32 devices in a mesh: parts: 2 (over x), cuts: 16 (over z, y, core).
Axes of the slice: x: 2, y: 2, z: 4, core: 2. Of those that a mesh axis runs over, the one named last changes fastest.
Arguments:
- objects: bfloat16 [32, 2, 384, 384], P(('parts', 'cuts')), parts along dimension 0, may hold values from -0.14941406 to 0.14941406
- propagators: bfloat16 [4, 2, 192, 192], replicated, may hold values from -1 to 1
- prop_index: int32 [32], P(('parts', 'cuts')), parts along dimension 0, may hold values from 0 to 3
- probes: bfloat16 [8, 2, 192, 192], replicated, may hold values from -6 to 6
- probe_group: int32 [6], replicated, may hold values from 0 to 7, as said below
- offsets: int32 [12, 2], P('parts'), parts along dimension 0, may hold values from 0 to 192
- measured: float32 [12, 192, 192], P('parts', 'cuts'), parts along dimension 0, may hold values from 0.3 to 4
Outputs:
- object_grad: float32 [32, 2, 384, 384], P(('parts', 'cuts')), parts along dimension 0
The draws below stay inside these ranges and needn't reach their ends.
There are 2 independent parts, one for each index of `parts`. The reference program is written for one: setup_inputs(seed, part) draws one part's arguments, and reference() takes and returns one part's arrays. A program takes and returns all parts, laid end to end along the dimension named above; an argument that names none is the same for every part. Nothing has to cross between parts.
Inputs may be any that keep to these rules, and one draw needn't show every extreme that they name: `probe_group`: within each run of 8 consecutive positions every group appears once.
All inputs are finite; a program needn't handle non-finite values.
Results may differ from the reference program's by a relative error of at most 0.035.
Values may be sent and summed in bfloat16 or wider, within the bound.
No kernel may reach another device: no remote copies, remote signals or barrier semaphores. Data moves between devices by JAX's collectives and lax.ppermute only.
A program may use at most 64 MiB of HBM per device.

```python
import math
import jax
import jax.numpy as jnp
from jax import lax

W = 192
OBJ = 384
POSITIONS = 6
GROUPS = 8
NPROP = 4
SLICES = 16


def draw_propagators(key, part):
    key = jax.random.fold_in(key, 7)
    angle_key, spread_key = jax.random.split(key)
    angle = jax.random.uniform(angle_key, (NPROP, W, W), jnp.float32, -math.pi, math.pi)
    spread = jax.random.normal(spread_key, (NPROP, 2, W, W), jnp.float32) * 0.0044
    diagonal = jnp.arange(W)[:, None] == jnp.arange(W)[None, :]
    real_part = jnp.where(diagonal[None], jnp.cos(angle), spread[:, 0])
    imag_part = jnp.where(diagonal[None], jnp.sin(angle), spread[:, 1])
    return jnp.stack([real_part, imag_part], axis=1).astype(jnp.bfloat16)


def draw_probe_group(key, part):
    key = jax.random.fold_in(key, 11)
    order = jax.random.permutation(key, GROUPS).astype(jnp.int32)
    slots = jnp.arange(POSITIONS, dtype=jnp.int32) % GROUPS
    return order[slots].astype(jnp.int32)


def set_ends(values, key, smallest, largest):
    longest = values.shape.index(max(values.shape))
    spots = []
    for shift in (0, 1):
        where = [jax.random.randint(jax.random.fold_in(key, axis), (), 0, length) for axis, length in enumerate(values.shape)]
        where[longest] = (where[longest] + shift) % values.shape[longest]
        spots.append(tuple(where))
    return values.at[spots[0]].set(smallest).at[spots[1]].set(largest)


def levels(key, dims, pieces, smallest, largest):
    gain = 1.0
    for dim, shards_of in pieces:
        draws = jax.random.uniform(jax.random.fold_in(jax.random.fold_in(key, 6), dim), (shards_of,), jnp.float32, smallest / len(pieces), largest / len(pieces))
        gain = gain * jnp.repeat(jnp.exp(draws), dims[dim] // shards_of).reshape((-1,) + (1,) * (len(dims) - 1 - dim))
    return gain


def scatter_about(own_key, shape, scale, limit, kind=jnp.bfloat16):
    return jnp.clip(scale * jax.random.normal(own_key, shape, jnp.float32), -limit, limit).astype(kind)


def setup_inputs(seed: int = 0, part: int = 0) -> dict:
    key_of = jax.random.split(jax.random.key(seed), 8)
    own_keys = jax.random.split(jax.random.fold_in(key_of[7], part), 8)
    return {
        "objects": jnp.clip(jax.random.uniform(own_keys[0], (SLICES, 2, OBJ, OBJ), jnp.float32, -0.14941406, 0.14941406) * levels(own_keys[0], (SLICES, 2, OBJ, OBJ), ((0, 16),), -0.4, 0.0), -0.14941406, 0.14941406).astype(jnp.bfloat16),
        "propagators": draw_propagators(jax.random.fold_in(key_of[7], 71), part),
        "prop_index": set_ends(jax.random.randint(own_keys[2], (SLICES,), 0, NPROP), jax.random.fold_in(own_keys[2], 1), 0, NPROP - 1).astype(jnp.int32),
        "probes": scatter_about(key_of[3], (GROUPS, 2, W, W), 1.0, 6.0),
        "probe_group": draw_probe_group(jax.random.fold_in(key_of[7], 71), part),
        "offsets": set_ends(jax.random.randint(own_keys[5], (POSITIONS, 2), 0, OBJ - W + 1), jax.random.fold_in(own_keys[5], 1), 0, OBJ - W).astype(jnp.int32),
        "measured": jnp.clip(jnp.exp(math.log(4.0) - 2.5902671 * jax.random.uniform(own_keys[6], (POSITIONS, W, W), jnp.float32) ** levels(own_keys[6], (POSITIONS, W, W), ((1, 16),), -0.2, 0.2)), 0.3, 4.0),
    }


TRANSMIT = 0.985

def plain_product(former, latter):
    return jnp.dot(former.astype(jnp.float32), latter.astype(jnp.float32), precision=lax.Precision.HIGHEST, preferred_element_type=jnp.float32)

def product_transposed(former, latter):
    return jnp.dot(former.astype(jnp.float32), latter.astype(jnp.float32).T, precision=lax.Precision.HIGHEST, preferred_element_type=jnp.float32)

def transposed_product(former, latter):
    return jnp.dot(former.astype(jnp.float32).T, latter.astype(jnp.float32), precision=lax.Precision.HIGHEST, preferred_element_type=jnp.float32)

def precise_product(former, latter):
    return jnp.dot(former, latter, precision=lax.Precision.HIGHEST, preferred_element_type=jnp.float32)

def dft_tables(wave_width):
    counter = jnp.arange(wave_width, dtype=jnp.int32)
    phase = counter[:, None] * counter[None, :] % wave_width
    angle = phase.astype(jnp.float32) * (2.0 * math.pi / wave_width)
    factor = 1.0 / math.sqrt(wave_width)
    return (jnp.cos(angle) * factor, -jnp.sin(angle) * factor)

def window_of(object_field, corner, wave_width):
    anchor = (jnp.zeros((), jnp.int32), corner[0].astype(jnp.int32), corner[1].astype(jnp.int32))
    window = lax.dynamic_slice(object_field, anchor, (2, wave_width, wave_width)).astype(jnp.float32)
    return (TRANSMIT + window[0], window[1])

def forward_slice(object_field, prop_pair, entering, corner):
    wave_width = entering.shape[-1]
    trans_real, trans_imag = window_of(object_field, corner, wave_width)
    wave_real = entering[0].astype(jnp.float32)
    wave_imag = entering[1].astype(jnp.float32)
    mixed_real = (trans_real * wave_real - trans_imag * wave_imag).astype(jnp.bfloat16)
    mixed_imag = (trans_real * wave_imag + trans_imag * wave_real).astype(jnp.bfloat16)
    prop_real = prop_pair[0]
    prop_imag = prop_pair[1]
    half_real = (plain_product(prop_real, mixed_real) - plain_product(prop_imag, mixed_imag)).astype(jnp.bfloat16)
    half_imag = (plain_product(prop_real, mixed_imag) + plain_product(prop_imag, mixed_real)).astype(jnp.bfloat16)
    out_real = product_transposed(half_real, prop_real) - product_transposed(half_imag, prop_imag)
    out_imag = product_transposed(half_real, prop_imag) + product_transposed(half_imag, prop_real)
    return jnp.stack([out_real, out_imag]).astype(jnp.bfloat16)

def detector(leaving, measured_here):
    wave_width = leaving.shape[-1]
    dft_real, dft_imag = dft_tables(wave_width)
    wave_real = leaving[0].astype(jnp.float32)
    wave_imag = leaving[1].astype(jnp.float32)
    near_real = precise_product(dft_real, wave_real) - precise_product(dft_imag, wave_imag)
    near_imag = precise_product(dft_real, wave_imag) + precise_product(dft_imag, wave_real)
    far_real = precise_product(near_real, dft_real) - precise_product(near_imag, dft_imag)
    far_imag = precise_product(near_real, dft_imag) + precise_product(near_imag, dft_real)
    misfit = far_real * far_real + far_imag * far_imag - measured_here
    push_real = misfit * far_real
    push_imag = misfit * far_imag
    back_real = precise_product(dft_real, push_real) + precise_product(dft_imag, push_imag)
    back_imag = precise_product(dft_real, push_imag) - precise_product(dft_imag, push_real)
    exit_real = precise_product(back_real, dft_real) + precise_product(back_imag, dft_imag)
    exit_imag = precise_product(back_imag, dft_real) - precise_product(back_real, dft_imag)
    return jnp.stack([exit_real, exit_imag]).astype(jnp.bfloat16)

def backward_slice(object_field, prop_pair, arriving, before, corner):
    wave_width = arriving.shape[-1]
    trans_real, trans_imag = window_of(object_field, corner, wave_width)
    prop_real = prop_pair[0]
    prop_imag = prop_pair[1]
    grad_real = arriving[0]
    grad_imag = arriving[1]
    back_real = (transposed_product(prop_real, grad_real) + transposed_product(prop_imag, grad_imag)).astype(jnp.bfloat16)
    back_imag = (transposed_product(prop_real, grad_imag) - transposed_product(prop_imag, grad_real)).astype(jnp.bfloat16)
    inner_real = plain_product(back_real, prop_real) + plain_product(back_imag, prop_imag)
    inner_imag = plain_product(back_imag, prop_real) - plain_product(back_real, prop_imag)
    before_real = before[0].astype(jnp.float32)
    before_imag = before[1].astype(jnp.float32)
    window_grad = jnp.stack([inner_real * before_real + inner_imag * before_imag, inner_imag * before_real - inner_real * before_imag])
    passed = jnp.stack([trans_real * inner_real + trans_imag * inner_imag, trans_real * inner_imag - trans_imag * inner_real]).astype(jnp.bfloat16)
    return (window_grad, passed)

def add_window(accumulated, window_grad, corner):
    anchor = (jnp.zeros((), jnp.int32), corner[0].astype(jnp.int32), corner[1].astype(jnp.int32))
    current = lax.dynamic_slice(accumulated, anchor, window_grad.shape)
    return lax.dynamic_update_slice(accumulated, current + window_grad, anchor)

def reference(objects, propagators, prop_index, probes, probe_group, offsets, measured):
    chosen = propagators[prop_index]
    starting = probes[probe_group]

    def forward_step(waves, slab):
        object_field, prop_pair = slab
        leaving = jax.vmap(forward_slice, (None, None, 0, 0))(object_field, prop_pair, waves, offsets)
        return (leaving, waves)
    final_waves, entering = lax.scan(forward_step, starting, (objects, chosen))
    exits = jax.vmap(detector)(final_waves, measured)

    def backward_step(grads, slab):
        object_field, prop_pair, before = slab
        window_grads, passed = jax.vmap(backward_slice, (None, None, 0, 0, 0))(object_field, prop_pair, grads, before, offsets)
        accumulated = jnp.zeros(object_field.shape, jnp.float32)
        for position in range(POSITIONS):
            accumulated = add_window(accumulated, window_grads[position], offsets[position])
        return (passed, accumulated)
    leftover, object_grad = lax.scan(backward_step, exits, (objects, chosen, entering), reverse=True)
    return object_grad
```

```python
import math

import jax
import jax.numpy as jnp
import ml_dtypes
import numpy as np
from jax import lax
from jax.experimental import pallas as pl
from jax.experimental.pallas import tpu as pltpu
from jax.sharding import PartitionSpec as P

TRANSMIT = 0.985
GROUP = 16
LANES = 128
ROWS = 16
F32 = jnp.float32
BF16 = jnp.bfloat16


def dot(former, latter):
    return jnp.dot(former, latter, preferred_element_type=F32)


def halves(x):
    return x[:, :LANES], x[:, LANES : 2 * LANES], x[:, 2 * LANES :]


def swapped(tail):
    return pltpu.roll(tail, LANES // 2, 1)


def low_half(rows):
    return lax.broadcasted_iota(jnp.int32, (rows, LANES), 1) < LANES // 2


def spread(tail):
    other = swapped(tail)
    low = low_half(tail.shape[0])
    return jnp.where(low, tail, other), jnp.where(low, other, tail)


def signed(tail, minus_low):
    low = low_half(tail.shape[0])
    return jnp.where(low == minus_low, -tail, tail)


def times(a, b):
    a0, a1, at = halves(a)
    b0, b1, bt = halves(b)
    b_real, b_imag = spread(bt)
    tail = at * b_real + signed(swapped(at), True) * b_imag
    return jnp.concatenate([a0 * b0 - a1 * b1, a1 * b0 + a0 * b1, tail], axis=1)


def times_conj(a, *others):
    a0, a1, at = halves(a)
    turned = signed(swapped(at), False)
    results = []
    for b in others:
        b0, b1, bt = halves(b)
        b_real, b_imag = spread(bt)
        tail = at * b_real + turned * b_imag
        results.append(jnp.concatenate([a0 * b0 + a1 * b1, a1 * b0 - a0 * b1, tail], axis=1))
    return results


def joined(both, conj):
    width = both.shape[0] // 2
    u0, u1, ut = halves(both[:width])
    v0, v1, vt = halves(both[width:])
    turned = signed(swapped(vt), not conj)
    if conj:
        return jnp.concatenate([u0 + v1, u1 - v0, ut + turned], axis=1)
    return jnp.concatenate([u0 - v1, u1 + v0, ut + turned], axis=1)


def with_mean(window):
    x = window.astype(F32)
    x0, x1, xt = halves(x)
    mean = jnp.where(low_half(xt.shape[0]), TRANSMIT, 0.0)
    return jnp.concatenate([TRANSMIT + x0, x1, mean + xt], axis=1)


def split2(x):
    high = x.astype(BF16)
    return high, (x - high.astype(F32)).astype(BF16)


def picker(columns, start, high_tail, transposed=False):
    shape = (2 * LANES, columns) if transposed else (columns, 2 * LANES)
    a = lax.broadcasted_iota(jnp.int32, shape, 1 if transposed else 0) - start
    q = lax.broadcasted_iota(jnp.int32, shape, 0 if transposed else 1)
    if high_tail:
        half = LANES // 2
        wanted = jnp.where(q < LANES, q, jnp.where(q < LANES + half, -columns, q - half))
    else:
        wanted = jnp.where(q < LANES + LANES // 2, q, -columns)
    return jnp.where(a == wanted, 1.0, 0.0).astype(BF16)


def row_picker(shape, distance):
    taken = lax.broadcasted_iota(jnp.int32, shape, 1)
    wanted = lax.broadcasted_iota(jnp.int32, shape, 0) + distance
    return jnp.where(taken == wanted, 1.0, 0.0).astype(BF16)


def packed(real, imag, columns, start):
    left = dot(real, picker(columns, start, False))
    right = dot(imag, picker(columns, start, True))
    return jnp.concatenate(
        [left[:, :LANES], right[:, :LANES], left[:, LANES:] + right[:, LANES:]], axis=1
    )


def dft_constants(width):
    counter = np.arange(width)
    angle = (counter[:, None] * counter[None, :] % width) * (2.0 * math.pi / width)
    real = np.cos(angle) / math.sqrt(width)
    imag = -np.sin(angle) / math.sqrt(width)
    order = np.concatenate(
        [
            np.arange(LANES),
            width + np.arange(LANES),
            np.arange(LANES, width),
            width + np.arange(LANES, width),
        ]
    )

    def right(mr, mi):
        full = np.block([[mr, mi], [-mi, mr]])
        return full[order][:, order]

    tables = []
    for table in (np.concatenate([real, imag]), right(real, imag), right(real, -imag)):
        high = table.astype(np.float32).astype(ml_dtypes.bfloat16)
        low = (table - high.astype(np.float64)).astype(np.float32).astype(ml_dtypes.bfloat16)
        tables += [high, low]
    return tables


def window_kernel(
    offsets_ref, index_ref, objects_ref, measured_ref, props_ref, blocks_ref, lb_ref, rf_ref, rb_ref
):
    positions, near_rows, width = measured_ref.shape
    extent = objects_ref.shape[-1]
    tag = jnp.full((ROWS, LANES), index_ref[0], jnp.int32).astype(F32).astype(BF16)
    lane = lax.broadcasted_iota(jnp.int32, (width, 2 * LANES), 0)
    spot = lax.broadcasted_iota(jnp.int32, (width, 2 * LANES), 1)
    doubled = jnp.where(lane == jnp.where(spot < LANES + LANES // 2, spot, spot - LANES // 2), 1.0, 0.0).astype(BF16)
    blank = jnp.zeros((ROWS - near_rows, width), F32)
    starts = [offsets_ref[p, 0] for p in range(positions)]
    rows = jnp.concatenate([row_picker((width, extent), start) for start in starts], axis=0)
    real, imag = (dot(rows, objects_ref[0, c]).astype(BF16) for c in range(2))
    for p in range(positions):
        here = slice(p * width, (p + 1) * width)
        window = packed(real[here], imag[here], extent, offsets_ref[p, 1])
        blocks_ref[p, :width, :] = window.astype(BF16)
        high, low = split2(jnp.concatenate([measured_ref[p], blank], axis=0))
        for place, part in ((width, high), (width + ROWS, low)):
            blocks_ref[p, place : place + ROWS, : 2 * LANES] = dot(part, doubled).astype(BF16)
            blocks_ref[p, place : place + ROWS, 2 * LANES :] = tag
    for k in range(props_ref.shape[0]):
        real, imag = props_ref[k, 0], props_ref[k, 1]
        lb_ref[k, :width, :] = real.astype(F32).T.astype(BF16)
        lb_ref[k, width:, :] = imag.astype(F32).T.astype(BF16)
        upper = packed(real, -imag, width, 0)
        lower = packed(imag, real, width, 0)
        table = jnp.concatenate(
            [upper[:LANES], lower[:LANES], upper[LANES:], lower[LANES:]], axis=0
        )
        rb_ref[k] = table.astype(BF16)
        rf_ref[k] = table.T.astype(BF16)


def forward_steps(blocks, waves, indices, lf, rf, first, last_out):
    width = blocks.shape[2] // 2
    sections = blocks.shape[0]

    def step(k, carried):
        which = indices[k]
        z = times(waves[k].astype(F32), with_mean(blocks[k, :width, :])).astype(BF16)
        left = lf[which].reshape(2 * width, width)
        h = joined(dot(left, z), False).astype(BF16)
        waves[k + 1] = dot(h, rf[which]).astype(BF16)
        return carried

    lax.fori_loop(0, sections, step, 0)


def backward_steps(blocks, waves, indices, lb, rb, grads, g):
    width = blocks.shape[2] // 2
    sections = blocks.shape[0]

    def step(n, carried):
        k = sections - 1 - n
        which = indices[k]
        c = joined(dot(lb[which], g[...]), True).astype(BF16)
        y = dot(c, rb[which])
        grad, passed = times_conj(y, waves[k].astype(F32), with_mean(blocks[k, :width, :]))
        grads[k] = grad.astype(BF16)
        g[...] = passed.astype(BF16)
        return carried

    lax.fori_loop(0, sections, step, 0)


def detector(psi, observed, lh, ll, rh, rl, ch, cl):
    def product(ah, al, bh, bl):
        return dot(ah, bh) + (dot(ah, bl) + dot(al, bh))

    near = joined(dot(lh, psi) + dot(ll, psi), False)
    nh, nl = split2(near)
    far = product(nh, nl, rh, rl)
    f0, f1, ft = halves(far)
    other = swapped(ft)
    main = f0 * f0 + f1 * f1 - observed[:, :LANES]
    tail = ft * ft + other * other - observed[:, LANES:]
    push = jnp.concatenate([main * f0, main * f1, tail * ft], axis=1)
    ph, pl_ = split2(push)
    back = joined(product(lh, ll, ph, pl_), True)
    bh, bl = split2(back)
    return product(bh, bl, ch, cl).astype(BF16)


def read_indices(blocks, indices, count):
    width = blocks.shape[2] // 2
    for k in range(blocks.shape[0]):
        tag = jnp.max(blocks[k, width : width + ROWS, 2 * LANES :].astype(F32))
        indices[k] = jnp.clip(tag.astype(jnp.int32), 0, count - 1)


def chain_kernel(near_rows):
    def kernel(
        who, group_ref, probes, blocks, lf, rf, lb, rb, lh, ll, rh, rl, ch, cl,
        grads, waves, g, observed, indices,
    ):
        width = blocks.shape[2] // 2
        sections = blocks.shape[0]
        probe = group_ref[who[0]]
        real, imag = probes[probe, 0], probes[probe, 1]
        waves[0] = packed(real, imag, width, 0).astype(BF16)
        read_indices(blocks, indices, lf.shape[0])
        for k in range(sections):
            high = blocks[k, width : width + ROWS, : 2 * LANES].astype(F32)
            low = blocks[k, width + ROWS : width + 2 * ROWS, : 2 * LANES].astype(F32)
            observed[k * near_rows : (k + 1) * near_rows, :] = (high + low)[:near_rows]
        forward_steps(blocks, waves, indices, lf, rf, None, None)
        g[...] = detector(
            waves[sections], observed[...], lh[...], ll[...], rh[...], rl[...], ch[...], cl[...]
        )
        backward_steps(blocks, waves, indices, lb, rb, grads, g)

    return kernel


def gather_kernel(offsets_ref, grads_ref, out_ref):
    positions = offsets_ref.shape[0]
    width = grads_ref.shape[1]
    extent = out_ref.shape[-1]
    spread_out = [[], []]
    for p in range(positions):
        x0, x1, xt = halves(grads_ref[p])
        for c, main in ((0, x0), (1, x1)):
            wide = jnp.concatenate([main, xt], axis=1)
            columns = picker(extent, offsets_ref[p, 1], c == 1, transposed=True)
            spread_out[c].append(dot(wide, columns).astype(BF16))
    rows = jnp.concatenate(
        [row_picker((extent, width), -offsets_ref[p, 0]) for p in range(positions)], axis=1
    )
    for c in range(2):
        out_ref[0, c] = dot(rows, jnp.concatenate(spread_out[c], axis=0))


VMEM = pl.BlockSpec(memory_space=pltpu.VMEM)
SMEM = pl.BlockSpec(memory_space=pltpu.SMEM)
PARAMS = pltpu.CompilerParams(vmem_limit_bytes=48 * 1024 * 1024)


def shards(objects, propagators, prop_index, probes, probe_group, offsets, measured):
    sections = lax.axis_size("cuts")
    rank = lax.axis_index("cuts")
    positions = probe_group.shape[0]
    width = probes.shape[-1]
    kinds = propagators.shape[0]
    near_rows = measured.shape[1]
    size = sections
    rows = width + 2 * ROWS

    blocks, lb, rf, rb = pl.pallas_call(
        window_kernel,
        out_shape=[
            jax.ShapeDtypeStruct((size, rows, 2 * width), BF16),
            jax.ShapeDtypeStruct((kinds, 2 * width, width), BF16),
            jax.ShapeDtypeStruct((kinds, 2 * width, 2 * width), BF16),
            jax.ShapeDtypeStruct((kinds, 2 * width, 2 * width), BF16),
        ],
        in_specs=[SMEM, SMEM, VMEM, VMEM, VMEM],
        out_specs=[VMEM] * 4,
        compiler_params=PARAMS,
        name="windows",
    )(offsets, prop_index, objects, measured, propagators)

    blocks = lax.all_to_all(blocks, "cuts", 0, 0, tiled=True)

    slot = jnp.minimum(rank, positions - 1).astype(jnp.int32)[None]
    constants = [jnp.asarray(table) for table in dft_constants(width)]
    grads = pl.pallas_call(
        chain_kernel(near_rows),
        out_shape=jax.ShapeDtypeStruct((size, width, 2 * width), BF16),
        in_specs=[SMEM, SMEM] + [VMEM] * 12,
        out_specs=VMEM,
        scratch_shapes=[
            pltpu.VMEM((size + 1, width, 2 * width), BF16),
            pltpu.VMEM((width, 2 * width), BF16),
            pltpu.VMEM((width, 2 * LANES), F32),
            pltpu.SMEM((size,), jnp.int32),
        ],
        compiler_params=PARAMS,
        name="chain",
    )(slot, probe_group, probes, blocks, propagators, rf, lb, rb, *constants)

    grads = lax.all_to_all(grads, "cuts", 0, 0, tiled=True)

    return pl.pallas_call(
        gather_kernel,
        out_shape=jax.ShapeDtypeStruct(objects.shape, F32),
        in_specs=[SMEM, VMEM],
        out_specs=VMEM,
        compiler_params=PARAMS,
        name="sum_windows",
    )(offsets, grads)


def solution(mesh):
    in_specs = (
        P(("parts", "cuts"), None, None, None),
        P(),
        P(("parts", "cuts")),
        P(),
        P(),
        P("parts", None),
        P("parts", "cuts", None),
    )
    out_specs = P(("parts", "cuts"), None, None, None)
    return jax.shard_map(shards, mesh=mesh, in_specs=in_specs, out_specs=out_specs, check_vma=False)
```

```python
import math

import jax
import jax.numpy as jnp
import ml_dtypes
import numpy as np
from jax import lax
from jax.experimental import pallas as pl
from jax.experimental.pallas import tpu as pltpu
from jax.sharding import PartitionSpec as P

TRANSMIT = 0.985
GROUP = 8
LANES = 128
ROWS = 16
F32 = jnp.float32
BF16 = jnp.bfloat16


def dot(former, latter):
    return jnp.dot(former, latter, preferred_element_type=F32)


def halves(x):
    return x[:, :LANES], x[:, LANES : 2 * LANES], x[:, 2 * LANES :]


def swapped(tail):
    return pltpu.roll(tail, LANES // 2, 1)


def low_half(rows):
    return lax.broadcasted_iota(jnp.int32, (rows, LANES), 1) < LANES // 2


def spread(tail):
    other = swapped(tail)
    low = low_half(tail.shape[0])
    return jnp.where(low, tail, other), jnp.where(low, other, tail)


def signed(tail, minus_low):
    low = low_half(tail.shape[0])
    return jnp.where(low == minus_low, -tail, tail)


def times(a, b):
    a0, a1, at = halves(a)
    b0, b1, bt = halves(b)
    b_real, b_imag = spread(bt)
    tail = at * b_real + signed(swapped(at), True) * b_imag
    return jnp.concatenate([a0 * b0 - a1 * b1, a1 * b0 + a0 * b1, tail], axis=1)


def times_conj(a, *others):
    a0, a1, at = halves(a)
    turned = signed(swapped(at), False)
    results = []
    for b in others:
        b0, b1, bt = halves(b)
        b_real, b_imag = spread(bt)
        tail = at * b_real + turned * b_imag
        results.append(jnp.concatenate([a0 * b0 + a1 * b1, a1 * b0 - a0 * b1, tail], axis=1))
    return results


def joined(both, conj):
    width = both.shape[0] // 2
    u0, u1, ut = halves(both[:width])
    v0, v1, vt = halves(both[width:])
    turned = signed(swapped(vt), not conj)
    if conj:
        return jnp.concatenate([u0 + v1, u1 - v0, ut + turned], axis=1)
    return jnp.concatenate([u0 - v1, u1 + v0, ut + turned], axis=1)


def with_mean(window):
    x = window.astype(F32)
    x0, x1, xt = halves(x)
    mean = jnp.where(low_half(xt.shape[0]), TRANSMIT, 0.0)
    return jnp.concatenate([TRANSMIT + x0, x1, mean + xt], axis=1)


def split2(x):
    high = x.astype(BF16)
    return high, (x - high.astype(F32)).astype(BF16)


def picker(columns, start, high_tail, transposed=False):
    shape = (2 * LANES, columns) if transposed else (columns, 2 * LANES)
    a = lax.broadcasted_iota(jnp.int32, shape, 1 if transposed else 0) - start
    q = lax.broadcasted_iota(jnp.int32, shape, 0 if transposed else 1)
    if high_tail:
        half = LANES // 2
        wanted = jnp.where(q < LANES, q, jnp.where(q < LANES + half, -columns, q - half))
    else:
        wanted = jnp.where(q < LANES + LANES // 2, q, -columns)
    return jnp.where(a == wanted, 1.0, 0.0).astype(BF16)


def row_picker(shape, distance):
    taken = lax.broadcasted_iota(jnp.int32, shape, 1)
    wanted = lax.broadcasted_iota(jnp.int32, shape, 0) + distance
    return jnp.where(taken == wanted, 1.0, 0.0).astype(BF16)


def packed(real, imag, columns, start):
    left = dot(real, picker(columns, start, False))
    right = dot(imag, picker(columns, start, True))
    return jnp.concatenate(
        [left[:, :LANES], right[:, :LANES], left[:, LANES:] + right[:, LANES:]], axis=1
    )


def dft_constants(width):
    counter = np.arange(width)
    angle = (counter[:, None] * counter[None, :] % width) * (2.0 * math.pi / width)
    real = np.cos(angle) / math.sqrt(width)
    imag = -np.sin(angle) / math.sqrt(width)
    order = np.concatenate(
        [
            np.arange(LANES),
            width + np.arange(LANES),
            np.arange(LANES, width),
            width + np.arange(LANES, width),
        ]
    )

    def right(mr, mi):
        full = np.block([[mr, mi], [-mi, mr]])
        return full[order][:, order]

    tables = []
    for table in (np.concatenate([real, imag]), right(real, imag), right(real, -imag)):
        high = table.astype(np.float32).astype(ml_dtypes.bfloat16)
        low = (table - high.astype(np.float64)).astype(np.float32).astype(ml_dtypes.bfloat16)
        tables += [high, low]
    return tables


def window_kernel(offsets_ref, index_ref, targets_ref, objects_ref, *blocks):
    extent = objects_ref.shape[-1]
    width = blocks[0].shape[1] // 2
    tag = jnp.full((ROWS, 2 * width), index_ref[0], jnp.int32).astype(F32).astype(BF16)
    for r, block in enumerate(blocks):
        p = targets_ref[r]

        @pl.when(p >= 0)
        def _(block=block, p=p):
            rows = row_picker((width, extent), offsets_ref[p, 0])
            real, imag = (dot(rows, objects_ref[0, c]).astype(BF16) for c in range(2))
            block[:width, :] = packed(real, imag, extent, offsets_ref[p, 1]).astype(BF16)
            block[width:, :] = tag


def doubled(rows):
    tail = jnp.concatenate([rows[:, LANES:]] * 2, axis=1)
    return jnp.concatenate([rows[:, :LANES], tail], axis=1)


def table_kernel(props_ref, lb_ref, rf_ref, rb_ref):
    width = props_ref.shape[-1]
    for k in range(props_ref.shape[0]):
        real, imag = props_ref[k, 0], props_ref[k, 1]
        lb_ref[k, :width, :] = real.astype(F32).T.astype(BF16)
        lb_ref[k, width:, :] = imag.astype(F32).T.astype(BF16)
        upper = packed(real, -imag, width, 0)
        lower = packed(imag, real, width, 0)
        table = jnp.concatenate(
            [upper[:LANES], lower[:LANES], upper[LANES:], lower[LANES:]], axis=0
        )
        rb_ref[k] = table.astype(BF16)
        rf_ref[k] = table.T.astype(BF16)


def forward_steps(blocks, waves, indices, lf, rf, arrived):
    sections, _, columns = blocks.shape
    width = columns // 2

    def step(k, carried):
        arrived(k)
        which = indices[k]
        z = times(waves[k].astype(F32), with_mean(blocks[k, :width, :])).astype(BF16)
        h = joined(dot(lf[which].reshape(columns, width), z), False).astype(BF16)
        waves[k + 1] = dot(h, rf[which]).astype(BF16)
        return carried

    lax.fori_loop(0, sections, step, 0)


def backward_steps(blocks, waves, indices, lb, rb, grads, g):
    sections, _, columns = blocks.shape
    width = columns // 2

    def step(n, carried):
        k = sections - 1 - n
        which = indices[k]
        c = joined(dot(lb[which], g[...]), True).astype(BF16)
        y = dot(c, rb[which])
        grad, passed = times_conj(y, waves[k].astype(F32), with_mean(blocks[k, :width, :]))
        grads[k] = grad.astype(BF16)
        g[...] = passed.astype(BF16)
        return carried

    lax.fori_loop(0, sections, step, 0)


def detector(psi, observed, lh, ll, rh, rl, ch, cl):
    def product(ah, al, bh, bl):
        return dot(ah, bh) + (dot(ah, bl) + dot(al, bh))

    near = joined(dot(lh, psi) + dot(ll, psi), False)
    nh, nl = split2(near)
    far = product(nh, nl, rh, rl)
    f0, f1, ft = halves(far)
    other = swapped(ft)
    main = f0 * f0 + f1 * f1 - observed[:, :LANES]
    tail = ft * ft + other * other - observed[:, LANES:]
    push = jnp.concatenate([main * f0, main * f1, tail * ft], axis=1)
    ph, pl_ = split2(push)
    back = joined(product(lh, ll, ph, pl_), True)
    bh, bl = split2(back)
    return product(bh, bl, ch, cl).astype(BF16)


def read_index(blocks, indices, k, count):
    width = blocks.shape[2] // 2
    tag = jnp.max(blocks[k, width:, :LANES].astype(F32))
    indices[k] = jnp.clip(tag.astype(jnp.int32), 0, count - 1)


def block_copies(blocks_in, order, blocks, sems):
    return [
        pltpu.make_async_copy(block, blocks.at[order[r]], sems.at[order[r]])
        for r, block in enumerate(blocks_in)
    ]


def forward_kernel(size, kept):
    def kernel(who, group_ref, order, probes, entering, lf_in, rf_in, *rest):
        blocks_in, rest = rest[:size], rest[size:]
        if kept:
            rest = rest[1:]
        leaving, waves_out, blocks, waves, lf, rf, probe, indices, block_sems, sems = rest
        columns = blocks.shape[2]

        @pl.when(who[2] > 0)
        def _():
            copies = block_copies(blocks_in, order, blocks, block_sems)
            tables = [
                pltpu.make_async_copy(lf_in, lf, sems.at[0]),
                pltpu.make_async_copy(rf_in, rf, sems.at[1]),
            ]
            for copy in tables + copies:
                copy.start()
            start_wave(who, group_ref, probes, entering, waves, probe, sems.at[2])
            for copy in tables:
                copy.wait()

            def arrived(k):
                pltpu.make_async_copy(blocks_in[0], blocks.at[k], block_sems.at[k]).wait()
                read_index(blocks, indices, k, lf.shape[0])

            forward_steps(blocks, waves, indices, lf, rf, arrived)
            leaving[...] = waves[size]
            keep = pltpu.make_async_copy(waves.at[pl.ds(0, size)], waves_out, sems.at[3])
            keep.start()
            keep.wait()

    return kernel


def start_wave(who, group_ref, probes, entering, waves, probe, sem):
    width = waves.shape[1]

    @pl.when(who[1] > 0)
    def _():
        copy = pltpu.make_async_copy(probes.at[group_ref[who[0]]], probe, sem)
        copy.start()
        copy.wait()
        waves[0] = packed(probe[0], probe[1], width, 0).astype(BF16)

    @pl.when(who[1] == 0)
    def _():
        copy = pltpu.make_async_copy(entering, waves.at[0], sem)
        copy.start()
        copy.wait()


def send_out(grads, order, grads_out, sems):
    copies = [
        pltpu.make_async_copy(grads.at[order[r]], out, sems.at[r]) for r, out in enumerate(grads_out)
    ]
    for copy in copies:
        copy.start()
    for copy in copies:
        copy.wait()


def middle_kernel(size, near_rows):
    def kernel(who, group_ref, order, out_order, probes, entering, lf_in, rf_in, lb_in, rb_in, *rest):
        constants_in, rest = rest[:6], rest[6:]
        measured, rest = rest[0], rest[1:]
        blocks_in, rest = rest[:size], rest[size:]
        leaving, grads_out, rest = rest[0], rest[1 : 1 + size], rest[1 + size :]
        blocks, waves, grads, lf, rf, lb, rb, probe, g, gathered, observed, indices = rest[:12]
        constants, block_sems, sems = rest[12:18], rest[18], rest[19]
        width, columns = waves.shape[1:]

        @pl.when(who[2] > 0)
        def _():
            copies = block_copies(blocks_in, order, blocks, block_sems)
            tables = [
                pltpu.make_async_copy(source, target, sems.at[n])
                for n, (source, target) in enumerate(
                    [(lf_in, lf), (rf_in, rf), (lb_in, lb), (rb_in, rb)]
                    + list(zip(constants_in, constants))
                )
            ]
            seen = pltpu.make_async_copy(measured.at[who[0]], gathered, sems.at[10])
            for copy in tables[:2] + copies + [seen] + tables[2:]:
                copy.start()
            start_wave(who, group_ref, probes, entering, waves, probe, sems.at[11])
            for copy in tables[:2]:
                copy.wait()

            def arrived(k):
                pltpu.make_async_copy(blocks_in[0], blocks.at[k], block_sems.at[k]).wait()
                read_index(blocks, indices, k, lf.shape[0])

            forward_steps(blocks, waves, indices, lf, rf, arrived)
            for copy in [seen] + tables[2:]:
                copy.wait()
            for n in range(gathered.shape[0]):
                observed[n * near_rows : (n + 1) * near_rows, :] = gathered[n]
            g[...] = detector(waves[size], doubled(observed[...]), *[table[...] for table in constants])
            backward_steps(blocks, waves, indices, lb, rb, grads, g)
            leaving[...] = g[...]
            send_out(grads, out_order, grads_out, block_sems)

    return kernel


def backward_kernel(size):
    def kernel(who, order, out_order, arriving, waves_in, lb_in, rb_in, *rest):
        blocks_in, rest = rest[:size], rest[2 * size :]
        leaving, grads_out, rest = rest[0], rest[1 : 1 + size], rest[1 + size :]
        blocks, waves, grads, lb, rb, g, indices, block_sems, sems = rest

        @pl.when(who[2] > 0)
        def _():
            copies = block_copies(blocks_in, order, blocks, block_sems)
            copies += [
                pltpu.make_async_copy(source, target, sems.at[n])
                for n, (source, target) in enumerate(
                    [(arriving, g), (waves_in, waves), (lb_in, lb), (rb_in, rb)]
                )
            ]
            for copy in copies:
                copy.start()
            for copy in copies:
                copy.wait()
            for k in range(size):
                read_index(blocks, indices, k, lb.shape[0])
            backward_steps(blocks, waves, indices, lb, rb, grads, g)
            leaving[...] = g[...]
            send_out(grads, out_order, grads_out, block_sems)

    return kernel


def gather_kernel(offsets_ref, sources_ref, *rest):
    grads_in, (out_ref, grads, sems) = rest[:-3], rest[-3:]
    positions = offsets_ref.shape[0]
    width = grads.shape[1]
    extent = out_ref.shape[-1]
    for r, block in enumerate(grads_in):
        p = sources_ref[r]

        @pl.when(p >= 0)
        def _(block=block, p=p, r=r):
            pltpu.make_async_copy(block, grads.at[p], sems.at[p]).start()

    rows = jnp.concatenate(
        [row_picker((extent, width), -offsets_ref[p, 0]) for p in range(positions)], axis=1
    )
    spread_out = [[], []]
    for p in range(positions):
        pltpu.make_async_copy(grads_in[0], grads.at[p], sems.at[p]).wait()
        x0, x1, xt = halves(grads[p])
        for c, main in ((0, x0), (1, x1)):
            wide = jnp.concatenate([main, xt], axis=1)
            columns = picker(extent, offsets_ref[p, 1], c == 1, transposed=True)
            spread_out[c].append(dot(wide, columns).astype(BF16))
    for c in range(2):
        out_ref[0, c] = dot(rows, jnp.concatenate(spread_out[c], axis=0))


VMEM = pl.BlockSpec(memory_space=pltpu.VMEM)
SMEM = pl.BlockSpec(memory_space=pltpu.SMEM)
HBM = pl.BlockSpec(memory_space=pl.ANY)
PARAMS = pltpu.CompilerParams(vmem_limit_bytes=56 * 1024 * 1024)


def positions_of_slots(size, positions):
    chips = size // 2
    inward = sorted(range(chips), key=lambda chip: bin(chip).count("1") % 2)
    slots = [2 * chip for chip in inward] + [2 * chip + 1 for chip in inward]
    held = [-1] * size
    for position, slot in enumerate(sorted(slots[:positions])):
        held[slot] = position
    return held


def shards(objects, propagators, prop_index, probes, probe_group, offsets, measured):
    sections = lax.axis_size("cuts")
    rank = lax.axis_index("cuts").astype(jnp.int32)
    positions = probe_group.shape[0]
    width = probes.shape[-1]
    kinds = propagators.shape[0]
    near_rows = measured.shape[1]
    size = GROUP
    groups = sections // size
    rows = width + ROWS
    held = positions_of_slots(size, positions)
    slot, group = rank % size, rank // size
    rounds = np.arange(size)
    held_here = jnp.asarray(np.array(held, np.int32))
    ahead = (slot + rounds) % size
    behind = (slot - rounds) % size
    targets = held_here[ahead]
    sources = held_here[behind]
    place = jnp.maximum(held_here[slot], 0)

    def who(stage):
        return jnp.stack([place, (group == 0).astype(jnp.int32), (group == stage).astype(jnp.int32)])

    def struct(*dims, kind=BF16):
        return jax.ShapeDtypeStruct(dims, kind)

    def across(block, r, inward):
        pairs = []
        for first in range(0, sections, size):
            for l in range(size):
                other = (l + r) % size
                if held[other if inward else l] >= 0:
                    pairs.append((first + l, first + other))
        return lax.ppermute(block, "cuts", pairs)

    def between(block, stage, distance):
        return lax.ppermute(
            block,
            "cuts",
            [(stage * size + l, (stage + distance) * size + l) for l in range(size) if held[l] >= 0],
        )

    gathered = lax.all_gather(measured, "cuts", axis=1, tiled=False)

    cut = pl.pallas_call(
        window_kernel,
        out_shape=[struct(rows, 2 * width)] * size,
        in_specs=[SMEM, SMEM, SMEM, VMEM],
        out_specs=[VMEM] * size,
        compiler_params=PARAMS,
        name="windows",
    )(offsets, prop_index, targets, objects)
    blocks = [cut[0]] + [across(cut[r], r, True) for r in range(1, size)]

    lb, rf, rb = pl.pallas_call(
        table_kernel,
        out_shape=[
            struct(kinds, 2 * width, width),
            struct(kinds, 2 * width, 2 * width),
            struct(kinds, 2 * width, 2 * width),
        ],
        in_specs=[VMEM],
        out_specs=[VMEM] * 3,
        compiler_params=PARAMS,
        cost_estimate=pl.CostEstimate(flops=10**9, bytes_accessed=4 * 10**6, transcendentals=0),
        name="tables",
    )(propagators)
    lf = propagators

    wave = (width, 2 * width)
    block_scratch = pltpu.VMEM((size, rows, 2 * width), BF16)
    waves_scratch = pltpu.VMEM((size + 1,) + wave, BF16)
    grads_scratch = pltpu.VMEM((size,) + wave, BF16)
    probe_scratch = pltpu.VMEM(probes.shape[1:], BF16)
    indices = pltpu.SMEM((size,), jnp.int32)

    def like(*arrays):
        return [pltpu.VMEM(array.shape, array.dtype) for array in arrays]

    entering, waves = jnp.zeros(wave, BF16), None
    for stage in range(groups - 1):
        kept = waves is not None
        leaving, waves = pl.pallas_call(
            forward_kernel(size, kept),
            out_shape=[struct(*wave), struct(size, *wave)],
            in_specs=[SMEM] * 3 + [HBM] * (4 + size + kept),
            out_specs=[VMEM, HBM],
            scratch_shapes=[block_scratch, waves_scratch]
            + like(lf, rf)
            + [probe_scratch, indices, pltpu.SemaphoreType.DMA((size,)), pltpu.SemaphoreType.DMA((4,))],
            input_output_aliases={7 + size: 1} if kept else {},
            compiler_params=PARAMS,
            name="forward",
        )(who(stage), probe_group, behind, probes, entering, lf, rf, *blocks, *([waves] if kept else []))
        entering = between(leaving, stage, 1)

    constants = [jnp.asarray(table) for table in dft_constants(width)]
    results = pl.pallas_call(
        middle_kernel(size, near_rows),
        out_shape=[struct(*wave)] * (1 + size),
        in_specs=[SMEM] * 4 + [HBM] * (13 + size),
        out_specs=[VMEM] + [HBM] * size,
        scratch_shapes=[block_scratch, waves_scratch, grads_scratch]
        + like(lf, rf, lb, rb)
        + [
            probe_scratch,
            pltpu.VMEM(wave, BF16),
            pltpu.VMEM(gathered.shape[1:], F32),
            pltpu.VMEM((width, width), F32),
            indices,
        ]
        + like(*constants)
        + [pltpu.SemaphoreType.DMA((size,)), pltpu.SemaphoreType.DMA((12,))],
        compiler_params=PARAMS,
        name="middle",
    )(
        who(groups - 1), probe_group, behind, ahead, probes, entering, lf, rf, lb, rb, *constants, gathered, *blocks
    )
    leaving, grads = results[0], results[1:]

    for stage in range(groups - 2, -1, -1):
        arriving = between(leaving, stage + 1, -1)
        results = pl.pallas_call(
            backward_kernel(size),
            out_shape=[struct(*wave)] * (1 + size),
            in_specs=[SMEM] * 3 + [HBM] * (4 + 2 * size),
            out_specs=[VMEM] + [HBM] * size,
            scratch_shapes=[block_scratch, pltpu.VMEM((size,) + wave, BF16), grads_scratch]
            + like(lb, rb)
            + [pltpu.VMEM(wave, BF16), indices, pltpu.SemaphoreType.DMA((size,)), pltpu.SemaphoreType.DMA((4,))],
            input_output_aliases={7 + size + r: 1 + r for r in range(size)},
            compiler_params=PARAMS,
            name="backward",
        )(who(stage), behind, ahead, arriving, waves, lb, rb, *blocks, *grads)
        leaving, grads = results[0], results[1:]

    grads = [grads[0]] + [across(grads[r], r, False) for r in range(1, size)]

    return pl.pallas_call(
        gather_kernel,
        out_shape=jax.ShapeDtypeStruct(objects.shape, F32),
        in_specs=[SMEM, SMEM] + [HBM] * size,
        out_specs=VMEM,
        scratch_shapes=[pltpu.VMEM((positions,) + wave, BF16), pltpu.SemaphoreType.DMA((positions,))],
        compiler_params=PARAMS,
        name="sum_windows",
    )(offsets, sources, *grads)


def solution(mesh):
    in_specs = (
        P(("parts", "cuts"), None, None, None),
        P(),
        P(("parts", "cuts")),
        P(),
        P(),
        P("parts", None),
        P("parts", "cuts", None),
    )
    out_specs = P(("parts", "cuts"), None, None, None)
    return jax.shard_map(shards, mesh=mesh, in_specs=in_specs, out_specs=out_specs, check_vma=False)
```

```python
import math

import jax
import jax.numpy as jnp
import numpy as np
from jax import lax
from jax.experimental import pallas as pl
from jax.experimental.pallas import tpu as pltpu
from jax.sharding import PartitionSpec as P

TRANSMIT = 0.985
GROUP = 8
LANES = 128
ROWS = 16
F32 = jnp.float32
BF16 = jnp.bfloat16


def dot(former, latter):
    return jnp.dot(former, latter, preferred_element_type=F32)


def halves(x):
    return x[:, :LANES], x[:, LANES : 2 * LANES], x[:, 2 * LANES :]


def swapped(tail):
    return pltpu.roll(tail, LANES // 2, 1)


def low_half(rows):
    return lax.broadcasted_iota(jnp.int32, (rows, LANES), 1) < LANES // 2


def spread(tail):
    other = swapped(tail)
    low = low_half(tail.shape[0])
    return jnp.where(low, tail, other), jnp.where(low, other, tail)


def signed(tail, minus_low):
    low = low_half(tail.shape[0])
    return jnp.where(low == minus_low, -tail, tail)


def times(a, b):
    a0, a1, at = halves(a)
    b0, b1, bt = halves(b)
    b_real, b_imag = spread(bt)
    tail = at * b_real + signed(swapped(at), True) * b_imag
    return jnp.concatenate([a0 * b0 - a1 * b1, a1 * b0 + a0 * b1, tail], axis=1)


def times_conj(a, *others):
    a0, a1, at = halves(a)
    turned = signed(swapped(at), False)
    results = []
    for b in others:
        b0, b1, bt = halves(b)
        b_real, b_imag = spread(bt)
        tail = at * b_real + turned * b_imag
        results.append(jnp.concatenate([a0 * b0 + a1 * b1, a1 * b0 - a0 * b1, tail], axis=1))
    return results


def joined(both, conj):
    width = both.shape[0] // 2
    u0, u1, ut = halves(both[:width])
    v0, v1, vt = halves(both[width:])
    turned = signed(swapped(vt), not conj)
    if conj:
        return jnp.concatenate([u0 + v1, u1 - v0, ut + turned], axis=1)
    return jnp.concatenate([u0 - v1, u1 + v0, ut + turned], axis=1)


def with_mean(window):
    x = window.astype(F32)
    x0, x1, xt = halves(x)
    mean = jnp.where(low_half(xt.shape[0]), TRANSMIT, 0.0)
    return jnp.concatenate([TRANSMIT + x0, x1, mean + xt], axis=1)


def split2(x):
    high = x.astype(BF16)
    return high, (x - high.astype(F32)).astype(BF16)


def picker(columns, start, high_tail, transposed=False):
    shape = (2 * LANES, columns) if transposed else (columns, 2 * LANES)
    a = lax.broadcasted_iota(jnp.int32, shape, 1 if transposed else 0) - start
    q = lax.broadcasted_iota(jnp.int32, shape, 0 if transposed else 1)
    if high_tail:
        half = LANES // 2
        wanted = jnp.where(q < LANES, q, jnp.where(q < LANES + half, -columns, q - half))
    else:
        wanted = jnp.where(q < LANES + LANES // 2, q, -columns)
    return jnp.where(a == wanted, 1.0, 0.0).astype(BF16)


def row_picker(shape, distance):
    taken = lax.broadcasted_iota(jnp.int32, shape, 1)
    wanted = lax.broadcasted_iota(jnp.int32, shape, 0) + distance
    return jnp.where(taken == wanted, 1.0, 0.0).astype(BF16)


def packed(real, imag, columns, start):
    left = dot(real, picker(columns, start, False))
    right = dot(imag, picker(columns, start, True))
    return jnp.concatenate(
        [left[:, :LANES], right[:, :LANES], left[:, LANES:] + right[:, LANES:]], axis=1
    )


def dft_constant(width):
    counter = np.arange(width)
    angle = (counter[:, None] * counter[None, :] % width) * (2.0 * math.pi / width)
    return (np.stack([np.cos(angle), -np.sin(angle)]) / math.sqrt(width)).astype(np.float32)


def window_kernel(offsets_ref, index_ref, objects_ref, measured_ref, blocks):
    positions, near_rows, width = measured_ref.shape
    extent = objects_ref.shape[-1]
    tag = jnp.full((ROWS, LANES), index_ref[0], jnp.int32).astype(F32).astype(BF16)
    blank = jnp.zeros((ROWS - near_rows, 2 * LANES), F32)
    field = jnp.concatenate([objects_ref[0, 0], objects_ref[0, 1]], axis=1)
    for p in range(positions):
        both = dot(row_picker((width, extent), offsets_ref[p, 0]), field).astype(BF16)
        window = packed(both[:, :extent], both[:, extent:], extent, offsets_ref[p, 1])
        blocks[p, :width, :] = window.astype(BF16)
        high, low = split2(jnp.concatenate([doubled(measured_ref[p]), blank], axis=0))
        for place, part in ((width, high), (width + ROWS, low)):
            blocks[p, place : place + ROWS, : 2 * LANES] = part
            blocks[p, place : place + ROWS, 2 * LANES :] = tag


def doubled(rows):
    tail = jnp.concatenate([rows[:, LANES:]] * 2, axis=1)
    return jnp.concatenate([rows[:, :LANES], tail], axis=1)


def right_table(real, imag):
    width = real.shape[0]
    upper = packed(real, imag, width, 0)
    lower = packed(-imag, real, width, 0)
    return jnp.concatenate([upper[:LANES], lower[:LANES], upper[LANES:], lower[LANES:]], axis=0)


def table_kernel(props_ref, dft_ref, lb_ref, rf_ref, rb_ref, dl_ref, dr_ref, dc_ref):
    width = props_ref.shape[-1]
    for k in range(props_ref.shape[0]):
        real, imag = props_ref[k, 0], props_ref[k, 1]
        lb_ref[k, :width, :] = real.astype(F32).T.astype(BF16)
        lb_ref[k, width:, :] = imag.astype(F32).T.astype(BF16)
        table = right_table(real, -imag)
        rb_ref[k] = table.astype(BF16)
        rf_ref[k] = table.T.astype(BF16)
    for n, (real, imag) in enumerate(zip(split2(dft_ref[0]), split2(dft_ref[1]))):
        dl_ref[n, :width, :] = real
        dl_ref[n, width:, :] = imag
        dr_ref[n] = right_table(real, imag).astype(BF16)
        dc_ref[n] = right_table(real, -imag).astype(BF16)


def forward_steps(blocks, waves, indices, lf, rf):
    sections, _, columns = blocks.shape
    width = columns // 2

    def step(k, carried):
        which = indices[k]
        z = times(waves[k].astype(F32), with_mean(blocks[k, :width, :])).astype(BF16)
        h = joined(dot(lf[which].reshape(columns, width), z), False).astype(BF16)
        waves[k + 1] = dot(h, rf[which]).astype(BF16)
        return carried

    lax.fori_loop(0, sections, step, 0)


def backward_steps(blocks, waves, indices, lb, rb, grads, g):
    sections, _, columns = blocks.shape
    width = columns // 2

    def step(n, carried):
        k = sections - 1 - n
        which = indices[k]
        c = joined(dot(lb[which], g[...]), True).astype(BF16)
        y = dot(c, rb[which])
        grad, passed = times_conj(y, waves[k].astype(F32), with_mean(blocks[k, :width, :]))
        grads[k] = grad.astype(BF16)
        g[...] = passed.astype(BF16)
        return carried

    lax.fori_loop(0, sections, step, 0)


def detector(psi, observed, left, right, right_conj):
    def product(ah, al, bh, bl):
        return dot(ah, bh) + (dot(ah, bl) + dot(al, bh))

    near = joined(dot(left[0], psi) + dot(left[1], psi), False)
    far = product(*split2(near), right[0], right[1])
    f0, f1, ft = halves(far)
    other = swapped(ft)
    main = f0 * f0 + f1 * f1 - observed[:, :LANES]
    tail = ft * ft + other * other - observed[:, LANES:]
    push = jnp.concatenate([main * f0, main * f1, tail * ft], axis=1)
    back = joined(product(left[0], left[1], *split2(push)), True)
    return product(*split2(back), right_conj[0], right_conj[1]).astype(BF16)


def read_indices(blocks, indices, count):
    for k in range(blocks.shape[0]):
        tag = jnp.max(blocks[k, -ROWS:, 2 * LANES :].astype(F32))
        indices[k] = jnp.clip(tag.astype(jnp.int32), 0, count - 1)


def place_in(size):
    rank = lax.axis_index("cuts")
    return lax.rem(rank, size), lax.div(rank, size)


def brought(pairs, sems):
    copies = [pltpu.make_async_copy(source, target, sems.at[n]) for n, (source, target) in enumerate(pairs)]
    for copy in copies:
        copy.start()
    return copies


def all_here(copies):
    for copy in copies:
        copy.wait()


def first_wave(group_ref, probes, probe, size, sem):
    slot, _ = place_in(size)
    which = group_ref[jnp.minimum(slot, group_ref.shape[0] - 1)]
    return pltpu.make_async_copy(probes.at[which], probe, sem)


def forward_kernel(size, stage):
    def kernel(*refs):
        if stage == 0:
            group_ref, probes, blocks_in, lf_in, rf_in, leaving, waves_out = refs[:7]
        else:
            entering, blocks_in, lf_in, rf_in, _, leaving, waves_out = refs[:7]
        blocks, waves, lf, rf, probe, indices, sems = refs[7:]
        _, group = place_in(size)

        @pl.when(group == stage)
        def _():
            copies = brought([(blocks_in, blocks), (lf_in, lf), (rf_in, rf)], sems)
            if stage == 0:
                copies.append(first_wave(group_ref, probes, probe, size, sems.at[3]))
                copies[-1].start()
            all_here(copies)
            read_indices(blocks, indices, lf.shape[0])
            if stage == 0:
                waves[0] = packed(probe[0], probe[1], probe.shape[-1], 0).astype(BF16)
            else:
                waves[0] = entering[...]
            forward_steps(blocks, waves, indices, lf, rf)
            leaving[...] = waves[size]
            all_here(brought([(waves.at[pl.ds(0, size)], waves_out)], sems))

    return kernel


def middle_kernel(size, groups, near_rows):
    def kernel(*refs):
        if groups == 1:
            group_ref, probes, *refs = refs
        else:
            entering, *refs = refs
        earlier, refs = refs[: groups - 1], refs[groups - 1 :]
        blocks_in, tables_in, refs = refs[0], refs[1:8], refs[8:]
        leaving, grads_out, blocks, waves, grads, probe, g, before, observed, indices, *refs = refs
        tables, sems = refs[:7], refs[7]
        lf, rf, lb, rb, left, right, right_conj = tables
        width = waves.shape[1]
        _, group = place_in(size)

        @pl.when(group == groups - 1)
        def _():
            pairs = [(blocks_in, blocks)] + list(zip(tables_in, tables))
            pairs += [(source, before.at[n]) for n, source in enumerate(earlier)]
            copies = brought(pairs, sems)
            if groups == 1:
                copies.insert(3, first_wave(group_ref, probes, probe, size, sems.at[len(pairs)]))
                copies[3].start()
            needed = 3 + (groups == 1)
            all_here(copies[:needed])
            read_indices(blocks, indices, lf.shape[0])
            if groups == 1:
                waves[0] = packed(probe[0], probe[1], width, 0).astype(BF16)
            else:
                waves[0] = entering[...]
            forward_steps(blocks, waves, indices, lf, rf)
            all_here(copies[needed:])

            def observe(at, block):
                high = block[-2 * ROWS : -ROWS, : 2 * LANES].astype(F32)
                low = block[-ROWS:, : 2 * LANES].astype(F32)
                observed[at * near_rows : (at + 1) * near_rows, :] = (high + low)[:near_rows]

            for k in range(size):
                for n in range(groups - 1):
                    observe(n * size + k, before[n, k])
                observe((groups - 1) * size + k, blocks[k, width:])
            g[...] = detector(waves[size], observed[...], left, right, right_conj)
            backward_steps(blocks, waves, indices, lb, rb, grads, g)
            leaving[...] = g[...]
            all_here(brought([(grads, grads_out)], sems))

    return kernel


def backward_kernel(size, stage):
    def kernel(
        arriving, waves_in, blocks_in, lb_in, rb_in, _, leaving, grads_out,
        blocks, waves, grads, lb, rb, g, indices, sems,
    ):
        _, group = place_in(size)

        @pl.when(group == stage)
        def _():
            all_here(brought([(blocks_in, blocks), (waves_in, waves), (lb_in, lb), (rb_in, rb)], sems))
            read_indices(blocks, indices, lb.shape[0])
            g[...] = arriving[...]
            backward_steps(blocks, waves, indices, lb, rb, grads, g)
            leaving[...] = g[...]
            all_here(brought([(grads, grads_out)], sems))

    return kernel


def gather_kernel(offsets_ref, grads_ref, out_ref):
    positions = offsets_ref.shape[0]
    width = grads_ref.shape[1]
    extent = out_ref.shape[-1]
    spread_out = []
    for p in range(positions):
        x0, x1, xt = halves(grads_ref[p])
        spread_out.append(
            jnp.concatenate(
                [
                    dot(
                        jnp.concatenate([main, xt], axis=1),
                        picker(extent, offsets_ref[p, 1], c == 1, transposed=True),
                    ).astype(BF16)
                    for c, main in ((0, x0), (1, x1))
                ],
                axis=1,
            )
        )
    rows = jnp.concatenate(
        [row_picker((extent, width), -offsets_ref[p, 0]) for p in range(positions)], axis=1
    )
    total = dot(rows, jnp.concatenate(spread_out, axis=0))
    out_ref[0, 0] = total[:, :extent]
    out_ref[0, 1] = total[:, extent:]


VMEM = pl.BlockSpec(memory_space=pltpu.VMEM)
SMEM = pl.BlockSpec(memory_space=pltpu.SMEM)
HBM = pl.BlockSpec(memory_space=pl.ANY)
PARAMS = pltpu.CompilerParams(vmem_limit_bytes=56 * 1024 * 1024)


def shards(objects, propagators, prop_index, probes, probe_group, offsets, measured):
    sections = lax.axis_size("cuts")
    width = probes.shape[-1]
    kinds = propagators.shape[0]
    near_rows = measured.shape[1]
    size = GROUP
    groups = sections // size
    rows = width + 2 * ROWS
    members = [list(range(first, first + size)) for first in range(0, sections, size)]

    def struct(*dims, kind=BF16):
        return jax.ShapeDtypeStruct(dims, kind)

    def exchanged(blocks):
        return lax.all_to_all(blocks, "cuts", 0, 0, axis_index_groups=members, tiled=True)

    def handed(block, stage, distance):
        route = [(stage * size + l, (stage + distance) * size + l) for l in range(probe_group.shape[0])]
        return lax.ppermute(block, "cuts", route)

    blocks = pl.pallas_call(
        window_kernel,
        out_shape=struct(size, rows, 2 * width),
        in_specs=[SMEM, SMEM, VMEM, VMEM],
        out_specs=VMEM,
        compiler_params=PARAMS,
        name="windows",
    )(offsets, prop_index, objects, measured)
    blocks = exchanged(blocks)

    tables = pl.pallas_call(
        table_kernel,
        out_shape=[
            struct(kinds, 2 * width, width),
            struct(kinds, 2 * width, 2 * width),
            struct(kinds, 2 * width, 2 * width),
            struct(2, 2 * width, width),
            struct(2, 2 * width, 2 * width),
            struct(2, 2 * width, 2 * width),
        ],
        in_specs=[VMEM, VMEM],
        out_specs=[VMEM] * 6,
        compiler_params=PARAMS,
        cost_estimate=pl.CostEstimate(flops=10**9, bytes_accessed=6 * 10**6, transcendentals=0),
        name="tables",
    )(propagators, jnp.asarray(dft_constant(width)))
    lf, lb, rf, rb = propagators, *tables[:3]
    dft = tables[3:]

    wave = (width, 2 * width)
    block_scratch = pltpu.VMEM((size, rows, 2 * width), BF16)
    waves_scratch = pltpu.VMEM((size + 1,) + wave, BF16)
    grads_scratch = pltpu.VMEM((size,) + wave, BF16)
    probe_scratch = pltpu.VMEM(probes.shape[1:], BF16)
    indices = pltpu.SMEM((size,), jnp.int32)

    def like(*arrays):
        return [pltpu.VMEM(array.shape, array.dtype) for array in arrays]

    entering, waves, nears = None, None, []
    for stage in range(groups - 1):
        nears.append(handed(blocks[:, width:], stage, groups - 1 - stage))
        first = stage == 0
        leaving, waves = pl.pallas_call(
            forward_kernel(size, stage),
            out_shape=[struct(*wave), struct(size, *wave)],
            in_specs=[SMEM] + [HBM] * 4 if first else [VMEM] + [HBM] * 4,
            out_specs=[VMEM, HBM],
            scratch_shapes=[block_scratch, waves_scratch]
            + like(lf, rf)
            + [probe_scratch, indices, pltpu.SemaphoreType.DMA((4,))],
            input_output_aliases={} if first else {4: 1},
            compiler_params=PARAMS,
            name="forward",
        )(*((probe_group, probes, blocks, lf, rf) if first else (entering, blocks, lf, rf, waves)))
        entering = handed(leaving, stage, 1)

    alone = groups == 1
    leaving, grads = pl.pallas_call(
        middle_kernel(size, groups, near_rows),
        out_shape=[struct(*wave), struct(size, *wave)],
        in_specs=([SMEM, HBM] if alone else [VMEM]) + [HBM] * (groups - 1 + 8),
        out_specs=[VMEM, HBM],
        scratch_shapes=[
            block_scratch,
            waves_scratch,
            grads_scratch,
            probe_scratch,
            pltpu.VMEM(wave, BF16),
            pltpu.VMEM((max(groups - 1, 1), size, 2 * ROWS, 2 * width), BF16),
            pltpu.VMEM((width, 2 * LANES), F32),
            indices,
        ]
        + like(lf, rf, lb, rb, *dft)
        + [pltpu.SemaphoreType.DMA((9 + groups,))],
        compiler_params=PARAMS,
        name="middle",
    )(*((probe_group, probes) if alone else (entering,)), *nears, blocks, lf, rf, lb, rb, *dft)

    for stage in range(groups - 2, -1, -1):
        arriving = handed(leaving, stage + 1, -1)
        leaving, grads = pl.pallas_call(
            backward_kernel(size, stage),
            out_shape=[struct(*wave), struct(size, *wave)],
            in_specs=[VMEM] + [HBM] * 5,
            out_specs=[VMEM, HBM],
            scratch_shapes=[block_scratch, pltpu.VMEM((size,) + wave, BF16), grads_scratch]
            + like(lb, rb)
            + [pltpu.VMEM(wave, BF16), indices, pltpu.SemaphoreType.DMA((4,))],
            input_output_aliases={5: 1},
            compiler_params=PARAMS,
            name="backward",
        )(arriving, waves, blocks, lb, rb, grads)

    return pl.pallas_call(
        gather_kernel,
        out_shape=jax.ShapeDtypeStruct(objects.shape, F32),
        in_specs=[SMEM, VMEM],
        out_specs=VMEM,
        compiler_params=PARAMS,
        name="sum_windows",
    )(offsets, exchanged(grads))


def solution(mesh):
    in_specs = (
        P(("parts", "cuts"), None, None, None),
        P(),
        P(("parts", "cuts")),
        P(),
        P(),
        P("parts", None),
        P("parts", "cuts", None),
    )
    out_specs = P(("parts", "cuts"), None, None, None)
    return jax.shard_map(shards, mesh=mesh, in_specs=in_specs, out_specs=out_specs, check_vma=False)
```

```python
import math

import jax
import jax.numpy as jnp
import numpy as np
from jax import lax
from jax.experimental import pallas as pl
from jax.experimental.pallas import tpu as pltpu
from jax.sharding import PartitionSpec as P

TRANSMIT = 0.985
GROUP = 8
LANES = 128
ROWS = 16
F32 = jnp.float32
BF16 = jnp.bfloat16


def dot(former, latter):
    return jnp.dot(former, latter, preferred_element_type=F32)


def halves(x):
    return x[:, :LANES], x[:, LANES : 2 * LANES], x[:, 2 * LANES :]


def swapped(tail):
    return pltpu.roll(tail, LANES // 2, 1)


def low_half(rows):
    return lax.broadcasted_iota(jnp.int32, (rows, LANES), 1) < LANES // 2


def spread(tail):
    other = swapped(tail)
    low = low_half(tail.shape[0])
    return jnp.where(low, tail, other), jnp.where(low, other, tail)


def signed(tail, minus_low):
    low = low_half(tail.shape[0])
    return jnp.where(low == minus_low, -tail, tail)


def times(a, b):
    a0, a1, at = halves(a)
    b0, b1, bt = halves(b)
    b_real, b_imag = spread(bt)
    tail = at * b_real + signed(swapped(at), True) * b_imag
    return jnp.concatenate([a0 * b0 - a1 * b1, a1 * b0 + a0 * b1, tail], axis=1)


def times_conj(a, *others):
    a0, a1, at = halves(a)
    turned = signed(swapped(at), False)
    results = []
    for b in others:
        b0, b1, bt = halves(b)
        b_real, b_imag = spread(bt)
        tail = at * b_real + turned * b_imag
        results.append(jnp.concatenate([a0 * b0 + a1 * b1, a1 * b0 - a0 * b1, tail], axis=1))
    return results


def joined(both, conj):
    width = both.shape[0] // 2
    u0, u1, ut = halves(both[:width])
    v0, v1, vt = halves(both[width:])
    turned = signed(swapped(vt), not conj)
    if conj:
        return jnp.concatenate([u0 + v1, u1 - v0, ut + turned], axis=1)
    return jnp.concatenate([u0 - v1, u1 + v0, ut + turned], axis=1)


def with_mean(window):
    x = window.astype(F32)
    x0, x1, xt = halves(x)
    mean = jnp.where(low_half(xt.shape[0]), TRANSMIT, 0.0)
    return jnp.concatenate([TRANSMIT + x0, x1, mean + xt], axis=1)


def split2(x):
    high = x.astype(BF16)
    return high, (x - high.astype(F32)).astype(BF16)


def picker(columns, start, high_tail, transposed=False):
    shape = (2 * LANES, columns) if transposed else (columns, 2 * LANES)
    a = lax.broadcasted_iota(jnp.int32, shape, 1 if transposed else 0) - start
    q = lax.broadcasted_iota(jnp.int32, shape, 0 if transposed else 1)
    if high_tail:
        half = LANES // 2
        wanted = jnp.where(q < LANES, q, jnp.where(q < LANES + half, -columns, q - half))
    else:
        wanted = jnp.where(q < LANES + LANES // 2, q, -columns)
    return jnp.where(a == wanted, 1.0, 0.0).astype(BF16)


def row_picker(shape, distance):
    taken = lax.broadcasted_iota(jnp.int32, shape, 1)
    wanted = lax.broadcasted_iota(jnp.int32, shape, 0) + distance
    return jnp.where(taken == wanted, 1.0, 0.0).astype(BF16)


def packed(real, imag, columns, start):
    left = dot(real, picker(columns, start, False))
    right = dot(imag, picker(columns, start, True))
    return jnp.concatenate(
        [left[:, :LANES], right[:, :LANES], left[:, LANES:] + right[:, LANES:]], axis=1
    )


def dft_constant(width):
    counter = np.arange(width)
    angle = (counter[:, None] * counter[None, :] % width) * (2.0 * math.pi / width)
    return (np.stack([np.cos(angle), -np.sin(angle)]) / math.sqrt(width)).astype(np.float32)


def window_kernel(offsets_ref, index_ref, objects_ref, measured_ref, blocks):
    positions, near_rows, width = measured_ref.shape
    extent = objects_ref.shape[-1]
    tag = jnp.full((ROWS, LANES), index_ref[0], jnp.int32).astype(F32).astype(BF16)
    blank = jnp.zeros((ROWS - near_rows, 2 * LANES), F32)
    field = jnp.concatenate([objects_ref[0, 0], objects_ref[0, 1]], axis=1)
    for p in range(positions):
        both = dot(row_picker((width, extent), offsets_ref[0, p]), field).astype(BF16)
        window = packed(both[:, :extent], both[:, extent:], extent, offsets_ref[1, p])
        blocks[p, :width, :] = window.astype(BF16)
        high, low = split2(jnp.concatenate([doubled(measured_ref[p]), blank], axis=0))
        for place, part in ((width, high), (width + ROWS, low)):
            blocks[p, place : place + ROWS, : 2 * LANES] = part
            blocks[p, place : place + ROWS, 2 * LANES :] = tag


def doubled(rows):
    tail = jnp.concatenate([rows[:, LANES:]] * 2, axis=1)
    return jnp.concatenate([rows[:, :LANES], tail], axis=1)


def right_table(real, imag):
    width = real.shape[0]
    upper = packed(real, imag, width, 0)
    lower = packed(-imag, real, width, 0)
    return jnp.concatenate([upper[:LANES], lower[:LANES], upper[LANES:], lower[LANES:]], axis=0)


def transposed(plane):
    return plane.astype(F32).T.astype(BF16)


def forward_tables(props, rf):
    for k in range(props.shape[0]):
        rf[k] = right_table(transposed(props[k, 0]), transposed(props[k, 1])).astype(BF16)


def backward_tables(props, lb, rb):
    width = props.shape[-1]
    for k in range(props.shape[0]):
        real, imag = props[k, 0], props[k, 1]
        lb[k, :width, :] = transposed(real)
        lb[k, width:, :] = transposed(imag)
        rb[k] = right_table(real, -imag).astype(BF16)


def detector_tables(dft, left, right, right_conj):
    width = dft.shape[-1]
    for n, (real, imag) in enumerate(zip(split2(dft[0]), split2(dft[1]))):
        left[n, :width, :] = real
        left[n, width:, :] = imag
        right[n] = right_table(real, imag).astype(BF16)
        right_conj[n] = right_table(real, -imag).astype(BF16)


def forward_steps(blocks, waves, indices, lf, rf):
    sections, _, columns = blocks.shape
    width = columns // 2

    def step(k, carried):
        which = indices[k]
        z = times(waves[k].astype(F32), with_mean(blocks[k, :width, :])).astype(BF16)
        h = joined(dot(lf[which].reshape(columns, width), z), False).astype(BF16)
        waves[k + 1] = dot(h, rf[which]).astype(BF16)
        return carried

    lax.fori_loop(0, sections, step, 0, unroll=2)


def backward_steps(blocks, waves, indices, lb, rb, grads, g):
    sections, _, columns = blocks.shape
    width = columns // 2

    def step(n, carried):
        k = sections - 1 - n
        which = indices[k]
        c = joined(dot(lb[which], g[...]), True).astype(BF16)
        y = dot(c, rb[which])
        grad, passed = times_conj(y, waves[k].astype(F32), with_mean(blocks[k, :width, :]))
        grads[k] = grad.astype(BF16)
        g[...] = passed.astype(BF16)
        return carried

    lax.fori_loop(0, sections, step, 0, unroll=2)


def detector(psi, observed, left, right, right_conj):
    def product(ah, al, bh, bl):
        return dot(ah, bh) + (dot(ah, bl) + dot(al, bh))

    near = joined(dot(left[0], psi) + dot(left[1], psi), False)
    far = product(*split2(near), right[0], right[1])
    f0, f1, ft = halves(far)
    other = swapped(ft)
    main = f0 * f0 + f1 * f1 - observed[:, :LANES]
    tail = ft * ft + other * other - observed[:, LANES:]
    push = jnp.concatenate([main * f0, main * f1, tail * ft], axis=1)
    back = joined(product(left[0], left[1], *split2(push)), True)
    return product(*split2(back), right_conj[0], right_conj[1]).astype(BF16)


def read_indices(blocks, indices, count):
    for k in range(blocks.shape[0]):
        tag = jnp.max(blocks[k, -ROWS:, 2 * LANES :].astype(F32))
        indices[k] = jnp.clip(tag.astype(jnp.int32), 0, count - 1)


def place_in(size):
    rank = lax.axis_index("cuts")
    return lax.rem(rank, size), lax.div(rank, size)


def observe(blocks, near_rows, observed, first):
    for k in range(blocks.shape[0]):
        high = blocks[k, -2 * ROWS : -ROWS, : 2 * LANES].astype(F32)
        low = blocks[k, -ROWS:, : 2 * LANES].astype(F32)
        at = first + k * near_rows
        observed[at : at + near_rows, :] = (high + low)[:near_rows]


def first_kernel(group_ref, probes, blocks, props, dft, leaving, near, waves, lb, rf, rb, left, right, right_conj, probe, indices, sem):
    size = blocks.shape[0]
    slot, group = place_in(size)

    @pl.when(group == 0)
    def _():
        which = group_ref[jnp.minimum(slot, group_ref.shape[0] - 1)]
        copy = pltpu.make_async_copy(probes.at[which], probe, sem)
        copy.start()
        forward_tables(props, rf)
        read_indices(blocks, indices, props.shape[0])
        copy.wait()
        waves[0] = packed(probe[0], probe[1], probe.shape[-1], 0).astype(BF16)
        forward_steps(blocks, waves, indices, props, rf)
        leaving[...] = waves[size]
        observe(blocks, near.shape[0] // size, near, 0)

    @pl.when(group > 0)
    def _():
        forward_tables(props, rf)
        backward_tables(props, lb, rb)
        detector_tables(dft, left, right, right_conj)


def forward_kernel(stage):
    def kernel(entering, blocks, props, rf, waves_in, leaving, near, waves, indices):
        size = blocks.shape[0]
        _, group = place_in(size)

        @pl.when(group == stage)
        def _():
            read_indices(blocks, indices, props.shape[0])
            waves[0] = entering[...]
            forward_steps(blocks, waves, indices, props, rf)
            leaving[...] = waves[size]
            observe(blocks, near.shape[0] // size, near, 0)

        @pl.when(group != stage)
        def _():
            waves[...] = waves_in[...]

    return kernel


def middle_kernel(groups):
    def kernel(entering, *refs):
        earlier, refs = refs[: groups - 1], refs[groups - 1 :]
        blocks, props, lb, rf, rb, left, right, right_conj, leaving, grads, lb_out, rb_out = refs[:12]
        waves, g, observed, indices = refs[12:]
        size = blocks.shape[0]
        _, group = place_in(size)

        @pl.when(group == groups - 1)
        def _():
            read_indices(blocks, indices, props.shape[0])
            waves[0] = entering[...]
            forward_steps(blocks, waves, indices, props, rf)
            rows = earlier[0].shape[0]
            for n, near in enumerate(earlier):
                observed[n * rows : (n + 1) * rows, :] = near[...]
            observe(blocks, rows // size, observed, (groups - 1) * rows)
            g[...] = detector(waves[size], observed[...], left, right, right_conj)
            backward_steps(blocks, waves, indices, lb, rb, grads, g)
            leaving[...] = g[...]

        @pl.when(group < groups - 1)
        def _():
            backward_tables(props, lb_out, rb_out)

    return kernel


def backward_kernel(stage):
    def kernel(arriving, waves, blocks, lb, rb, grads_in, leaving, grads, g, indices):
        _, group = place_in(blocks.shape[0])

        @pl.when(group == stage)
        def _():
            read_indices(blocks, indices, lb.shape[0])
            g[...] = arriving[...]
            backward_steps(blocks, waves, indices, lb, rb, grads, g)
            leaving[...] = g[...]

        @pl.when(group != stage)
        def _():
            grads[...] = grads_in[...]

    return kernel


def gather_kernel(offsets_ref, grads_ref, out_ref):
    positions = offsets_ref.shape[1]
    width = grads_ref.shape[1]
    extent = out_ref.shape[-1]
    spread_out = []
    for p in range(positions):
        x0, x1, xt = halves(grads_ref[p])
        spread_out.append(
            jnp.concatenate(
                [
                    dot(
                        jnp.concatenate([main, xt], axis=1),
                        picker(extent, offsets_ref[1, p], c == 1, transposed=True),
                    ).astype(BF16)
                    for c, main in ((0, x0), (1, x1))
                ],
                axis=1,
            )
        )
    rows = jnp.concatenate(
        [row_picker((extent, width), -offsets_ref[0, p]) for p in range(positions)], axis=1
    )
    total = dot(rows, jnp.concatenate(spread_out, axis=0))
    out_ref[0, 0] = total[:, :extent]
    out_ref[0, 1] = total[:, extent:]


VMEM = pl.BlockSpec(memory_space=pltpu.VMEM)
SMEM = pl.BlockSpec(memory_space=pltpu.SMEM)
HBM = pl.BlockSpec(memory_space=pl.ANY)
PARAMS = pltpu.CompilerParams(vmem_limit_bytes=20 * 1024 * 1024)


def shards(objects, propagators, prop_index, probes, probe_group, offsets, measured):
    sections = lax.axis_size("cuts")
    width = probes.shape[-1]
    kinds = propagators.shape[0]
    near_rows = measured.shape[1]
    size = GROUP
    groups = sections // size
    rows = width + 2 * ROWS
    members = [list(range(first, first + size)) for first in range(0, sections, size)]

    def struct(*dims, kind=BF16):
        return jax.ShapeDtypeStruct(dims, kind)

    def exchanged(blocks):
        return lax.all_to_all(blocks, "cuts", 0, 0, axis_index_groups=members, tiled=True)

    def handed(block, stage, distance):
        route = [(stage * size + l, (stage + distance) * size + l) for l in range(probe_group.shape[0])]
        return lax.ppermute(block, "cuts", route)

    blocks = pl.pallas_call(
        window_kernel,
        out_shape=struct(size, rows, 2 * width),
        in_specs=[SMEM, SMEM, VMEM, VMEM],
        out_specs=VMEM,
        compiler_params=PARAMS,
        name="windows",
    )(offsets.T, prop_index, objects, measured)
    blocks = exchanged(blocks)

    wave = struct(width, 2 * width)
    near = struct(size * near_rows, 2 * LANES, kind=F32)
    waves_shape = struct(size + 1, width, 2 * width)
    grads_shape = struct(size, width, 2 * width)
    left_table = struct(kinds, 2 * width, width)
    square_table = struct(kinds, 2 * width, 2 * width)
    detector_left = struct(2, 2 * width, width)
    detector_right = struct(2, 2 * width, 2 * width)
    indices = pltpu.SMEM((size,), jnp.int32)

    def scratch(shape):
        return pltpu.VMEM(shape.shape, shape.dtype)

    def call(kernel, name, out_shape, in_specs, scratch_shapes, operands):
        return pl.pallas_call(
            kernel,
            out_shape=out_shape,
            in_specs=in_specs,
            out_specs=[VMEM] * len(out_shape),
            scratch_shapes=scratch_shapes,
            compiler_params=PARAMS,
            name=name,
        )(*operands)

    leaving, near_out, waves, lb, rf, rb, *dft = call(
        first_kernel,
        "first_forward",
        [wave, near, waves_shape, left_table, square_table, square_table]
        + [detector_left, detector_right, detector_right],
        [SMEM, HBM, VMEM, VMEM, VMEM],
        [pltpu.VMEM(probes.shape[1:], BF16), indices, pltpu.SemaphoreType.DMA],
        (probe_group, probes, blocks, propagators, jnp.asarray(dft_constant(width))),
    )
    entering = handed(leaving, 0, 1)
    nears = [handed(near_out, 0, groups - 1)]
    for stage in range(1, groups - 1):
        leaving, near_out, waves = call(
            forward_kernel(stage),
            "forward",
            [wave, near, waves_shape],
            [VMEM] * 5,
            [indices],
            (entering, blocks, propagators, rf, waves),
        )
        entering = handed(leaving, stage, 1)
        nears.append(handed(near_out, stage, groups - 1 - stage))

    leaving, grads, lb, rb = call(
        middle_kernel(groups),
        "middle",
        [wave, grads_shape, left_table, square_table],
        [VMEM] * (groups + 8),
        [scratch(waves_shape), scratch(wave), pltpu.VMEM((width, 2 * LANES), F32), indices],
        (entering, *nears, blocks, propagators, lb, rf, rb, *dft),
    )

    for stage in range(groups - 2, -1, -1):
        arriving = handed(leaving, stage + 1, -1)
        leaving, grads = call(
            backward_kernel(stage),
            "backward",
            [wave, grads_shape],
            [VMEM] * 6,
            [scratch(wave), indices],
            (arriving, waves, blocks, lb, rb, grads),
        )

    return pl.pallas_call(
        gather_kernel,
        out_shape=jax.ShapeDtypeStruct(objects.shape, F32),
        in_specs=[SMEM, VMEM],
        out_specs=VMEM,
        compiler_params=PARAMS,
        name="sum_windows",
    )(offsets.T, exchanged(grads))


def solution(mesh):
    in_specs = (
        P(("parts", "cuts"), None, None, None),
        P(),
        P(("parts", "cuts")),
        P(),
        P(),
        P("parts", None),
        P("parts", "cuts", None),
    )
    out_specs = P(("parts", "cuts"), None, None, None)
    return jax.shard_map(shards, mesh=mesh, in_specs=in_specs, out_specs=out_specs, check_vma=False)
```

```python
import math

import jax
import jax.numpy as jnp
import numpy as np
from jax import lax
from jax.experimental import pallas as pl
from jax.experimental.pallas import tpu as pltpu
from jax.sharding import PartitionSpec as P

TRANSMIT = 0.985
GROUP = 8
LANES = 128
ROWS = 16
F32 = jnp.float32
BF16 = jnp.bfloat16


def dot(former, latter):
    return jnp.dot(former, latter, preferred_element_type=F32)


def halves(x):
    return x[:, :LANES], x[:, LANES : 2 * LANES], x[:, 2 * LANES :]


def swapped(tail):
    return pltpu.roll(tail, LANES // 2, 1)


def low_half(rows):
    return lax.broadcasted_iota(jnp.int32, (rows, LANES), 1) < LANES // 2


def spread(tail):
    other = swapped(tail)
    low = low_half(tail.shape[0])
    return jnp.where(low, tail, other), jnp.where(low, other, tail)


def signed(tail, minus_low):
    low = low_half(tail.shape[0])
    return jnp.where(low == minus_low, -tail, tail)


def times(a, b):
    a0, a1, at = halves(a)
    b0, b1, bt = halves(b)
    b_real, b_imag = spread(bt)
    tail = at * b_real + signed(swapped(at), True) * b_imag
    return jnp.concatenate([a0 * b0 - a1 * b1, a1 * b0 + a0 * b1, tail], axis=1)


def times_conj(a, *others):
    a0, a1, at = halves(a)
    turned = signed(swapped(at), False)
    results = []
    for b in others:
        b0, b1, bt = halves(b)
        b_real, b_imag = spread(bt)
        tail = at * b_real + turned * b_imag
        results.append(jnp.concatenate([a0 * b0 + a1 * b1, a1 * b0 - a0 * b1, tail], axis=1))
    return results


def joined(both, conj):
    width = both.shape[0] // 2
    u0, u1, ut = halves(both[:width])
    v0, v1, vt = halves(both[width:])
    turned = signed(swapped(vt), not conj)
    if conj:
        return jnp.concatenate([u0 + v1, u1 - v0, ut + turned], axis=1)
    return jnp.concatenate([u0 - v1, u1 + v0, ut + turned], axis=1)


def with_mean(window):
    x = window.astype(F32)
    x0, x1, xt = halves(x)
    mean = jnp.where(low_half(xt.shape[0]), TRANSMIT, 0.0)
    return jnp.concatenate([TRANSMIT + x0, x1, mean + xt], axis=1)


def split2(x):
    high = x.astype(BF16)
    return high, (x - high.astype(F32)).astype(BF16)


def picker(columns, start, high_tail, transposed=False):
    shape = (2 * LANES, columns) if transposed else (columns, 2 * LANES)
    a = lax.broadcasted_iota(jnp.int32, shape, 1 if transposed else 0) - start
    q = lax.broadcasted_iota(jnp.int32, shape, 0 if transposed else 1)
    if high_tail:
        half = LANES // 2
        wanted = jnp.where(q < LANES, q, jnp.where(q < LANES + half, -columns, q - half))
    else:
        wanted = jnp.where(q < LANES + LANES // 2, q, -columns)
    return jnp.where(a == wanted, 1.0, 0.0).astype(BF16)


def row_picker(shape, distance):
    taken = lax.broadcasted_iota(jnp.int32, shape, 1)
    wanted = lax.broadcasted_iota(jnp.int32, shape, 0) + distance
    return jnp.where(taken == wanted, 1.0, 0.0).astype(BF16)


def packed(real, imag, columns, start):
    left = dot(real, picker(columns, start, False))
    right = dot(imag, picker(columns, start, True))
    return jnp.concatenate(
        [left[:, :LANES], right[:, :LANES], left[:, LANES:] + right[:, LANES:]], axis=1
    )


def dft_constant(width):
    counter = np.arange(width)
    angle = (counter[:, None] * counter[None, :] % width) * (2.0 * math.pi / width)
    return (np.stack([np.cos(angle), -np.sin(angle)]) / math.sqrt(width)).astype(np.float32)


def slots_of(positions, size):
    order = list(range(0, size, 2)) + list(range(1, size, 2))
    return sorted(order[:positions])


def window_kernel(offsets_ref, index_ref, objects_in, measured_in, blocks, objects, measured, sems):
    positions, near_rows, width = measured.shape
    extent = objects.shape[-1]
    copies = [
        pltpu.make_async_copy(objects_in.at[0, 0], objects.at[0], sems.at[0]),
        pltpu.make_async_copy(objects_in.at[0, 1], objects.at[1], sems.at[1]),
        pltpu.make_async_copy(measured_in, measured, sems.at[2]),
    ]
    for copy in copies:
        copy.start()
    tag = jnp.full((ROWS - near_rows, 2 * width), index_ref[0], jnp.int32).astype(F32)
    for copy in copies:
        copy.wait()
    field = jnp.concatenate([objects[0], objects[1]], axis=1)
    for p, slot in enumerate(slots_of(positions, blocks.shape[0])):
        both = dot(row_picker((width, extent), offsets_ref[0, p]), field).astype(BF16)
        window = packed(both[:, :extent], both[:, extent:], extent, offsets_ref[1, p])
        blocks[slot, :width, :] = window.astype(BF16)
        high = measured[p].astype(BF16).astype(F32)
        low = measured[p] - high
        seen = jnp.concatenate([high[:, :LANES], low[:, :LANES], high[:, LANES:], low[:, LANES:]], axis=1)
        blocks[slot, width:, :] = jnp.concatenate([seen, tag], axis=0).astype(BF16)


def right_table(real, imag):
    width = real.shape[0]
    upper = packed(real, imag, width, 0)
    lower = packed(-imag, real, width, 0)
    return jnp.concatenate([upper[:LANES], lower[:LANES], upper[LANES:], lower[LANES:]], axis=0)


def transposed(plane):
    return plane.astype(F32).T.astype(BF16)


def forward_tables(props, rf):
    for k in range(props.shape[0]):
        rf[k] = right_table(transposed(props[k, 0]), transposed(props[k, 1])).astype(BF16)


def backward_tables(props, lb, rb):
    width = props.shape[-1]
    for k in range(props.shape[0]):
        real, imag = props[k, 0], props[k, 1]
        lb[k, :width, :] = transposed(real)
        lb[k, width:, :] = transposed(imag)
        rb[k] = right_table(real, -imag).astype(BF16)


def detector_tables(dft, left, right, right_conj):
    width = dft.shape[-1]
    for n, (real, imag) in enumerate(zip(split2(dft[0]), split2(dft[1]))):
        left[n, :width, :] = real
        left[n, width:, :] = imag
        right[n] = right_table(real, imag).astype(BF16)
        right_conj[n] = right_table(real, -imag).astype(BF16)


def forward_steps(blocks, waves, indices, lf, rf):
    sections, _, columns = blocks.shape
    width = columns // 2

    def step(k, carried):
        which = indices[k]
        z = times(waves[k].astype(F32), with_mean(blocks[k, :width, :])).astype(BF16)
        h = joined(dot(lf[which].reshape(columns, width), z), False).astype(BF16)
        waves[k + 1] = dot(h, rf[which]).astype(BF16)
        return carried

    lax.fori_loop(0, sections, step, 0, unroll=2)


def backward_steps(blocks, waves, indices, lb, rb, grads, g):
    sections, _, columns = blocks.shape
    width = columns // 2

    def step(n, carried):
        k = sections - 1 - n
        which = indices[k]
        c = joined(dot(lb[which], g[...]), True).astype(BF16)
        y = dot(c, rb[which])
        grad, passed = times_conj(y, waves[k].astype(F32), with_mean(blocks[k, :width, :]))
        grads[k] = grad.astype(BF16)
        g[...] = passed.astype(BF16)
        return carried

    lax.fori_loop(0, sections, step, 0, unroll=2)


def detector(psi, observed, left, right, right_conj):
    def product(ah, al, bh, bl):
        return dot(ah, bh) + (dot(ah, bl) + dot(al, bh))

    near = joined(dot(left[0], psi) + dot(left[1], psi), False)
    far = product(*split2(near), right[0], right[1])
    f0, f1, ft = halves(far)
    other = swapped(ft)
    main = f0 * f0 + f1 * f1 - observed[:, :LANES]
    tail = ft * ft + other * other - observed[:, LANES:]
    push = jnp.concatenate([main * f0, main * f1, tail * ft], axis=1)
    back = joined(product(left[0], left[1], *split2(push)), True)
    return product(*split2(back), right_conj[0], right_conj[1]).astype(BF16)


def read_indices(blocks, indices, count):
    for k in range(blocks.shape[0]):
        tag = jnp.max(blocks[k, -ROWS:, :LANES].astype(F32)[ROWS - 1 :])
        indices[k] = jnp.clip(tag.astype(jnp.int32), 0, count - 1)


def place_in(size):
    rank = lax.axis_index("cuts")
    return lax.rem(rank, size), lax.div(rank, size)


def observe(blocks, near_rows, observed, first):
    for k in range(blocks.shape[0]):
        high, low, tail = halves(blocks[k, -ROWS:, :].astype(F32))
        rows = jnp.concatenate([high + low, tail + swapped(tail)], axis=1)
        at = first + k * near_rows
        observed[at : at + near_rows, :] = rows[:near_rows]


def near_kernel(blocks, _, near):
    observe(blocks, near.shape[0] // blocks.shape[0], near, 0)


def first_kernel(group_ref, probes, blocks, props, dft, leaving, waves, lb, rf, rb, left, right, right_conj, probe, indices, sem):
    size = blocks.shape[0]
    slot, group = place_in(size)

    @pl.when(group == 0)
    def _():
        position = 0
        for p, held in enumerate(slots_of(group_ref.shape[0], size)):
            position = jnp.where(slot == held, p, position)
        which = group_ref[position]
        copy = pltpu.make_async_copy(probes.at[which], probe, sem)
        copy.start()
        forward_tables(props, rf)
        read_indices(blocks, indices, props.shape[0])
        copy.wait()
        waves[0] = packed(probe[0], probe[1], probe.shape[-1], 0).astype(BF16)
        forward_steps(blocks, waves, indices, props, rf)
        leaving[...] = waves[size]

    @pl.when(group > 0)
    def _():
        forward_tables(props, rf)
        backward_tables(props, lb, rb)
        detector_tables(dft, left, right, right_conj)


def forward_kernel(stage):
    def kernel(entering, blocks, props, rf, waves_in, leaving, waves, indices):
        size = blocks.shape[0]
        _, group = place_in(size)

        @pl.when(group == stage)
        def _():
            read_indices(blocks, indices, props.shape[0])
            waves[0] = entering[...]
            forward_steps(blocks, waves, indices, props, rf)
            leaving[...] = waves[size]

        @pl.when(group != stage)
        def _():
            waves[...] = waves_in[...]

    return kernel


def middle_kernel(groups):
    def kernel(waves, *refs):
        earlier, refs = refs[: groups - 1], refs[groups - 1 :]
        blocks, props, lb, rb, left, right, right_conj, leaving, grads, lb_out, rb_out, g, observed, indices = refs
        size = blocks.shape[0]
        _, group = place_in(size)

        @pl.when(group == groups - 1)
        def _():
            read_indices(blocks, indices, props.shape[0])
            rows = earlier[0].shape[0]
            for n, near in enumerate(earlier):
                observed[n * rows : (n + 1) * rows, :] = near[...]
            observe(blocks, rows // size, observed, (groups - 1) * rows)
            g[...] = detector(waves[size], observed[...], left, right, right_conj)
            backward_steps(blocks, waves, indices, lb, rb, grads, g)
            leaving[...] = g[...]

        @pl.when(group < groups - 1)
        def _():
            backward_tables(props, lb_out, rb_out)

    return kernel


def backward_kernel(stage):
    def kernel(arriving, waves, blocks, lb, rb, grads_in, leaving, grads, g, indices):
        _, group = place_in(blocks.shape[0])

        @pl.when(group == stage)
        def _():
            read_indices(blocks, indices, lb.shape[0])
            g[...] = arriving[...]
            backward_steps(blocks, waves, indices, lb, rb, grads, g)
            leaving[...] = g[...]

        @pl.when(group != stage)
        def _():
            grads[...] = grads_in[...]

    return kernel


def gather_kernel(offsets_ref, grads_ref, out_ref):
    positions = offsets_ref.shape[1]
    width = grads_ref.shape[1]
    extent = out_ref.shape[-1]
    spread_out = []
    for p, slot in enumerate(slots_of(positions, grads_ref.shape[0])):
        x0, x1, xt = halves(grads_ref[slot])
        spread_out.append(
            jnp.concatenate(
                [
                    dot(
                        jnp.concatenate([main, xt], axis=1),
                        picker(extent, offsets_ref[1, p], c == 1, transposed=True),
                    ).astype(BF16)
                    for c, main in ((0, x0), (1, x1))
                ],
                axis=1,
            )
        )
    rows = jnp.concatenate(
        [row_picker((extent, width), -offsets_ref[0, p]) for p in range(positions)], axis=1
    )
    total = dot(rows, jnp.concatenate(spread_out, axis=0))
    out_ref[0, 0] = total[:, :extent]
    out_ref[0, 1] = total[:, extent:]


VMEM = pl.BlockSpec(memory_space=pltpu.VMEM)
SMEM = pl.BlockSpec(memory_space=pltpu.SMEM)
HBM = pl.BlockSpec(memory_space=pl.ANY)
PARAMS = pltpu.CompilerParams(vmem_limit_bytes=20 * 1024 * 1024)


def shards(objects, propagators, prop_index, probes, probe_group, offsets, measured):
    sections = lax.axis_size("cuts")
    width = probes.shape[-1]
    kinds = propagators.shape[0]
    near_rows = measured.shape[1]
    size = GROUP
    groups = sections // size
    rows = width + ROWS
    slots = slots_of(probe_group.shape[0], size)
    members = [list(range(first, first + size)) for first in range(0, sections, size)]

    def struct(*dims, kind=BF16):
        return jax.ShapeDtypeStruct(dims, kind)

    def exchanged(blocks):
        return lax.all_to_all(blocks, "cuts", 0, 0, axis_index_groups=members, tiled=True)

    def handed(block, stage, distance):
        route = [(stage * size + l, (stage + distance) * size + l) for l in slots]
        return lax.ppermute(block, "cuts", route)

    blocks = pl.pallas_call(
        window_kernel,
        out_shape=struct(size, rows, 2 * width),
        in_specs=[SMEM, SMEM, HBM, HBM],
        out_specs=VMEM,
        scratch_shapes=[
            pltpu.VMEM(objects.shape[1:], BF16),
            pltpu.VMEM(measured.shape, F32),
            pltpu.SemaphoreType.DMA((3,)),
        ],
        compiler_params=PARAMS,
        name="windows",
    )(offsets.T, prop_index, objects, measured)
    blocks = exchanged(blocks)

    wave = struct(width, 2 * width)
    near = struct(size * near_rows, 2 * LANES, kind=F32)
    waves_shape = struct(size + 1, width, 2 * width)
    grads_shape = struct(size, width, 2 * width)
    left_table = struct(kinds, 2 * width, width)
    square_table = struct(kinds, 2 * width, 2 * width)
    detector_left = struct(2, 2 * width, width)
    detector_right = struct(2, 2 * width, 2 * width)
    indices = pltpu.SMEM((size,), jnp.int32)

    def scratch(shape):
        return pltpu.VMEM(shape.shape, shape.dtype)

    def call(kernel, name, out_shape, in_specs, scratch_shapes, operands):
        return pl.pallas_call(
            kernel,
            out_shape=out_shape,
            in_specs=in_specs,
            out_specs=[VMEM] * len(out_shape),
            scratch_shapes=scratch_shapes,
            compiler_params=PARAMS,
            name=name,
        )(*operands)

    leaving, waves, lb, rf, rb, *dft = call(
        first_kernel,
        "first_forward",
        [wave, waves_shape, left_table, square_table, square_table]
        + [detector_left, detector_right, detector_right],
        [SMEM, HBM, VMEM, VMEM, VMEM],
        [pltpu.VMEM(probes.shape[1:], BF16), indices, pltpu.SemaphoreType.DMA],
        (probe_group, probes, blocks, propagators, jnp.asarray(dft_constant(width))),
    )
    entering = handed(leaving, 0, 1)
    (near_out,) = call(near_kernel, "near_rows", [near], [VMEM, HBM], [], (blocks, leaving))
    nears = [handed(near_out, stage, groups - 1 - stage) for stage in range(groups - 1)]
    for stage in range(1, groups):
        leaving, waves = call(
            forward_kernel(stage),
            "forward",
            [wave, waves_shape],
            [VMEM] * 5,
            [indices],
            (entering, blocks, propagators, rf, waves),
        )
        if stage < groups - 1:
            entering = handed(leaving, stage, 1)

    leaving, grads, lb, rb = call(
        middle_kernel(groups),
        "middle",
        [wave, grads_shape, left_table, square_table],
        [VMEM] * (groups + 7),
        [scratch(wave), pltpu.VMEM((width, 2 * LANES), F32), indices],
        (waves, *nears, blocks, propagators, lb, rb, *dft),
    )

    for stage in range(groups - 2, -1, -1):
        arriving = handed(leaving, stage + 1, -1)
        leaving, grads = call(
            backward_kernel(stage),
            "backward",
            [wave, grads_shape],
            [VMEM] * 6,
            [scratch(wave), indices],
            (arriving, waves, blocks, lb, rb, grads),
        )

    return pl.pallas_call(
        gather_kernel,
        out_shape=jax.ShapeDtypeStruct(objects.shape, F32),
        in_specs=[SMEM, VMEM],
        out_specs=VMEM,
        compiler_params=PARAMS,
        name="sum_windows",
    )(offsets.T, exchanged(grads))


def solution(mesh):
    in_specs = (
        P(("parts", "cuts"), None, None, None),
        P(),
        P(("parts", "cuts")),
        P(),
        P(),
        P("parts", None),
        P("parts", "cuts", None),
    )
    out_specs = P(("parts", "cuts"), None, None, None)
    return jax.shard_map(shards, mesh=mesh, in_specs=in_specs, out_specs=out_specs, check_vma=False)
```

```python
import math

import jax
import jax.numpy as jnp
import numpy as np
from jax import lax
from jax.experimental import pallas as pl
from jax.experimental.pallas import tpu as pltpu
from jax.sharding import PartitionSpec as P

TRANSMIT = 0.985
GROUP = 8
LANES = 128
ROWS = 16
F32 = jnp.float32
BF16 = jnp.bfloat16


def dot(former, latter):
    return jnp.dot(former, latter, preferred_element_type=F32)


def halves(x):
    return x[:, :LANES], x[:, LANES : 2 * LANES], x[:, 2 * LANES :]


def swapped(tail):
    return pltpu.roll(tail, LANES // 2, 1)


def low_half(rows):
    return lax.broadcasted_iota(jnp.int32, (rows, LANES), 1) < LANES // 2


def spread(tail):
    other = swapped(tail)
    low = low_half(tail.shape[0])
    return jnp.where(low, tail, other), jnp.where(low, other, tail)


def signed(tail, minus_low):
    low = low_half(tail.shape[0])
    return jnp.where(low == minus_low, -tail, tail)


def times(a, b):
    a0, a1, at = halves(a)
    b0, b1, bt = halves(b)
    b_real, b_imag = spread(bt)
    tail = at * b_real + signed(swapped(at), True) * b_imag
    return jnp.concatenate([a0 * b0 - a1 * b1, a1 * b0 + a0 * b1, tail], axis=1)


def times_conj(a, *others):
    a0, a1, at = halves(a)
    turned = signed(swapped(at), False)
    results = []
    for b in others:
        b0, b1, bt = halves(b)
        b_real, b_imag = spread(bt)
        tail = at * b_real + turned * b_imag
        results.append(jnp.concatenate([a0 * b0 + a1 * b1, a1 * b0 - a0 * b1, tail], axis=1))
    return results


def joined(both, conj):
    width = both.shape[0] // 2
    u0, u1, ut = halves(both[:width])
    v0, v1, vt = halves(both[width:])
    turned = signed(swapped(vt), not conj)
    if conj:
        return jnp.concatenate([u0 + v1, u1 - v0, ut + turned], axis=1)
    return jnp.concatenate([u0 - v1, u1 + v0, ut + turned], axis=1)


def with_mean(window):
    x = window.astype(F32)
    x0, x1, xt = halves(x)
    mean = jnp.where(low_half(xt.shape[0]), TRANSMIT, 0.0)
    return jnp.concatenate([TRANSMIT + x0, x1, mean + xt], axis=1)


def split2(x):
    high = x.astype(BF16)
    return high, (x - high.astype(F32)).astype(BF16)


def picker(columns, start, high_tail, transposed=False):
    shape = (2 * LANES, columns) if transposed else (columns, 2 * LANES)
    a = lax.broadcasted_iota(jnp.int32, shape, 1 if transposed else 0) - start
    q = lax.broadcasted_iota(jnp.int32, shape, 0 if transposed else 1)
    if high_tail:
        half = LANES // 2
        wanted = jnp.where(q < LANES, q, jnp.where(q < LANES + half, -columns, q - half))
    else:
        wanted = jnp.where(q < LANES + LANES // 2, q, -columns)
    return jnp.where(a == wanted, 1.0, 0.0).astype(BF16)


def row_picker(shape, distance):
    taken = lax.broadcasted_iota(jnp.int32, shape, 1)
    wanted = lax.broadcasted_iota(jnp.int32, shape, 0) + distance
    return jnp.where(taken == wanted, 1.0, 0.0).astype(BF16)


def packed(real, imag, columns, start):
    left = dot(real, picker(columns, start, False))
    right = dot(imag, picker(columns, start, True))
    return jnp.concatenate(
        [left[:, :LANES], right[:, :LANES], left[:, LANES:] + right[:, LANES:]], axis=1
    )


def dft_constant(width):
    counter = np.arange(width)
    angle = (counter[:, None] * counter[None, :] % width) * (2.0 * math.pi / width)
    return (np.stack([np.cos(angle), -np.sin(angle)]) / math.sqrt(width)).astype(np.float32)


def slots_of(positions, size):
    order = list(range(0, size, 2)) + list(range(1, size, 2))
    return sorted(order[:positions])


def partner(rank, size, r):
    return lax.bitwise_xor(lax.rem(rank, size), r)


def shuffled(pairs, sems):
    copies = [pltpu.make_async_copy(source, target, sems.at[n]) for n, (source, target) in enumerate(pairs)]
    for copy in copies:
        copy.start()
    for copy in copies:
        copy.wait()


def window_kernel(offsets_ref, index_ref, objects_in, measured_in, *refs):
    outs, (blocks, objects, measured, sems) = refs[:-4], refs[-4:]
    positions, near_rows, width = measured.shape
    extent = objects.shape[-1]
    copies = [
        pltpu.make_async_copy(objects_in.at[0, 0], objects.at[0], sems.at[0]),
        pltpu.make_async_copy(objects_in.at[0, 1], objects.at[1], sems.at[1]),
        pltpu.make_async_copy(measured_in, measured, sems.at[2]),
    ]
    for copy in copies:
        copy.start()
    tag = jnp.full((ROWS - near_rows, 2 * width), index_ref[0], jnp.int32).astype(F32)
    for copy in copies:
        copy.wait()
    field = jnp.concatenate([objects[0], objects[1]], axis=1)
    for p, slot in enumerate(slots_of(positions, blocks.shape[0])):
        both = dot(row_picker((width, extent), offsets_ref[0, p]), field).astype(BF16)
        window = packed(both[:, :extent], both[:, extent:], extent, offsets_ref[1, p])
        blocks[slot, :width, :] = window.astype(BF16)
        high = measured[p].astype(BF16).astype(F32)
        low = measured[p] - high
        seen = jnp.concatenate([high[:, :LANES], low[:, :LANES], high[:, LANES:], low[:, LANES:]], axis=1)
        blocks[slot, width:, :] = jnp.concatenate([seen, tag], axis=0).astype(BF16)
    shuffled([(blocks.at[partner(lax.axis_index("cuts"), len(outs), r)], out) for r, out in enumerate(outs)], sems)


def right_table(real, imag):
    width = real.shape[0]
    upper = packed(real, imag, width, 0)
    lower = packed(-imag, real, width, 0)
    return jnp.concatenate([upper[:LANES], lower[:LANES], upper[LANES:], lower[LANES:]], axis=0)


def transposed(plane):
    return plane.astype(F32).T.astype(BF16)


def forward_tables(props, rf):
    for k in range(props.shape[0]):
        rf[k] = right_table(transposed(props[k, 0]), transposed(props[k, 1])).astype(BF16)


def backward_tables(props, lb, rb):
    width = props.shape[-1]
    for k in range(props.shape[0]):
        real, imag = props[k, 0], props[k, 1]
        lb[k, :width, :] = transposed(real)
        lb[k, width:, :] = transposed(imag)
        rb[k] = right_table(real, -imag).astype(BF16)


def detector_tables(dft, left, right, right_conj):
    width = dft.shape[-1]
    for n, (real, imag) in enumerate(zip(split2(dft[0]), split2(dft[1]))):
        left[n, :width, :] = real
        left[n, width:, :] = imag
        right[n] = right_table(real, imag).astype(BF16)
        right_conj[n] = right_table(real, -imag).astype(BF16)


def forward_steps(blocks, waves, indices, lf, rf):
    sections, _, columns = blocks.shape
    width = columns // 2

    def step(k, carried):
        which = indices[k]
        z = times(waves[k].astype(F32), with_mean(blocks[k, :width, :])).astype(BF16)
        h = joined(dot(lf[which].reshape(columns, width), z), False).astype(BF16)
        waves[k + 1] = dot(h, rf[which]).astype(BF16)
        return carried

    lax.fori_loop(0, sections, step, 0, unroll=2)


def backward_steps(blocks, waves, indices, lb, rb, grads, g):
    sections, _, columns = blocks.shape
    width = columns // 2

    def step(n, carried):
        k = sections - 1 - n
        which = indices[k]
        c = joined(dot(lb[which], g[...]), True).astype(BF16)
        y = dot(c, rb[which])
        grad, passed = times_conj(y, waves[k].astype(F32), with_mean(blocks[k, :width, :]))
        grads[k] = grad.astype(BF16)
        g[...] = passed.astype(BF16)
        return carried

    lax.fori_loop(0, sections, step, 0, unroll=2)


def detector(psi, observed, left, right, right_conj):
    def product(ah, al, bh, bl):
        return dot(ah, bh) + (dot(ah, bl) + dot(al, bh))

    near = joined(dot(left[0], psi) + dot(left[1], psi), False)
    far = product(*split2(near), right[0], right[1])
    f0, f1, ft = halves(far)
    other = swapped(ft)
    main = f0 * f0 + f1 * f1 - observed[:, :LANES]
    tail = ft * ft + other * other - observed[:, LANES:]
    push = jnp.concatenate([main * f0, main * f1, tail * ft], axis=1)
    back = joined(product(left[0], left[1], *split2(push)), True)
    return product(*split2(back), right_conj[0], right_conj[1]).astype(BF16)


def read_indices(blocks, indices, count):
    for k in range(blocks.shape[0]):
        tag = jnp.max(blocks[k, -ROWS:, :LANES].astype(F32)[ROWS - 1 :])
        indices[k] = jnp.clip(tag.astype(jnp.int32), 0, count - 1)


def place_in(size):
    rank = lax.axis_index("cuts")
    return lax.rem(rank, size), lax.div(rank, size)


def observe(blocks, near_rows, observed, first):
    for k in range(blocks.shape[0]):
        high, low, tail = halves(blocks[k, -ROWS:, :].astype(F32))
        rows = jnp.concatenate([high + low, tail + swapped(tail)], axis=1)
        at = first + k * near_rows
        observed[at : at + near_rows, :] = rows[:near_rows]


def near_kernel(blocks, _, near):
    observe(blocks, near.shape[0] // blocks.shape[0], near, 0)


def first_kernel(group_ref, probes, props, dft, *refs):
    blocks_in, refs = refs[:-13], refs[-13:]
    leaving, blocks, waves, lb, rf, rb, left, right, right_conj, probe, indices, sem, sems = refs
    size = blocks.shape[0]
    shifts = [
        pltpu.make_async_copy(block, blocks.at[partner(lax.axis_index("cuts"), size, r)], sems.at[r])
        for r, block in enumerate(blocks_in)
    ]
    for shift in shifts:
        shift.start()
    slot, group = place_in(size)

    @pl.when(group == 0)
    def _():
        position = 0
        for p, held in enumerate(slots_of(group_ref.shape[0], size)):
            position = jnp.where(slot == held, p, position)
        which = group_ref[position]
        copy = pltpu.make_async_copy(probes.at[which], probe, sem)
        copy.start()
        forward_tables(props, rf)
        for shift in shifts:
            shift.wait()
        read_indices(blocks, indices, props.shape[0])
        copy.wait()
        waves[0] = packed(probe[0], probe[1], probe.shape[-1], 0).astype(BF16)
        forward_steps(blocks, waves, indices, props, rf)
        leaving[...] = waves[size]

    @pl.when(group > 0)
    def _():
        forward_tables(props, rf)
        backward_tables(props, lb, rb)
        detector_tables(dft, left, right, right_conj)
        for shift in shifts:
            shift.wait()


def forward_kernel(stage):
    def kernel(entering, blocks, props, rf, waves_in, leaving, waves, indices):
        size = blocks.shape[0]
        _, group = place_in(size)

        @pl.when(group == stage)
        def _():
            read_indices(blocks, indices, props.shape[0])
            waves[0] = entering[...]
            forward_steps(blocks, waves, indices, props, rf)
            leaving[...] = waves[size]

        @pl.when(group != stage)
        def _():
            waves[...] = waves_in[...]

    return kernel


def middle_kernel(groups):
    def kernel(waves, *refs):
        earlier, refs = refs[: groups - 1], refs[groups - 1 :]
        blocks, props, lb, rb, left, right, right_conj, leaving, grads, lb_out, rb_out, g, observed, indices = refs
        size = blocks.shape[0]
        _, group = place_in(size)

        @pl.when(group == groups - 1)
        def _():
            read_indices(blocks, indices, props.shape[0])
            rows = earlier[0].shape[0]
            for n, near in enumerate(earlier):
                observed[n * rows : (n + 1) * rows, :] = near[...]
            observe(blocks, rows // size, observed, (groups - 1) * rows)
            g[...] = detector(waves[size], observed[...], left, right, right_conj)
            backward_steps(blocks, waves, indices, lb, rb, grads, g)
            leaving[...] = g[...]

        @pl.when(group < groups - 1)
        def _():
            backward_tables(props, lb_out, rb_out)

    return kernel


def backward_kernel(stage):
    def kernel(arriving, waves, blocks, lb, rb, grads_in, leaving, *refs):
        outs, (grads, g, indices, sems) = refs[:-4], refs[-4:]
        size = blocks.shape[0]
        _, group = place_in(size)
        order = [partner(lax.axis_index("cuts"), size, r) if stage == 0 else r for r in range(size)]

        @pl.when(group == stage)
        def _():
            read_indices(blocks, indices, lb.shape[0])
            g[...] = arriving[...]
            backward_steps(blocks, waves, indices, lb, rb, grads, g)
            leaving[...] = g[...]
            shuffled([(grads.at[order[r]], out) for r, out in enumerate(outs)], sems)

        @pl.when(group != stage)
        def _():
            shuffled([(grads_in.at[order[r]], out) for r, out in enumerate(outs)], sems)

    return kernel


def gather_kernel(offsets_ref, *refs):
    grads_in, (out_ref, grads, sems) = refs[:-3], refs[-3:]
    size = len(grads_in)
    rank = lax.axis_index("cuts")
    shuffled([(block, grads.at[partner(rank, size, r)]) for r, block in enumerate(grads_in)], sems)
    positions = offsets_ref.shape[1]
    width = grads.shape[1]
    extent = out_ref.shape[-1]
    spread_out = []
    for p, slot in enumerate(slots_of(positions, size)):
        x0, x1, xt = halves(grads[slot])
        spread_out.append(
            jnp.concatenate(
                [
                    dot(
                        jnp.concatenate([main, xt], axis=1),
                        picker(extent, offsets_ref[1, p], c == 1, transposed=True),
                    ).astype(BF16)
                    for c, main in ((0, x0), (1, x1))
                ],
                axis=1,
            )
        )
    rows = jnp.concatenate(
        [row_picker((extent, width), -offsets_ref[0, p]) for p in range(positions)], axis=1
    )
    total = dot(rows, jnp.concatenate(spread_out, axis=0))
    out_ref[0, 0] = total[:, :extent]
    out_ref[0, 1] = total[:, extent:]


VMEM = pl.BlockSpec(memory_space=pltpu.VMEM)
SMEM = pl.BlockSpec(memory_space=pltpu.SMEM)
HBM = pl.BlockSpec(memory_space=pl.ANY)
PARAMS = pltpu.CompilerParams(vmem_limit_bytes=20 * 1024 * 1024)


def shards(objects, propagators, prop_index, probes, probe_group, offsets, measured):
    sections = lax.axis_size("cuts")
    width = probes.shape[-1]
    kinds = propagators.shape[0]
    near_rows = measured.shape[1]
    size = GROUP
    groups = sections // size
    rows = width + ROWS
    slots = slots_of(probe_group.shape[0], size)

    def struct(*dims, kind=BF16):
        return jax.ShapeDtypeStruct(dims, kind)

    def exchanged(blocks, inward):
        results = list(blocks)
        for r in sorted(range(1, size), key=lambda r: (r % 2, -r)):
            route = [
                (first + l, first + (l ^ r))
                for first in range(0, sections, size)
                for l in range(size)
                if (l ^ r if inward else l) in slots
            ]
            results[r] = lax.ppermute(blocks[r], "cuts", route)
        return results

    def handed(block, stage, distance):
        route = [(stage * size + l, (stage + distance) * size + l) for l in slots]
        return lax.ppermute(block, "cuts", route)

    blocks = pl.pallas_call(
        window_kernel,
        out_shape=[struct(rows, 2 * width)] * size,
        in_specs=[SMEM, SMEM, HBM, HBM],
        out_specs=[VMEM] * size,
        scratch_shapes=[
            pltpu.VMEM((size, rows, 2 * width), BF16),
            pltpu.VMEM(objects.shape[1:], BF16),
            pltpu.VMEM(measured.shape, F32),
            pltpu.SemaphoreType.DMA((size,)),
        ],
        compiler_params=PARAMS,
        name="windows",
    )(offsets.T, prop_index, objects, measured)
    blocks = exchanged(blocks, True)

    wave = struct(width, 2 * width)
    near = struct(size * near_rows, 2 * LANES, kind=F32)
    waves_shape = struct(size + 1, width, 2 * width)
    grads_shape = struct(size, width, 2 * width)
    left_table = struct(kinds, 2 * width, width)
    square_table = struct(kinds, 2 * width, 2 * width)
    detector_left = struct(2, 2 * width, width)
    detector_right = struct(2, 2 * width, 2 * width)
    indices = pltpu.SMEM((size,), jnp.int32)

    def scratch(shape):
        return pltpu.VMEM(shape.shape, shape.dtype)

    def call(kernel, name, out_shape, in_specs, scratch_shapes, operands):
        return pl.pallas_call(
            kernel,
            out_shape=out_shape,
            in_specs=in_specs,
            out_specs=[VMEM] * len(out_shape),
            scratch_shapes=scratch_shapes,
            compiler_params=PARAMS,
            name=name,
        )(*operands)

    leaving, blocks, waves, lb, rf, rb, *dft = call(
        first_kernel,
        "first_forward",
        [wave, struct(size, rows, 2 * width), waves_shape, left_table, square_table, square_table]
        + [detector_left, detector_right, detector_right],
        [SMEM, HBM, VMEM, VMEM] + [VMEM] * size,
        [pltpu.VMEM(probes.shape[1:], BF16), indices, pltpu.SemaphoreType.DMA, pltpu.SemaphoreType.DMA((size,))],
        (probe_group, probes, propagators, jnp.asarray(dft_constant(width)), *blocks),
    )
    entering = handed(leaving, 0, 1)
    (near_out,) = call(near_kernel, "near_rows", [near], [VMEM, HBM], [], (blocks, leaving))
    nears = [handed(near_out, stage, groups - 1 - stage) for stage in range(groups - 1)]
    for stage in range(1, groups):
        leaving, waves = call(
            forward_kernel(stage),
            "forward",
            [wave, waves_shape],
            [VMEM] * 5,
            [indices],
            (entering, blocks, propagators, rf, waves),
        )
        if stage < groups - 1:
            entering = handed(leaving, stage, 1)

    leaving, grads, lb, rb = call(
        middle_kernel(groups),
        "middle",
        [wave, grads_shape, left_table, square_table],
        [VMEM] * (groups + 7),
        [scratch(wave), pltpu.VMEM((width, 2 * LANES), F32), indices],
        (waves, *nears, blocks, propagators, lb, rb, *dft),
    )

    for stage in range(groups - 2, -1, -1):
        arriving = handed(leaving, stage + 1, -1)
        last = stage == 0
        leaving, *grads = call(
            backward_kernel(stage),
            "backward",
            [wave] + [struct(width, 2 * width)] * size,
            [VMEM] * 6,
            [scratch(grads_shape), scratch(wave), indices, pltpu.SemaphoreType.DMA((size,))],
            (arriving, waves, blocks, lb, rb, grads),
        )
        if not last:
            grads = jnp.stack(grads)

    return call(
        gather_kernel,
        "sum_windows",
        [struct(*objects.shape, kind=F32)],
        [SMEM] + [VMEM] * size,
        [scratch(grads_shape), pltpu.SemaphoreType.DMA((size,))],
        (offsets.T, *exchanged(grads, False)),
    )[0]


def solution(mesh):
    in_specs = (
        P(("parts", "cuts"), None, None, None),
        P(),
        P(("parts", "cuts")),
        P(),
        P(),
        P("parts", None),
        P("parts", "cuts", None),
    )
    out_specs = P(("parts", "cuts"), None, None, None)
    return jax.shard_map(shards, mesh=mesh, in_specs=in_specs, out_specs=out_specs, check_vma=False)
```

```python
import math

import jax
import jax.numpy as jnp
import numpy as np
from jax import lax
from jax.experimental import pallas as pl
from jax.experimental.pallas import tpu as pltpu
from jax.sharding import PartitionSpec as P

TRANSMIT = 0.985
GROUP = 8
LANES = 128
ROWS = 16
F32 = jnp.float32
BF16 = jnp.bfloat16


def dot(former, latter):
    return jnp.dot(former, latter, preferred_element_type=F32)


def halves(x):
    return x[:, :LANES], x[:, LANES : 2 * LANES], x[:, 2 * LANES :]


def swapped(tail):
    return pltpu.roll(tail, LANES // 2, 1)


def low_half(rows):
    return lax.broadcasted_iota(jnp.int32, (rows, LANES), 1) < LANES // 2


def spread(tail):
    other = swapped(tail)
    low = low_half(tail.shape[0])
    return jnp.where(low, tail, other), jnp.where(low, other, tail)


def signed(tail, minus_low):
    low = low_half(tail.shape[0])
    return jnp.where(low == minus_low, -tail, tail)


def times(a, b):
    a0, a1, at = halves(a)
    b0, b1, bt = halves(b)
    b_real, b_imag = spread(bt)
    tail = at * b_real + signed(swapped(at), True) * b_imag
    return jnp.concatenate([a0 * b0 - a1 * b1, a1 * b0 + a0 * b1, tail], axis=1)


def times_conj(a, *others):
    a0, a1, at = halves(a)
    turned = signed(swapped(at), False)
    results = []
    for b in others:
        b0, b1, bt = halves(b)
        b_real, b_imag = spread(bt)
        tail = at * b_real + turned * b_imag
        results.append(jnp.concatenate([a0 * b0 + a1 * b1, a1 * b0 - a0 * b1, tail], axis=1))
    return results


def joined(both, conj):
    width = both.shape[0] // 2
    u0, u1, ut = halves(both[:width])
    v0, v1, vt = halves(both[width:])
    turned = signed(swapped(vt), not conj)
    if conj:
        return jnp.concatenate([u0 + v1, u1 - v0, ut + turned], axis=1)
    return jnp.concatenate([u0 - v1, u1 + v0, ut + turned], axis=1)


def with_mean(window):
    x = window.astype(F32)
    x0, x1, xt = halves(x)
    mean = jnp.where(low_half(xt.shape[0]), TRANSMIT, 0.0)
    return jnp.concatenate([TRANSMIT + x0, x1, mean + xt], axis=1)


def split2(x):
    high = x.astype(BF16)
    return high, (x - high.astype(F32)).astype(BF16)


def picker(columns, start, high_tail, transposed=False):
    shape = (2 * LANES, columns) if transposed else (columns, 2 * LANES)
    a = lax.broadcasted_iota(jnp.int32, shape, 1 if transposed else 0) - start
    q = lax.broadcasted_iota(jnp.int32, shape, 0 if transposed else 1)
    if high_tail:
        half = LANES // 2
        wanted = jnp.where(q < LANES, q, jnp.where(q < LANES + half, -columns, q - half))
    else:
        wanted = jnp.where(q < LANES + LANES // 2, q, -columns)
    return jnp.where(a == wanted, 1.0, 0.0).astype(BF16)


def row_picker(shape, distance):
    taken = lax.broadcasted_iota(jnp.int32, shape, 1)
    wanted = lax.broadcasted_iota(jnp.int32, shape, 0) + distance
    return jnp.where(taken == wanted, 1.0, 0.0).astype(BF16)


def packed(real, imag, columns, start):
    left = dot(real, picker(columns, start, False))
    right = dot(imag, picker(columns, start, True))
    return jnp.concatenate(
        [left[:, :LANES], right[:, :LANES], left[:, LANES:] + right[:, LANES:]], axis=1
    )


def dft_constant(width):
    counter = np.arange(width)
    angle = (counter[:, None] * counter[None, :] % width) * (2.0 * math.pi / width)
    return (np.stack([np.cos(angle), -np.sin(angle)]) / math.sqrt(width)).astype(np.float32)


def slots_of(positions, size):
    order = list(range(0, size, 2)) + list(range(1, size, 2))
    return sorted(order[:positions])


def window_kernel(offsets_in, index_ref, objects_in, measured_in, blocks, offsets_ref, objects, measured, sems):
    positions, near_rows, width = measured.shape
    extent = objects.shape[-1]
    copies = [
        pltpu.make_async_copy(objects_in.at[0, 0], objects.at[0], sems.at[0]),
        pltpu.make_async_copy(objects_in.at[0, 1], objects.at[1], sems.at[1]),
        pltpu.make_async_copy(measured_in, measured, sems.at[2]),
        pltpu.make_async_copy(offsets_in, offsets_ref, sems.at[3]),
    ]
    for copy in copies:
        copy.start()
    tag = jnp.full((ROWS - near_rows, 2 * width), index_ref[0], jnp.int32).astype(F32)
    for copy in copies:
        copy.wait()
    field = jnp.concatenate([objects[0], objects[1]], axis=1)
    for p, slot in enumerate(slots_of(positions, blocks.shape[0])):
        both = dot(row_picker((width, extent), offsets_ref[0, p]), field).astype(BF16)
        window = packed(both[:, :extent], both[:, extent:], extent, offsets_ref[1, p])
        blocks[slot, :width, :] = window.astype(BF16)
        high = measured[p].astype(BF16).astype(F32)
        low = measured[p] - high
        seen = jnp.concatenate([high[:, :LANES], low[:, :LANES], high[:, LANES:], low[:, LANES:]], axis=1)
        blocks[slot, width:, :] = jnp.concatenate([seen, tag], axis=0).astype(BF16)


def right_table(real, imag):
    width = real.shape[0]
    upper = packed(real, imag, width, 0)
    lower = packed(-imag, real, width, 0)
    return jnp.concatenate([upper[:LANES], lower[:LANES], upper[LANES:], lower[LANES:]], axis=0)


def transposed(plane):
    return plane.astype(F32).T.astype(BF16)


def forward_tables(props, rf):
    for k in range(props.shape[0]):
        rf[k] = right_table(transposed(props[k, 0]), transposed(props[k, 1])).astype(BF16)


def backward_tables(props, lb, rb):
    width = props.shape[-1]
    for k in range(props.shape[0]):
        real, imag = props[k, 0], props[k, 1]
        lb[k, :width, :] = transposed(real)
        lb[k, width:, :] = transposed(imag)
        rb[k] = right_table(real, -imag).astype(BF16)


def detector_tables(dft, left, right, right_conj):
    width = dft.shape[-1]
    for n, (real, imag) in enumerate(zip(split2(dft[0]), split2(dft[1]))):
        left[n, :width, :] = real
        left[n, width:, :] = imag
        right[n] = right_table(real, imag).astype(BF16)
        right_conj[n] = right_table(real, -imag).astype(BF16)


def forward_steps(blocks, waves, indices, lf, rf):
    sections, _, columns = blocks.shape
    width = columns // 2

    def step(k, carried):
        which = indices[k]
        z = times(waves[k].astype(F32), with_mean(blocks[k, :width, :])).astype(BF16)
        h = joined(dot(lf[which].reshape(columns, width), z), False).astype(BF16)
        waves[k + 1] = dot(h, rf[which]).astype(BF16)
        return carried

    lax.fori_loop(0, sections, step, 0, unroll=True)


def backward_steps(blocks, waves, indices, lb, rb, grads, g):
    sections, _, columns = blocks.shape
    width = columns // 2

    def step(n, carried):
        k = sections - 1 - n
        which = indices[k]
        c = joined(dot(lb[which], g[...]), True).astype(BF16)
        y = dot(c, rb[which])
        grad, passed = times_conj(y, waves[k].astype(F32), with_mean(blocks[k, :width, :]))
        grads[k] = grad.astype(BF16)
        g[...] = passed.astype(BF16)
        return carried

    lax.fori_loop(0, sections, step, 0, unroll=True)


def detector(psi, observed, left, right, right_conj):
    def product(ah, al, bh, bl):
        return dot(ah, bh) + (dot(ah, bl) + dot(al, bh))

    near = joined(dot(left[0], psi) + dot(left[1], psi), False)
    far = product(*split2(near), right[0], right[1])
    f0, f1, ft = halves(far)
    other = swapped(ft)
    main = f0 * f0 + f1 * f1 - observed[:, :LANES]
    tail = ft * ft + other * other - observed[:, LANES:]
    push = jnp.concatenate([main * f0, main * f1, tail * ft], axis=1)
    back = joined(product(left[0], left[1], *split2(push)), True)
    return product(*split2(back), right_conj[0], right_conj[1]).astype(BF16)


def read_indices(blocks, indices, count):
    for k in range(blocks.shape[0]):
        tag = jnp.max(blocks[k, -ROWS:, :LANES].astype(F32)[ROWS - 1 :])
        indices[k] = jnp.clip(tag.astype(jnp.int32), 0, count - 1)


def place_in(size):
    rank = lax.axis_index("cuts")
    return lax.rem(rank, size), lax.div(rank, size)


def observe(blocks, near_rows, observed, first):
    for k in range(blocks.shape[0]):
        high, low, tail = halves(blocks[k, -ROWS:, :].astype(F32))
        rows = jnp.concatenate([high + low, tail + swapped(tail)], axis=1)
        at = first + k * near_rows
        observed[at : at + near_rows, :] = rows[:near_rows]


def near_kernel(blocks, _, near):
    observe(blocks, near.shape[0] // blocks.shape[0], near, 0)


def first_kernel(group_ref, probes, blocks, props, dft, leaving, waves, lb, rf, rb, left, right, right_conj, probe, indices, sem):
    size = blocks.shape[0]
    slot, group = place_in(size)

    @pl.when(group == 0)
    def _():
        position = 0
        for p, held in enumerate(slots_of(group_ref.shape[0], size)):
            position = jnp.where(slot == held, p, position)
        which = group_ref[position]
        copy = pltpu.make_async_copy(probes.at[which], probe, sem)
        copy.start()
        forward_tables(props, rf)
        read_indices(blocks, indices, props.shape[0])
        copy.wait()
        waves[0] = packed(probe[0], probe[1], probe.shape[-1], 0).astype(BF16)
        forward_steps(blocks, waves, indices, props, rf)
        leaving[...] = waves[size]

    @pl.when(group > 0)
    def _():
        forward_tables(props, rf)
        backward_tables(props, lb, rb)
        detector_tables(dft, left, right, right_conj)


def forward_kernel(stage):
    def kernel(entering, blocks, props, rf, waves_in, leaving, waves, indices):
        size = blocks.shape[0]
        _, group = place_in(size)

        @pl.when(group == stage)
        def _():
            read_indices(blocks, indices, props.shape[0])
            waves[0] = entering[...]
            forward_steps(blocks, waves, indices, props, rf)
            leaving[...] = waves[size]

        @pl.when(group != stage)
        def _():
            waves[...] = waves_in[...]

    return kernel


def middle_kernel(groups):
    def kernel(waves, *refs):
        earlier, refs = refs[: groups - 1], refs[groups - 1 :]
        blocks, props, lb, rb, left, right, right_conj, leaving, grads, lb_out, rb_out, g, observed, indices = refs
        size = blocks.shape[0]
        _, group = place_in(size)

        @pl.when(group == groups - 1)
        def _():
            read_indices(blocks, indices, props.shape[0])
            rows = earlier[0].shape[0]
            for n, near in enumerate(earlier):
                observed[n * rows : (n + 1) * rows, :] = near[...]
            observe(blocks, rows // size, observed, (groups - 1) * rows)
            g[...] = detector(waves[size], observed[...], left, right, right_conj)
            backward_steps(blocks, waves, indices, lb, rb, grads, g)
            leaving[...] = g[...]

        @pl.when(group < groups - 1)
        def _():
            backward_tables(props, lb_out, rb_out)

    return kernel


def backward_kernel(stage):
    def kernel(arriving, waves, blocks, lb, rb, grads_in, leaving, grads, g, indices):
        _, group = place_in(blocks.shape[0])

        @pl.when(group == stage)
        def _():
            read_indices(blocks, indices, lb.shape[0])
            g[...] = arriving[...]
            backward_steps(blocks, waves, indices, lb, rb, grads, g)
            leaving[...] = g[...]

        @pl.when(group != stage)
        def _():
            grads[...] = grads_in[...]

    return kernel


def gather_kernel(offsets_ref, grads_ref, out_ref):
    positions = offsets_ref.shape[1]
    width = grads_ref.shape[1]
    extent = out_ref.shape[-1]
    spread_out = []
    for p, slot in enumerate(slots_of(positions, grads_ref.shape[0])):
        x0, x1, xt = halves(grads_ref[slot])
        spread_out.append(
            jnp.concatenate(
                [
                    dot(
                        jnp.concatenate([main, xt], axis=1),
                        picker(extent, offsets_ref[1, p], c == 1, transposed=True),
                    ).astype(BF16)
                    for c, main in ((0, x0), (1, x1))
                ],
                axis=1,
            )
        )
    rows = jnp.concatenate(
        [row_picker((extent, width), -offsets_ref[0, p]) for p in range(positions)], axis=1
    )
    total = dot(rows, jnp.concatenate(spread_out, axis=0))
    out_ref[0, 0] = total[:, :extent]
    out_ref[0, 1] = total[:, extent:]


VMEM = pl.BlockSpec(memory_space=pltpu.VMEM)
SMEM = pl.BlockSpec(memory_space=pltpu.SMEM)
HBM = pl.BlockSpec(memory_space=pl.ANY)
ALONE = pltpu.CompilerParams(vmem_limit_bytes=60 * 1024 * 1024)
PARAMS = pltpu.CompilerParams(vmem_limit_bytes=20 * 1024 * 1024)


def shards(objects, propagators, prop_index, probes, probe_group, offsets, measured):
    sections = lax.axis_size("cuts")
    width = probes.shape[-1]
    kinds = propagators.shape[0]
    near_rows = measured.shape[1]
    size = GROUP
    groups = sections // size
    rows = width + ROWS
    slots = slots_of(probe_group.shape[0], size)
    members = [list(range(first, first + size)) for first in range(0, sections, size)]

    def struct(*dims, kind=BF16):
        return jax.ShapeDtypeStruct(dims, kind)

    def exchanged(blocks):
        return lax.all_to_all(blocks, "cuts", 0, 0, axis_index_groups=members, tiled=True)

    def handed(block, stage, distance):
        route = [(stage * size + l, (stage + distance) * size + l) for l in slots]
        return lax.ppermute(block, "cuts", route)

    blocks = pl.pallas_call(
        window_kernel,
        out_shape=struct(size, rows, 2 * width),
        in_specs=[HBM, SMEM, HBM, HBM],
        out_specs=VMEM,
        scratch_shapes=[
            pltpu.SMEM(offsets.shape[::-1], jnp.int32),
            pltpu.VMEM(objects.shape[1:], BF16),
            pltpu.VMEM(measured.shape, F32),
            pltpu.SemaphoreType.DMA((4,)),
        ],
        compiler_params=ALONE,
        name="windows",
    )(offsets.T, prop_index, objects, measured)
    blocks = exchanged(blocks)

    wave = struct(width, 2 * width)
    near = struct(size * near_rows, 2 * LANES, kind=F32)
    waves_shape = struct(size + 1, width, 2 * width)
    grads_shape = struct(size, width, 2 * width)
    left_table = struct(kinds, 2 * width, width)
    square_table = struct(kinds, 2 * width, 2 * width)
    detector_left = struct(2, 2 * width, width)
    detector_right = struct(2, 2 * width, 2 * width)
    indices = pltpu.SMEM((size,), jnp.int32)

    def scratch(shape):
        return pltpu.VMEM(shape.shape, shape.dtype)

    def call(kernel, name, out_shape, in_specs, scratch_shapes, operands):
        return pl.pallas_call(
            kernel,
            out_shape=out_shape,
            in_specs=in_specs,
            out_specs=[VMEM] * len(out_shape),
            scratch_shapes=scratch_shapes,
            compiler_params=PARAMS,
            name=name,
        )(*operands)

    leaving, waves, lb, rf, rb, *dft = call(
        first_kernel,
        "first_forward",
        [wave, waves_shape, left_table, square_table, square_table]
        + [detector_left, detector_right, detector_right],
        [SMEM, HBM, VMEM, VMEM, VMEM],
        [pltpu.VMEM(probes.shape[1:], BF16), indices, pltpu.SemaphoreType.DMA],
        (probe_group, probes, blocks, propagators, jnp.asarray(dft_constant(width))),
    )
    entering = handed(leaving, 0, 1)
    (near_out,) = call(near_kernel, "near_rows", [near], [VMEM, HBM], [], (blocks, leaving))
    nears = [handed(near_out, stage, groups - 1 - stage) for stage in range(groups - 1)]
    for stage in range(1, groups):
        leaving, waves = call(
            forward_kernel(stage),
            "forward",
            [wave, waves_shape],
            [VMEM] * 5,
            [indices],
            (entering, blocks, propagators, rf, waves),
        )
        if stage < groups - 1:
            entering = handed(leaving, stage, 1)

    leaving, grads, lb, rb = call(
        middle_kernel(groups),
        "middle",
        [wave, grads_shape, left_table, square_table],
        [VMEM] * (groups + 7),
        [scratch(wave), pltpu.VMEM((width, 2 * LANES), F32), indices],
        (waves, *nears, blocks, propagators, lb, rb, *dft),
    )

    for stage in range(groups - 2, -1, -1):
        arriving = handed(leaving, stage + 1, -1)
        leaving, grads = call(
            backward_kernel(stage),
            "backward",
            [wave, grads_shape],
            [VMEM] * 6,
            [scratch(wave), indices],
            (arriving, waves, blocks, lb, rb, grads),
        )

    return pl.pallas_call(
        gather_kernel,
        out_shape=jax.ShapeDtypeStruct(objects.shape, F32),
        in_specs=[SMEM, VMEM],
        out_specs=VMEM,
        compiler_params=PARAMS,
        name="sum_windows",
    )(offsets.T, exchanged(grads))


def solution(mesh):
    in_specs = (
        P(("parts", "cuts"), None, None, None),
        P(),
        P(("parts", "cuts")),
        P(),
        P(),
        P("parts", None),
        P("parts", "cuts", None),
    )
    out_specs = P(("parts", "cuts"), None, None, None)
    return jax.shard_map(shards, mesh=mesh, in_specs=in_specs, out_specs=out_specs, check_vma=False)
```

```python
import math

import jax
import jax.numpy as jnp
import numpy as np
from jax import lax
from jax.experimental import pallas as pl
from jax.experimental.pallas import tpu as pltpu
from jax.sharding import PartitionSpec as P

TRANSMIT = 0.985
GROUP = 8
LANES = 128
ROWS = 16
F32 = jnp.float32
BF16 = jnp.bfloat16


def dot(former, latter):
    return jnp.dot(former, latter, preferred_element_type=F32)


def halves(x):
    return x[:, :LANES], x[:, LANES : 2 * LANES], x[:, 2 * LANES :]


def swapped(tail):
    return pltpu.roll(tail, LANES // 2, 1)


def low_half(rows):
    return lax.broadcasted_iota(jnp.int32, (rows, LANES), 1) < LANES // 2


def spread(tail):
    other = swapped(tail)
    low = low_half(tail.shape[0])
    return jnp.where(low, tail, other), jnp.where(low, other, tail)


def signed(tail, minus_low):
    low = low_half(tail.shape[0])
    return jnp.where(low == minus_low, -tail, tail)


def times(a, b):
    a0, a1, at = halves(a)
    b0, b1, bt = halves(b)
    b_real, b_imag = spread(bt)
    tail = at * b_real + signed(swapped(at), True) * b_imag
    return jnp.concatenate([a0 * b0 - a1 * b1, a1 * b0 + a0 * b1, tail], axis=1)


def times_conj(a, *others):
    a0, a1, at = halves(a)
    turned = signed(swapped(at), False)
    results = []
    for b in others:
        b0, b1, bt = halves(b)
        b_real, b_imag = spread(bt)
        tail = at * b_real + turned * b_imag
        results.append(jnp.concatenate([a0 * b0 + a1 * b1, a1 * b0 - a0 * b1, tail], axis=1))
    return results


def joined(both, conj):
    width = both.shape[0] // 2
    u0, u1, ut = halves(both[:width])
    v0, v1, vt = halves(both[width:])
    turned = signed(swapped(vt), not conj)
    if conj:
        return jnp.concatenate([u0 + v1, u1 - v0, ut + turned], axis=1)
    return jnp.concatenate([u0 - v1, u1 + v0, ut + turned], axis=1)


def with_mean(window):
    x = window.astype(F32)
    x0, x1, xt = halves(x)
    mean = jnp.where(low_half(xt.shape[0]), TRANSMIT, 0.0)
    return jnp.concatenate([TRANSMIT + x0, x1, mean + xt], axis=1)


def split2(x):
    high = x.astype(BF16)
    return high, (x - high.astype(F32)).astype(BF16)


def picker(columns, start, high_tail, transposed=False):
    shape = (2 * LANES, columns) if transposed else (columns, 2 * LANES)
    a = lax.broadcasted_iota(jnp.int32, shape, 1 if transposed else 0) - start
    q = lax.broadcasted_iota(jnp.int32, shape, 0 if transposed else 1)
    if high_tail:
        half = LANES // 2
        wanted = jnp.where(q < LANES, q, jnp.where(q < LANES + half, -columns, q - half))
    else:
        wanted = jnp.where(q < LANES + LANES // 2, q, -columns)
    return jnp.where(a == wanted, 1.0, 0.0).astype(BF16)


def row_picker(shape, distance):
    taken = lax.broadcasted_iota(jnp.int32, shape, 1)
    wanted = lax.broadcasted_iota(jnp.int32, shape, 0) + distance
    return jnp.where(taken == wanted, 1.0, 0.0).astype(BF16)


def rows_near(x, start, count):
    limit = x.shape[0] - count
    bit = 1 << (limit.bit_length() - 1)
    while bit >= ROWS:
        length = count + bit
        short = bit + length - x.shape[0]
        if short > 0:
            x = jnp.concatenate([x, jnp.zeros((short, x.shape[1]), x.dtype)], axis=0)
        x = jnp.where(lax.bitwise_and(start, bit) != 0, x[bit : bit + length], x[:length])
        bit //= 2
    return x


def packed(real, imag, columns, start):
    left = dot(real, picker(columns, start, False))
    right = dot(imag, picker(columns, start, True))
    return jnp.concatenate(
        [left[:, :LANES], right[:, :LANES], left[:, LANES:] + right[:, LANES:]], axis=1
    )


def dft_constant(width):
    counter = np.arange(width)
    angle = (counter[:, None] * counter[None, :] % width) * (2.0 * math.pi / width)
    return (np.stack([np.cos(angle), -np.sin(angle)]) / math.sqrt(width)).astype(np.float32)


def slots_of(positions, size):
    order = list(range(0, size, 2)) + list(range(size - 1, 0, -2))
    return sorted(order[:positions])


def window_kernel(offsets_in, index_ref, objects_in, measured_in, blocks_out, blocks, offsets_ref, objects, measured, sems):
    positions, near_rows, width = measured.shape
    extent = objects.shape[-1]
    copies = [
        pltpu.make_async_copy(objects_in.at[0, 0], objects.at[0], sems.at[0]),
        pltpu.make_async_copy(objects_in.at[0, 1], objects.at[1], sems.at[1]),
        pltpu.make_async_copy(measured_in, measured, sems.at[2]),
        pltpu.make_async_copy(offsets_in, offsets_ref, sems.at[3]),
    ]
    for copy in copies:
        copy.start()
    tag = jnp.full((ROWS, LANES), index_ref[0], jnp.int32).astype(F32)
    for copy in copies:
        copy.wait()
    sending = []
    for p, slot in enumerate(slots_of(positions, blocks.shape[0])):
        start = offsets_ref[0, p]
        real, imag = (rows_near(objects[c], start, width) for c in range(2))
        window = packed(real, imag, extent, offsets_ref[1, p]).astype(BF16)
        shift = lax.bitwise_and(start, ROWS - 1)
        blocks[slot, :width, :] = dot(row_picker((width, width + ROWS), shift), window).astype(BF16)
        tail = measured[p, :, LANES:]
        seen = jnp.concatenate([measured[p, :, :LANES], tail, tail, tag[:near_rows]], axis=1)
        left_over = jnp.concatenate([tag[near_rows:]] * 3, axis=1)
        blocks[slot, width:, :] = jnp.concatenate([seen, left_over], axis=0).astype(BF16)
        sending.append(pltpu.make_async_copy(blocks.at[slot], blocks_out.at[slot], sems.at[4 + p]))
        sending[-1].start()
    for copy in sending:
        copy.wait()


def right_table(real, imag):
    width = real.shape[0]
    upper = packed(real, imag, width, 0)
    lower = packed(-imag, real, width, 0)
    return jnp.concatenate([upper[:LANES], lower[:LANES], upper[LANES:], lower[LANES:]], axis=0)


def transposed(plane):
    return plane.astype(F32).T.astype(BF16)


def forward_tables(props, rf):
    for k in range(props.shape[0]):
        rf[k] = right_table(transposed(props[k, 0]), transposed(props[k, 1])).astype(BF16)


def backward_tables(props, lb, rb):
    width = props.shape[-1]
    for k in range(props.shape[0]):
        real, imag = props[k, 0], props[k, 1]
        lb[k, :width, :] = transposed(real)
        lb[k, width:, :] = transposed(imag)
        rb[k] = right_table(real, -imag).astype(BF16)


def detector_tables(dft, left, right, right_conj):
    width = dft.shape[-1]
    for n, (real, imag) in enumerate(zip(split2(dft[0]), split2(dft[1]))):
        left[n, :width, :] = real
        left[n, width:, :] = imag
        right[n] = right_table(real, imag).astype(BF16)
        right_conj[n] = right_table(real, -imag).astype(BF16)


def forward_steps(blocks, waves, indices, lf, rf):
    sections, _, columns = blocks.shape
    width = columns // 2

    def step(k, carried):
        which = indices[k]
        z = times(waves[k].astype(F32), with_mean(blocks[k, :width, :])).astype(BF16)
        h = joined(dot(lf[which].reshape(columns, width), z), False).astype(BF16)
        waves[k + 1] = dot(h, rf[which]).astype(BF16)
        return carried

    lax.fori_loop(0, sections, step, 0, unroll=True)


def backward_steps(blocks, waves, indices, lb, rb, grads, g):
    sections, _, columns = blocks.shape
    width = columns // 2

    def step(n, carried):
        k = sections - 1 - n
        which = indices[k]
        c = joined(dot(lb[which], g[...]), True).astype(BF16)
        y = dot(c, rb[which])
        grad, passed = times_conj(y, waves[k].astype(F32), with_mean(blocks[k, :width, :]))
        grads[k] = grad.astype(BF16)
        g[...] = passed.astype(BF16)
        return carried

    lax.fori_loop(0, sections, step, 0, unroll=True)


def detector(psi, observed, left, right, right_conj):
    def product(ah, al, bh, bl):
        return dot(ah, bh) + (dot(ah, bl) + dot(al, bh))

    near = joined(dot(left[0], psi) + dot(left[1], psi), False)
    far = product(*split2(near), right[0], right[1])
    f0, f1, ft = halves(far)
    other = swapped(ft)
    main = f0 * f0 + f1 * f1 - observed[:, :LANES]
    tail = ft * ft + other * other - observed[:, LANES:]
    push = jnp.concatenate([main * f0, main * f1, tail * ft], axis=1)
    back = joined(product(left[0], left[1], *split2(push)), True)
    return product(*split2(back), right_conj[0], right_conj[1]).astype(BF16)


def read_indices(blocks, indices, count):
    for k in range(blocks.shape[0]):
        tag = jnp.max(blocks[k, -ROWS:, 2 * LANES :].astype(F32))
        indices[k] = jnp.clip(tag.astype(jnp.int32), 0, count - 1)


def place_in(size):
    rank = lax.axis_index("cuts")
    return lax.rem(rank, size), lax.div(rank, size)


def observe(blocks, near_rows, observed, first):
    for k in range(blocks.shape[0]):
        at = first + k * near_rows
        observed[at : at + near_rows, :] = blocks[k, -ROWS:, : 2 * LANES].astype(F32)[:near_rows]


def near_kernel(blocks, _, near, observed):
    observe(blocks, near.shape[0] // blocks.shape[0], observed, 0)
    near[...] = observed[...].astype(BF16)


def first_kernel(group_ref, probes, blocks, props, dft, leaving, waves, lb, rf, rb, left, right, right_conj, probe, indices, sem):
    size = blocks.shape[0]
    slot, group = place_in(size)

    @pl.when(group == 0)
    def _():
        position = 0
        for p, held in enumerate(slots_of(group_ref.shape[0], size)):
            position = jnp.where(slot == held, p, position)
        which = group_ref[position]
        copy = pltpu.make_async_copy(probes.at[which], probe, sem)
        copy.start()
        forward_tables(props, rf)
        read_indices(blocks, indices, props.shape[0])
        copy.wait()
        waves[0] = packed(probe[0], probe[1], probe.shape[-1], 0).astype(BF16)
        forward_steps(blocks, waves, indices, props, rf)
        leaving[...] = waves[size]

    @pl.when(group > 0)
    def _():
        forward_tables(props, rf)
        backward_tables(props, lb, rb)
        detector_tables(dft, left, right, right_conj)


def forward_kernel(stage):
    def kernel(entering, blocks, props, rf, waves_in, leaving, waves, indices):
        size = blocks.shape[0]
        _, group = place_in(size)

        @pl.when(group == stage)
        def _():
            read_indices(blocks, indices, props.shape[0])
            waves[0] = entering[...]
            forward_steps(blocks, waves, indices, props, rf)
            leaving[...] = waves[size]

        @pl.when(group != stage)
        def _():
            waves[...] = waves_in[...]

    return kernel


def middle_kernel(groups):
    def kernel(waves, *refs):
        earlier, refs = refs[: groups - 1], refs[groups - 1 :]
        blocks, props, lb, rb, left, right, right_conj, leaving, grads, lb_out, rb_out, g, observed, indices = refs
        size = blocks.shape[0]
        _, group = place_in(size)

        @pl.when(group == groups - 1)
        def _():
            read_indices(blocks, indices, props.shape[0])
            rows = earlier[0].shape[0]
            for n, near in enumerate(earlier):
                observed[n * rows : (n + 1) * rows, :] = near[...].astype(F32)
            observe(blocks, rows // size, observed, (groups - 1) * rows)
            g[...] = detector(waves[size], observed[...], left, right, right_conj)
            backward_steps(blocks, waves, indices, lb, rb, grads, g)
            leaving[...] = g[...]

        @pl.when(group < groups - 1)
        def _():
            backward_tables(props, lb_out, rb_out)

    return kernel


def backward_kernel(stage):
    def kernel(arriving, waves, blocks, lb, rb, grads_in, leaving, grads, g, indices):
        _, group = place_in(blocks.shape[0])

        @pl.when(group == stage)
        def _():
            read_indices(blocks, indices, lb.shape[0])
            g[...] = arriving[...]
            backward_steps(blocks, waves, indices, lb, rb, grads, g)
            leaving[...] = g[...]

        @pl.when(group != stage)
        def _():
            grads[...] = grads_in[...]

    return kernel


def gather_kernel(offsets_ref, grads_ref, out_ref):
    positions = offsets_ref.shape[1]
    width = grads_ref.shape[1]
    extent = out_ref.shape[-1]
    spread_out = []
    for p, slot in enumerate(slots_of(positions, grads_ref.shape[0])):
        x0, x1, xt = halves(grads_ref[slot])
        spread_out.append(
            jnp.concatenate(
                [
                    dot(
                        jnp.concatenate([main, xt], axis=1),
                        picker(extent, offsets_ref[1, p], c == 1, transposed=True),
                    ).astype(BF16)
                    for c, main in ((0, x0), (1, x1))
                ],
                axis=1,
            )
        )
    rows = jnp.concatenate(
        [row_picker((extent, width), -offsets_ref[0, p]) for p in range(positions)], axis=1
    )
    total = dot(rows, jnp.concatenate(spread_out, axis=0))
    out_ref[0, 0] = total[:, :extent]
    out_ref[0, 1] = total[:, extent:]


VMEM = pl.BlockSpec(memory_space=pltpu.VMEM)
SMEM = pl.BlockSpec(memory_space=pltpu.SMEM)
HBM = pl.BlockSpec(memory_space=pl.ANY)
ALONE = pltpu.CompilerParams(vmem_limit_bytes=60 * 1024 * 1024)
PARAMS = pltpu.CompilerParams(vmem_limit_bytes=20 * 1024 * 1024)


def shards(objects, propagators, prop_index, probes, probe_group, offsets, measured):
    sections = lax.axis_size("cuts")
    width = probes.shape[-1]
    kinds = propagators.shape[0]
    near_rows = measured.shape[1]
    size = GROUP
    groups = sections // size
    rows = width + ROWS
    slots = slots_of(probe_group.shape[0], size)
    members = [list(range(first, first + size)) for first in range(0, sections, size)]

    def struct(*dims, kind=BF16):
        return jax.ShapeDtypeStruct(dims, kind)

    def exchanged(blocks):
        return lax.all_to_all(blocks, "cuts", 0, 0, axis_index_groups=members, tiled=True)

    def handed(block, stage, distance):
        route = [(stage * size + l, (stage + distance) * size + l) for l in slots]
        return lax.ppermute(block, "cuts", route)

    blocks = pl.pallas_call(
        window_kernel,
        out_shape=struct(size, rows, 2 * width),
        in_specs=[HBM, SMEM, HBM, HBM],
        out_specs=HBM,
        scratch_shapes=[
            pltpu.VMEM((size, rows, 2 * width), BF16),
            pltpu.SMEM(offsets.shape[::-1], jnp.int32),
            pltpu.VMEM(objects.shape[1:], BF16),
            pltpu.VMEM(measured.shape, F32),
            pltpu.SemaphoreType.DMA((4 + len(slots),)),
        ],
        compiler_params=ALONE,
        name="windows",
    )(offsets.T, prop_index, objects, measured)
    blocks = exchanged(blocks)

    wave = struct(width, 2 * width)
    near = struct(size * near_rows, 2 * LANES)
    waves_shape = struct(size + 1, width, 2 * width)
    grads_shape = struct(size, width, 2 * width)
    left_table = struct(kinds, 2 * width, width)
    square_table = struct(kinds, 2 * width, 2 * width)
    detector_left = struct(2, 2 * width, width)
    detector_right = struct(2, 2 * width, 2 * width)
    indices = pltpu.SMEM((size,), jnp.int32)

    def scratch(shape):
        return pltpu.VMEM(shape.shape, shape.dtype)

    def call(kernel, name, out_shape, in_specs, scratch_shapes, operands, slices=0):
        return pl.pallas_call(
            kernel,
            out_shape=out_shape,
            in_specs=in_specs,
            out_specs=[VMEM] * len(out_shape),
            scratch_shapes=scratch_shapes,
            compiler_params=PARAMS,
            cost_estimate=pl.CostEstimate(
                flops=16 * slices * width**3,
                bytes_accessed=sum(math.prod(x.shape) * x.dtype.itemsize for x in list(operands) + out_shape),
                transcendentals=0,
            ),
            name=name,
        )(*operands)

    leaving, waves, lb, rf, rb, *dft = call(
        first_kernel,
        "first_forward",
        [wave, waves_shape, left_table, square_table, square_table]
        + [detector_left, detector_right, detector_right],
        [SMEM, HBM, VMEM, VMEM, VMEM],
        [pltpu.VMEM(probes.shape[1:], BF16), indices, pltpu.SemaphoreType.DMA],
        (probe_group, probes, blocks, propagators, jnp.asarray(dft_constant(width))),
        size,
    )
    entering = handed(leaving, 0, 1)
    (near_out,) = call(near_kernel, "near_rows", [near], [VMEM, HBM], [pltpu.VMEM(near.shape, F32)], (blocks, leaving))
    nears = [handed(near_out, stage, groups - 1 - stage) for stage in range(groups - 1)]
    for stage in range(1, groups):
        leaving, waves = call(
            forward_kernel(stage),
            "forward",
            [wave, waves_shape],
            [VMEM] * 5,
            [indices],
            (entering, blocks, propagators, rf, waves),
            size,
        )
        if stage < groups - 1:
            entering = handed(leaving, stage, 1)

    leaving, grads, lb, rb = call(
        middle_kernel(groups),
        "middle",
        [wave, grads_shape, left_table, square_table],
        [VMEM] * (groups + 7),
        [scratch(wave), pltpu.VMEM((width, 2 * LANES), F32), indices],
        (waves, *nears, blocks, propagators, lb, rb, *dft),
        size,
    )

    for stage in range(groups - 2, -1, -1):
        arriving = handed(leaving, stage + 1, -1)
        leaving, grads = call(
            backward_kernel(stage),
            "backward",
            [wave, grads_shape],
            [VMEM] * 6,
            [scratch(wave), indices],
            (arriving, waves, blocks, lb, rb, grads),
            size,
        )

    return pl.pallas_call(
        gather_kernel,
        out_shape=jax.ShapeDtypeStruct(objects.shape, F32),
        in_specs=[SMEM, VMEM],
        out_specs=VMEM,
        compiler_params=PARAMS,
        name="sum_windows",
    )(offsets.T, exchanged(grads))


def solution(mesh):
    in_specs = (
        P(("parts", "cuts"), None, None, None),
        P(),
        P(("parts", "cuts")),
        P(),
        P(),
        P("parts", None),
        P("parts", "cuts", None),
    )
    out_specs = P(("parts", "cuts"), None, None, None)
    return jax.shard_map(shards, mesh=mesh, in_specs=in_specs, out_specs=out_specs, check_vma=False)
```

```python
import math

import jax
import jax.numpy as jnp
import numpy as np
from jax import lax
from jax.experimental import pallas as pl
from jax.experimental.pallas import tpu as pltpu
from jax.sharding import PartitionSpec as P

TRANSMIT = 0.985
GROUP = 8
LANES = 128
ROWS = 16
F32 = jnp.float32
BF16 = jnp.bfloat16


def dot(former, latter):
    return jnp.dot(former, latter, preferred_element_type=F32)


def halves(x):
    return x[:, :LANES], x[:, LANES : 2 * LANES], x[:, 2 * LANES :]


def swapped(tail):
    return pltpu.roll(tail, LANES // 2, 1)


def low_half(rows):
    return lax.broadcasted_iota(jnp.int32, (rows, LANES), 1) < LANES // 2


def spread(tail):
    other = swapped(tail)
    low = low_half(tail.shape[0])
    return jnp.where(low, tail, other), jnp.where(low, other, tail)


def signed(tail, minus_low):
    low = low_half(tail.shape[0])
    return jnp.where(low == minus_low, -tail, tail)


def factor(b):
    b0, b1, bt = halves(b)
    return (b0, b1) + spread(bt)


def times(a, parts):
    a0, a1, at = halves(a)
    b0, b1, b_real, b_imag = parts
    tail = at * b_real + signed(swapped(at), True) * b_imag
    return jnp.concatenate([a0 * b0 - a1 * b1, a1 * b0 + a0 * b1, tail], axis=1)


def times_conj(a, turned, parts):
    a0, a1, at = halves(a)
    b0, b1, b_real, b_imag = parts
    tail = at * b_real + turned * b_imag
    return jnp.concatenate([a0 * b0 + a1 * b1, a1 * b0 - a0 * b1, tail], axis=1)


def joined(both, conj):
    width = both.shape[0] // 2
    u0, u1, ut = halves(both[:width])
    v0, v1, vt = halves(both[width:])
    turned = signed(swapped(vt), not conj)
    if conj:
        return jnp.concatenate([u0 + v1, u1 - v0, ut + turned], axis=1)
    return jnp.concatenate([u0 - v1, u1 + v0, ut + turned], axis=1)


def with_mean(window):
    x = window.astype(F32)
    x0, x1, xt = halves(x)
    mean = jnp.where(low_half(xt.shape[0]), TRANSMIT, 0.0)
    return jnp.concatenate([TRANSMIT + x0, x1, mean + xt], axis=1)


def split2(x):
    high = x.astype(BF16)
    return high, (x - high.astype(F32)).astype(BF16)


def picker(columns, start, high_tail, transposed=False):
    shape = (2 * LANES, columns) if transposed else (columns, 2 * LANES)
    a = lax.broadcasted_iota(jnp.int32, shape, 1 if transposed else 0) - start
    q = lax.broadcasted_iota(jnp.int32, shape, 0 if transposed else 1)
    if high_tail:
        half = LANES // 2
        wanted = jnp.where(q < LANES, q, jnp.where(q < LANES + half, -columns, q - half))
    else:
        wanted = jnp.where(q < LANES + LANES // 2, q, -columns)
    return jnp.where(a == wanted, 1.0, 0.0).astype(BF16)


def row_picker(shape, distance):
    taken = lax.broadcasted_iota(jnp.int32, shape, 1)
    wanted = lax.broadcasted_iota(jnp.int32, shape, 0) + distance
    return jnp.where(taken == wanted, 1.0, 0.0).astype(BF16)


def rows_near(x, start, count):
    limit = x.shape[0] - count
    bit = 1 << (limit.bit_length() - 1)
    while bit >= ROWS:
        length = count + bit
        short = bit + length - x.shape[0]
        if short > 0:
            x = jnp.concatenate([x, jnp.zeros((short, x.shape[1]), x.dtype)], axis=0)
        x = jnp.where(lax.bitwise_and(start, bit) != 0, x[bit : bit + length], x[:length])
        bit //= 2
    return x


def packed(real, imag, columns, start):
    left = dot(real, picker(columns, start, False))
    right = dot(imag, picker(columns, start, True))
    return jnp.concatenate(
        [left[:, :LANES], right[:, :LANES], left[:, LANES:] + right[:, LANES:]], axis=1
    )


def dft_constant(width):
    counter = np.arange(width)
    angle = (counter[:, None] * counter[None, :] % width) * (2.0 * math.pi / width)
    return (np.stack([np.cos(angle), -np.sin(angle)]) / math.sqrt(width)).astype(np.float32)


def slots_of(positions, size):
    order = list(range(0, size, 2)) + list(range(size - 1, 0, -2))
    return sorted(order[:positions])


def window_kernel(offsets_in, index_ref, objects_in, measured_in, blocks_out, blocks, offsets_ref, objects, measured, sems):
    positions, near_rows, width = measured.shape
    extent = objects.shape[-1]
    copies = [
        pltpu.make_async_copy(objects_in.at[0, 0], objects.at[0], sems.at[0]),
        pltpu.make_async_copy(objects_in.at[0, 1], objects.at[1], sems.at[1]),
        pltpu.make_async_copy(measured_in, measured, sems.at[2]),
        pltpu.make_async_copy(offsets_in, offsets_ref, sems.at[3]),
    ]
    for copy in copies:
        copy.start()
    tag = jnp.full((ROWS, LANES), index_ref[0], jnp.int32).astype(F32)
    for copy in copies:
        copy.wait()
    sending = []
    for p, slot in enumerate(slots_of(positions, blocks.shape[0])):
        start = offsets_ref[0, p]
        real, imag = (rows_near(objects[c], start, width) for c in range(2))
        window = packed(real, imag, extent, offsets_ref[1, p]).astype(BF16)
        shift = lax.bitwise_and(start, ROWS - 1)
        blocks[slot, :width, :] = dot(row_picker((width, width + ROWS), shift), window).astype(BF16)
        tail = measured[p, :, LANES:]
        seen = jnp.concatenate([measured[p, :, :LANES], tail, tail, tag[:near_rows]], axis=1)
        left_over = jnp.concatenate([tag[near_rows:]] * 3, axis=1)
        blocks[slot, width:, :] = jnp.concatenate([seen, left_over], axis=0).astype(BF16)
        sending.append(pltpu.make_async_copy(blocks.at[slot], blocks_out.at[slot], sems.at[4 + p]))
        sending[-1].start()
    for copy in sending:
        copy.wait()


def right_table(real, imag):
    width = real.shape[0]
    upper = packed(real, imag, width, 0)
    lower = packed(-imag, real, width, 0)
    return jnp.concatenate([upper[:LANES], lower[:LANES], upper[LANES:], lower[LANES:]], axis=0)


def transposed(plane):
    return plane.astype(F32).T.astype(BF16)


def forward_tables(props, rf):
    for k in range(props.shape[0]):
        rf[k] = right_table(transposed(props[k, 0]), transposed(props[k, 1])).astype(BF16)


def backward_tables(props, lb, rb):
    width = props.shape[-1]
    for k in range(props.shape[0]):
        real, imag = props[k, 0], props[k, 1]
        lb[k, :width, :] = transposed(real)
        lb[k, width:, :] = transposed(imag)
        rb[k] = right_table(real, -imag).astype(BF16)


def detector_tables(dft, left, right, right_conj):
    width = dft.shape[-1]
    for n, (real, imag) in enumerate(zip(split2(dft[0]), split2(dft[1]))):
        left[n, :width, :] = real
        left[n, width:, :] = imag
        right[n] = right_table(real, imag).astype(BF16)
        if n == 0:
            right_conj[...] = right_table(real, -imag).astype(BF16)


def forward_steps(blocks, waves, indices, lf, rf):
    sections, _, columns = blocks.shape
    width = columns // 2
    psi = waves[0]
    parts = factor(with_mean(blocks[0, :width, :]))
    for k in range(sections):
        which = indices[k]
        z = times(psi.astype(F32), parts).astype(BF16)
        h = joined(dot(lf[which].reshape(columns, width), z), False).astype(BF16)
        if k + 1 < sections:
            parts = factor(with_mean(blocks[k + 1, :width, :]))
        psi = dot(h, rf[which]).astype(BF16)
        waves[k + 1] = psi


def backward_steps(blocks, waves, indices, lb, rb, grads, g):
    sections, _, columns = blocks.shape
    width = columns // 2

    def leave(k, y, turned, wave_parts):
        grads[k] = times_conj(y, turned, wave_parts).astype(BF16)

    late = None
    for k in reversed(range(sections)):
        which = indices[k]
        both = dot(lb[which], g)
        if late is not None:
            leave(*late)
        c = joined(both, True).astype(BF16)
        wave_parts = factor(waves[k].astype(F32))
        window_parts = factor(with_mean(blocks[k, :width, :]))
        y = dot(c, rb[which])
        turned = signed(swapped(halves(y)[2]), False)
        g = times_conj(y, turned, window_parts).astype(BF16)
        late = (k, y, turned, wave_parts)
    leave(*late)
    return g


def detector(psi, observed, left, right, right_conj):
    def product(ah, al, bh, bl):
        return dot(ah, bh) + (dot(ah, bl) + dot(al, bh))

    near = joined(dot(left[0], psi) + dot(left[1], psi), False)
    far = product(*split2(near), right[0], right[1])
    f0, f1, ft = halves(far)
    other = swapped(ft)
    main = f0 * f0 + f1 * f1 - observed[:, :LANES]
    tail = ft * ft + other * other - observed[:, LANES:]
    push = jnp.concatenate([main * f0, main * f1, tail * ft], axis=1)
    back = joined(dot(left[0], push.astype(BF16)), True)
    return dot(back.astype(BF16), right_conj[...]).astype(BF16)


def read_indices(blocks, indices, count):
    for k in range(blocks.shape[0]):
        tag = jnp.max(blocks[k, -ROWS:, 2 * LANES :].astype(F32))
        indices[k] = jnp.clip(tag.astype(jnp.int32), 0, count - 1)


def place_in(size):
    rank = lax.axis_index("cuts")
    return lax.rem(rank, size), lax.div(rank, size)


def observe(blocks, near_rows, observed, first):
    for k in range(blocks.shape[0]):
        at = first + k * near_rows
        observed[at : at + near_rows, :] = blocks[k, -ROWS:, : 2 * LANES].astype(F32)[:near_rows]


def near_kernel(blocks, _, near, observed):
    observe(blocks, near.shape[0] // blocks.shape[0], observed, 0)
    near[...] = observed[...].astype(BF16)


def first_kernel(group_ref, probes, blocks, props, dft, leaving, waves, lb, rf, rb, left, right, right_conj, probe, indices, sem):
    size = blocks.shape[0]
    slot, group = place_in(size)

    @pl.when(group == 0)
    def _():
        position = 0
        for p, held in enumerate(slots_of(group_ref.shape[0], size)):
            position = jnp.where(slot == held, p, position)
        which = group_ref[position]
        copy = pltpu.make_async_copy(probes.at[which], probe, sem)
        copy.start()
        forward_tables(props, rf)
        read_indices(blocks, indices, props.shape[0])
        copy.wait()
        waves[0] = packed(probe[0], probe[1], probe.shape[-1], 0).astype(BF16)
        forward_steps(blocks, waves, indices, props, rf)
        leaving[...] = waves[size]

    @pl.when(group > 0)
    def _():
        forward_tables(props, rf)
        backward_tables(props, lb, rb)
        detector_tables(dft, left, right, right_conj)


def forward_kernel(stage):
    def kernel(entering, blocks, props, rf, waves_in, leaving, waves, indices):
        size = blocks.shape[0]
        _, group = place_in(size)

        @pl.when(group == stage)
        def _():
            read_indices(blocks, indices, props.shape[0])
            waves[0] = entering[...]
            forward_steps(blocks, waves, indices, props, rf)
            leaving[...] = waves[size]

        @pl.when(group != stage)
        def _():
            waves[...] = waves_in[...]

    return kernel


def middle_kernel(groups):
    def kernel(waves, *refs):
        earlier, refs = refs[: groups - 1], refs[groups - 1 :]
        blocks, props, lb, rb, left, right, right_conj, leaving, grads, lb_out, rb_out, observed, indices = refs
        size = blocks.shape[0]
        _, group = place_in(size)

        @pl.when(group == groups - 1)
        def _():
            read_indices(blocks, indices, props.shape[0])
            rows = earlier[0].shape[0]
            for n, near in enumerate(earlier):
                observed[n * rows : (n + 1) * rows, :] = near[...].astype(F32)
            observe(blocks, rows // size, observed, (groups - 1) * rows)
            g = detector(waves[size], observed[...], left, right, right_conj)
            leaving[...] = backward_steps(blocks, waves, indices, lb, rb, grads, g)

        @pl.when(group < groups - 1)
        def _():
            backward_tables(props, lb_out, rb_out)

    return kernel


def backward_kernel(stage):
    def kernel(arriving, waves, blocks, lb, rb, grads_in, leaving, grads, indices):
        _, group = place_in(blocks.shape[0])

        @pl.when(group == stage)
        def _():
            read_indices(blocks, indices, lb.shape[0])
            leaving[...] = backward_steps(blocks, waves, indices, lb, rb, grads, arriving[...])

        @pl.when(group != stage)
        def _():
            grads[...] = grads_in[...]

    return kernel


def gather_kernel(offsets_ref, grads_ref, out_ref):
    positions = offsets_ref.shape[1]
    width = grads_ref.shape[1]
    extent = out_ref.shape[-1]
    spread_out = []
    for p, slot in enumerate(slots_of(positions, grads_ref.shape[0])):
        x0, x1, xt = halves(grads_ref[slot])
        spread_out.append(
            jnp.concatenate(
                [
                    dot(
                        jnp.concatenate([main, xt], axis=1),
                        picker(extent, offsets_ref[1, p], c == 1, transposed=True),
                    ).astype(BF16)
                    for c, main in ((0, x0), (1, x1))
                ],
                axis=1,
            )
        )
    rows = jnp.concatenate(
        [row_picker((extent, width), -offsets_ref[0, p]) for p in range(positions)], axis=1
    )
    total = dot(rows, jnp.concatenate(spread_out, axis=0))
    out_ref[0, 0] = total[:, :extent]
    out_ref[0, 1] = total[:, extent:]


VMEM = pl.BlockSpec(memory_space=pltpu.VMEM)
SMEM = pl.BlockSpec(memory_space=pltpu.SMEM)
HBM = pl.BlockSpec(memory_space=pl.ANY)
ALONE = pltpu.CompilerParams(vmem_limit_bytes=60 * 1024 * 1024)
PARAMS = pltpu.CompilerParams(vmem_limit_bytes=20 * 1024 * 1024)


def shards(objects, propagators, prop_index, probes, probe_group, offsets, measured):
    sections = lax.axis_size("cuts")
    width = probes.shape[-1]
    kinds = propagators.shape[0]
    near_rows = measured.shape[1]
    size = GROUP
    groups = sections // size
    rows = width + ROWS
    slots = slots_of(probe_group.shape[0], size)
    members = [list(range(first, first + size)) for first in range(0, sections, size)]

    def struct(*dims, kind=BF16):
        return jax.ShapeDtypeStruct(dims, kind)

    def exchanged(blocks):
        return lax.all_to_all(blocks, "cuts", 0, 0, axis_index_groups=members, tiled=True)

    def handed(block, stage, distance):
        route = [(stage * size + l, (stage + distance) * size + l) for l in slots]
        return lax.ppermute(block, "cuts", route)

    blocks = pl.pallas_call(
        window_kernel,
        out_shape=struct(size, rows, 2 * width),
        in_specs=[HBM, SMEM, HBM, HBM],
        out_specs=HBM,
        scratch_shapes=[
            pltpu.VMEM((size, rows, 2 * width), BF16),
            pltpu.SMEM(offsets.shape[::-1], jnp.int32),
            pltpu.VMEM(objects.shape[1:], BF16),
            pltpu.VMEM(measured.shape, F32),
            pltpu.SemaphoreType.DMA((4 + len(slots),)),
        ],
        compiler_params=ALONE,
        name="windows",
    )(offsets.T, prop_index, objects, measured)
    blocks = exchanged(blocks)

    wave = struct(width, 2 * width)
    near = struct(size * near_rows, 2 * LANES)
    waves_shape = struct(size + 1, width, 2 * width)
    grads_shape = struct(size, width, 2 * width)
    left_table = struct(kinds, 2 * width, width)
    square_table = struct(kinds, 2 * width, 2 * width)
    detector_left = struct(2, 2 * width, width)
    detector_right = struct(2, 2 * width, 2 * width)
    indices = pltpu.SMEM((size,), jnp.int32)

    def call(kernel, name, out_shape, in_specs, scratch_shapes, operands, slices=0):
        return pl.pallas_call(
            kernel,
            out_shape=out_shape,
            in_specs=in_specs,
            out_specs=[VMEM] * len(out_shape),
            scratch_shapes=scratch_shapes,
            compiler_params=PARAMS,
            cost_estimate=pl.CostEstimate(
                flops=16 * slices * width**3,
                bytes_accessed=sum(math.prod(x.shape) * x.dtype.itemsize for x in list(operands) + out_shape),
                transcendentals=0,
            ),
            name=name,
        )(*operands)

    leaving, waves, lb, rf, rb, *dft = call(
        first_kernel,
        "first_forward",
        [wave, waves_shape, left_table, square_table, square_table]
        + [detector_left, detector_right, struct(2 * width, 2 * width)],
        [SMEM, HBM, VMEM, VMEM, VMEM],
        [pltpu.VMEM(probes.shape[1:], BF16), indices, pltpu.SemaphoreType.DMA],
        (probe_group, probes, blocks, propagators, jnp.asarray(dft_constant(width))),
        size,
    )
    entering = handed(leaving, 0, 1)
    (near_out,) = call(near_kernel, "near_rows", [near], [VMEM, HBM], [pltpu.VMEM(near.shape, F32)], (blocks, leaving))
    nears = [handed(near_out, stage, groups - 1 - stage) for stage in range(groups - 1)]
    for stage in range(1, groups):
        leaving, waves = call(
            forward_kernel(stage),
            "forward",
            [wave, waves_shape],
            [VMEM] * 5,
            [indices],
            (entering, blocks, propagators, rf, waves),
            size,
        )
        if stage < groups - 1:
            entering = handed(leaving, stage, 1)

    leaving, grads, lb, rb = call(
        middle_kernel(groups),
        "middle",
        [wave, grads_shape, left_table, square_table],
        [VMEM] * (groups + 7),
        [pltpu.VMEM((width, 2 * LANES), F32), indices],
        (waves, *nears, blocks, propagators, lb, rb, *dft),
        size,
    )

    for stage in range(groups - 2, -1, -1):
        arriving = handed(leaving, stage + 1, -1)
        leaving, grads = call(
            backward_kernel(stage),
            "backward",
            [wave, grads_shape],
            [VMEM] * 6,
            [indices],
            (arriving, waves, blocks, lb, rb, grads),
            size,
        )

    return pl.pallas_call(
        gather_kernel,
        out_shape=jax.ShapeDtypeStruct(objects.shape, F32),
        in_specs=[SMEM, VMEM],
        out_specs=VMEM,
        compiler_params=PARAMS,
        name="sum_windows",
    )(offsets.T, exchanged(grads))


def solution(mesh):
    in_specs = (
        P(("parts", "cuts"), None, None, None),
        P(),
        P(("parts", "cuts")),
        P(),
        P(),
        P("parts", None),
        P("parts", "cuts", None),
    )
    out_specs = P(("parts", "cuts"), None, None, None)
    return jax.shard_map(shards, mesh=mesh, in_specs=in_specs, out_specs=out_specs, check_vma=False)
```

```python
import math

import jax
import jax.numpy as jnp
import numpy as np
from jax import lax
from jax.experimental import pallas as pl
from jax.experimental.pallas import tpu as pltpu
from jax.sharding import PartitionSpec as P

TRANSMIT = 0.985
GROUP = 8
LANES = 128
ROWS = 16
F32 = jnp.float32
BF16 = jnp.bfloat16


def dot(former, latter):
    return jnp.dot(former, latter, preferred_element_type=F32)


def halves(x):
    return x[:, :LANES], x[:, LANES : 2 * LANES], x[:, 2 * LANES :]


def swapped(tail):
    return pltpu.roll(tail, LANES // 2, 1)


def low_half(rows):
    return lax.broadcasted_iota(jnp.int32, (rows, LANES), 1) < LANES // 2


def spread(tail):
    other = swapped(tail)
    low = low_half(tail.shape[0])
    return jnp.where(low, tail, other), jnp.where(low, other, tail)


def signed(tail, minus_low):
    low = low_half(tail.shape[0])
    return jnp.where(low == minus_low, -tail, tail)


def factor(b):
    b0, b1, bt = halves(b)
    return (b0, b1) + spread(bt)


def times(a, parts):
    a0, a1, at = halves(a)
    b0, b1, b_real, b_imag = parts
    tail = at * b_real + signed(swapped(at), True) * b_imag
    return jnp.concatenate([a0 * b0 - a1 * b1, a1 * b0 + a0 * b1, tail], axis=1)


def times_conj(a, turned, parts):
    a0, a1, at = halves(a)
    b0, b1, b_real, b_imag = parts
    tail = at * b_real + turned * b_imag
    return jnp.concatenate([a0 * b0 + a1 * b1, a1 * b0 - a0 * b1, tail], axis=1)


def joined(both, conj):
    width = both.shape[0] // 2
    u0, u1, ut = halves(both[:width])
    v0, v1, vt = halves(both[width:])
    turned = signed(swapped(vt), not conj)
    if conj:
        return jnp.concatenate([u0 + v1, u1 - v0, ut + turned], axis=1)
    return jnp.concatenate([u0 - v1, u1 + v0, ut + turned], axis=1)


def stacked(x):
    x0, x1, xt = halves(x)
    half = LANES // 2
    return jnp.concatenate(
        [
            jnp.concatenate([x0, xt[:, :half]], axis=1),
            jnp.concatenate([x1, swapped(xt)[:, :half]], axis=1),
        ],
        axis=0,
    )


def with_mean(window):
    x = window.astype(F32)
    x0, x1, xt = halves(x)
    mean = jnp.where(low_half(xt.shape[0]), TRANSMIT, 0.0)
    return jnp.concatenate([TRANSMIT + x0, x1, mean + xt], axis=1)


def split2(x):
    high = x.astype(BF16)
    return high, (x - high.astype(F32)).astype(BF16)


def picker(columns, start, high_tail, transposed=False):
    shape = (2 * LANES, columns) if transposed else (columns, 2 * LANES)
    a = lax.broadcasted_iota(jnp.int32, shape, 1 if transposed else 0) - start
    q = lax.broadcasted_iota(jnp.int32, shape, 0 if transposed else 1)
    if high_tail:
        half = LANES // 2
        wanted = jnp.where(q < LANES, q, jnp.where(q < LANES + half, -columns, q - half))
    else:
        wanted = jnp.where(q < LANES + LANES // 2, q, -columns)
    return jnp.where(a == wanted, 1.0, 0.0).astype(BF16)


def row_picker(shape, distance):
    taken = lax.broadcasted_iota(jnp.int32, shape, 1)
    wanted = lax.broadcasted_iota(jnp.int32, shape, 0) + distance
    return jnp.where(taken == wanted, 1.0, 0.0).astype(BF16)


def rows_near(x, start, count):
    limit = x.shape[0] - count
    bit = 1 << (limit.bit_length() - 1)
    while bit >= ROWS:
        length = count + bit
        short = bit + length - x.shape[0]
        if short > 0:
            x = jnp.concatenate([x, jnp.zeros((short, x.shape[1]), x.dtype)], axis=0)
        x = jnp.where(lax.bitwise_and(start, bit) != 0, x[bit : bit + length], x[:length])
        bit //= 2
    return x


def packed(real, imag, columns, start):
    left = dot(real, picker(columns, start, False))
    right = dot(imag, picker(columns, start, True))
    return jnp.concatenate(
        [left[:, :LANES], right[:, :LANES], left[:, LANES:] + right[:, LANES:]], axis=1
    )


def dft_constant(width):
    counter = np.arange(width)
    angle = (counter[:, None] * counter[None, :] % width) * (2.0 * math.pi / width)
    return (np.stack([np.cos(angle), -np.sin(angle)]) / math.sqrt(width)).astype(np.float32)


def slots_of(positions, size):
    order = list(range(0, size, 2)) + list(range(size - 1, 0, -2))
    return sorted(order[:positions])


def window_kernel(offsets_in, index_ref, objects_in, measured_in, blocks_out, blocks, offsets_ref, objects, measured, sems):
    positions, near_rows, width = measured.shape
    extent = objects.shape[-1]
    copies = [
        pltpu.make_async_copy(objects_in.at[0, 0], objects.at[0], sems.at[0]),
        pltpu.make_async_copy(objects_in.at[0, 1], objects.at[1], sems.at[1]),
        pltpu.make_async_copy(measured_in, measured, sems.at[2]),
        pltpu.make_async_copy(offsets_in, offsets_ref, sems.at[3]),
    ]
    for copy in copies:
        copy.start()
    tag = jnp.full((ROWS, LANES), index_ref[0], jnp.int32).astype(F32)
    for copy in copies:
        copy.wait()
    sending = []
    for p, slot in enumerate(slots_of(positions, blocks.shape[0])):
        start = offsets_ref[0, p]
        real, imag = (rows_near(objects[c], start, width) for c in range(2))
        window = packed(real, imag, extent, offsets_ref[1, p]).astype(BF16)
        shift = lax.bitwise_and(start, ROWS - 1)
        blocks[slot, :width, :] = dot(row_picker((width, width + ROWS), shift), window).astype(BF16)
        tail = measured[p, :, LANES:]
        seen = jnp.concatenate([measured[p, :, :LANES], tail, tail, tag[:near_rows]], axis=1)
        left_over = jnp.concatenate([tag[near_rows:]] * 3, axis=1)
        blocks[slot, width:, :] = jnp.concatenate([seen, left_over], axis=0).astype(BF16)
        sending.append(pltpu.make_async_copy(blocks.at[slot], blocks_out.at[slot], sems.at[4 + p]))
        sending[-1].start()
    for copy in sending:
        copy.wait()


def transposed(plane):
    return plane.astype(F32).T.astype(BF16)


def forward_tables(props, rf):
    for k in range(props.shape[0]):
        rf[k] = packed(transposed(props[k, 0]), transposed(props[k, 1]), props.shape[-1], 0).astype(BF16)


def backward_tables(props, lb, rb):
    width = props.shape[-1]
    for k in range(props.shape[0]):
        real, imag = props[k, 0], props[k, 1]
        lb[k, :width, :] = transposed(real)
        lb[k, width:, :] = transposed(imag)
        rb[k] = packed(real, -imag, width, 0).astype(BF16)


def detector_tables(dft, left, right, right_conj):
    width = dft.shape[-1]
    for n, (real, imag) in enumerate(zip(split2(dft[0]), split2(dft[1]))):
        left[n, :width, :] = real
        left[n, width:, :] = imag
        right[n] = packed(real, imag, width, 0).astype(BF16)
        if n == 0:
            right_conj[...] = packed(real, -imag, width, 0).astype(BF16)


def forward_steps(blocks, waves, indices, lf, rf):
    sections, _, columns = blocks.shape
    width = columns // 2
    psi = waves[0]
    parts = factor(with_mean(blocks[0, :width, :]))
    for k in range(sections):
        which = indices[k]
        z = times(psi.astype(F32), parts).astype(BF16)
        h = joined(dot(lf[which].reshape(columns, width), z), False)
        if k + 1 < sections:
            parts = factor(with_mean(blocks[k + 1, :width, :]))
        psi = joined(dot(stacked(h).astype(BF16), rf[which]), False).astype(BF16)
        waves[k + 1] = psi


def backward_steps(blocks, waves, indices, lb, rb, grads, g):
    sections, _, columns = blocks.shape
    width = columns // 2

    def leave(k, y, turned, wave_parts):
        grads[k] = times_conj(y, turned, wave_parts).astype(BF16)

    late = None
    for k in reversed(range(sections)):
        which = indices[k]
        both = dot(lb[which], g)
        if late is not None:
            leave(*late)
        c = joined(both, True)
        wave_parts = factor(waves[k].astype(F32))
        window_parts = factor(with_mean(blocks[k, :width, :]))
        y = joined(dot(stacked(c).astype(BF16), rb[which]), False)
        turned = signed(swapped(halves(y)[2]), False)
        g = times_conj(y, turned, window_parts).astype(BF16)
        late = (k, y, turned, wave_parts)
    leave(*late)
    return g


def detector(psi, observed, left, right, right_conj):
    def product(ah, al, bh, bl):
        return dot(ah, bh) + (dot(ah, bl) + dot(al, bh))

    near = joined(dot(left[0], psi) + dot(left[1], psi), False)
    far = joined(product(*split2(stacked(near)), right[0], right[1]), False)
    f0, f1, ft = halves(far)
    other = swapped(ft)
    main = f0 * f0 + f1 * f1 - observed[:, :LANES]
    tail = ft * ft + other * other - observed[:, LANES:]
    push = jnp.concatenate([main * f0, main * f1, tail * ft], axis=1)
    back = joined(dot(left[0], push.astype(BF16)), True)
    return joined(dot(stacked(back).astype(BF16), right_conj[...]), False).astype(BF16)


def read_indices(blocks, indices, count):
    for k in range(blocks.shape[0]):
        tag = jnp.max(blocks[k, -ROWS:, 2 * LANES :].astype(F32))
        indices[k] = jnp.clip(tag.astype(jnp.int32), 0, count - 1)


def place_in(size):
    rank = lax.axis_index("cuts")
    return lax.rem(rank, size), lax.div(rank, size)


def observe(blocks, near_rows, observed, first):
    for k in range(blocks.shape[0]):
        at = first + k * near_rows
        observed[at : at + near_rows, :] = blocks[k, -ROWS:, : 2 * LANES].astype(F32)[:near_rows]


def near_kernel(blocks, _, near, observed):
    observe(blocks, near.shape[0] // blocks.shape[0], observed, 0)
    near[...] = observed[...].astype(BF16)


def first_kernel(group_ref, probes, blocks, props, dft, leaving, waves, lb, rf, rb, left, right, right_conj, probe, indices, sem):
    size = blocks.shape[0]
    slot, group = place_in(size)

    @pl.when(group == 0)
    def _():
        position = 0
        for p, held in enumerate(slots_of(group_ref.shape[0], size)):
            position = jnp.where(slot == held, p, position)
        which = group_ref[position]
        copy = pltpu.make_async_copy(probes.at[which], probe, sem)
        copy.start()
        forward_tables(props, rf)
        read_indices(blocks, indices, props.shape[0])
        copy.wait()
        waves[0] = packed(probe[0], probe[1], probe.shape[-1], 0).astype(BF16)
        forward_steps(blocks, waves, indices, props, rf)
        leaving[...] = waves[size]

    @pl.when(group > 0)
    def _():
        forward_tables(props, rf)
        backward_tables(props, lb, rb)
        detector_tables(dft, left, right, right_conj)


def forward_kernel(stage):
    def kernel(entering, blocks, props, rf, waves_in, leaving, waves, indices):
        size = blocks.shape[0]
        _, group = place_in(size)

        @pl.when(group == stage)
        def _():
            read_indices(blocks, indices, props.shape[0])
            waves[0] = entering[...]
            forward_steps(blocks, waves, indices, props, rf)
            leaving[...] = waves[size]

        @pl.when(group != stage)
        def _():
            waves[...] = waves_in[...]

    return kernel


def middle_kernel(groups):
    def kernel(waves, *refs):
        earlier, refs = refs[: groups - 1], refs[groups - 1 :]
        blocks, props, lb, rb, left, right, right_conj, leaving, grads, lb_out, rb_out, observed, indices = refs
        size = blocks.shape[0]
        _, group = place_in(size)

        @pl.when(group == groups - 1)
        def _():
            read_indices(blocks, indices, props.shape[0])
            rows = earlier[0].shape[0]
            for n, near in enumerate(earlier):
                observed[n * rows : (n + 1) * rows, :] = near[...].astype(F32)
            observe(blocks, rows // size, observed, (groups - 1) * rows)
            g = detector(waves[size], observed[...], left, right, right_conj)
            leaving[...] = backward_steps(blocks, waves, indices, lb, rb, grads, g)

        @pl.when(group < groups - 1)
        def _():
            backward_tables(props, lb_out, rb_out)

    return kernel


def backward_kernel(stage):
    def kernel(arriving, waves, blocks, lb, rb, grads_in, leaving, grads, indices):
        _, group = place_in(blocks.shape[0])

        @pl.when(group == stage)
        def _():
            read_indices(blocks, indices, lb.shape[0])
            leaving[...] = backward_steps(blocks, waves, indices, lb, rb, grads, arriving[...])

        @pl.when(group != stage)
        def _():
            grads[...] = grads_in[...]

    return kernel


def gather_kernel(offsets_ref, grads_ref, out_ref):
    positions = offsets_ref.shape[1]
    width = grads_ref.shape[1]
    extent = out_ref.shape[-1]
    spread_out = []
    for p, slot in enumerate(slots_of(positions, grads_ref.shape[0])):
        x0, x1, xt = halves(grads_ref[slot])
        spread_out.append(
            jnp.concatenate(
                [
                    dot(
                        jnp.concatenate([main, xt], axis=1),
                        picker(extent, offsets_ref[1, p], c == 1, transposed=True),
                    ).astype(BF16)
                    for c, main in ((0, x0), (1, x1))
                ],
                axis=1,
            )
        )
    rows = jnp.concatenate(
        [row_picker((extent, width), -offsets_ref[0, p]) for p in range(positions)], axis=1
    )
    total = dot(rows, jnp.concatenate(spread_out, axis=0))
    out_ref[0, 0] = total[:, :extent]
    out_ref[0, 1] = total[:, extent:]


VMEM = pl.BlockSpec(memory_space=pltpu.VMEM)
SMEM = pl.BlockSpec(memory_space=pltpu.SMEM)
HBM = pl.BlockSpec(memory_space=pl.ANY)
ALONE = pltpu.CompilerParams(vmem_limit_bytes=60 * 1024 * 1024)
PARAMS = pltpu.CompilerParams(vmem_limit_bytes=20 * 1024 * 1024)


def shards(objects, propagators, prop_index, probes, probe_group, offsets, measured):
    sections = lax.axis_size("cuts")
    width = probes.shape[-1]
    kinds = propagators.shape[0]
    near_rows = measured.shape[1]
    size = GROUP
    groups = sections // size
    rows = width + ROWS
    slots = slots_of(probe_group.shape[0], size)
    members = [list(range(first, first + size)) for first in range(0, sections, size)]

    def struct(*dims, kind=BF16):
        return jax.ShapeDtypeStruct(dims, kind)

    def exchanged(blocks):
        return lax.all_to_all(blocks, "cuts", 0, 0, axis_index_groups=members, tiled=True)

    def handed(block, stage, distance):
        route = [(stage * size + l, (stage + distance) * size + l) for l in slots]
        return lax.ppermute(block, "cuts", route)

    blocks = pl.pallas_call(
        window_kernel,
        out_shape=struct(size, rows, 2 * width),
        in_specs=[HBM, SMEM, HBM, HBM],
        out_specs=HBM,
        scratch_shapes=[
            pltpu.VMEM((size, rows, 2 * width), BF16),
            pltpu.SMEM(offsets.shape[::-1], jnp.int32),
            pltpu.VMEM(objects.shape[1:], BF16),
            pltpu.VMEM(measured.shape, F32),
            pltpu.SemaphoreType.DMA((4 + len(slots),)),
        ],
        compiler_params=ALONE,
        name="windows",
    )(offsets.T, prop_index, objects, measured)
    blocks = exchanged(blocks)

    wave = struct(width, 2 * width)
    near = struct(size * near_rows, 2 * LANES)
    waves_shape = struct(size + 1, width, 2 * width)
    grads_shape = struct(size, width, 2 * width)
    left_table = struct(kinds, 2 * width, width)
    right_table = struct(kinds, width, 2 * width)
    detector_left = struct(2, 2 * width, width)
    detector_right = struct(2, width, 2 * width)
    indices = pltpu.SMEM((size,), jnp.int32)

    def call(kernel, name, out_shape, in_specs, scratch_shapes, operands, slices=0):
        return pl.pallas_call(
            kernel,
            out_shape=out_shape,
            in_specs=in_specs,
            out_specs=[VMEM] * len(out_shape),
            scratch_shapes=scratch_shapes,
            compiler_params=PARAMS,
            cost_estimate=pl.CostEstimate(
                flops=16 * slices * width**3,
                bytes_accessed=sum(math.prod(x.shape) * x.dtype.itemsize for x in list(operands) + out_shape),
                transcendentals=0,
            ),
            name=name,
        )(*operands)

    leaving, waves, lb, rf, rb, *dft = call(
        first_kernel,
        "first_forward",
        [wave, waves_shape, left_table, right_table, right_table]
        + [detector_left, detector_right, wave],
        [SMEM, HBM, VMEM, VMEM, VMEM],
        [pltpu.VMEM(probes.shape[1:], BF16), indices, pltpu.SemaphoreType.DMA],
        (probe_group, probes, blocks, propagators, jnp.asarray(dft_constant(width))),
        size,
    )
    entering = handed(leaving, 0, 1)
    (near_out,) = call(near_kernel, "near_rows", [near], [VMEM, HBM], [pltpu.VMEM(near.shape, F32)], (blocks, leaving))
    nears = [handed(near_out, stage, groups - 1 - stage) for stage in range(groups - 1)]
    for stage in range(1, groups):
        leaving, waves = call(
            forward_kernel(stage),
            "forward",
            [wave, waves_shape],
            [VMEM] * 5,
            [indices],
            (entering, blocks, propagators, rf, waves),
            size,
        )
        if stage < groups - 1:
            entering = handed(leaving, stage, 1)

    leaving, grads, lb, rb = call(
        middle_kernel(groups),
        "middle",
        [wave, grads_shape, left_table, right_table],
        [VMEM] * (groups + 7),
        [pltpu.VMEM((width, 2 * LANES), F32), indices],
        (waves, *nears, blocks, propagators, lb, rb, *dft),
        size,
    )

    for stage in range(groups - 2, -1, -1):
        arriving = handed(leaving, stage + 1, -1)
        leaving, grads = call(
            backward_kernel(stage),
            "backward",
            [wave, grads_shape],
            [VMEM] * 6,
            [indices],
            (arriving, waves, blocks, lb, rb, grads),
            size,
        )

    return pl.pallas_call(
        gather_kernel,
        out_shape=jax.ShapeDtypeStruct(objects.shape, F32),
        in_specs=[SMEM, VMEM],
        out_specs=VMEM,
        compiler_params=PARAMS,
        name="sum_windows",
    )(offsets.T, exchanged(grads))


def solution(mesh):
    in_specs = (
        P(("parts", "cuts"), None, None, None),
        P(),
        P(("parts", "cuts")),
        P(),
        P(),
        P("parts", None),
        P("parts", "cuts", None),
    )
    out_specs = P(("parts", "cuts"), None, None, None)
    return jax.shard_map(shards, mesh=mesh, in_specs=in_specs, out_specs=out_specs, check_vma=False)
```

```python
import math

import jax
import jax.numpy as jnp
import numpy as np
from jax import lax
from jax.experimental import pallas as pl
from jax.experimental.pallas import tpu as pltpu
from jax.sharding import PartitionSpec as P

TRANSMIT = 0.985
GROUP = 8
LANES = 128
ROWS = 16
F32 = jnp.float32
BF16 = jnp.bfloat16


def dot(former, latter):
    return jnp.dot(former, latter, preferred_element_type=F32)


def halves(x):
    return x[:, :LANES], x[:, LANES : 2 * LANES], x[:, 2 * LANES :]


def swapped(tail):
    return pltpu.roll(tail, LANES // 2, 1)


def low_half(rows):
    return lax.broadcasted_iota(jnp.int32, (rows, LANES), 1) < LANES // 2


def wide(x):
    x0, x1, xt = halves(x)
    low = low_half(xt.shape[0])
    return jnp.concatenate([x0, jnp.where(low, xt, 0.0), x1, jnp.where(low, swapped(xt), 0.0)], axis=1)


def narrow(x):
    x0, xt, x1, yt = (x[:, n * LANES : (n + 1) * LANES] for n in range(4))
    return jnp.concatenate([x0, x1, jnp.where(low_half(xt.shape[0]), xt, swapped(yt))], axis=1)


def parts(x):
    return x[:, : 2 * LANES], x[:, 2 * LANES :]


def upright(x):
    return jnp.concatenate(parts(x), axis=0)


def abreast(x):
    half = x.shape[0] // 2
    return jnp.concatenate([x[:half], x[half:]], axis=1)


def times(a, b):
    (ar, ai), (br, bi) = parts(a), parts(b)
    return jnp.concatenate([ar * br - ai * bi, ai * br + ar * bi], axis=1)


def times_conj(a, b):
    (ar, ai), (br, bi) = parts(a), parts(b)
    return jnp.concatenate([ar * br + ai * bi, ai * br - ar * bi], axis=1)


def transmission(window):
    real, imag = parts(wide(window.astype(F32)))
    return jnp.concatenate([TRANSMIT + real, imag], axis=1)


def split2(x):
    high = x.astype(BF16)
    return high, (x - high.astype(F32)).astype(BF16)


def picker(columns, start, high_tail, transposed=False):
    shape = (2 * LANES, columns) if transposed else (columns, 2 * LANES)
    a = lax.broadcasted_iota(jnp.int32, shape, 1 if transposed else 0) - start
    q = lax.broadcasted_iota(jnp.int32, shape, 0 if transposed else 1)
    if high_tail:
        half = LANES // 2
        wanted = jnp.where(q < LANES, q, jnp.where(q < LANES + half, -columns, q - half))
    else:
        wanted = jnp.where(q < LANES + LANES // 2, q, -columns)
    return jnp.where(a == wanted, 1.0, 0.0).astype(BF16)


def row_picker(shape, distance):
    taken = lax.broadcasted_iota(jnp.int32, shape, 1)
    wanted = lax.broadcasted_iota(jnp.int32, shape, 0) + distance
    return jnp.where(taken == wanted, 1.0, 0.0).astype(BF16)


def rows_near(x, start, count):
    limit = x.shape[0] - count
    bit = 1 << (limit.bit_length() - 1)
    while bit >= ROWS:
        length = count + bit
        short = bit + length - x.shape[0]
        if short > 0:
            x = jnp.concatenate([x, jnp.zeros((short, x.shape[1]), x.dtype)], axis=0)
        x = jnp.where(lax.bitwise_and(start, bit) != 0, x[bit : bit + length], x[:length])
        bit //= 2
    return x


def packed(real, imag, columns, start):
    left = dot(real, picker(columns, start, False))
    right = dot(imag, picker(columns, start, True))
    return jnp.concatenate(
        [left[:, :LANES], right[:, :LANES], left[:, LANES:] + right[:, LANES:]], axis=1
    )


def dft_constant(width):
    counter = np.arange(width)
    angle = (counter[:, None] * counter[None, :] % width) * (2.0 * math.pi / width)
    return (np.stack([np.cos(angle), -np.sin(angle)]) / math.sqrt(width)).astype(np.float32)


def slots_of(positions, size):
    order = list(range(0, size, 2)) + list(range(size - 1, 0, -2))
    return sorted(order[:positions])


def window_kernel(offsets_in, index_ref, objects_in, measured_in, blocks_out, blocks, offsets_ref, objects, measured, sems):
    positions, near_rows, width = measured.shape
    extent = objects.shape[-1]
    copies = [
        pltpu.make_async_copy(objects_in.at[0, 0], objects.at[0], sems.at[0]),
        pltpu.make_async_copy(objects_in.at[0, 1], objects.at[1], sems.at[1]),
        pltpu.make_async_copy(measured_in, measured, sems.at[2]),
        pltpu.make_async_copy(offsets_in, offsets_ref, sems.at[3]),
    ]
    for copy in copies:
        copy.start()
    tag = jnp.full((ROWS, LANES), index_ref[0], jnp.int32).astype(F32)
    for copy in copies:
        copy.wait()
    sending = []
    for p, slot in enumerate(slots_of(positions, blocks.shape[0])):
        start = offsets_ref[0, p]
        real, imag = (rows_near(objects[c], start, width) for c in range(2))
        window = packed(real, imag, extent, offsets_ref[1, p]).astype(BF16)
        shift = lax.bitwise_and(start, ROWS - 1)
        blocks[slot, :width, :] = dot(row_picker((width, width + ROWS), shift), window).astype(BF16)
        tail = measured[p, :, LANES:]
        seen = jnp.concatenate([measured[p, :, :LANES], tail, tail, tag[:near_rows]], axis=1)
        left_over = jnp.concatenate([tag[near_rows:]] * 3, axis=1)
        blocks[slot, width:, :] = jnp.concatenate([seen, left_over], axis=0).astype(BF16)
        sending.append(pltpu.make_async_copy(blocks.at[slot], blocks_out.at[slot], sems.at[4 + p]))
        sending[-1].start()
    for copy in sending:
        copy.wait()


def left_table(table, at, real, imag):
    width = real.shape[0]
    table[at, :width, :] = jnp.concatenate([real, -imag], axis=1).astype(BF16)
    table[at, width:, :] = jnp.concatenate([imag, real], axis=1).astype(BF16)


def right_table(table, at, real, imag):
    width = real.shape[0]
    second = 2 * LANES
    table[at] = jnp.zeros(table.shape[1:], BF16)
    for row, column, plane in (
        (0, 0, real),
        (0, second, imag),
        (second, 0, -imag),
        (second, second, real),
    ):
        table[at, row : row + width, column : column + width] = plane.astype(BF16)


def forward_tables(props, lf, rf):
    for k in range(props.shape[0]):
        real, imag = props[k, 0].astype(F32), props[k, 1].astype(F32)
        left_table(lf, k, real, imag)
        right_table(rf, k, real.T, imag.T)


def backward_tables(props, lb, rb):
    for k in range(props.shape[0]):
        real, imag = props[k, 0].astype(F32), props[k, 1].astype(F32)
        left_table(lb, k, real.T, -imag.T)
        right_table(rb, k, real, -imag)


def detector_tables(dft, left, right):
    for n, (real, imag) in enumerate(zip(split2(dft[0]), split2(dft[1]))):
        real, imag = real.astype(F32), imag.astype(F32)
        for at, sign in ((n, 1.0), (n + 2, -1.0)):
            if at < 3:
                left_table(left, at, real, sign * imag)
                right_table(right, at, real, sign * imag)


def forward_steps(blocks, waves, indices, lf, rf):
    sections, _, columns = blocks.shape
    width = columns // 2
    psi = waves[0]
    for k in range(sections):
        which = indices[k]
        z = times(psi.astype(F32), transmission(blocks[k, :width, :])).astype(BF16)
        h = dot(lf[which], upright(z)).astype(BF16)
        psi = dot(abreast(h), rf[which]).astype(BF16)
        waves[k + 1] = psi


def backward_steps(blocks, waves, indices, lb, rb, grads, g):
    sections, _, columns = blocks.shape
    width = columns // 2
    for k in reversed(range(sections)):
        which = indices[k]
        c = dot(lb[which], upright(g)).astype(BF16)
        y = dot(abreast(c), rb[which])
        g = times_conj(y, transmission(blocks[k, :width, :])).astype(BF16)
        grads[k] = narrow(times_conj(y, waves[k].astype(F32))).astype(BF16)
    return g


def sent(wave):
    return narrow(wave.astype(F32)).astype(BF16)


def received(wave):
    return wide(wave.astype(F32)).astype(BF16)


def detector(psi, observed, left, right):
    def product(ah, al, bh, bl):
        return dot(ah, bh) + (dot(ah, bl) + dot(al, bh))

    psi = upright(psi)
    near = abreast(dot(left[0], psi) + dot(left[1], psi))
    far = product(*split2(near), right[0], right[1])
    real, imag = parts(far)
    misfit = real * real + imag * imag - observed
    push = jnp.concatenate([misfit * real, misfit * imag], axis=0)
    back = dot(left[2], push.astype(BF16)).astype(BF16)
    return dot(abreast(back), right[2]).astype(BF16)


def read_indices(blocks, indices, count):
    for k in range(blocks.shape[0]):
        tag = jnp.max(blocks[k, -ROWS:, 2 * LANES :].astype(F32))
        indices[k] = jnp.clip(tag.astype(jnp.int32), 0, count - 1)


def place_in(size):
    rank = lax.axis_index("cuts")
    return lax.rem(rank, size), lax.div(rank, size)


def observe(blocks, near_rows, observed, first):
    for k in range(blocks.shape[0]):
        at = first + k * near_rows
        observed[at : at + near_rows, :] = blocks[k, -ROWS:, : 2 * LANES].astype(F32)[:near_rows]


def near_kernel(blocks, _, near, observed):
    observe(blocks, near.shape[0] // blocks.shape[0], observed, 0)
    near[...] = observed[...].astype(BF16)


def first_kernel(group_ref, probes, blocks, props, dft, leaving, waves, lf, rf, lb, rb, left, right, probe, indices, sem):
    size = blocks.shape[0]
    slot, group = place_in(size)

    @pl.when(group == 0)
    def _():
        position = 0
        for p, held in enumerate(slots_of(group_ref.shape[0], size)):
            position = jnp.where(slot == held, p, position)
        which = group_ref[position]
        copy = pltpu.make_async_copy(probes.at[which], probe, sem)
        copy.start()
        forward_tables(props, lf, rf)
        read_indices(blocks, indices, props.shape[0])
        copy.wait()
        waves[0] = wide(packed(probe[0], probe[1], probe.shape[-1], 0)).astype(BF16)
        forward_steps(blocks, waves, indices, lf, rf)
        leaving[...] = sent(waves[size])

    @pl.when(group > 0)
    def _():
        forward_tables(props, lf, rf)
        backward_tables(props, lb, rb)
        detector_tables(dft, left, right)


def forward_kernel(stage):
    def kernel(entering, blocks, lf, rf, waves_in, leaving, waves, indices):
        size = blocks.shape[0]
        _, group = place_in(size)

        @pl.when(group == stage)
        def _():
            read_indices(blocks, indices, lf.shape[0])
            waves[0] = received(entering[...])
            forward_steps(blocks, waves, indices, lf, rf)
            leaving[...] = sent(waves[size])

        @pl.when(group != stage)
        def _():
            waves[...] = waves_in[...]

    return kernel


def middle_kernel(groups):
    def kernel(waves, *refs):
        earlier, refs = refs[: groups - 1], refs[groups - 1 :]
        blocks, props, lb, rb, left, right, leaving, grads, lb_out, rb_out, observed, indices = refs
        size = blocks.shape[0]
        _, group = place_in(size)

        @pl.when(group == groups - 1)
        def _():
            read_indices(blocks, indices, props.shape[0])
            rows = earlier[0].shape[0]
            for n, near in enumerate(earlier):
                observed[n * rows : (n + 1) * rows, :] = near[...].astype(F32)
            observe(blocks, rows // size, observed, (groups - 1) * rows)
            g = detector(waves[size], observed[...], left, right)
            leaving[...] = sent(backward_steps(blocks, waves, indices, lb, rb, grads, g))

        @pl.when(group < groups - 1)
        def _():
            backward_tables(props, lb_out, rb_out)

    return kernel


def backward_kernel(stage):
    def kernel(arriving, waves, blocks, lb, rb, grads_in, leaving, grads, indices):
        _, group = place_in(blocks.shape[0])

        @pl.when(group == stage)
        def _():
            read_indices(blocks, indices, lb.shape[0])
            g = received(arriving[...])
            leaving[...] = sent(backward_steps(blocks, waves, indices, lb, rb, grads, g))

        @pl.when(group != stage)
        def _():
            grads[...] = grads_in[...]

    return kernel


def gather_kernel(offsets_ref, grads_ref, out_ref):
    positions = offsets_ref.shape[1]
    width = grads_ref.shape[1]
    extent = out_ref.shape[-1]
    spread_out = []
    for p, slot in enumerate(slots_of(positions, grads_ref.shape[0])):
        x0, x1, xt = halves(grads_ref[slot])
        spread_out.append(
            jnp.concatenate(
                [
                    dot(
                        jnp.concatenate([main, xt], axis=1),
                        picker(extent, offsets_ref[1, p], c == 1, transposed=True),
                    ).astype(BF16)
                    for c, main in ((0, x0), (1, x1))
                ],
                axis=1,
            )
        )
    rows = jnp.concatenate(
        [row_picker((extent, width), -offsets_ref[0, p]) for p in range(positions)], axis=1
    )
    total = dot(rows, jnp.concatenate(spread_out, axis=0))
    out_ref[0, 0] = total[:, :extent]
    out_ref[0, 1] = total[:, extent:]


VMEM = pl.BlockSpec(memory_space=pltpu.VMEM)
SMEM = pl.BlockSpec(memory_space=pltpu.SMEM)
HBM = pl.BlockSpec(memory_space=pl.ANY)
ALONE = pltpu.CompilerParams(vmem_limit_bytes=60 * 1024 * 1024)
PARAMS = pltpu.CompilerParams(vmem_limit_bytes=20 * 1024 * 1024)


def shards(objects, propagators, prop_index, probes, probe_group, offsets, measured):
    sections = lax.axis_size("cuts")
    width = probes.shape[-1]
    kinds = propagators.shape[0]
    near_rows = measured.shape[1]
    size = GROUP
    groups = sections // size
    rows = width + ROWS
    slots = slots_of(probe_group.shape[0], size)
    members = [list(range(first, first + size)) for first in range(0, sections, size)]

    def struct(*dims, kind=BF16):
        return jax.ShapeDtypeStruct(dims, kind)

    def exchanged(blocks):
        return lax.all_to_all(blocks, "cuts", 0, 0, axis_index_groups=members, tiled=True)

    def handed(block, stage, distance):
        route = [(stage * size + l, (stage + distance) * size + l) for l in slots]
        return lax.ppermute(block, "cuts", route)

    blocks = pl.pallas_call(
        window_kernel,
        out_shape=struct(size, rows, 2 * width),
        in_specs=[HBM, SMEM, HBM, HBM],
        out_specs=HBM,
        scratch_shapes=[
            pltpu.VMEM((size, rows, 2 * width), BF16),
            pltpu.SMEM(offsets.shape[::-1], jnp.int32),
            pltpu.VMEM(objects.shape[1:], BF16),
            pltpu.VMEM(measured.shape, F32),
            pltpu.SemaphoreType.DMA((4 + len(slots),)),
        ],
        compiler_params=ALONE,
        name="windows",
    )(offsets.T, prop_index, objects, measured)
    blocks = exchanged(blocks)

    wave = struct(width, 2 * width)
    near = struct(size * near_rows, 2 * LANES)
    full = 4 * LANES
    waves_shape = struct(size + 1, width, full)
    grads_shape = struct(size, width, 2 * width)
    lefts, rights = struct(kinds, 2 * width, 2 * width), struct(kinds, full, full)
    detector_tables_shapes = [struct(3, 2 * width, 2 * width), struct(3, full, full)]
    indices = pltpu.SMEM((size,), jnp.int32)

    def call(kernel, name, out_shape, in_specs, scratch_shapes, operands, slices=0):
        return pl.pallas_call(
            kernel,
            out_shape=out_shape,
            in_specs=in_specs,
            out_specs=[VMEM] * len(out_shape),
            scratch_shapes=scratch_shapes,
            compiler_params=PARAMS,
            cost_estimate=pl.CostEstimate(
                flops=16 * slices * width**3,
                bytes_accessed=sum(math.prod(x.shape) * x.dtype.itemsize for x in list(operands) + out_shape),
                transcendentals=0,
            ),
            name=name,
        )(*operands)

    leaving, waves, lf, rf, lb, rb, *dft = call(
        first_kernel,
        "first_forward",
        [wave, waves_shape, lefts, rights, lefts, rights] + detector_tables_shapes,
        [SMEM, HBM, VMEM, VMEM, VMEM],
        [pltpu.VMEM(probes.shape[1:], BF16), indices, pltpu.SemaphoreType.DMA],
        (probe_group, probes, blocks, propagators, jnp.asarray(dft_constant(width))),
        size,
    )
    entering = handed(leaving, 0, 1)
    (near_out,) = call(near_kernel, "near_rows", [near], [VMEM, HBM], [pltpu.VMEM(near.shape, F32)], (blocks, leaving))
    nears = [handed(near_out, stage, groups - 1 - stage) for stage in range(groups - 1)]
    for stage in range(1, groups):
        leaving, waves = call(
            forward_kernel(stage),
            "forward",
            [wave, waves_shape],
            [VMEM] * 5,
            [indices],
            (entering, blocks, lf, rf, waves),
            size,
        )
        if stage < groups - 1:
            entering = handed(leaving, stage, 1)

    leaving, grads, lb, rb = call(
        middle_kernel(groups),
        "middle",
        [wave, grads_shape, lefts, rights],
        [VMEM] * (groups + 6),
        [pltpu.VMEM((width, 2 * LANES), F32), indices],
        (waves, *nears, blocks, propagators, lb, rb, *dft),
        size,
    )

    for stage in range(groups - 2, -1, -1):
        arriving = handed(leaving, stage + 1, -1)
        leaving, grads = call(
            backward_kernel(stage),
            "backward",
            [wave, grads_shape],
            [VMEM] * 6,
            [indices],
            (arriving, waves, blocks, lb, rb, grads),
            size,
        )

    return pl.pallas_call(
        gather_kernel,
        out_shape=jax.ShapeDtypeStruct(objects.shape, F32),
        in_specs=[SMEM, VMEM],
        out_specs=VMEM,
        compiler_params=PARAMS,
        name="sum_windows",
    )(offsets.T, exchanged(grads))


def solution(mesh):
    in_specs = (
        P(("parts", "cuts"), None, None, None),
        P(),
        P(("parts", "cuts")),
        P(),
        P(),
        P("parts", None),
        P("parts", "cuts", None),
    )
    out_specs = P(("parts", "cuts"), None, None, None)
    return jax.shard_map(shards, mesh=mesh, in_specs=in_specs, out_specs=out_specs, check_vma=False)
```

```python
import math

import jax
import jax.numpy as jnp
import numpy as np
from jax import lax
from jax.experimental import pallas as pl
from jax.experimental.pallas import tpu as pltpu
from jax.sharding import PartitionSpec as P

TRANSMIT = 0.985
GROUP = 8
LANES = 128
ROWS = 16
F32 = jnp.float32
BF16 = jnp.bfloat16


def dot(former, latter):
    return jnp.dot(former, latter, preferred_element_type=F32)


def halves(x):
    return x[:, :LANES], x[:, LANES : 2 * LANES], x[:, 2 * LANES :]


def swapped(tail):
    return pltpu.roll(tail, LANES // 2, 1)


def low_half(rows):
    return lax.broadcasted_iota(jnp.int32, (rows, LANES), 1) < LANES // 2


def spread(tail):
    other = swapped(tail)
    low = low_half(tail.shape[0])
    return jnp.where(low, tail, other), jnp.where(low, other, tail)


def signed(tail, minus_low):
    low = low_half(tail.shape[0])
    return jnp.where(low == minus_low, -tail, tail)


def factor(b):
    b0, b1, bt = halves(b)
    return (b0, b1) + spread(bt)


def times(a, parts):
    a0, a1, at = halves(a)
    b0, b1, b_real, b_imag = parts
    tail = at * b_real + signed(swapped(at), True) * b_imag
    return jnp.concatenate([a0 * b0 - a1 * b1, a1 * b0 + a0 * b1, tail], axis=1)


def times_conj(a, turned, parts):
    a0, a1, at = halves(a)
    b0, b1, b_real, b_imag = parts
    tail = at * b_real + turned * b_imag
    return jnp.concatenate([a0 * b0 + a1 * b1, a1 * b0 - a0 * b1, tail], axis=1)


def joined(both, conj):
    width = both.shape[0] // 2
    u0, u1, ut = halves(both[:width])
    v0, v1, vt = halves(both[width:])
    turned = signed(swapped(vt), not conj)
    if conj:
        return jnp.concatenate([u0 + v1, u1 - v0, ut + turned], axis=1)
    return jnp.concatenate([u0 - v1, u1 + v0, ut + turned], axis=1)


def with_mean(window):
    x = window.astype(F32)
    x0, x1, xt = halves(x)
    mean = jnp.where(low_half(xt.shape[0]), TRANSMIT, 0.0)
    return jnp.concatenate([TRANSMIT + x0, x1, mean + xt], axis=1)


def split2(x):
    high = x.astype(BF16)
    return high, (x - high.astype(F32)).astype(BF16)


def picker(shape, start):
    columns, across = (0, 1) if shape[0] > shape[1] else (1, 0)
    taken = lax.broadcasted_iota(jnp.int32, shape, columns) - start
    place = lax.broadcasted_iota(jnp.int32, shape, across)
    wanted = jnp.where(place < LANES + LANES // 2, place, -shape[columns])
    return jnp.where(taken == wanted, 1.0, 0.0).astype(BF16)


def row_picker(shape, distance):
    taken = lax.broadcasted_iota(jnp.int32, shape, 1)
    wanted = lax.broadcasted_iota(jnp.int32, shape, 0) + distance
    return jnp.where(taken == wanted, 1.0, 0.0).astype(BF16)


def rows_near(x, start, count):
    limit = x.shape[0] - count
    bit = 1 << (limit.bit_length() - 1)
    while bit >= ROWS:
        length = count + bit
        short = bit + length - x.shape[0]
        if short > 0:
            x = jnp.concatenate([x, jnp.zeros((short, x.shape[1]), x.dtype)], axis=0)
        x = jnp.where(lax.bitwise_and(start, bit) != 0, x[bit : bit + length], x[:length])
        bit //= 2
    return x


def packed(real, imag):
    return jnp.concatenate([real[:, :LANES], imag[:, :LANES], real[:, LANES:], imag[:, LANES:]], axis=1)


def dft_constant(width):
    counter = np.arange(width)
    angle = (counter[:, None] * counter[None, :] % width) * (2.0 * math.pi / width)
    return (np.stack([np.cos(angle), -np.sin(angle)]) / math.sqrt(width)).astype(np.float32)


def slots_of(positions, size):
    half = size // 2
    order = list(range(half, size)) + list(range(0, half, 2)) + list(range(1, half, 2))
    return order[:positions]


def slots_in(group, positions, size):
    flip = (group % 2) * (size // 2)
    return [slot ^ flip for slot in slots_of(positions, size)]


def window_kernel(offsets_in, index_ref, objects_in, measured_in, blocks_out, blocks, offsets_ref, objects, measured, sems):
    positions, near_rows, width = measured.shape
    extent = objects.shape[-1]
    copies = [
        pltpu.make_async_copy(objects_in.at[0, 0], objects.at[0], sems.at[0]),
        pltpu.make_async_copy(objects_in.at[0, 1], objects.at[1], sems.at[1]),
        pltpu.make_async_copy(measured_in, measured, sems.at[2]),
        pltpu.make_async_copy(offsets_in, offsets_ref, sems.at[3]),
    ]
    for copy in copies:
        copy.start()
    tag = jnp.full((ROWS, LANES), index_ref[0], jnp.int32).astype(F32)
    for copy in copies:
        copy.wait()
    size = blocks_out.shape[0]
    _, group = place_in(size)
    flip = lax.rem(group, 2) * (size // 2)
    sending = []
    for p, slot in enumerate(slots_of(positions, size)):
        start = offsets_ref[0, p]
        both = jnp.concatenate([rows_near(objects[c], start, width) for c in range(2)], axis=0)
        picked = dot(both, picker((extent, 2 * LANES), offsets_ref[1, p]))
        real, imag = picked[: width + ROWS], picked[width + ROWS :]
        tail = jnp.where(low_half(width + ROWS), real[:, LANES:], swapped(imag[:, LANES:]))
        window = jnp.concatenate([real[:, :LANES], imag[:, :LANES], tail], axis=1).astype(BF16)
        shift = lax.bitwise_and(start, ROWS - 1)
        blocks[p, :width, :] = dot(row_picker((width, width + ROWS), shift), window).astype(BF16)
        tail = measured[p, :, LANES:]
        seen = jnp.concatenate([measured[p, :, :LANES], tail, tail, tag[:near_rows]], axis=1)
        left_over = jnp.concatenate([tag[near_rows:]] * 3, axis=1)
        blocks[p, width:, :] = jnp.concatenate([seen, left_over], axis=0).astype(BF16)
        target = blocks_out.at[lax.bitwise_xor(slot, flip)]
        sending.append(pltpu.make_async_copy(blocks.at[p], target, sems.at[4 + p]))
        sending[-1].start()
    for copy in sending:
        copy.wait()


def right_table(real, imag):
    upper, lower = packed(real, imag), packed(-imag, real)
    return jnp.concatenate([upper[:LANES], lower[:LANES], upper[LANES:], lower[LANES:]], axis=0).astype(BF16)


def forward_tables(props, rf):
    for k in range(props.shape[0]):
        rf[k] = right_table(props[k, 0].astype(F32).T, props[k, 1].astype(F32).T)


def backward_tables(props, lb, rb):
    width = props.shape[-1]
    for k in range(props.shape[0]):
        real, imag = props[k, 0].astype(F32), props[k, 1].astype(F32)
        lb[k, :width, :] = real.T.astype(BF16)
        lb[k, width:, :] = imag.T.astype(BF16)
        rb[k] = right_table(real, -imag)


def detector_tables(dft, left, right, right_conj):
    width = dft.shape[-1]
    for n, (real, imag) in enumerate(zip(split2(dft[0]), split2(dft[1]))):
        left[n, :width, :] = real
        left[n, width:, :] = imag
        real, imag = real.astype(F32), imag.astype(F32)
        right[n] = right_table(real, imag)
        if n == 0:
            right_conj[...] = right_table(real, -imag)


def forward_steps(blocks, waves, indices, lf, rf):
    sections, _, columns = blocks.shape
    width = columns // 2
    psi = waves[0]
    parts = factor(with_mean(blocks[0, :width, :]))
    for k in range(sections):
        which = indices[k]
        z = times(psi.astype(F32), parts).astype(BF16)
        h = joined(dot(lf[which].reshape(columns, width), z), False).astype(BF16)
        if k + 1 < sections:
            parts = factor(with_mean(blocks[k + 1, :width, :]))
        psi = dot(h, rf[which]).astype(BF16)
        waves[k + 1] = psi


def backward_steps(blocks, waves, indices, lb, rb, grads, g):
    sections, _, columns = blocks.shape
    width = columns // 2

    def leave(k, y, turned, wave_parts):
        grads[k] = times_conj(y, turned, wave_parts).astype(BF16)

    late = None
    for k in reversed(range(sections)):
        which = indices[k]
        both = dot(lb[which], g)
        if late is not None:
            leave(*late)
        c = joined(both, True).astype(BF16)
        wave_parts = factor(waves[k].astype(F32))
        window_parts = factor(with_mean(blocks[k, :width, :]))
        y = dot(c, rb[which])
        turned = signed(swapped(halves(y)[2]), False)
        g = times_conj(y, turned, window_parts).astype(BF16)
        late = (k, y, turned, wave_parts)
    leave(*late)
    return g


def detector(psi, observed, left, right, right_conj):
    def product(ah, al, bh, bl):
        return dot(ah, bh) + (dot(ah, bl) + dot(al, bh))

    near = joined(dot(left[0], psi) + dot(left[1], psi), False)
    far = product(*split2(near), right[0], right[1])
    f0, f1, ft = halves(far)
    other = swapped(ft)
    main = f0 * f0 + f1 * f1 - observed[:, :LANES]
    tail = ft * ft + other * other - observed[:, LANES:]
    push = jnp.concatenate([main * f0, main * f1, tail * ft], axis=1)
    back = joined(dot(left[0], push.astype(BF16)), True)
    return dot(back.astype(BF16), right_conj[...]).astype(BF16)


def read_indices(blocks, indices, count):
    for k in range(blocks.shape[0]):
        tag = jnp.max(blocks[k, -ROWS:, 2 * LANES :].astype(F32))
        indices[k] = jnp.clip(tag.astype(jnp.int32), 0, count - 1)


def place_in(size):
    rank = lax.axis_index("cuts")
    return lax.rem(rank, size), lax.div(rank, size)


def observe(blocks, near_rows, observed, first):
    for k in range(blocks.shape[0]):
        at = first + k * near_rows
        observed[at : at + near_rows, :] = blocks[k, -ROWS:, : 2 * LANES].astype(F32)[:near_rows]


def near_kernel(blocks, _, near, observed):
    observe(blocks, near.shape[0] // blocks.shape[0], observed, 0)
    near[...] = observed[...].astype(BF16)


def first_kernel(group_ref, probes, blocks, props, dft, leaving, waves, lb, rf, rb, left, right, right_conj, probe, indices, sem):
    size = blocks.shape[0]
    slot, group = place_in(size)

    @pl.when(group == 0)
    def _():
        position = 0
        for p, held in enumerate(slots_of(group_ref.shape[0], size)):
            position = jnp.where(slot == held, p, position)
        which = group_ref[position]
        copy = pltpu.make_async_copy(probes.at[which], probe, sem)
        copy.start()
        forward_tables(props, rf)
        read_indices(blocks, indices, props.shape[0])
        copy.wait()
        waves[0] = packed(probe[0].astype(F32), probe[1].astype(F32)).astype(BF16)
        forward_steps(blocks, waves, indices, props, rf)
        leaving[...] = waves[size]

    @pl.when(group > 0)
    def _():
        forward_tables(props, rf)
        backward_tables(props, lb, rb)
        detector_tables(dft, left, right, right_conj)


def forward_kernel(stage):
    def kernel(entering, blocks, props, rf, waves_in, leaving, waves, indices):
        size = blocks.shape[0]
        _, group = place_in(size)

        @pl.when(group == stage)
        def _():
            read_indices(blocks, indices, props.shape[0])
            waves[0] = entering[...]
            forward_steps(blocks, waves, indices, props, rf)
            leaving[...] = waves[size]

        @pl.when(group != stage)
        def _():
            waves[...] = waves_in[...]

    return kernel


def middle_kernel(groups):
    def kernel(waves, *refs):
        earlier, refs = refs[: groups - 1], refs[groups - 1 :]
        blocks, props, lb, rb, left, right, right_conj, leaving, grads, lb_out, rb_out, observed, indices = refs
        size = blocks.shape[0]
        _, group = place_in(size)

        @pl.when(group == groups - 1)
        def _():
            read_indices(blocks, indices, props.shape[0])
            rows = earlier[0].shape[0]
            for n, near in enumerate(earlier):
                observed[n * rows : (n + 1) * rows, :] = near[...].astype(F32)
            observe(blocks, rows // size, observed, (groups - 1) * rows)
            g = detector(waves[size], observed[...], left, right, right_conj)
            leaving[...] = backward_steps(blocks, waves, indices, lb, rb, grads, g)

        @pl.when(group < groups - 1)
        def _():
            backward_tables(props, lb_out, rb_out)

    return kernel


def backward_kernel(stage):
    def kernel(arriving, waves, blocks, lb, rb, grads_in, leaving, grads, indices):
        _, group = place_in(blocks.shape[0])

        @pl.when(group == stage)
        def _():
            read_indices(blocks, indices, lb.shape[0])
            leaving[...] = backward_steps(blocks, waves, indices, lb, rb, grads, arriving[...])

        @pl.when(group != stage)
        def _():
            grads[...] = grads_in[...]

    return kernel


def gather_kernel(offsets_ref, grads_ref, out_ref, planes, sems):
    positions = offsets_ref.shape[1]
    size, width, _ = grads_ref.shape
    extent = out_ref.shape[-1]
    _, group = place_in(size)
    flip = lax.rem(group, 2) * (size // 2)
    spread_out = []
    for p, slot in enumerate(slots_of(positions, size)):
        x0, x1, xt = halves(grads_ref[lax.bitwise_xor(slot, flip)])
        other = swapped(xt.astype(F32)).astype(BF16)
        both = jnp.concatenate(
            [jnp.concatenate([x0, xt], axis=1), jnp.concatenate([x1, other], axis=1)], axis=0
        )
        spread_out.append(dot(both, picker((2 * LANES, extent), offsets_ref[1, p])).astype(BF16))
    rows = jnp.concatenate(
        [row_picker((extent, width), -offsets_ref[0, p]) for p in range(positions)], axis=1
    )
    copies = []
    for c in range(2):
        here = slice(c * width, (c + 1) * width)
        planes[c] = dot(rows, jnp.concatenate([x[here] for x in spread_out], axis=0))
        copies.append(pltpu.make_async_copy(planes.at[c], out_ref.at[0, c], sems.at[c]))
        copies[-1].start()
    for copy in copies:
        copy.wait()


VMEM = pl.BlockSpec(memory_space=pltpu.VMEM)
SMEM = pl.BlockSpec(memory_space=pltpu.SMEM)
HBM = pl.BlockSpec(memory_space=pl.ANY)
ALONE = pltpu.CompilerParams(vmem_limit_bytes=60 * 1024 * 1024)
PARAMS = pltpu.CompilerParams(vmem_limit_bytes=20 * 1024 * 1024)


def shards(objects, propagators, prop_index, probes, probe_group, offsets, measured):
    sections = lax.axis_size("cuts")
    width = probes.shape[-1]
    kinds = propagators.shape[0]
    near_rows = measured.shape[1]
    size = GROUP
    groups = sections // size
    rows = width + ROWS
    slots = slots_of(probe_group.shape[0], size)
    members = [list(range(first, first + size)) for first in range(0, sections, size)]

    def struct(*dims, kind=BF16):
        return jax.ShapeDtypeStruct(dims, kind)

    def exchanged(blocks):
        return lax.all_to_all(blocks, "cuts", 0, 0, axis_index_groups=members, tiled=True)

    def handed(block, stage, distance):
        ends = (slots_in(at, len(slots), size) for at in (stage, stage + distance))
        route = [(stage * size + l, (stage + distance) * size + m) for l, m in zip(*ends)]
        return lax.ppermute(block, "cuts", route)

    blocks = pl.pallas_call(
        window_kernel,
        out_shape=struct(size, rows, 2 * width),
        in_specs=[HBM, SMEM, HBM, HBM],
        out_specs=HBM,
        scratch_shapes=[
            pltpu.VMEM((size, rows, 2 * width), BF16),
            pltpu.SMEM(offsets.shape[::-1], jnp.int32),
            pltpu.VMEM(objects.shape[1:], BF16),
            pltpu.VMEM(measured.shape, F32),
            pltpu.SemaphoreType.DMA((4 + len(slots),)),
        ],
        compiler_params=ALONE,
        name="windows",
    )(offsets.T, prop_index, objects, measured)
    blocks = exchanged(blocks)

    wave = struct(width, 2 * width)
    near = struct(size * near_rows, 2 * LANES)
    waves_shape = struct(size + 1, width, 2 * width)
    grads_shape = struct(size, width, 2 * width)
    left_table = struct(kinds, 2 * width, width)
    square_table = struct(kinds, 2 * width, 2 * width)
    detector_left = struct(2, 2 * width, width)
    detector_right = struct(2, 2 * width, 2 * width)
    indices = pltpu.SMEM((size,), jnp.int32)

    def call(kernel, name, out_shape, in_specs, scratch_shapes, operands, slices=0):
        return pl.pallas_call(
            kernel,
            out_shape=out_shape,
            in_specs=in_specs,
            out_specs=[VMEM] * len(out_shape),
            scratch_shapes=scratch_shapes,
            compiler_params=PARAMS,
            cost_estimate=pl.CostEstimate(
                flops=16 * slices * width**3,
                bytes_accessed=sum(math.prod(x.shape) * x.dtype.itemsize for x in list(operands) + out_shape),
                transcendentals=0,
            ),
            name=name,
        )(*operands)

    leaving, waves, lb, rf, rb, *dft = call(
        first_kernel,
        "first_forward",
        [wave, waves_shape, left_table, square_table, square_table]
        + [detector_left, detector_right, struct(2 * width, 2 * width)],
        [SMEM, HBM, VMEM, VMEM, VMEM],
        [pltpu.VMEM(probes.shape[1:], BF16), indices, pltpu.SemaphoreType.DMA],
        (probe_group, probes, blocks, propagators, jnp.asarray(dft_constant(width))),
        size,
    )
    entering = handed(leaving, 0, 1)
    (near_out,) = call(near_kernel, "near_rows", [near], [VMEM, HBM], [pltpu.VMEM(near.shape, F32)], (blocks, leaving))
    nears = [handed(near_out, stage, groups - 1 - stage) for stage in range(groups - 1)]
    for stage in range(1, groups):
        leaving, waves = call(
            forward_kernel(stage),
            "forward",
            [wave, waves_shape],
            [VMEM] * 5,
            [indices],
            (entering, blocks, propagators, rf, waves),
            size,
        )
        if stage < groups - 1:
            entering = handed(leaving, stage, 1)

    leaving, grads, lb, rb = call(
        middle_kernel(groups),
        "middle",
        [wave, grads_shape, left_table, square_table],
        [VMEM] * (groups + 7),
        [pltpu.VMEM((width, 2 * LANES), F32), indices],
        (waves, *nears, blocks, propagators, lb, rb, *dft),
        size,
    )

    for stage in range(groups - 2, -1, -1):
        arriving = handed(leaving, stage + 1, -1)
        leaving, grads = call(
            backward_kernel(stage),
            "backward",
            [wave, grads_shape],
            [VMEM] * 6,
            [indices],
            (arriving, waves, blocks, lb, rb, grads),
            size,
        )

    return pl.pallas_call(
        gather_kernel,
        out_shape=jax.ShapeDtypeStruct(objects.shape, F32),
        in_specs=[SMEM, VMEM],
        out_specs=HBM,
        scratch_shapes=[pltpu.VMEM(objects.shape[1:], F32), pltpu.SemaphoreType.DMA((2,))],
        compiler_params=PARAMS,
        name="sum_windows",
    )(offsets.T, exchanged(grads))


def solution(mesh):
    in_specs = (
        P(("parts", "cuts"), None, None, None),
        P(),
        P(("parts", "cuts")),
        P(),
        P(),
        P("parts", None),
        P("parts", "cuts", None),
    )
    out_specs = P(("parts", "cuts"), None, None, None)
    return jax.shard_map(shards, mesh=mesh, in_specs=in_specs, out_specs=out_specs, check_vma=False)
```

```python
import math

import jax
import jax.numpy as jnp
import numpy as np
from jax import lax
from jax.experimental import pallas as pl
from jax.experimental.pallas import tpu as pltpu
from jax.sharding import PartitionSpec as P

TRANSMIT = 0.985
GROUP = 8
LANES = 128
ROWS = 16
F32 = jnp.float32
BF16 = jnp.bfloat16


def dot(former, latter):
    return jnp.dot(former, latter, preferred_element_type=F32)


def halves(x):
    return x[:, :LANES], x[:, LANES : 2 * LANES], x[:, 2 * LANES :]


def swapped(tail):
    return pltpu.roll(tail, LANES // 2, 1)


def low_half(rows):
    return lax.broadcasted_iota(jnp.int32, (rows, LANES), 1) < LANES // 2


def spread(tail):
    other = swapped(tail)
    low = low_half(tail.shape[0])
    return jnp.where(low, tail, other), jnp.where(low, other, tail)


def signed(tail, minus_low):
    low = low_half(tail.shape[0])
    return jnp.where(low == minus_low, -tail, tail)


def factor(b):
    b0, b1, bt = halves(b)
    return (b0, b1) + spread(bt)


def times(a, parts):
    a0, a1, at = halves(a)
    b0, b1, b_real, b_imag = parts
    tail = at * b_real + signed(swapped(at), True) * b_imag
    return jnp.concatenate([a0 * b0 - a1 * b1, a1 * b0 + a0 * b1, tail], axis=1)


def times_conj(a, turned, parts):
    a0, a1, at = halves(a)
    b0, b1, b_real, b_imag = parts
    tail = at * b_real + turned * b_imag
    return jnp.concatenate([a0 * b0 + a1 * b1, a1 * b0 - a0 * b1, tail], axis=1)


def left_product(table, x, conj):
    width = x.shape[0]
    u0, u1, ut = halves(dot(table[:width], x))
    v0, v1, vt = halves(dot(table[width:], x))
    turned = signed(swapped(vt), not conj)
    if conj:
        return jnp.concatenate([u0 + v1, u1 - v0, ut + turned], axis=1)
    return jnp.concatenate([u0 - v1, u1 + v0, ut + turned], axis=1)


def right_product(x, table):
    half = x.shape[0] // 2
    return jnp.concatenate([dot(x[:half], table), dot(x[half:], table)], axis=0)


def with_mean(window):
    x = window.astype(F32)
    x0, x1, xt = halves(x)
    mean = jnp.where(low_half(xt.shape[0]), TRANSMIT, 0.0)
    return jnp.concatenate([TRANSMIT + x0, x1, mean + xt], axis=1)


def split2(x):
    high = x.astype(BF16)
    return high, (x - high.astype(F32)).astype(BF16)


def picker(shape, start, high_tail=False):
    columns, across = (0, 1) if shape[0] > shape[1] else (1, 0)
    half = LANES // 2
    taken = lax.broadcasted_iota(jnp.int32, shape, columns) - start
    place = lax.broadcasted_iota(jnp.int32, shape, across)
    if high_tail:
        wanted = jnp.where(place < LANES, place, jnp.where(place < LANES + half, -shape[columns], place - half))
    else:
        wanted = jnp.where(place < LANES + half, place, -shape[columns])
    return jnp.where(taken == wanted, 1.0, 0.0).astype(BF16)


def row_picker(shape, distance):
    taken = lax.broadcasted_iota(jnp.int32, shape, 1)
    wanted = lax.broadcasted_iota(jnp.int32, shape, 0) + distance
    return jnp.where(taken == wanted, 1.0, 0.0).astype(BF16)


def rows_near(x, start, count):
    limit = x.shape[0] - count
    bit = 1 << (limit.bit_length() - 1)
    while bit >= ROWS:
        length = count + bit
        short = bit + length - x.shape[0]
        if short > 0:
            x = jnp.concatenate([x, jnp.zeros((short, x.shape[1]), x.dtype)], axis=0)
        x = jnp.where(lax.bitwise_and(start, bit) != 0, x[bit : bit + length], x[:length])
        bit //= 2
    return x


def packed(real, imag):
    return jnp.concatenate([real[:, :LANES], imag[:, :LANES], real[:, LANES:], imag[:, LANES:]], axis=1)


def dft_constant(width):
    counter = np.arange(width)
    angle = (counter[:, None] * counter[None, :] % width) * (2.0 * math.pi / width)
    return (np.stack([np.cos(angle), -np.sin(angle)]) / math.sqrt(width)).astype(np.float32)


def slots_of(positions, size):
    half = size // 2
    order = list(range(half, size)) + list(range(0, half, 2)) + list(range(1, half, 2))
    return order[:positions]


def slots_in(group, positions, size):
    flip = (group % 2) * (size // 2)
    return [slot ^ flip for slot in slots_of(positions, size)]


def window_kernel(offsets_in, index_ref, objects_in, measured_in, blocks_out, blocks, offsets_ref, objects, measured, sems):
    positions, near_rows, width = measured.shape
    extent = objects.shape[-1]
    copies = [
        pltpu.make_async_copy(objects_in.at[0, 0], objects.at[0], sems.at[0]),
        pltpu.make_async_copy(objects_in.at[0, 1], objects.at[1], sems.at[1]),
        pltpu.make_async_copy(measured_in, measured, sems.at[2]),
        pltpu.make_async_copy(offsets_in, offsets_ref, sems.at[3]),
    ]
    for copy in copies:
        copy.start()
    tag = jnp.full((ROWS, LANES), index_ref[0], jnp.int32).astype(F32)
    for copy in copies:
        copy.wait()
    size = blocks_out.shape[0]
    _, group = place_in(size)
    flip = lax.rem(group, 2) * (size // 2)
    sending = []
    for p, slot in enumerate(slots_of(positions, size)):
        start = offsets_ref[0, p]
        real, imag = (
            dot(rows_near(objects[c], start, width), picker((extent, 2 * LANES), offsets_ref[1, p], c == 1))
            for c in range(2)
        )
        tail = real[:, LANES:] + imag[:, LANES:]
        window = jnp.concatenate([real[:, :LANES], imag[:, :LANES], tail], axis=1).astype(BF16)
        shift = lax.bitwise_and(start, ROWS - 1)
        blocks[p, :width, :] = dot(row_picker((width, width + ROWS), shift), window).astype(BF16)
        tail = measured[p, :, LANES:]
        seen = jnp.concatenate([measured[p, :, :LANES], tail, tail, tag[:near_rows]], axis=1)
        left_over = jnp.concatenate([tag[near_rows:]] * 3, axis=1)
        blocks[p, width:, :] = jnp.concatenate([seen, left_over], axis=0).astype(BF16)
        target = blocks_out.at[lax.bitwise_xor(slot, flip)]
        sending.append(pltpu.make_async_copy(blocks.at[p], target, sems.at[4 + p]))
        sending[-1].start()
    for copy in sending:
        copy.wait()


def right_table(real, imag):
    upper, lower = packed(real, imag), packed(-imag, real)
    return jnp.concatenate([upper[:LANES], lower[:LANES], upper[LANES:], lower[LANES:]], axis=0).astype(BF16)


def forward_tables(props, rf):
    for k in range(props.shape[0]):
        rf[k] = right_table(props[k, 0].astype(F32).T, props[k, 1].astype(F32).T)


def backward_tables(props, lb, rb):
    width = props.shape[-1]
    for k in range(props.shape[0]):
        real, imag = props[k, 0].astype(F32), props[k, 1].astype(F32)
        lb[k, :width, :] = real.T.astype(BF16)
        lb[k, width:, :] = imag.T.astype(BF16)
        rb[k] = right_table(real, -imag)


def detector_tables(dft, left, right, right_conj):
    width = dft.shape[-1]
    for n, (real, imag) in enumerate(zip(split2(dft[0]), split2(dft[1]))):
        left[n, :width, :] = real
        left[n, width:, :] = imag
        real, imag = real.astype(F32), imag.astype(F32)
        right[n] = right_table(real, imag)
        if n == 0:
            right_conj[...] = right_table(real, -imag)


def forward_steps(blocks, waves, indices, lf, rf):
    sections, _, columns = blocks.shape
    width = columns // 2
    psi = waves[0]
    parts = factor(with_mean(blocks[0, :width, :]))
    for k in range(sections):
        which = indices[k]
        z = times(psi.astype(F32), parts).astype(BF16)
        h = left_product(lf[which].reshape(columns, width), z, False).astype(BF16)
        if k + 1 < sections:
            parts = factor(with_mean(blocks[k + 1, :width, :]))
        psi = right_product(h, rf[which]).astype(BF16)
        waves[k + 1] = psi


def backward_steps(blocks, waves, indices, lb, rb, grads, g):
    sections, _, columns = blocks.shape
    width = columns // 2

    def leave(k, y, turned, wave_parts):
        grads[k] = times_conj(y, turned, wave_parts).astype(BF16)

    late = None
    for k in reversed(range(sections)):
        which = indices[k]
        c = left_product(lb[which], g, True).astype(BF16)
        if late is not None:
            leave(*late)
        wave_parts = factor(waves[k].astype(F32))
        window_parts = factor(with_mean(blocks[k, :width, :]))
        y = right_product(c, rb[which])
        turned = signed(swapped(halves(y)[2]), False)
        g = times_conj(y, turned, window_parts).astype(BF16)
        late = (k, y, turned, wave_parts)
    leave(*late)
    return g


def detector(psi, observed, left, right, right_conj):
    def product(ah, al, bh, bl):
        return dot(ah, bh) + (dot(ah, bl) + dot(al, bh))

    near = left_product(left[0], psi, False) + left_product(left[1], psi, False)
    far = product(*split2(near), right[0], right[1])
    f0, f1, ft = halves(far)
    other = swapped(ft)
    main = f0 * f0 + f1 * f1 - observed[:, :LANES]
    tail = ft * ft + other * other - observed[:, LANES:]
    push = jnp.concatenate([main * f0, main * f1, tail * ft], axis=1)
    back = left_product(left[0], push.astype(BF16), True)
    return dot(back.astype(BF16), right_conj[...]).astype(BF16)


def read_indices(blocks, indices, count):
    for k in range(blocks.shape[0]):
        tag = jnp.max(blocks[k, -ROWS:, 2 * LANES :].astype(F32))
        indices[k] = jnp.clip(tag.astype(jnp.int32), 0, count - 1)


def place_in(size):
    rank = lax.axis_index("cuts")
    return lax.rem(rank, size), lax.div(rank, size)


def observe(blocks, near_rows, observed, first):
    for k in range(blocks.shape[0]):
        at = first + k * near_rows
        observed[at : at + near_rows, :] = blocks[k, -ROWS:, : 2 * LANES].astype(F32)[:near_rows]


def near_kernel(blocks, _, near, observed):
    observe(blocks, near.shape[0] // blocks.shape[0], observed, 0)
    near[...] = observed[...].astype(BF16)


def first_kernel(group_ref, probes, blocks, props, dft, leaving, waves, lb, rf, rb, left, right, right_conj, probe, indices, sem):
    size = blocks.shape[0]
    slot, group = place_in(size)

    @pl.when(group == 0)
    def _():
        position = 0
        for p, held in enumerate(slots_of(group_ref.shape[0], size)):
            position = jnp.where(slot == held, p, position)
        which = group_ref[position]
        copy = pltpu.make_async_copy(probes.at[which], probe, sem)
        copy.start()
        forward_tables(props, rf)
        read_indices(blocks, indices, props.shape[0])
        copy.wait()
        waves[0] = packed(probe[0].astype(F32), probe[1].astype(F32)).astype(BF16)
        forward_steps(blocks, waves, indices, props, rf)
        leaving[...] = waves[size]

    @pl.when(group > 0)
    def _():
        forward_tables(props, rf)
        backward_tables(props, lb, rb)
        detector_tables(dft, left, right, right_conj)


def forward_kernel(stage):
    def kernel(entering, blocks, props, rf, waves_in, leaving, waves, indices):
        size = blocks.shape[0]
        _, group = place_in(size)

        @pl.when(group == stage)
        def _():
            read_indices(blocks, indices, props.shape[0])
            waves[0] = entering[...]
            forward_steps(blocks, waves, indices, props, rf)
            leaving[...] = waves[size]

        @pl.when(group != stage)
        def _():
            waves[...] = waves_in[...]

    return kernel


def middle_kernel(groups):
    def kernel(waves, *refs):
        earlier, refs = refs[: groups - 1], refs[groups - 1 :]
        blocks, props, lb, rb, left, right, right_conj, leaving, grads, lb_out, rb_out, observed, indices = refs
        size = blocks.shape[0]
        _, group = place_in(size)

        @pl.when(group == groups - 1)
        def _():
            read_indices(blocks, indices, props.shape[0])
            rows = earlier[0].shape[0]
            for n, near in enumerate(earlier):
                observed[n * rows : (n + 1) * rows, :] = near[...].astype(F32)
            observe(blocks, rows // size, observed, (groups - 1) * rows)
            g = detector(waves[size], observed[...], left, right, right_conj)
            leaving[...] = backward_steps(blocks, waves, indices, lb, rb, grads, g)

        @pl.when(group < groups - 1)
        def _():
            backward_tables(props, lb_out, rb_out)

    return kernel


def backward_kernel(stage):
    def kernel(arriving, waves, blocks, lb, rb, grads_in, leaving, grads, indices):
        _, group = place_in(blocks.shape[0])

        @pl.when(group == stage)
        def _():
            read_indices(blocks, indices, lb.shape[0])
            leaving[...] = backward_steps(blocks, waves, indices, lb, rb, grads, arriving[...])

        @pl.when(group != stage)
        def _():
            grads[...] = grads_in[...]

    return kernel


def gather_kernel(offsets_ref, grads_ref, out_ref, planes, sems):
    positions = offsets_ref.shape[1]
    size, width, _ = grads_ref.shape
    extent = out_ref.shape[-1]
    _, group = place_in(size)
    flip = lax.rem(group, 2) * (size // 2)
    spread_out = []
    for p, slot in enumerate(slots_of(positions, size)):
        x0, x1, xt = halves(grads_ref[lax.bitwise_xor(slot, flip)])
        other = swapped(xt.astype(F32)).astype(BF16)
        both = jnp.concatenate(
            [jnp.concatenate([x0, xt], axis=1), jnp.concatenate([x1, other], axis=1)], axis=0
        )
        spread_out.append(dot(both, picker((2 * LANES, extent), offsets_ref[1, p])).astype(BF16))
    rows = jnp.concatenate(
        [row_picker((extent, width), -offsets_ref[0, p]) for p in range(positions)], axis=1
    )
    copies = []
    for c in range(2):
        here = slice(c * width, (c + 1) * width)
        planes[c] = dot(rows, jnp.concatenate([x[here] for x in spread_out], axis=0))
        copies.append(pltpu.make_async_copy(planes.at[c], out_ref.at[0, c], sems.at[c]))
        copies[-1].start()
    for copy in copies:
        copy.wait()


VMEM = pl.BlockSpec(memory_space=pltpu.VMEM)
SMEM = pl.BlockSpec(memory_space=pltpu.SMEM)
HBM = pl.BlockSpec(memory_space=pl.ANY)
ALONE = pltpu.CompilerParams(vmem_limit_bytes=60 * 1024 * 1024)
PARAMS = pltpu.CompilerParams(vmem_limit_bytes=20 * 1024 * 1024)


def shards(objects, propagators, prop_index, probes, probe_group, offsets, measured):
    sections = lax.axis_size("cuts")
    width = probes.shape[-1]
    kinds = propagators.shape[0]
    near_rows = measured.shape[1]
    size = GROUP
    groups = sections // size
    rows = width + ROWS
    slots = slots_of(probe_group.shape[0], size)
    members = [list(range(first, first + size)) for first in range(0, sections, size)]

    def struct(*dims, kind=BF16):
        return jax.ShapeDtypeStruct(dims, kind)

    def exchanged(blocks):
        return lax.all_to_all(blocks, "cuts", 0, 0, axis_index_groups=members, tiled=True)

    def handed(block, stage, distance):
        ends = (slots_in(at, len(slots), size) for at in (stage, stage + distance))
        route = [(stage * size + l, (stage + distance) * size + m) for l, m in zip(*ends)]
        return lax.ppermute(block, "cuts", route)

    blocks = pl.pallas_call(
        window_kernel,
        out_shape=struct(size, rows, 2 * width),
        in_specs=[HBM, SMEM, HBM, HBM],
        out_specs=HBM,
        scratch_shapes=[
            pltpu.VMEM((size, rows, 2 * width), BF16),
            pltpu.SMEM(offsets.shape[::-1], jnp.int32),
            pltpu.VMEM(objects.shape[1:], BF16),
            pltpu.VMEM(measured.shape, F32),
            pltpu.SemaphoreType.DMA((4 + len(slots),)),
        ],
        compiler_params=ALONE,
        name="windows",
    )(offsets.T, prop_index, objects, measured)
    blocks = exchanged(blocks)

    wave = struct(width, 2 * width)
    near = struct(size * near_rows, 2 * LANES)
    waves_shape = struct(size + 1, width, 2 * width)
    grads_shape = struct(size, width, 2 * width)
    left_table = struct(kinds, 2 * width, width)
    square_table = struct(kinds, 2 * width, 2 * width)
    detector_left = struct(2, 2 * width, width)
    detector_right = struct(2, 2 * width, 2 * width)
    indices = pltpu.SMEM((size,), jnp.int32)

    def call(kernel, name, out_shape, in_specs, scratch_shapes, operands, slices=0):
        return pl.pallas_call(
            kernel,
            out_shape=out_shape,
            in_specs=in_specs,
            out_specs=[VMEM] * len(out_shape),
            scratch_shapes=scratch_shapes,
            compiler_params=PARAMS,
            cost_estimate=pl.CostEstimate(
                flops=16 * slices * width**3,
                bytes_accessed=sum(math.prod(x.shape) * x.dtype.itemsize for x in list(operands) + out_shape),
                transcendentals=0,
            ),
            name=name,
        )(*operands)

    leaving, waves, lb, rf, rb, *dft = call(
        first_kernel,
        "first_forward",
        [wave, waves_shape, left_table, square_table, square_table]
        + [detector_left, detector_right, struct(2 * width, 2 * width)],
        [SMEM, HBM, VMEM, VMEM, VMEM],
        [pltpu.VMEM(probes.shape[1:], BF16), indices, pltpu.SemaphoreType.DMA],
        (probe_group, probes, blocks, propagators, jnp.asarray(dft_constant(width))),
        size,
    )
    entering = handed(leaving, 0, 1)
    (near_out,) = call(near_kernel, "near_rows", [near], [VMEM, HBM], [pltpu.VMEM(near.shape, F32)], (blocks, leaving))
    nears = [handed(near_out, stage, groups - 1 - stage) for stage in range(groups - 1)]
    for stage in range(1, groups):
        leaving, waves = call(
            forward_kernel(stage),
            "forward",
            [wave, waves_shape],
            [VMEM] * 5,
            [indices],
            (entering, blocks, propagators, rf, waves),
            size,
        )
        if stage < groups - 1:
            entering = handed(leaving, stage, 1)

    leaving, grads, lb, rb = call(
        middle_kernel(groups),
        "middle",
        [wave, grads_shape, left_table, square_table],
        [VMEM] * (groups + 7),
        [pltpu.VMEM((width, 2 * LANES), F32), indices],
        (waves, *nears, blocks, propagators, lb, rb, *dft),
        size,
    )

    for stage in range(groups - 2, -1, -1):
        arriving = handed(leaving, stage + 1, -1)
        leaving, grads = call(
            backward_kernel(stage),
            "backward",
            [wave, grads_shape],
            [VMEM] * 6,
            [indices],
            (arriving, waves, blocks, lb, rb, grads),
            size,
        )

    return pl.pallas_call(
        gather_kernel,
        out_shape=jax.ShapeDtypeStruct(objects.shape, F32),
        in_specs=[SMEM, VMEM],
        out_specs=HBM,
        scratch_shapes=[pltpu.VMEM(objects.shape[1:], F32), pltpu.SemaphoreType.DMA((2,))],
        compiler_params=PARAMS,
        name="sum_windows",
    )(offsets.T, exchanged(grads))


def solution(mesh):
    in_specs = (
        P(("parts", "cuts"), None, None, None),
        P(),
        P(("parts", "cuts")),
        P(),
        P(),
        P("parts", None),
        P("parts", "cuts", None),
    )
    out_specs = P(("parts", "cuts"), None, None, None)
    return jax.shard_map(shards, mesh=mesh, in_specs=in_specs, out_specs=out_specs, check_vma=False)
```

```python
import math

import jax
import jax.numpy as jnp
import numpy as np
from jax import lax
from jax.experimental import pallas as pl
from jax.experimental.pallas import tpu as pltpu
from jax.sharding import PartitionSpec as P

TRANSMIT = 0.985
GROUP = 8
LANES = 128
ROWS = 16
F32 = jnp.float32
BF16 = jnp.bfloat16


def dot(former, latter):
    return jnp.dot(former, latter, preferred_element_type=F32)


def halves(x):
    return x[:, :LANES], x[:, LANES : 2 * LANES], x[:, 2 * LANES :]


def swapped(tail):
    return pltpu.roll(tail, LANES // 2, 1)


def low_half(rows):
    return lax.broadcasted_iota(jnp.int32, (rows, LANES), 1) < LANES // 2


def spread(tail):
    other = swapped(tail)
    low = low_half(tail.shape[0])
    return jnp.where(low, tail, other), jnp.where(low, other, tail)


def signed(tail, minus_low):
    low = low_half(tail.shape[0])
    return jnp.where(low == minus_low, -tail, tail)


def factor(b):
    b0, b1, bt = halves(b)
    return (b0, b1) + spread(bt)


def upright(real, real_tail, imag, imag_tail):
    return jnp.concatenate(
        [jnp.concatenate([real, real_tail], axis=1), jnp.concatenate([imag, imag_tail], axis=1)], axis=0
    ).astype(BF16)


def from_upright(x):
    width = x.shape[0] // 2
    real, imag = x[:width], x[width:]
    tail = jnp.where(low_half(width), real[:, LANES:], swapped(imag[:, LANES:]))
    return jnp.concatenate([real[:, :LANES], imag[:, :LANES], tail], axis=1)


def to_upright(x):
    x0, x1, xt = halves(x)
    return upright(x0, xt, x1, swapped(xt))


def times_upright(a, parts):
    a0, a1, at = halves(a)
    b0, b1, b_real, b_imag = parts
    other = swapped(at)
    return upright(
        a0 * b0 - a1 * b1, at * b_real - other * b_imag, a1 * b0 + a0 * b1, other * b_real + at * b_imag
    )


def times_conj_upright(a, other, parts):
    a0, a1, at = halves(a)
    b0, b1, b_real, b_imag = parts
    return upright(
        a0 * b0 + a1 * b1, at * b_real + other * b_imag, a1 * b0 - a0 * b1, other * b_real - at * b_imag
    )


def times_conj(a, other, parts):
    a0, a1, at = halves(a)
    b0, b1, b_real, b_imag = parts
    tail = at * b_real + signed(other, False) * b_imag
    return jnp.concatenate([a0 * b0 + a1 * b1, a1 * b0 - a0 * b1, tail], axis=1)


def with_mean(window):
    x = window.astype(F32)
    x0, x1, xt = halves(x)
    mean = jnp.where(low_half(xt.shape[0]), TRANSMIT, 0.0)
    return jnp.concatenate([TRANSMIT + x0, x1, mean + xt], axis=1)


def split2(x):
    high = x.astype(BF16)
    return high, (x - high.astype(F32)).astype(BF16)


def picker(shape, start, high_tail=False):
    columns, across = (0, 1) if shape[0] > shape[1] else (1, 0)
    half = LANES // 2
    taken = lax.broadcasted_iota(jnp.int32, shape, columns) - start
    place = lax.broadcasted_iota(jnp.int32, shape, across)
    if high_tail:
        wanted = jnp.where(place < LANES, place, jnp.where(place < LANES + half, -shape[columns], place - half))
    else:
        wanted = jnp.where(place < LANES + half, place, -shape[columns])
    return jnp.where(taken == wanted, 1.0, 0.0).astype(BF16)


def row_picker(shape, distance):
    taken = lax.broadcasted_iota(jnp.int32, shape, 1)
    wanted = lax.broadcasted_iota(jnp.int32, shape, 0) + distance
    return jnp.where(taken == wanted, 1.0, 0.0).astype(BF16)


def rows_near(x, start, count):
    limit = x.shape[0] - count
    bit = 1 << (limit.bit_length() - 1)
    while bit >= ROWS:
        length = count + bit
        short = bit + length - x.shape[0]
        if short > 0:
            x = jnp.concatenate([x, jnp.zeros((short, x.shape[1]), x.dtype)], axis=0)
        x = jnp.where(lax.bitwise_and(start, bit) != 0, x[bit : bit + length], x[:length])
        bit //= 2
    return x


def packed(real, imag):
    return jnp.concatenate([real[:, :LANES], imag[:, :LANES], real[:, LANES:], imag[:, LANES:]], axis=1)


def dft_constant(width):
    counter = np.arange(width)
    angle = (counter[:, None] * counter[None, :] % width) * (2.0 * math.pi / width)
    return (np.stack([np.cos(angle), -np.sin(angle)]) / math.sqrt(width)).astype(np.float32)


def slots_of(positions, size):
    half = size // 2
    order = list(range(half, size)) + list(range(0, half, 2)) + list(range(1, half, 2))
    return order[:positions]


def slots_in(group, positions, size):
    flip = (group % 2) * (size // 2)
    return [slot ^ flip for slot in slots_of(positions, size)]


def window_kernel(offsets_in, index_ref, objects_in, measured_in, blocks_out, blocks, offsets_ref, objects, measured, sems):
    positions, near_rows, width = measured.shape
    extent = objects.shape[-1]
    copies = [
        pltpu.make_async_copy(objects_in.at[0, 0], objects.at[0], sems.at[0]),
        pltpu.make_async_copy(objects_in.at[0, 1], objects.at[1], sems.at[1]),
        pltpu.make_async_copy(measured_in, measured, sems.at[2]),
        pltpu.make_async_copy(offsets_in, offsets_ref, sems.at[3]),
    ]
    for copy in copies:
        copy.start()
    tag = jnp.full((ROWS, LANES), index_ref[0], jnp.int32).astype(F32)
    for copy in copies:
        copy.wait()
    size = blocks_out.shape[0]
    _, group = place_in(size)
    flip = lax.rem(group, 2) * (size // 2)
    sending = []
    for p, slot in enumerate(slots_of(positions, size)):
        start = offsets_ref[0, p]
        real, imag = (
            dot(rows_near(objects[c], start, width), picker((extent, 2 * LANES), offsets_ref[1, p], c == 1))
            for c in range(2)
        )
        tail = real[:, LANES:] + imag[:, LANES:]
        window = jnp.concatenate([real[:, :LANES], imag[:, :LANES], tail], axis=1).astype(BF16)
        shift = lax.bitwise_and(start, ROWS - 1)
        blocks[p, :width, :] = dot(row_picker((width, width + ROWS), shift), window).astype(BF16)
        tail = measured[p, :, LANES:]
        seen = jnp.concatenate([measured[p, :, :LANES], tail, tail, tag[:near_rows]], axis=1)
        left_over = jnp.concatenate([tag[near_rows:]] * 3, axis=1)
        blocks[p, width:, :] = jnp.concatenate([seen, left_over], axis=0).astype(BF16)
        target = blocks_out.at[lax.bitwise_xor(slot, flip)]
        sending.append(pltpu.make_async_copy(blocks.at[p], target, sems.at[4 + p]))
        sending[-1].start()
    for copy in sending:
        copy.wait()


def right_table(real, imag):
    upper, lower = packed(real, imag), packed(-imag, real)
    return jnp.concatenate([upper[:LANES], lower[:LANES], upper[LANES:], lower[LANES:]], axis=0).astype(BF16)


def left_table(real, imag):
    return jnp.concatenate(
        [jnp.concatenate([real, -imag], axis=1), jnp.concatenate([imag, real], axis=1)], axis=0
    ).astype(BF16)


def forward_tables(props, lf, rf):
    for k in range(props.shape[0]):
        real, imag = props[k, 0].astype(F32), props[k, 1].astype(F32)
        lf[k] = left_table(real, imag)
        rf[k] = right_table(real.T, imag.T)


def backward_tables(props, lb, rb):
    for k in range(props.shape[0]):
        real, imag = props[k, 0].astype(F32), props[k, 1].astype(F32)
        lb[k] = left_table(real.T, -imag.T)
        rb[k] = right_table(real, -imag)


def detector_tables(dft, left, right):
    for n, (real, imag) in enumerate(zip(split2(dft[0]), split2(dft[1]))):
        real, imag = real.astype(F32), imag.astype(F32)
        left[n] = left_table(real, imag)
        right[n] = right_table(real, imag)
        if n == 0:
            left[2] = left_table(real, -imag)
            right[2] = right_table(real, -imag)


def forward_steps(blocks, waves, indices, lf, rf):
    sections, _, columns = blocks.shape
    width = columns // 2
    psi = waves[0]
    for k in range(sections):
        which = indices[k]
        z = times_upright(psi.astype(F32), factor(with_mean(blocks[k, :width, :])))
        h = from_upright(dot(lf[which], z)).astype(BF16)
        psi = dot(h, rf[which]).astype(BF16)
        waves[k + 1] = psi


def backward_steps(blocks, waves, indices, lb, rb, grads, g):
    sections, _, columns = blocks.shape
    width = columns // 2
    for k in reversed(range(sections)):
        which = indices[k]
        c = from_upright(dot(lb[which], g)).astype(BF16)
        y = dot(c, rb[which])
        other = swapped(halves(y)[2])
        g = times_conj_upright(y, other, factor(with_mean(blocks[k, :width, :])))
        grads[k] = times_conj(y, other, factor(waves[k].astype(F32))).astype(BF16)
    return from_upright(g.astype(F32)).astype(BF16)


def detector(psi, observed, left, right):
    def product(ah, al, bh, bl):
        return dot(ah, bh) + (dot(ah, bl) + dot(al, bh))

    psi = to_upright(psi.astype(F32))
    near = from_upright(dot(left[0], psi) + dot(left[1], psi))
    far = product(*split2(near), right[0], right[1])
    f0, f1, ft = halves(far)
    other = swapped(ft)
    main = f0 * f0 + f1 * f1 - observed[:, :LANES]
    tail = ft * ft + other * other - observed[:, LANES:]
    push = upright(main * f0, tail * ft, main * f1, tail * other)
    back = from_upright(dot(left[2], push)).astype(BF16)
    return to_upright(dot(back, right[2]))


def read_indices(blocks, indices, count):
    for k in range(blocks.shape[0]):
        tag = jnp.max(blocks[k, -ROWS:, 2 * LANES :].astype(F32))
        indices[k] = jnp.clip(tag.astype(jnp.int32), 0, count - 1)


def place_in(size):
    rank = lax.axis_index("cuts")
    return lax.rem(rank, size), lax.div(rank, size)


def observe(blocks, near_rows, observed, first):
    for k in range(blocks.shape[0]):
        at = first + k * near_rows
        observed[at : at + near_rows, :] = blocks[k, -ROWS:, : 2 * LANES].astype(F32)[:near_rows]


def near_kernel(blocks, _, near, observed):
    observe(blocks, near.shape[0] // blocks.shape[0], observed, 0)
    near[...] = observed[...].astype(BF16)


def first_kernel(group_ref, probes, blocks, props, dft, leaving, waves, lf, rf, lb, rb, left, right, probe, indices, sem):
    size = blocks.shape[0]
    slot, group = place_in(size)

    @pl.when(group == 0)
    def _():
        position = 0
        for p, held in enumerate(slots_of(group_ref.shape[0], size)):
            position = jnp.where(slot == held, p, position)
        which = group_ref[position]
        copy = pltpu.make_async_copy(probes.at[which], probe, sem)
        copy.start()
        forward_tables(props, lf, rf)
        read_indices(blocks, indices, props.shape[0])
        copy.wait()
        waves[0] = packed(probe[0].astype(F32), probe[1].astype(F32)).astype(BF16)
        forward_steps(blocks, waves, indices, lf, rf)
        leaving[...] = waves[size]

    @pl.when(group > 0)
    def _():
        forward_tables(props, lf, rf)
        backward_tables(props, lb, rb)
        detector_tables(dft, left, right)


def forward_kernel(stage):
    def kernel(entering, blocks, lf, rf, waves_in, leaving, waves, indices):
        size = blocks.shape[0]
        _, group = place_in(size)

        @pl.when(group == stage)
        def _():
            read_indices(blocks, indices, lf.shape[0])
            waves[0] = entering[...]
            forward_steps(blocks, waves, indices, lf, rf)
            leaving[...] = waves[size]

        @pl.when(group != stage)
        def _():
            waves[...] = waves_in[...]

    return kernel


def middle_kernel(groups):
    def kernel(waves, *refs):
        earlier, refs = refs[: groups - 1], refs[groups - 1 :]
        blocks, props, lb, rb, left, right, leaving, grads, lb_out, rb_out, observed, indices = refs
        size = blocks.shape[0]
        _, group = place_in(size)

        @pl.when(group == groups - 1)
        def _():
            read_indices(blocks, indices, props.shape[0])
            rows = earlier[0].shape[0]
            for n, near in enumerate(earlier):
                observed[n * rows : (n + 1) * rows, :] = near[...].astype(F32)
            observe(blocks, rows // size, observed, (groups - 1) * rows)
            g = detector(waves[size], observed[...], left, right)
            leaving[...] = backward_steps(blocks, waves, indices, lb, rb, grads, g)

        @pl.when(group < groups - 1)
        def _():
            backward_tables(props, lb_out, rb_out)

    return kernel


def backward_kernel(stage):
    def kernel(arriving, waves, blocks, lb, rb, grads_in, leaving, grads, indices):
        _, group = place_in(blocks.shape[0])

        @pl.when(group == stage)
        def _():
            read_indices(blocks, indices, lb.shape[0])
            g = to_upright(arriving[...].astype(F32))
            leaving[...] = backward_steps(blocks, waves, indices, lb, rb, grads, g)

        @pl.when(group != stage)
        def _():
            grads[...] = grads_in[...]

    return kernel


def gather_kernel(offsets_ref, grads_ref, out_ref, planes, sems):
    positions = offsets_ref.shape[1]
    size, width, _ = grads_ref.shape
    extent = out_ref.shape[-1]
    _, group = place_in(size)
    flip = lax.rem(group, 2) * (size // 2)
    spread_out = []
    for p, slot in enumerate(slots_of(positions, size)):
        x0, x1, xt = halves(grads_ref[lax.bitwise_xor(slot, flip)])
        other = swapped(xt.astype(F32)).astype(BF16)
        both = jnp.concatenate(
            [jnp.concatenate([x0, xt], axis=1), jnp.concatenate([x1, other], axis=1)], axis=0
        )
        spread_out.append(dot(both, picker((2 * LANES, extent), offsets_ref[1, p])).astype(BF16))
    rows = jnp.concatenate(
        [row_picker((extent, width), -offsets_ref[0, p]) for p in range(positions)], axis=1
    )
    copies = []
    for c in range(2):
        here = slice(c * width, (c + 1) * width)
        planes[c] = dot(rows, jnp.concatenate([x[here] for x in spread_out], axis=0))
        copies.append(pltpu.make_async_copy(planes.at[c], out_ref.at[0, c], sems.at[c]))
        copies[-1].start()
    for copy in copies:
        copy.wait()


VMEM = pl.BlockSpec(memory_space=pltpu.VMEM)
SMEM = pl.BlockSpec(memory_space=pltpu.SMEM)
HBM = pl.BlockSpec(memory_space=pl.ANY)
ALONE = pltpu.CompilerParams(vmem_limit_bytes=60 * 1024 * 1024)
PARAMS = pltpu.CompilerParams(vmem_limit_bytes=20 * 1024 * 1024)


def shards(objects, propagators, prop_index, probes, probe_group, offsets, measured):
    sections = lax.axis_size("cuts")
    width = probes.shape[-1]
    kinds = propagators.shape[0]
    near_rows = measured.shape[1]
    size = GROUP
    groups = sections // size
    rows = width + ROWS
    slots = slots_of(probe_group.shape[0], size)
    members = [list(range(first, first + size)) for first in range(0, sections, size)]

    def struct(*dims, kind=BF16):
        return jax.ShapeDtypeStruct(dims, kind)

    def exchanged(blocks):
        return lax.all_to_all(blocks, "cuts", 0, 0, axis_index_groups=members, tiled=True)

    def handed(block, stage, distance):
        ends = (slots_in(at, len(slots), size) for at in (stage, stage + distance))
        route = [(stage * size + l, (stage + distance) * size + m) for l, m in zip(*ends)]
        return lax.ppermute(block, "cuts", route)

    blocks = pl.pallas_call(
        window_kernel,
        out_shape=struct(size, rows, 2 * width),
        in_specs=[HBM, SMEM, HBM, HBM],
        out_specs=HBM,
        scratch_shapes=[
            pltpu.VMEM((size, rows, 2 * width), BF16),
            pltpu.SMEM(offsets.shape[::-1], jnp.int32),
            pltpu.VMEM(objects.shape[1:], BF16),
            pltpu.VMEM(measured.shape, F32),
            pltpu.SemaphoreType.DMA((4 + len(slots),)),
        ],
        compiler_params=ALONE,
        name="windows",
    )(offsets.T, prop_index, objects, measured)
    blocks = exchanged(blocks)

    wave = struct(width, 2 * width)
    near = struct(size * near_rows, 2 * LANES)
    waves_shape = struct(size + 1, width, 2 * width)
    grads_shape = struct(size, width, 2 * width)
    table = struct(kinds, 2 * width, 2 * width)
    detector_table = struct(3, 2 * width, 2 * width)
    indices = pltpu.SMEM((size,), jnp.int32)

    def call(kernel, name, out_shape, in_specs, scratch_shapes, operands, slices=0):
        return pl.pallas_call(
            kernel,
            out_shape=out_shape,
            in_specs=in_specs,
            out_specs=[VMEM] * len(out_shape),
            scratch_shapes=scratch_shapes,
            compiler_params=PARAMS,
            cost_estimate=pl.CostEstimate(
                flops=16 * slices * width**3,
                bytes_accessed=sum(math.prod(x.shape) * x.dtype.itemsize for x in list(operands) + out_shape),
                transcendentals=0,
            ),
            name=name,
        )(*operands)

    leaving, waves, lf, rf, lb, rb, *dft = call(
        first_kernel,
        "first_forward",
        [wave, waves_shape, table, table, table, table, detector_table, detector_table],
        [SMEM, HBM, VMEM, VMEM, VMEM],
        [pltpu.VMEM(probes.shape[1:], BF16), indices, pltpu.SemaphoreType.DMA],
        (probe_group, probes, blocks, propagators, jnp.asarray(dft_constant(width))),
        size,
    )
    entering = handed(leaving, 0, 1)
    (near_out,) = call(near_kernel, "near_rows", [near], [VMEM, HBM], [pltpu.VMEM(near.shape, F32)], (blocks, leaving))
    nears = [handed(near_out, stage, groups - 1 - stage) for stage in range(groups - 1)]
    for stage in range(1, groups):
        leaving, waves = call(
            forward_kernel(stage),
            "forward",
            [wave, waves_shape],
            [VMEM] * 5,
            [indices],
            (entering, blocks, lf, rf, waves),
            size,
        )
        if stage < groups - 1:
            entering = handed(leaving, stage, 1)

    leaving, grads, lb, rb = call(
        middle_kernel(groups),
        "middle",
        [wave, grads_shape, table, table],
        [VMEM] * (groups + 6),
        [pltpu.VMEM((width, 2 * LANES), F32), indices],
        (waves, *nears, blocks, propagators, lb, rb, *dft),
        size,
    )

    for stage in range(groups - 2, -1, -1):
        arriving = handed(leaving, stage + 1, -1)
        leaving, grads = call(
            backward_kernel(stage),
            "backward",
            [wave, grads_shape],
            [VMEM] * 6,
            [indices],
            (arriving, waves, blocks, lb, rb, grads),
            size,
        )

    return pl.pallas_call(
        gather_kernel,
        out_shape=jax.ShapeDtypeStruct(objects.shape, F32),
        in_specs=[SMEM, VMEM],
        out_specs=HBM,
        scratch_shapes=[pltpu.VMEM(objects.shape[1:], F32), pltpu.SemaphoreType.DMA((2,))],
        compiler_params=PARAMS,
        name="sum_windows",
    )(offsets.T, exchanged(grads))


def solution(mesh):
    in_specs = (
        P(("parts", "cuts"), None, None, None),
        P(),
        P(("parts", "cuts")),
        P(),
        P(),
        P("parts", None),
        P("parts", "cuts", None),
    )
    out_specs = P(("parts", "cuts"), None, None, None)
    return jax.shard_map(shards, mesh=mesh, in_specs=in_specs, out_specs=out_specs, check_vma=False)
```

```python
import math

import jax
import jax.numpy as jnp
import numpy as np
from jax import lax
from jax.experimental import pallas as pl
from jax.experimental.pallas import tpu as pltpu
from jax.sharding import PartitionSpec as P

TRANSMIT = 0.985
GROUP = 8
LANES = 128
ROWS = 16
F32 = jnp.float32
BF16 = jnp.bfloat16


def dot(former, latter):
    return jnp.dot(former, latter, preferred_element_type=F32)


def halves(x):
    return x[:, :LANES], x[:, LANES : 2 * LANES], x[:, 2 * LANES :]


def swapped(tail):
    return pltpu.roll(tail, LANES // 2, 1)


def low_half(rows):
    return lax.broadcasted_iota(jnp.int32, (rows, LANES), 1) < LANES // 2


def spread(tail):
    other = swapped(tail)
    low = low_half(tail.shape[0])
    return jnp.where(low, tail, other), jnp.where(low, other, tail)


def signed(tail, minus_low):
    low = low_half(tail.shape[0])
    return jnp.where(low == minus_low, -tail, tail)


def factor(b):
    b0, b1, bt = halves(b)
    return (b0, b1) + spread(bt)


def times(a, parts):
    a0, a1, at = halves(a)
    b0, b1, b_real, b_imag = parts
    tail = at * b_real + signed(swapped(at), True) * b_imag
    return jnp.concatenate([a0 * b0 - a1 * b1, a1 * b0 + a0 * b1, tail], axis=1)


def times_conj(a, turned, parts):
    a0, a1, at = halves(a)
    b0, b1, b_real, b_imag = parts
    tail = at * b_real + turned * b_imag
    return jnp.concatenate([a0 * b0 + a1 * b1, a1 * b0 - a0 * b1, tail], axis=1)


def left_product(table, x, conj):
    width = x.shape[0]
    both = dot(table, x)
    u0, u1, ut = halves(both[:width])
    v0, v1, vt = halves(both[width:])
    turned = signed(swapped(vt), not conj)
    if conj:
        return jnp.concatenate([u0 + v1, u1 - v0, ut + turned], axis=1)
    return jnp.concatenate([u0 - v1, u1 + v0, ut + turned], axis=1)


def spread_tails(blocks, tails):
    size, _, columns = blocks.shape
    for k in range(size):
        pair = spread(blocks[k, : columns // 2, 2 * LANES :].astype(F32))
        tails[k] = jnp.concatenate(pair, axis=1).astype(BF16)


def transmission(blocks, tails, k):
    window = blocks[k, : blocks.shape[2] // 2, :].astype(F32)
    b0, b1, bt = halves(window)
    if tails is None:
        b_real, b_imag = spread(bt)
    else:
        pair = tails[k].astype(F32)
        b_real, b_imag = pair[:, :LANES], pair[:, LANES:]
    return TRANSMIT + b0, b1, TRANSMIT + b_real, b_imag


def split2(x):
    high = x.astype(BF16)
    return high, (x - high.astype(F32)).astype(BF16)


def picker(shape, start, high_tail=False):
    columns, across = (0, 1) if shape[0] > shape[1] else (1, 0)
    half = LANES // 2
    taken = lax.broadcasted_iota(jnp.int32, shape, columns) - start
    place = lax.broadcasted_iota(jnp.int32, shape, across)
    if high_tail:
        wanted = jnp.where(place < LANES, place, jnp.where(place < LANES + half, -shape[columns], place - half))
    else:
        wanted = jnp.where(place < LANES + half, place, -shape[columns])
    return jnp.where(taken == wanted, 1.0, 0.0).astype(BF16)


def row_picker(shape, distance):
    taken = lax.broadcasted_iota(jnp.int32, shape, 1)
    wanted = lax.broadcasted_iota(jnp.int32, shape, 0) + distance
    return jnp.where(taken == wanted, 1.0, 0.0).astype(BF16)


def rows_near(x, start, count):
    limit = x.shape[0] - count
    bit = 1 << (limit.bit_length() - 1)
    while bit >= ROWS:
        length = count + bit
        short = bit + length - x.shape[0]
        if short > 0:
            x = jnp.concatenate([x, jnp.zeros((short, x.shape[1]), x.dtype)], axis=0)
        x = jnp.where(lax.bitwise_and(start, bit) != 0, x[bit : bit + length], x[:length])
        bit //= 2
    return x


def packed(real, imag):
    return jnp.concatenate([real[:, :LANES], imag[:, :LANES], real[:, LANES:], imag[:, LANES:]], axis=1)


def dft_constant(width):
    counter = np.arange(width)
    angle = (counter[:, None] * counter[None, :] % width) * (2.0 * math.pi / width)
    return (np.stack([np.cos(angle), -np.sin(angle)]) / math.sqrt(width)).astype(np.float32)


def slots_of(positions, size):
    half = size // 2
    order = list(range(half, size)) + list(range(0, half, 2)) + list(range(1, half, 2))
    return order[:positions]


def slots_in(group, positions, size):
    flip = (group % 2) * (size // 2)
    return [slot ^ flip for slot in slots_of(positions, size)]


def window_kernel(offsets_in, index_ref, objects_in, measured_in, blocks_out, blocks, offsets_ref, objects, measured, sems):
    positions, near_rows, width = measured.shape
    extent = objects.shape[-1]
    copies = [
        pltpu.make_async_copy(objects_in.at[0, 0], objects.at[0], sems.at[0]),
        pltpu.make_async_copy(objects_in.at[0, 1], objects.at[1], sems.at[1]),
        pltpu.make_async_copy(measured_in, measured, sems.at[2]),
        pltpu.make_async_copy(offsets_in, offsets_ref, sems.at[3]),
    ]
    for copy in copies:
        copy.start()
    tag = jnp.full((ROWS, LANES), index_ref[0], jnp.int32).astype(F32)
    for copy in copies:
        copy.wait()
    size = blocks_out.shape[0]
    _, group = place_in(size)
    flip = lax.rem(group, 2) * (size // 2)
    sending = []
    for p, slot in enumerate(slots_of(positions, size)):
        start = offsets_ref[0, p]
        real, imag = (
            dot(rows_near(objects[c], start, width), picker((extent, 2 * LANES), offsets_ref[1, p], c == 1))
            for c in range(2)
        )
        tail = real[:, LANES:] + imag[:, LANES:]
        window = jnp.concatenate([real[:, :LANES], imag[:, :LANES], tail], axis=1).astype(BF16)
        shift = lax.bitwise_and(start, ROWS - 1)
        blocks[p, :width, :] = dot(row_picker((width, width + ROWS), shift), window).astype(BF16)
        tail = measured[p, :, LANES:]
        seen = jnp.concatenate([measured[p, :, :LANES], tail, tail, tag[:near_rows]], axis=1)
        left_over = jnp.concatenate([tag[near_rows:]] * 3, axis=1)
        blocks[p, width:, :] = jnp.concatenate([seen, left_over], axis=0).astype(BF16)
        target = blocks_out.at[lax.bitwise_xor(slot, flip)]
        sending.append(pltpu.make_async_copy(blocks.at[p], target, sems.at[4 + p]))
        sending[-1].start()
    for copy in sending:
        copy.wait()


def right_table(real, imag):
    upper, lower = packed(real, imag), packed(-imag, real)
    return jnp.concatenate([upper[:LANES], lower[:LANES], upper[LANES:], lower[LANES:]], axis=0).astype(BF16)


def forward_tables(props, rf):
    for k in range(props.shape[0]):
        rf[k] = right_table(props[k, 0].astype(F32).T, props[k, 1].astype(F32).T)


def backward_tables(props, lb, rb):
    width = props.shape[-1]
    for k in range(props.shape[0]):
        real, imag = props[k, 0].astype(F32), props[k, 1].astype(F32)
        lb[k, :width, :] = real.T.astype(BF16)
        lb[k, width:, :] = imag.T.astype(BF16)
        rb[k] = right_table(real, -imag)


def detector_tables(dft, left, right, right_conj):
    width = dft.shape[-1]
    for n, (real, imag) in enumerate(zip(split2(dft[0]), split2(dft[1]))):
        left[n, :width, :] = real
        left[n, width:, :] = imag
        real, imag = real.astype(F32), imag.astype(F32)
        right[n] = right_table(real, imag)
        if n == 0:
            right_conj[...] = right_table(real, -imag)


def forward_steps(blocks, tails, waves, indices, lf, rf):
    sections, _, columns = blocks.shape
    width = columns // 2
    psi = waves[0]
    parts = transmission(blocks, tails, 0)
    for k in range(sections):
        which = indices[k]
        z = times(psi.astype(F32), parts).astype(BF16)
        h = left_product(lf[which].reshape(columns, width), z, False).astype(BF16)
        if k + 1 < sections:
            parts = transmission(blocks, tails, k + 1)
        psi = dot(h, rf[which]).astype(BF16)
        waves[k + 1] = psi


def backward_steps(blocks, tails, waves, indices, lb, rb, grads, g):
    sections, _, columns = blocks.shape
    width = columns // 2

    def leave(k, y, turned, wave_parts):
        grads[k] = times_conj(y, turned, wave_parts).astype(BF16)

    late = None
    for k in reversed(range(sections)):
        which = indices[k]
        c = left_product(lb[which], g, True).astype(BF16)
        if late is not None:
            leave(*late)
        wave_parts = factor(waves[k].astype(F32))
        window_parts = transmission(blocks, tails, k)
        y = dot(c, rb[which])
        turned = signed(swapped(halves(y)[2]), False)
        g = times_conj(y, turned, window_parts).astype(BF16)
        late = (k, y, turned, wave_parts)
    leave(*late)
    return g


def detector(psi, observed, left, right, right_conj):
    def product(ah, al, bh, bl):
        return dot(ah, bh) + (dot(ah, bl) + dot(al, bh))

    near = left_product(left[0], psi, False) + left_product(left[1], psi, False)
    far = product(*split2(near), right[0], right[1])
    f0, f1, ft = halves(far)
    other = swapped(ft)
    main = f0 * f0 + f1 * f1 - observed[:, :LANES]
    tail = ft * ft + other * other - observed[:, LANES:]
    push = jnp.concatenate([main * f0, main * f1, tail * ft], axis=1)
    back = left_product(left[0], push.astype(BF16), True)
    return dot(back.astype(BF16), right_conj[...]).astype(BF16)


def read_indices(blocks, indices, count):
    for k in range(blocks.shape[0]):
        tag = jnp.max(blocks[k, -ROWS:, 2 * LANES :].astype(F32))
        indices[k] = jnp.clip(tag.astype(jnp.int32), 0, count - 1)


def place_in(size):
    rank = lax.axis_index("cuts")
    return lax.rem(rank, size), lax.div(rank, size)


def observe(blocks, near_rows, observed, first):
    for k in range(blocks.shape[0]):
        at = first + k * near_rows
        observed[at : at + near_rows, :] = blocks[k, -ROWS:, : 2 * LANES].astype(F32)[:near_rows]


def near_kernel(blocks, _, near, observed):
    observe(blocks, near.shape[0] // blocks.shape[0], observed, 0)
    near[...] = observed[...].astype(BF16)


def first_kernel(group_ref, probes, blocks, props, dft, leaving, waves, tails, lb, rf, rb, left, right, right_conj, probe, indices, sem):
    size = blocks.shape[0]
    slot, group = place_in(size)

    @pl.when(group == 0)
    def _():
        position = 0
        for p, held in enumerate(slots_of(group_ref.shape[0], size)):
            position = jnp.where(slot == held, p, position)
        which = group_ref[position]
        copy = pltpu.make_async_copy(probes.at[which], probe, sem)
        copy.start()
        forward_tables(props, rf)
        read_indices(blocks, indices, props.shape[0])
        copy.wait()
        waves[0] = packed(probe[0].astype(F32), probe[1].astype(F32)).astype(BF16)
        forward_steps(blocks, None, waves, indices, props, rf)
        leaving[...] = waves[size]

    @pl.when(group > 0)
    def _():
        spread_tails(blocks, tails)
        forward_tables(props, rf)
        backward_tables(props, lb, rb)
        detector_tables(dft, left, right, right_conj)


def forward_kernel(stage):
    def kernel(entering, blocks, tails, props, rf, waves_in, leaving, waves, first_tails, indices):
        size = blocks.shape[0]
        _, group = place_in(size)

        @pl.when(group == stage)
        def _():
            read_indices(blocks, indices, props.shape[0])
            waves[0] = entering[...]
            forward_steps(blocks, tails, waves, indices, props, rf)
            leaving[...] = waves[size]

        @pl.when(group != stage)
        def _():
            waves[...] = waves_in[...]

        @pl.when(group == 0)
        def _():
            spread_tails(blocks, first_tails)

    return kernel


def middle_kernel(groups):
    def kernel(waves, *refs):
        earlier, refs = refs[: groups - 1], refs[groups - 1 :]
        blocks, tails, props, lb, rb, left, right, right_conj, leaving, grads, lb_out, rb_out, observed, indices = refs
        size = blocks.shape[0]
        _, group = place_in(size)

        @pl.when(group == groups - 1)
        def _():
            read_indices(blocks, indices, props.shape[0])
            rows = earlier[0].shape[0]
            for n, near in enumerate(earlier):
                observed[n * rows : (n + 1) * rows, :] = near[...].astype(F32)
            observe(blocks, rows // size, observed, (groups - 1) * rows)
            g = detector(waves[size], observed[...], left, right, right_conj)
            leaving[...] = backward_steps(blocks, tails, waves, indices, lb, rb, grads, g)

        @pl.when(group < groups - 1)
        def _():
            backward_tables(props, lb_out, rb_out)

    return kernel


def backward_kernel(stage):
    def kernel(arriving, waves, blocks, tails, lb, rb, grads_in, leaving, grads, indices):
        _, group = place_in(blocks.shape[0])

        @pl.when(group == stage)
        def _():
            read_indices(blocks, indices, lb.shape[0])
            leaving[...] = backward_steps(blocks, tails, waves, indices, lb, rb, grads, arriving[...])

        @pl.when(group != stage)
        def _():
            grads[...] = grads_in[...]

    return kernel


def gather_kernel(offsets_ref, grads_ref, out_ref, planes, sems):
    positions = offsets_ref.shape[1]
    size, width, _ = grads_ref.shape
    extent = out_ref.shape[-1]
    _, group = place_in(size)
    flip = lax.rem(group, 2) * (size // 2)
    spread_out = []
    for p, slot in enumerate(slots_of(positions, size)):
        x0, x1, xt = halves(grads_ref[lax.bitwise_xor(slot, flip)])
        other = swapped(xt.astype(F32)).astype(BF16)
        both = jnp.concatenate(
            [jnp.concatenate([x0, xt], axis=1), jnp.concatenate([x1, other], axis=1)], axis=0
        )
        spread_out.append(dot(both, picker((2 * LANES, extent), offsets_ref[1, p])).astype(BF16))
    rows = jnp.concatenate(
        [row_picker((extent, width), -offsets_ref[0, p]) for p in range(positions)], axis=1
    )
    copies = []
    for c in range(2):
        here = slice(c * width, (c + 1) * width)
        planes[c] = dot(rows, jnp.concatenate([x[here] for x in spread_out], axis=0))
        copies.append(pltpu.make_async_copy(planes.at[c], out_ref.at[0, c], sems.at[c]))
        copies[-1].start()
    for copy in copies:
        copy.wait()


VMEM = pl.BlockSpec(memory_space=pltpu.VMEM)
SMEM = pl.BlockSpec(memory_space=pltpu.SMEM)
HBM = pl.BlockSpec(memory_space=pl.ANY)
ALONE = pltpu.CompilerParams(vmem_limit_bytes=60 * 1024 * 1024)
PARAMS = pltpu.CompilerParams(vmem_limit_bytes=20 * 1024 * 1024)


def shards(objects, propagators, prop_index, probes, probe_group, offsets, measured):
    sections = lax.axis_size("cuts")
    width = probes.shape[-1]
    kinds = propagators.shape[0]
    near_rows = measured.shape[1]
    size = GROUP
    groups = sections // size
    rows = width + ROWS
    slots = slots_of(probe_group.shape[0], size)
    members = [list(range(first, first + size)) for first in range(0, sections, size)]

    def struct(*dims, kind=BF16):
        return jax.ShapeDtypeStruct(dims, kind)

    def exchanged(blocks):
        return lax.all_to_all(blocks, "cuts", 0, 0, axis_index_groups=members, tiled=True)

    def handed(block, stage, distance):
        ends = (slots_in(at, len(slots), size) for at in (stage, stage + distance))
        route = [(stage * size + l, (stage + distance) * size + m) for l, m in zip(*ends)]
        return lax.ppermute(block, "cuts", route)

    blocks = pl.pallas_call(
        window_kernel,
        out_shape=struct(size, rows, 2 * width),
        in_specs=[HBM, SMEM, HBM, HBM],
        out_specs=HBM,
        scratch_shapes=[
            pltpu.VMEM((size, rows, 2 * width), BF16),
            pltpu.SMEM(offsets.shape[::-1], jnp.int32),
            pltpu.VMEM(objects.shape[1:], BF16),
            pltpu.VMEM(measured.shape, F32),
            pltpu.SemaphoreType.DMA((4 + len(slots),)),
        ],
        compiler_params=ALONE,
        name="windows",
    )(offsets.T, prop_index, objects, measured)
    blocks = exchanged(blocks)

    wave = struct(width, 2 * width)
    near = struct(size * near_rows, 2 * LANES)
    waves_shape = struct(size + 1, width, 2 * width)
    grads_shape = struct(size, width, 2 * width)
    tails_shape = struct(size, width, 2 * LANES)
    left_table = struct(kinds, 2 * width, width)
    square_table = struct(kinds, 2 * width, 2 * width)
    detector_left = struct(2, 2 * width, width)
    detector_right = struct(2, 2 * width, 2 * width)
    indices = pltpu.SMEM((size,), jnp.int32)

    def call(kernel, name, out_shape, in_specs, scratch_shapes, operands, slices=0):
        return pl.pallas_call(
            kernel,
            out_shape=out_shape,
            in_specs=in_specs,
            out_specs=[VMEM] * len(out_shape),
            scratch_shapes=scratch_shapes,
            compiler_params=PARAMS,
            cost_estimate=pl.CostEstimate(
                flops=16 * slices * width**3,
                bytes_accessed=sum(math.prod(x.shape) * x.dtype.itemsize for x in list(operands) + out_shape),
                transcendentals=0,
            ),
            name=name,
        )(*operands)

    leaving, waves, tails, lb, rf, rb, *dft = call(
        first_kernel,
        "first_forward",
        [wave, waves_shape, tails_shape, left_table, square_table, square_table]
        + [detector_left, detector_right, struct(2 * width, 2 * width)],
        [SMEM, HBM, VMEM, VMEM, VMEM],
        [pltpu.VMEM(probes.shape[1:], BF16), indices, pltpu.SemaphoreType.DMA],
        (probe_group, probes, blocks, propagators, jnp.asarray(dft_constant(width))),
        size,
    )
    entering = handed(leaving, 0, 1)
    (near_out,) = call(near_kernel, "near_rows", [near], [VMEM, HBM], [pltpu.VMEM(near.shape, F32)], (blocks, leaving))
    nears = [handed(near_out, stage, groups - 1 - stage) for stage in range(groups - 1)]
    for stage in range(1, groups):
        leaving, waves, first_tails = call(
            forward_kernel(stage),
            "forward",
            [wave, waves_shape, tails_shape],
            [VMEM] * 6,
            [indices],
            (entering, blocks, tails, propagators, rf, waves),
            size,
        )
        if stage < groups - 1:
            entering = handed(leaving, stage, 1)

    leaving, grads, lb, rb = call(
        middle_kernel(groups),
        "middle",
        [wave, grads_shape, left_table, square_table],
        [VMEM] * (groups + 8),
        [pltpu.VMEM((width, 2 * LANES), F32), indices],
        (waves, *nears, blocks, tails, propagators, lb, rb, *dft),
        size,
    )

    for stage in range(groups - 2, -1, -1):
        arriving = handed(leaving, stage + 1, -1)
        leaving, grads = call(
            backward_kernel(stage),
            "backward",
            [wave, grads_shape],
            [VMEM] * 7,
            [indices],
            (arriving, waves, blocks, first_tails if stage == 0 else tails, lb, rb, grads),
            size,
        )

    return pl.pallas_call(
        gather_kernel,
        out_shape=jax.ShapeDtypeStruct(objects.shape, F32),
        in_specs=[SMEM, VMEM],
        out_specs=HBM,
        scratch_shapes=[pltpu.VMEM(objects.shape[1:], F32), pltpu.SemaphoreType.DMA((2,))],
        compiler_params=PARAMS,
        name="sum_windows",
    )(offsets.T, exchanged(grads))


def solution(mesh):
    in_specs = (
        P(("parts", "cuts"), None, None, None),
        P(),
        P(("parts", "cuts")),
        P(),
        P(),
        P("parts", None),
        P("parts", "cuts", None),
    )
    out_specs = P(("parts", "cuts"), None, None, None)
    return jax.shard_map(shards, mesh=mesh, in_specs=in_specs, out_specs=out_specs, check_vma=False)
```

```python
import math

import jax
import jax.numpy as jnp
import numpy as np
from jax import lax
from jax.experimental import pallas as pl
from jax.experimental.pallas import tpu as pltpu
from jax.sharding import PartitionSpec as P

TRANSMIT = 0.985
GROUP = 8
LANES = 128
ROWS = 16
F32 = jnp.float32
BF16 = jnp.bfloat16


def dot(former, latter):
    return jnp.dot(former, latter, preferred_element_type=F32)


def halves(x):
    return x[:, :LANES], x[:, LANES : 2 * LANES], x[:, 2 * LANES :]


def swapped(tail):
    return pltpu.roll(tail, LANES // 2, 1)


def low_half(rows):
    return lax.broadcasted_iota(jnp.int32, (rows, LANES), 1) < LANES // 2


def spread(tail):
    other = swapped(tail)
    low = low_half(tail.shape[0])
    return jnp.where(low, tail, other), jnp.where(low, other, tail)


def signed(tail, minus_low):
    low = low_half(tail.shape[0])
    return jnp.where(low == minus_low, -tail, tail)


def factor(b):
    b0, b1, bt = halves(b)
    return (b0, b1) + spread(bt)


def times(a, parts):
    a0, a1, at = halves(a)
    b0, b1, b_real, b_imag = parts
    tail = at * b_real + signed(swapped(at), True) * b_imag
    return jnp.concatenate([a0 * b0 - a1 * b1, a1 * b0 + a0 * b1, tail], axis=1)


def times_conj(a, turned, parts):
    a0, a1, at = halves(a)
    b0, b1, b_real, b_imag = parts
    tail = at * b_real + turned * b_imag
    return jnp.concatenate([a0 * b0 + a1 * b1, a1 * b0 - a0 * b1, tail], axis=1)


def left_product(table, x, conj):
    width = x.shape[0]
    both = dot(table, x)
    u0, u1, ut = halves(both[:width])
    v0, v1, vt = halves(both[width:])
    turned = signed(swapped(vt), not conj)
    if conj:
        return jnp.concatenate([u0 + v1, u1 - v0, ut + turned], axis=1)
    return jnp.concatenate([u0 - v1, u1 + v0, ut + turned], axis=1)


def spread_tails(blocks, tails):
    size, _, columns = blocks.shape
    for k in range(size):
        pair = spread(blocks[k, : columns // 2, 2 * LANES :].astype(F32))
        tails[k] = jnp.concatenate(pair, axis=1).astype(BF16)


def transmission(blocks, tails, k):
    window = blocks[k, : blocks.shape[2] // 2, :].astype(F32)
    b0, b1, bt = halves(window)
    if tails is None:
        b_real, b_imag = spread(bt)
    else:
        pair = tails[k].astype(F32)
        b_real, b_imag = pair[:, :LANES], pair[:, LANES:]
    return TRANSMIT + b0, b1, TRANSMIT + b_real, b_imag


def split2(x):
    high = x.astype(BF16)
    return high, (x - high.astype(F32)).astype(BF16)


def picker(shape, start, high_tail=False):
    columns, across = (0, 1) if shape[0] > shape[1] else (1, 0)
    half = LANES // 2
    taken = lax.broadcasted_iota(jnp.int32, shape, columns) - start
    place = lax.broadcasted_iota(jnp.int32, shape, across)
    if high_tail:
        wanted = jnp.where(place < LANES, place, jnp.where(place < LANES + half, -shape[columns], place - half))
    else:
        wanted = jnp.where(place < LANES + half, place, -shape[columns])
    return jnp.where(taken == wanted, 1.0, 0.0).astype(BF16)


def row_picker(shape, distance):
    taken = lax.broadcasted_iota(jnp.int32, shape, 1)
    wanted = lax.broadcasted_iota(jnp.int32, shape, 0) + distance
    return jnp.where(taken == wanted, 1.0, 0.0).astype(BF16)


def rows_near(x, start, count):
    limit = x.shape[0] - count
    bit = 1 << (limit.bit_length() - 1)
    while bit >= ROWS:
        length = count + bit
        short = bit + length - x.shape[0]
        if short > 0:
            x = jnp.concatenate([x, jnp.zeros((short, x.shape[1]), x.dtype)], axis=0)
        x = jnp.where(lax.bitwise_and(start, bit) != 0, x[bit : bit + length], x[:length])
        bit //= 2
    return x


def packed(real, imag):
    return jnp.concatenate([real[:, :LANES], imag[:, :LANES], real[:, LANES:], imag[:, LANES:]], axis=1)


def dft_constant(width):
    counter = np.arange(width)
    angle = (counter[:, None] * counter[None, :] % width) * (2.0 * math.pi / width)
    return (np.stack([np.cos(angle), -np.sin(angle)]) / math.sqrt(width)).astype(np.float32)


def slots_of(positions, size):
    half = size // 2
    order = list(range(half, size)) + list(range(0, half, 2)) + list(range(1, half, 2))
    return order[:positions]


def slots_in(group, positions, size):
    flip = (group % 2) * (size // 2)
    return [slot ^ flip for slot in slots_of(positions, size)]


def window_kernel(offsets_in, index_ref, objects_in, measured_in, blocks_out, blocks, offsets_ref, objects, measured, pickers, sems):
    positions, near_rows, width = measured.shape
    extent = objects.shape[-1]
    copies = [
        pltpu.make_async_copy(objects_in.at[0, 0], objects.at[0], sems.at[0]),
        pltpu.make_async_copy(objects_in.at[0, 1], objects.at[1], sems.at[1]),
        pltpu.make_async_copy(measured_in, measured, sems.at[2]),
        pltpu.make_async_copy(offsets_in, offsets_ref, sems.at[3]),
    ]
    for copy in reversed(copies):
        copy.start()
    tag = jnp.full((ROWS, LANES), index_ref[0], jnp.int32).astype(F32)
    size = blocks_out.shape[0]
    _, group = place_in(size)
    flip = lax.rem(group, 2) * (size // 2)
    copies.pop().wait()
    for p in range(positions):
        for c in range(2):
            pickers[p, c] = picker((extent, 2 * LANES), offsets_ref[1, p], c == 1)
    for copy in copies:
        copy.wait()
    sending = []
    for p, slot in enumerate(slots_of(positions, size)):
        start = offsets_ref[0, p]
        real, imag = (
            dot(rows_near(objects[c], start, width), pickers[p, c])
            for c in range(2)
        )
        tail = real[:, LANES:] + imag[:, LANES:]
        window = jnp.concatenate([real[:, :LANES], imag[:, :LANES], tail], axis=1).astype(BF16)
        shift = lax.bitwise_and(start, ROWS - 1)
        blocks[p, :width, :] = dot(row_picker((width, width + ROWS), shift), window).astype(BF16)
        tail = measured[p, :, LANES:]
        seen = jnp.concatenate([measured[p, :, :LANES], tail, tail, tag[:near_rows]], axis=1)
        left_over = jnp.concatenate([tag[near_rows:]] * 3, axis=1)
        blocks[p, width:, :] = jnp.concatenate([seen, left_over], axis=0).astype(BF16)
        target = blocks_out.at[lax.bitwise_xor(slot, flip)]
        sending.append(pltpu.make_async_copy(blocks.at[p], target, sems.at[4 + p]))
        sending[-1].start()
    for copy in sending:
        copy.wait()


def right_table(real, imag):
    upper, lower = packed(real, imag), packed(-imag, real)
    return jnp.concatenate([upper[:LANES], lower[:LANES], upper[LANES:], lower[LANES:]], axis=0).astype(BF16)


def forward_tables(props, rf):
    for k in range(props.shape[0]):
        rf[k] = right_table(props[k, 0].astype(F32).T, props[k, 1].astype(F32).T)


def backward_tables(props, lb, rb):
    width = props.shape[-1]
    for k in range(props.shape[0]):
        real, imag = props[k, 0].astype(F32), props[k, 1].astype(F32)
        lb[k, :width, :] = real.T.astype(BF16)
        lb[k, width:, :] = imag.T.astype(BF16)
        rb[k] = right_table(real, -imag)


def detector_tables(dft, left, right, right_conj):
    width = dft.shape[-1]
    for n, (real, imag) in enumerate(zip(split2(dft[0]), split2(dft[1]))):
        left[n, :width, :] = real
        left[n, width:, :] = imag
        real, imag = real.astype(F32), imag.astype(F32)
        right[n] = right_table(real, imag)
        if n == 0:
            right_conj[...] = right_table(real, -imag)


def forward_steps(blocks, tails, waves, indices, lf, rf):
    sections, _, columns = blocks.shape
    width = columns // 2
    psi = waves[0]
    parts = transmission(blocks, tails, 0)
    for k in range(sections):
        which = indices[k]
        z = times(psi.astype(F32), parts).astype(BF16)
        h = left_product(lf[which].reshape(columns, width), z, False).astype(BF16)
        if k + 1 < sections:
            parts = transmission(blocks, tails, k + 1)
        psi = dot(h, rf[which]).astype(BF16)
        waves[k + 1] = psi


def backward_steps(blocks, tails, waves, indices, lb, rb, grads, g):
    sections, _, columns = blocks.shape
    width = columns // 2

    def leave(k, y, turned, wave_parts):
        grads[k] = times_conj(y, turned, wave_parts).astype(BF16)

    late = None
    for k in reversed(range(sections)):
        which = indices[k]
        c = left_product(lb[which], g, True).astype(BF16)
        if late is not None:
            leave(*late)
        wave_parts = factor(waves[k].astype(F32))
        window_parts = transmission(blocks, tails, k)
        y = dot(c, rb[which])
        turned = signed(swapped(halves(y)[2]), False)
        g = times_conj(y, turned, window_parts).astype(BF16)
        late = (k, y, turned, wave_parts)
    leave(*late)
    return g


def detector(psi, observed, left, right, right_conj):
    def product(ah, al, bh, bl):
        return dot(ah, bh) + (dot(ah, bl) + dot(al, bh))

    near = left_product(left[0], psi, False) + left_product(left[1], psi, False)
    far = product(*split2(near), right[0], right[1])
    f0, f1, ft = halves(far)
    other = swapped(ft)
    main = f0 * f0 + f1 * f1 - observed[:, :LANES]
    tail = ft * ft + other * other - observed[:, LANES:]
    push = jnp.concatenate([main * f0, main * f1, tail * ft], axis=1)
    back = left_product(left[0], push.astype(BF16), True)
    return dot(back.astype(BF16), right_conj[...]).astype(BF16)


def read_indices(blocks, indices, count):
    for k in range(blocks.shape[0]):
        tag = jnp.max(blocks[k, -ROWS:, 2 * LANES :].astype(F32))
        indices[k] = jnp.clip(tag.astype(jnp.int32), 0, count - 1)


def place_in(size):
    rank = lax.axis_index("cuts")
    return lax.rem(rank, size), lax.div(rank, size)


def observe(blocks, near_rows, observed, first):
    for k in range(blocks.shape[0]):
        at = first + k * near_rows
        observed[at : at + near_rows, :] = blocks[k, -ROWS:, : 2 * LANES].astype(F32)[:near_rows]


def near_kernel(blocks, _, near, observed):
    observe(blocks, near.shape[0] // blocks.shape[0], observed, 0)
    near[...] = observed[...].astype(BF16)


def first_kernel(group_ref, probes, blocks, props, dft, leaving, waves, tails, lb, rf, rb, left, right, right_conj, probe, indices, sem):
    size = blocks.shape[0]
    slot, group = place_in(size)

    @pl.when(group == 0)
    def _():
        position = 0
        for p, held in enumerate(slots_of(group_ref.shape[0], size)):
            position = jnp.where(slot == held, p, position)
        which = group_ref[position]
        copy = pltpu.make_async_copy(probes.at[which], probe, sem)
        copy.start()
        forward_tables(props, rf)
        read_indices(blocks, indices, props.shape[0])
        copy.wait()
        waves[0] = packed(probe[0].astype(F32), probe[1].astype(F32)).astype(BF16)
        forward_steps(blocks, None, waves, indices, props, rf)
        leaving[...] = waves[size]

    @pl.when(group > 0)
    def _():
        spread_tails(blocks, tails)
        forward_tables(props, rf)
        backward_tables(props, lb, rb)
        detector_tables(dft, left, right, right_conj)


def forward_kernel(stage):
    def kernel(entering, blocks, tails, props, rf, waves_in, leaving, waves, first_tails, indices):
        size = blocks.shape[0]
        _, group = place_in(size)

        @pl.when(group == stage)
        def _():
            read_indices(blocks, indices, props.shape[0])
            waves[0] = entering[...]
            forward_steps(blocks, tails, waves, indices, props, rf)
            leaving[...] = waves[size]

        @pl.when(group != stage)
        def _():
            waves[...] = waves_in[...]

        @pl.when(group == 0)
        def _():
            spread_tails(blocks, first_tails)

    return kernel


def middle_kernel(groups):
    def kernel(waves, *refs):
        earlier, refs = refs[: groups - 1], refs[groups - 1 :]
        blocks, tails, props, lb, rb, left, right, right_conj, leaving, grads, lb_out, rb_out, observed, indices = refs
        size = blocks.shape[0]
        _, group = place_in(size)

        @pl.when(group == groups - 1)
        def _():
            read_indices(blocks, indices, props.shape[0])
            rows = earlier[0].shape[0]
            for n, near in enumerate(earlier):
                observed[n * rows : (n + 1) * rows, :] = near[...].astype(F32)
            observe(blocks, rows // size, observed, (groups - 1) * rows)
            g = detector(waves[size], observed[...], left, right, right_conj)
            leaving[...] = backward_steps(blocks, tails, waves, indices, lb, rb, grads, g)

        @pl.when(group < groups - 1)
        def _():
            backward_tables(props, lb_out, rb_out)

    return kernel


def backward_kernel(stage):
    def kernel(arriving, waves, blocks, tails, lb, rb, grads_in, leaving, grads, indices):
        _, group = place_in(blocks.shape[0])

        @pl.when(group == stage)
        def _():
            read_indices(blocks, indices, lb.shape[0])
            leaving[...] = backward_steps(blocks, tails, waves, indices, lb, rb, grads, arriving[...])

        @pl.when(group != stage)
        def _():
            grads[...] = grads_in[...]

    return kernel


def gather_kernel(offsets_ref, grads_ref, out_ref, planes, sems):
    positions = offsets_ref.shape[1]
    size, width, _ = grads_ref.shape
    extent = out_ref.shape[-1]
    _, group = place_in(size)
    flip = lax.rem(group, 2) * (size // 2)
    spread_out = []
    for p, slot in enumerate(slots_of(positions, size)):
        x0, x1, xt = halves(grads_ref[lax.bitwise_xor(slot, flip)])
        other = swapped(xt.astype(F32)).astype(BF16)
        both = jnp.concatenate(
            [jnp.concatenate([x0, xt], axis=1), jnp.concatenate([x1, other], axis=1)], axis=0
        )
        spread_out.append(dot(both, picker((2 * LANES, extent), offsets_ref[1, p])).astype(BF16))
    rows = jnp.concatenate(
        [row_picker((extent, width), -offsets_ref[0, p]) for p in range(positions)], axis=1
    )
    copies = []
    for c in range(2):
        here = slice(c * width, (c + 1) * width)
        planes[c] = dot(rows, jnp.concatenate([x[here] for x in spread_out], axis=0))
        copies.append(pltpu.make_async_copy(planes.at[c], out_ref.at[0, c], sems.at[c]))
        copies[-1].start()
    for copy in copies:
        copy.wait()


VMEM = pl.BlockSpec(memory_space=pltpu.VMEM)
SMEM = pl.BlockSpec(memory_space=pltpu.SMEM)
HBM = pl.BlockSpec(memory_space=pl.ANY)
ALONE = pltpu.CompilerParams(vmem_limit_bytes=60 * 1024 * 1024)
PARAMS = pltpu.CompilerParams(vmem_limit_bytes=20 * 1024 * 1024)


def shards(objects, propagators, prop_index, probes, probe_group, offsets, measured):
    sections = lax.axis_size("cuts")
    width = probes.shape[-1]
    kinds = propagators.shape[0]
    near_rows = measured.shape[1]
    size = GROUP
    groups = sections // size
    rows = width + ROWS
    slots = slots_of(probe_group.shape[0], size)
    members = [list(range(first, first + size)) for first in range(0, sections, size)]

    def struct(*dims, kind=BF16):
        return jax.ShapeDtypeStruct(dims, kind)

    def exchanged(blocks):
        return lax.all_to_all(blocks, "cuts", 0, 0, axis_index_groups=members, tiled=True)

    def handed(block, stage, distance):
        ends = (slots_in(at, len(slots), size) for at in (stage, stage + distance))
        route = [(stage * size + l, (stage + distance) * size + m) for l, m in zip(*ends)]
        return lax.ppermute(block, "cuts", route)

    blocks = pl.pallas_call(
        window_kernel,
        out_shape=struct(size, rows, 2 * width),
        in_specs=[HBM, SMEM, HBM, HBM],
        out_specs=HBM,
        scratch_shapes=[
            pltpu.VMEM((size, rows, 2 * width), BF16),
            pltpu.SMEM(offsets.shape[::-1], jnp.int32),
            pltpu.VMEM(objects.shape[1:], BF16),
            pltpu.VMEM(measured.shape, F32),
            pltpu.VMEM((len(slots), 2, objects.shape[-1], 2 * LANES), BF16),
            pltpu.SemaphoreType.DMA((4 + len(slots),)),
        ],
        compiler_params=ALONE,
        name="windows",
    )(offsets.T, prop_index, objects, measured)
    blocks = exchanged(blocks)

    wave = struct(width, 2 * width)
    near = struct(size * near_rows, 2 * LANES)
    waves_shape = struct(size + 1, width, 2 * width)
    grads_shape = struct(size, width, 2 * width)
    tails_shape = struct(size, width, 2 * LANES)
    left_table = struct(kinds, 2 * width, width)
    square_table = struct(kinds, 2 * width, 2 * width)
    detector_left = struct(2, 2 * width, width)
    detector_right = struct(2, 2 * width, 2 * width)
    indices = pltpu.SMEM((size,), jnp.int32)

    def call(kernel, name, out_shape, in_specs, scratch_shapes, operands, slices=0):
        return pl.pallas_call(
            kernel,
            out_shape=out_shape,
            in_specs=in_specs,
            out_specs=[VMEM] * len(out_shape),
            scratch_shapes=scratch_shapes,
            compiler_params=PARAMS,
            cost_estimate=pl.CostEstimate(
                flops=16 * slices * width**3,
                bytes_accessed=sum(math.prod(x.shape) * x.dtype.itemsize for x in list(operands) + out_shape),
                transcendentals=0,
            ),
            name=name,
        )(*operands)

    leaving, waves, tails, lb, rf, rb, *dft = call(
        first_kernel,
        "first_forward",
        [wave, waves_shape, tails_shape, left_table, square_table, square_table]
        + [detector_left, detector_right, struct(2 * width, 2 * width)],
        [SMEM, HBM, VMEM, VMEM, VMEM],
        [pltpu.VMEM(probes.shape[1:], BF16), indices, pltpu.SemaphoreType.DMA],
        (probe_group, probes, blocks, propagators, jnp.asarray(dft_constant(width))),
        size,
    )
    entering = handed(leaving, 0, 1)
    (near_out,) = call(near_kernel, "near_rows", [near], [VMEM, HBM], [pltpu.VMEM(near.shape, F32)], (blocks, leaving))
    nears = [handed(near_out, stage, groups - 1 - stage) for stage in range(groups - 1)]
    for stage in range(1, groups):
        leaving, waves, first_tails = call(
            forward_kernel(stage),
            "forward",
            [wave, waves_shape, tails_shape],
            [VMEM] * 6,
            [indices],
            (entering, blocks, tails, propagators, rf, waves),
            size,
        )
        if stage < groups - 1:
            entering = handed(leaving, stage, 1)

    leaving, grads, lb, rb = call(
        middle_kernel(groups),
        "middle",
        [wave, grads_shape, left_table, square_table],
        [VMEM] * (groups + 8),
        [pltpu.VMEM((width, 2 * LANES), F32), indices],
        (waves, *nears, blocks, tails, propagators, lb, rb, *dft),
        size,
    )

    for stage in range(groups - 2, -1, -1):
        arriving = handed(leaving, stage + 1, -1)
        leaving, grads = call(
            backward_kernel(stage),
            "backward",
            [wave, grads_shape],
            [VMEM] * 7,
            [indices],
            (arriving, waves, blocks, first_tails if stage == 0 else tails, lb, rb, grads),
            size,
        )

    return pl.pallas_call(
        gather_kernel,
        out_shape=jax.ShapeDtypeStruct(objects.shape, F32),
        in_specs=[SMEM, VMEM],
        out_specs=HBM,
        scratch_shapes=[pltpu.VMEM(objects.shape[1:], F32), pltpu.SemaphoreType.DMA((2,))],
        compiler_params=PARAMS,
        name="sum_windows",
    )(offsets.T, exchanged(grads))


def solution(mesh):
    in_specs = (
        P(("parts", "cuts"), None, None, None),
        P(),
        P(("parts", "cuts")),
        P(),
        P(),
        P("parts", None),
        P("parts", "cuts", None),
    )
    out_specs = P(("parts", "cuts"), None, None, None)
    return jax.shard_map(shards, mesh=mesh, in_specs=in_specs, out_specs=out_specs, check_vma=False)
```

```python
import math

import jax
import jax.numpy as jnp
import numpy as np
from jax import lax
from jax.experimental import pallas as pl
from jax.experimental.pallas import tpu as pltpu
from jax.sharding import PartitionSpec as P

TRANSMIT = 0.985
GROUP = 8
LANES = 128
ROWS = 16
F32 = jnp.float32
BF16 = jnp.bfloat16


def dot(former, latter):
    return jnp.dot(former, latter, preferred_element_type=F32)


def halves(x):
    return x[:, :LANES], x[:, LANES : 2 * LANES], x[:, 2 * LANES :]


def swapped(tail):
    return pltpu.roll(tail, LANES // 2, 1)


def low_half(rows):
    return lax.broadcasted_iota(jnp.int32, (rows, LANES), 1) < LANES // 2


def spread(tail):
    other = swapped(tail)
    low = low_half(tail.shape[0])
    return jnp.where(low, tail, other), jnp.where(low, other, tail)


def signed(tail, minus_low):
    low = low_half(tail.shape[0])
    return jnp.where(low == minus_low, -tail, tail)


def factor(b):
    b0, b1, bt = halves(b)
    return (b0, b1) + spread(bt)


def times(a, parts):
    a0, a1, at = halves(a)
    b0, b1, b_real, b_imag = parts
    tail = at * b_real + signed(swapped(at), True) * b_imag
    return jnp.concatenate([a0 * b0 - a1 * b1, a1 * b0 + a0 * b1, tail], axis=1)


def times_conj(a, turned, parts):
    a0, a1, at = halves(a)
    b0, b1, b_real, b_imag = parts
    tail = at * b_real + turned * b_imag
    return jnp.concatenate([a0 * b0 + a1 * b1, a1 * b0 - a0 * b1, tail], axis=1)


def left_product(table, x, conj):
    width = x.shape[0]
    both = dot(table, x)
    u0, u1, ut = halves(both[:width])
    v0, v1, vt = halves(both[width:])
    turned = signed(swapped(vt), not conj)
    if conj:
        return jnp.concatenate([u0 + v1, u1 - v0, ut + turned], axis=1)
    return jnp.concatenate([u0 - v1, u1 + v0, ut + turned], axis=1)


def spread_tails(blocks, tails):
    size, _, columns = blocks.shape
    for k in range(size):
        pair = spread(blocks[k, : columns // 2, 2 * LANES :].astype(F32))
        tails[k] = jnp.concatenate(pair, axis=1).astype(BF16)


def transmission(blocks, tails, k):
    window = blocks[k, : blocks.shape[2] // 2, :].astype(F32)
    b0, b1, bt = halves(window)
    if tails is None:
        b_real, b_imag = spread(bt)
    else:
        pair = tails[k].astype(F32)
        b_real, b_imag = pair[:, :LANES], pair[:, LANES:]
    return TRANSMIT + b0, b1, TRANSMIT + b_real, b_imag


def split2(x):
    high = x.astype(BF16)
    return high, (x - high.astype(F32)).astype(BF16)


def picker(shape, start, high_tail=False):
    columns, across = (0, 1) if shape[0] > shape[1] else (1, 0)
    half = LANES // 2
    taken = lax.broadcasted_iota(jnp.int32, shape, columns) - start
    place = lax.broadcasted_iota(jnp.int32, shape, across)
    if high_tail:
        wanted = jnp.where(place < LANES, place, jnp.where(place < LANES + half, -shape[columns], place - half))
    else:
        wanted = jnp.where(place < LANES + half, place, -shape[columns])
    return jnp.where(taken == wanted, 1.0, 0.0).astype(BF16)


def row_picker(shape, distance):
    taken = lax.broadcasted_iota(jnp.int32, shape, 1)
    wanted = lax.broadcasted_iota(jnp.int32, shape, 0) + distance
    return jnp.where(taken == wanted, 1.0, 0.0).astype(BF16)


def rows_near(x, start, count):
    limit = x.shape[0] - count
    bit = 1 << (limit.bit_length() - 1)
    while bit >= ROWS:
        length = count + bit
        short = bit + length - x.shape[0]
        if short > 0:
            x = jnp.concatenate([x, jnp.zeros((short, x.shape[1]), x.dtype)], axis=0)
        x = jnp.where(lax.bitwise_and(start, bit) != 0, x[bit : bit + length], x[:length])
        bit //= 2
    return x


def packed(real, imag):
    return jnp.concatenate([real[:, :LANES], imag[:, :LANES], real[:, LANES:], imag[:, LANES:]], axis=1)


def dft_constant(width):
    counter = np.arange(width)
    angle = (counter[:, None] * counter[None, :] % width) * (2.0 * math.pi / width)
    return (np.stack([np.cos(angle), -np.sin(angle)]) / math.sqrt(width)).astype(np.float32)


def slots_of(positions, size):
    half = size // 2
    order = list(range(half, size)) + list(range(0, half, 2)) + list(range(1, half, 2))
    return order[:positions]


def slots_in(group, positions, size):
    flip = (group % 2) * (size // 2)
    return [slot ^ flip for slot in slots_of(positions, size)]


def window_kernel(
    offsets_in, index_ref, objects_in, measured_in, props_in, blocks_out, rf_out,
    blocks, rf, offsets_ref, objects, measured, props, pickers, sems,
):
    positions, near_rows, width = measured.shape
    extent = objects.shape[-1]
    copies = [
        pltpu.make_async_copy(objects_in.at[0, 0], objects.at[0], sems.at[0]),
        pltpu.make_async_copy(objects_in.at[0, 1], objects.at[1], sems.at[1]),
        pltpu.make_async_copy(measured_in, measured, sems.at[2]),
        pltpu.make_async_copy(props_in, props, sems.at[3]),
        pltpu.make_async_copy(offsets_in, offsets_ref, sems.at[4]),
    ]
    for copy in copies[-1:] + copies[:-1]:
        copy.start()
    tag = jnp.full((ROWS, LANES), index_ref[0], jnp.int32).astype(F32)
    size = blocks_out.shape[0]
    _, group = place_in(size)
    flip = lax.rem(group, 2) * (size // 2)
    copies.pop().wait()
    for p in range(positions):
        for c in range(2):
            pickers[p, c] = picker((extent, 2 * LANES), offsets_ref[1, p], c == 1)
    for copy in copies:
        copy.wait()
    sending = []
    for p, slot in enumerate(slots_of(positions, size)):
        start = offsets_ref[0, p]
        real, imag = (
            dot(rows_near(objects[c], start, width), pickers[p, c])
            for c in range(2)
        )
        tail = real[:, LANES:] + imag[:, LANES:]
        window = jnp.concatenate([real[:, :LANES], imag[:, :LANES], tail], axis=1).astype(BF16)
        shift = lax.bitwise_and(start, ROWS - 1)
        blocks[p, :width, :] = dot(row_picker((width, width + ROWS), shift), window).astype(BF16)
        tail = measured[p, :, LANES:]
        seen = jnp.concatenate([measured[p, :, :LANES], tail, tail, tag[:near_rows]], axis=1)
        left_over = jnp.concatenate([tag[near_rows:]] * 3, axis=1)
        blocks[p, width:, :] = jnp.concatenate([seen, left_over], axis=0).astype(BF16)
        target = blocks_out.at[lax.bitwise_xor(slot, flip)]
        sending.append(pltpu.make_async_copy(blocks.at[p], target, sems.at[5 + p]))
        sending[-1].start()
        for k in range(p, props.shape[0], positions):
            rf[k] = right_table(props[k, 0].astype(F32).T, props[k, 1].astype(F32).T)
            sending.append(pltpu.make_async_copy(rf.at[k], rf_out.at[k], sems.at[5 + positions + k]))
            sending[-1].start()
    for copy in sending:
        copy.wait()


def right_table(real, imag):
    upper, lower = packed(real, imag), packed(-imag, real)
    return jnp.concatenate([upper[:LANES], lower[:LANES], upper[LANES:], lower[LANES:]], axis=0).astype(BF16)


def backward_tables(props, lb, rb):
    width = props.shape[-1]
    for k in range(props.shape[0]):
        real, imag = props[k, 0].astype(F32), props[k, 1].astype(F32)
        lb[k, :width, :] = real.T.astype(BF16)
        lb[k, width:, :] = imag.T.astype(BF16)
        rb[k] = right_table(real, -imag)


def detector_tables(dft, left, right, right_conj):
    width = dft.shape[-1]
    for n, (real, imag) in enumerate(zip(split2(dft[0]), split2(dft[1]))):
        left[n, :width, :] = real
        left[n, width:, :] = imag
        real, imag = real.astype(F32), imag.astype(F32)
        right[n] = right_table(real, imag)
        if n == 0:
            right_conj[...] = right_table(real, -imag)


def forward_steps(blocks, tails, waves, indices, lf, rf):
    sections, _, columns = blocks.shape
    width = columns // 2
    psi = waves[0]
    parts = transmission(blocks, tails, 0)
    for k in range(sections):
        which = indices[k]
        z = times(psi.astype(F32), parts).astype(BF16)
        h = left_product(lf[which].reshape(columns, width), z, False).astype(BF16)
        if k + 1 < sections:
            parts = transmission(blocks, tails, k + 1)
        psi = dot(h, rf[which]).astype(BF16)
        waves[k + 1] = psi


def backward_steps(blocks, tails, waves, indices, lb, rb, grads, g):
    sections, _, columns = blocks.shape
    width = columns // 2

    def leave(k, y, turned, wave_parts):
        grads[k] = times_conj(y, turned, wave_parts).astype(BF16)

    late = None
    for k in reversed(range(sections)):
        which = indices[k]
        c = left_product(lb[which], g, True).astype(BF16)
        if late is not None:
            leave(*late)
        wave_parts = factor(waves[k].astype(F32))
        window_parts = transmission(blocks, tails, k)
        y = dot(c, rb[which])
        turned = signed(swapped(halves(y)[2]), False)
        g = times_conj(y, turned, window_parts).astype(BF16)
        late = (k, y, turned, wave_parts)
    leave(*late)
    return g


def detector(psi, observed, left, right, right_conj):
    def product(ah, al, bh, bl):
        return dot(ah, bh) + (dot(ah, bl) + dot(al, bh))

    near = left_product(left[0], psi, False) + left_product(left[1], psi, False)
    far = product(*split2(near), right[0], right[1])
    f0, f1, ft = halves(far)
    other = swapped(ft)
    main = f0 * f0 + f1 * f1 - observed[:, :LANES]
    tail = ft * ft + other * other - observed[:, LANES:]
    push = jnp.concatenate([main * f0, main * f1, tail * ft], axis=1)
    back = left_product(left[0], push.astype(BF16), True)
    return dot(back.astype(BF16), right_conj[...]).astype(BF16)


def read_indices(blocks, indices, count):
    for k in range(blocks.shape[0]):
        tag = jnp.max(blocks[k, -ROWS:, 2 * LANES :].astype(F32))
        indices[k] = jnp.clip(tag.astype(jnp.int32), 0, count - 1)


def place_in(size):
    rank = lax.axis_index("cuts")
    return lax.rem(rank, size), lax.div(rank, size)


def observe(blocks, near_rows, observed, first):
    for k in range(blocks.shape[0]):
        at = first + k * near_rows
        observed[at : at + near_rows, :] = blocks[k, -ROWS:, : 2 * LANES].astype(F32)[:near_rows]


def near_kernel(blocks, _, near, observed):
    observe(blocks, near.shape[0] // blocks.shape[0], observed, 0)
    near[...] = observed[...].astype(BF16)


def first_kernel(group_ref, probes, blocks, props, rf, dft, leaving, waves, tails, lb, rb, left, right, right_conj, probe, indices, sem):
    size = blocks.shape[0]
    slot, group = place_in(size)

    @pl.when(group == 0)
    def _():
        position = 0
        for p, held in enumerate(slots_of(group_ref.shape[0], size)):
            position = jnp.where(slot == held, p, position)
        which = group_ref[position]
        copy = pltpu.make_async_copy(probes.at[which], probe, sem)
        copy.start()
        read_indices(blocks, indices, props.shape[0])
        copy.wait()
        waves[0] = packed(probe[0].astype(F32), probe[1].astype(F32)).astype(BF16)
        forward_steps(blocks, None, waves, indices, props, rf)
        leaving[...] = waves[size]

    @pl.when(group > 0)
    def _():
        spread_tails(blocks, tails)
        backward_tables(props, lb, rb)
        detector_tables(dft, left, right, right_conj)


def forward_kernel(stage):
    def kernel(entering, blocks, tails, props, rf, waves_in, leaving, waves, first_tails, indices):
        size = blocks.shape[0]
        _, group = place_in(size)

        @pl.when(group == stage)
        def _():
            read_indices(blocks, indices, props.shape[0])
            waves[0] = entering[...]
            forward_steps(blocks, tails, waves, indices, props, rf)
            leaving[...] = waves[size]

        @pl.when(group != stage)
        def _():
            waves[...] = waves_in[...]

        @pl.when(group == 0)
        def _():
            spread_tails(blocks, first_tails)

    return kernel


def middle_kernel(groups):
    def kernel(waves, *refs):
        earlier, refs = refs[: groups - 1], refs[groups - 1 :]
        blocks, tails, props, lb, rb, left, right, right_conj, leaving, grads, lb_out, rb_out, observed, indices = refs
        size = blocks.shape[0]
        _, group = place_in(size)

        @pl.when(group == groups - 1)
        def _():
            read_indices(blocks, indices, props.shape[0])
            rows = earlier[0].shape[0]
            for n, near in enumerate(earlier):
                observed[n * rows : (n + 1) * rows, :] = near[...].astype(F32)
            observe(blocks, rows // size, observed, (groups - 1) * rows)
            g = detector(waves[size], observed[...], left, right, right_conj)
            leaving[...] = backward_steps(blocks, tails, waves, indices, lb, rb, grads, g)

        @pl.when(group < groups - 1)
        def _():
            backward_tables(props, lb_out, rb_out)

    return kernel


def backward_kernel(stage):
    def kernel(arriving, waves, blocks, tails, lb, rb, grads_in, leaving, grads, indices):
        _, group = place_in(blocks.shape[0])

        @pl.when(group == stage)
        def _():
            read_indices(blocks, indices, lb.shape[0])
            leaving[...] = backward_steps(blocks, tails, waves, indices, lb, rb, grads, arriving[...])

        @pl.when(group != stage)
        def _():
            grads[...] = grads_in[...]

    return kernel


def gather_kernel(offsets_ref, grads_ref, out_ref, planes, sems):
    positions = offsets_ref.shape[1]
    size, width, _ = grads_ref.shape
    extent = out_ref.shape[-1]
    _, group = place_in(size)
    flip = lax.rem(group, 2) * (size // 2)
    spread_out = []
    for p, slot in enumerate(slots_of(positions, size)):
        x0, x1, xt = halves(grads_ref[lax.bitwise_xor(slot, flip)])
        other = swapped(xt.astype(F32)).astype(BF16)
        both = jnp.concatenate(
            [jnp.concatenate([x0, xt], axis=1), jnp.concatenate([x1, other], axis=1)], axis=0
        )
        spread_out.append(dot(both, picker((2 * LANES, extent), offsets_ref[1, p])).astype(BF16))
    rows = jnp.concatenate(
        [row_picker((extent, width), -offsets_ref[0, p]) for p in range(positions)], axis=1
    )
    copies = []
    for c in range(2):
        here = slice(c * width, (c + 1) * width)
        planes[c] = dot(rows, jnp.concatenate([x[here] for x in spread_out], axis=0))
        copies.append(pltpu.make_async_copy(planes.at[c], out_ref.at[0, c], sems.at[c]))
        copies[-1].start()
    for copy in copies:
        copy.wait()


VMEM = pl.BlockSpec(memory_space=pltpu.VMEM)
SMEM = pl.BlockSpec(memory_space=pltpu.SMEM)
HBM = pl.BlockSpec(memory_space=pl.ANY)
ALONE = pltpu.CompilerParams(vmem_limit_bytes=60 * 1024 * 1024)
PARAMS = pltpu.CompilerParams(vmem_limit_bytes=20 * 1024 * 1024)


def shards(objects, propagators, prop_index, probes, probe_group, offsets, measured):
    sections = lax.axis_size("cuts")
    width = probes.shape[-1]
    kinds = propagators.shape[0]
    near_rows = measured.shape[1]
    size = GROUP
    groups = sections // size
    rows = width + ROWS
    slots = slots_of(probe_group.shape[0], size)
    members = [list(range(first, first + size)) for first in range(0, sections, size)]

    def struct(*dims, kind=BF16):
        return jax.ShapeDtypeStruct(dims, kind)

    def exchanged(blocks):
        return lax.all_to_all(blocks, "cuts", 0, 0, axis_index_groups=members, tiled=True)

    def handed(block, stage, distance):
        ends = (slots_in(at, len(slots), size) for at in (stage, stage + distance))
        route = [(stage * size + l, (stage + distance) * size + m) for l, m in zip(*ends)]
        return lax.ppermute(block, "cuts", route)

    blocks, rf = pl.pallas_call(
        window_kernel,
        out_shape=[struct(size, rows, 2 * width), struct(kinds, 2 * width, 2 * width)],
        in_specs=[HBM, SMEM, HBM, HBM, HBM],
        out_specs=[HBM, HBM],
        scratch_shapes=[
            pltpu.VMEM((size, rows, 2 * width), BF16),
            pltpu.VMEM((kinds, 2 * width, 2 * width), BF16),
            pltpu.SMEM(offsets.shape[::-1], jnp.int32),
            pltpu.VMEM(objects.shape[1:], BF16),
            pltpu.VMEM(measured.shape, F32),
            pltpu.VMEM(propagators.shape, BF16),
            pltpu.VMEM((len(slots), 2, objects.shape[-1], 2 * LANES), BF16),
            pltpu.SemaphoreType.DMA((5 + len(slots) + kinds,)),
        ],
        compiler_params=ALONE,
        name="windows",
    )(offsets.T, prop_index, objects, measured, propagators)
    blocks = exchanged(blocks)

    wave = struct(width, 2 * width)
    near = struct(size * near_rows, 2 * LANES)
    waves_shape = struct(size + 1, width, 2 * width)
    grads_shape = struct(size, width, 2 * width)
    tails_shape = struct(size, width, 2 * LANES)
    left_table = struct(kinds, 2 * width, width)
    square_table = struct(kinds, 2 * width, 2 * width)
    detector_left = struct(2, 2 * width, width)
    detector_right = struct(2, 2 * width, 2 * width)
    indices = pltpu.SMEM((size,), jnp.int32)

    def call(kernel, name, out_shape, in_specs, scratch_shapes, operands, slices=0):
        return pl.pallas_call(
            kernel,
            out_shape=out_shape,
            in_specs=in_specs,
            out_specs=[VMEM] * len(out_shape),
            scratch_shapes=scratch_shapes,
            compiler_params=PARAMS,
            cost_estimate=pl.CostEstimate(
                flops=16 * slices * width**3,
                bytes_accessed=sum(math.prod(x.shape) * x.dtype.itemsize for x in list(operands) + out_shape),
                transcendentals=0,
            ),
            name=name,
        )(*operands)

    leaving, waves, tails, lb, rb, *dft = call(
        first_kernel,
        "first_forward",
        [wave, waves_shape, tails_shape, left_table, square_table]
        + [detector_left, detector_right, struct(2 * width, 2 * width)],
        [SMEM, HBM, VMEM, VMEM, VMEM, VMEM],
        [pltpu.VMEM(probes.shape[1:], BF16), indices, pltpu.SemaphoreType.DMA],
        (probe_group, probes, blocks, propagators, rf, jnp.asarray(dft_constant(width))),
        size,
    )
    entering = handed(leaving, 0, 1)
    (near_out,) = call(near_kernel, "near_rows", [near], [VMEM, HBM], [pltpu.VMEM(near.shape, F32)], (blocks, leaving))
    nears = [handed(near_out, stage, groups - 1 - stage) for stage in range(groups - 1)]
    for stage in range(1, groups):
        leaving, waves, first_tails = call(
            forward_kernel(stage),
            "forward",
            [wave, waves_shape, tails_shape],
            [VMEM] * 6,
            [indices],
            (entering, blocks, tails, propagators, rf, waves),
            size,
        )
        if stage < groups - 1:
            entering = handed(leaving, stage, 1)

    leaving, grads, lb, rb = call(
        middle_kernel(groups),
        "middle",
        [wave, grads_shape, left_table, square_table],
        [VMEM] * (groups + 8),
        [pltpu.VMEM((width, 2 * LANES), F32), indices],
        (waves, *nears, blocks, tails, propagators, lb, rb, *dft),
        size,
    )

    for stage in range(groups - 2, -1, -1):
        arriving = handed(leaving, stage + 1, -1)
        leaving, grads = call(
            backward_kernel(stage),
            "backward",
            [wave, grads_shape],
            [VMEM] * 7,
            [indices],
            (arriving, waves, blocks, first_tails if stage == 0 else tails, lb, rb, grads),
            size,
        )

    return pl.pallas_call(
        gather_kernel,
        out_shape=jax.ShapeDtypeStruct(objects.shape, F32),
        in_specs=[SMEM, VMEM],
        out_specs=HBM,
        scratch_shapes=[pltpu.VMEM(objects.shape[1:], F32), pltpu.SemaphoreType.DMA((2,))],
        compiler_params=PARAMS,
        name="sum_windows",
    )(offsets.T, exchanged(grads))


def solution(mesh):
    in_specs = (
        P(("parts", "cuts"), None, None, None),
        P(),
        P(("parts", "cuts")),
        P(),
        P(),
        P("parts", None),
        P("parts", "cuts", None),
    )
    out_specs = P(("parts", "cuts"), None, None, None)
    return jax.shard_map(shards, mesh=mesh, in_specs=in_specs, out_specs=out_specs, check_vma=False)
```

```python
import math

import jax
import jax.numpy as jnp
import numpy as np
from jax import lax
from jax.experimental import pallas as pl
from jax.experimental.pallas import tpu as pltpu
from jax.sharding import PartitionSpec as P

TRANSMIT = 0.985
GROUP = 8
LANES = 128
ROWS = 16
EXTRA = 8
F32 = jnp.float32
BF16 = jnp.bfloat16


def dot(former, latter):
    return jnp.dot(former, latter, preferred_element_type=F32)


def halves(x):
    return x[:, :LANES], x[:, LANES : 2 * LANES], x[:, 2 * LANES :]


def swapped(tail):
    return pltpu.roll(tail, LANES // 2, 1)


def low_half(rows):
    return lax.broadcasted_iota(jnp.int32, (rows, LANES), 1) < LANES // 2


def spread(tail):
    other = swapped(tail)
    low = low_half(tail.shape[0])
    return jnp.where(low, tail, other), jnp.where(low, other, tail)


def signed(tail, minus_low):
    low = low_half(tail.shape[0])
    return jnp.where(low == minus_low, -tail, tail)


def factor(b):
    b0, b1, bt = halves(b)
    return (b0, b1) + spread(bt)


def times(a, parts):
    a0, a1, at = halves(a)
    b0, b1, b_real, b_imag = parts
    tail = at * b_real + signed(swapped(at), True) * b_imag
    return jnp.concatenate([a0 * b0 - a1 * b1, a1 * b0 + a0 * b1, tail], axis=1)


def times_conj(a, turned, parts):
    a0, a1, at = halves(a)
    b0, b1, b_real, b_imag = parts
    tail = at * b_real + turned * b_imag
    return jnp.concatenate([a0 * b0 + a1 * b1, a1 * b0 - a0 * b1, tail], axis=1)


def left_product(table, x, conj):
    width = x.shape[0]
    both = dot(table, x)
    u0, u1, ut = halves(both[:width])
    v0, v1, vt = halves(both[width:])
    turned = signed(swapped(vt), not conj)
    if conj:
        return jnp.concatenate([u0 + v1, u1 - v0, ut + turned], axis=1)
    return jnp.concatenate([u0 - v1, u1 + v0, ut + turned], axis=1)


def spread_tails(blocks, tails):
    size, _, columns = blocks.shape
    for k in range(size):
        pair = spread(blocks[k, : columns // 2, 2 * LANES :].astype(F32))
        tails[k] = jnp.concatenate(pair, axis=1).astype(BF16)


def transmission(blocks, tails, k):
    window = blocks[k, : blocks.shape[2] // 2, :].astype(F32)
    b0, b1, bt = halves(window)
    if tails is None:
        b_real, b_imag = spread(bt)
    else:
        pair = tails[k].astype(F32)
        b_real, b_imag = pair[:, :LANES], pair[:, LANES:]
    return TRANSMIT + b0, b1, TRANSMIT + b_real, b_imag


def split2(x):
    high = x.astype(BF16)
    return high, (x - high.astype(F32)).astype(BF16)


def picker(shape, start, high_tail=False):
    columns, across = (0, 1) if shape[0] > shape[1] else (1, 0)
    half = LANES // 2
    taken = lax.broadcasted_iota(jnp.int32, shape, columns) - start
    place = lax.broadcasted_iota(jnp.int32, shape, across)
    if high_tail:
        wanted = jnp.where(place < LANES, place, jnp.where(place < LANES + half, -shape[columns], place - half))
    else:
        wanted = jnp.where(place < LANES + half, place, -shape[columns])
    return jnp.where(taken == wanted, 1.0, 0.0).astype(BF16)


def row_picker(shape, distance):
    taken = lax.broadcasted_iota(jnp.int32, shape, 1)
    wanted = lax.broadcasted_iota(jnp.int32, shape, 0) + distance
    return jnp.where(taken == wanted, 1.0, 0.0).astype(BF16)


def rows_near(x, start, count):
    limit = x.shape[0] - count
    bit = 1 << (limit.bit_length() - 1)
    while bit >= ROWS:
        length = count + bit
        short = bit + length - x.shape[0]
        if short > 0:
            x = jnp.concatenate([x, jnp.zeros((short, x.shape[1]), x.dtype)], axis=0)
        x = jnp.where(lax.bitwise_and(start, bit) != 0, x[bit : bit + length], x[:length])
        bit //= 2
    return x


def packed(real, imag):
    return jnp.concatenate([real[:, :LANES], imag[:, :LANES], real[:, LANES:], imag[:, LANES:]], axis=1)


def dft_constant(width):
    counter = np.arange(width)
    angle = (counter[:, None] * counter[None, :] % width) * (2.0 * math.pi / width)
    return (np.stack([np.cos(angle), -np.sin(angle)]) / math.sqrt(width)).astype(np.float32)


def slots_of(positions, size):
    half = size // 2
    order = list(range(half, size)) + list(range(0, half, 2)) + list(range(1, half, 2))
    return order[:positions]


def slots_in(group, positions, size):
    flip = (group % 2) * (size // 2)
    return [slot ^ flip for slot in slots_of(positions, size)]


def window_kernel(offsets_in, index_ref, objects_in, measured_in, blocks_out, blocks, offsets_ref, objects, measured, pickers, sems):
    positions, near_rows, width = measured.shape
    extent = objects.shape[-1]
    copies = [
        pltpu.make_async_copy(objects_in.at[0, 0], objects.at[0], sems.at[0]),
        pltpu.make_async_copy(objects_in.at[0, 1], objects.at[1], sems.at[1]),
        pltpu.make_async_copy(measured_in, measured, sems.at[2]),
        pltpu.make_async_copy(offsets_in, offsets_ref, sems.at[3]),
    ]
    for copy in reversed(copies):
        copy.start()
    half = (near_rows + 1) // 2
    tag = jnp.full((EXTRA - half, 2 * width), index_ref[0], jnp.int32).astype(F32)
    size = blocks_out.shape[0]
    _, group = place_in(size)
    flip = lax.rem(group, 2) * (size // 2)
    copies.pop().wait()
    for p in range(positions):
        for c in range(2):
            pickers[p, c] = picker((extent, 2 * LANES), offsets_ref[1, p], c == 1)
    for copy in copies:
        copy.wait()
    sending = []
    for p, slot in enumerate(slots_of(positions, size)):
        start = offsets_ref[0, p]
        real, imag = (
            dot(rows_near(objects[c], start, width), pickers[p, c])
            for c in range(2)
        )
        tail = real[:, LANES:] + imag[:, LANES:]
        window = jnp.concatenate([real[:, :LANES], imag[:, :LANES], tail], axis=1).astype(BF16)
        shift = lax.bitwise_and(start, ROWS - 1)
        blocks[p, :width, :] = dot(row_picker((width, width + ROWS), shift), window).astype(BF16)
        rows = jnp.concatenate([measured[p], measured[p, : 2 * half - near_rows]], axis=0) if near_rows % 2 else measured[p]
        seen = packed(rows[:half], rows[half:])
        blocks[p, width:, :] = jnp.concatenate([seen, tag], axis=0).astype(BF16)
        target = blocks_out.at[lax.bitwise_xor(slot, flip)]
        sending.append(pltpu.make_async_copy(blocks.at[p], target, sems.at[4 + p]))
        sending[-1].start()
    for copy in sending:
        copy.wait()


def right_table(real, imag):
    upper, lower = packed(real, imag), packed(-imag, real)
    return jnp.concatenate([upper[:LANES], lower[:LANES], upper[LANES:], lower[LANES:]], axis=0).astype(BF16)


def forward_tables(props, rf):
    for k in range(props.shape[0]):
        rf[k] = right_table(props[k, 0].astype(F32).T, props[k, 1].astype(F32).T)


def backward_tables(props, lb, rb):
    width = props.shape[-1]
    for k in range(props.shape[0]):
        real, imag = props[k, 0].astype(F32), props[k, 1].astype(F32)
        lb[k, :width, :] = real.T.astype(BF16)
        lb[k, width:, :] = imag.T.astype(BF16)
        rb[k] = right_table(real, -imag)


def detector_tables(dft, left, right, right_conj):
    width = dft.shape[-1]
    for n, (real, imag) in enumerate(zip(split2(dft[0]), split2(dft[1]))):
        left[n, :width, :] = real
        left[n, width:, :] = imag
        real, imag = real.astype(F32), imag.astype(F32)
        right[n] = right_table(real, imag)
        if n == 0:
            right_conj[...] = right_table(real, -imag)


def forward_steps(blocks, tails, waves, indices, lf, rf):
    sections, _, columns = blocks.shape
    width = columns // 2
    psi = waves[0]
    parts = transmission(blocks, tails, 0)
    for k in range(sections):
        which = indices[k]
        z = times(psi.astype(F32), parts).astype(BF16)
        h = left_product(lf[which].reshape(columns, width), z, False).astype(BF16)
        if k + 1 < sections:
            parts = transmission(blocks, tails, k + 1)
        psi = dot(h, rf[which]).astype(BF16)
        waves[k + 1] = psi


def backward_steps(blocks, tails, waves, indices, lb, rb, grads, g):
    sections, _, columns = blocks.shape
    width = columns // 2

    def leave(k, y, turned, wave_parts):
        grads[k] = times_conj(y, turned, wave_parts).astype(BF16)

    late = None
    for k in reversed(range(sections)):
        which = indices[k]
        c = left_product(lb[which], g, True).astype(BF16)
        if late is not None:
            leave(*late)
        wave_parts = factor(waves[k].astype(F32))
        window_parts = transmission(blocks, tails, k)
        y = dot(c, rb[which])
        turned = signed(swapped(halves(y)[2]), False)
        g = times_conj(y, turned, window_parts).astype(BF16)
        late = (k, y, turned, wave_parts)
    leave(*late)
    return g


def detector(psi, observed, left, right, right_conj):
    def product(ah, al, bh, bl):
        return dot(ah, bh) + (dot(ah, bl) + dot(al, bh))

    near = left_product(left[0], psi, False) + left_product(left[1], psi, False)
    far = product(*split2(near), right[0], right[1])
    f0, f1, ft = halves(far)
    other = swapped(ft)
    main = f0 * f0 + f1 * f1 - observed[:, :LANES]
    tail = ft * ft + other * other - observed[:, LANES:]
    push = jnp.concatenate([main * f0, main * f1, tail * ft], axis=1)
    back = left_product(left[0], push.astype(BF16), True)
    return dot(back.astype(BF16), right_conj[...]).astype(BF16)


def read_indices(blocks, indices, count):
    for k in range(blocks.shape[0]):
        tag = jnp.max(blocks[k, -EXTRA:, :LANES].astype(F32)[EXTRA - 1 :])
        indices[k] = jnp.clip(tag.astype(jnp.int32), 0, count - 1)


def place_in(size):
    rank = lax.axis_index("cuts")
    return lax.rem(rank, size), lax.div(rank, size)


def observe(blocks, near_rows, observed, first):
    half = (near_rows + 1) // 2
    for k in range(blocks.shape[0]):
        early, late, tail = halves(blocks[k, -EXTRA:, :].astype(F32))
        early_tail, late_tail = spread(tail)
        at = first + k * near_rows
        observed[at : at + half, :] = jnp.concatenate([early, early_tail], axis=1)[:half]
        observed[at + half : at + near_rows, :] = jnp.concatenate([late, late_tail], axis=1)[: near_rows - half]


def near_kernel(blocks, _, near, observed):
    observe(blocks, near.shape[0] // blocks.shape[0], observed, 0)
    near[...] = observed[...].astype(BF16)


def first_kernel(group_ref, probes, blocks, props, dft, leaving, waves, tails, lb, rf, rb, left, right, right_conj, probe, indices, sem):
    size = blocks.shape[0]
    slot, group = place_in(size)

    @pl.when(group == 0)
    def _():
        position = 0
        for p, held in enumerate(slots_of(group_ref.shape[0], size)):
            position = jnp.where(slot == held, p, position)
        which = group_ref[position]
        copy = pltpu.make_async_copy(probes.at[which], probe, sem)
        copy.start()
        forward_tables(props, rf)
        read_indices(blocks, indices, props.shape[0])
        copy.wait()
        waves[0] = packed(probe[0].astype(F32), probe[1].astype(F32)).astype(BF16)
        forward_steps(blocks, None, waves, indices, props, rf)
        leaving[...] = waves[size]

    @pl.when(group > 0)
    def _():
        spread_tails(blocks, tails)
        forward_tables(props, rf)
        backward_tables(props, lb, rb)
        detector_tables(dft, left, right, right_conj)


def forward_kernel(stage):
    def kernel(entering, blocks, tails, props, rf, waves_in, leaving, waves, first_tails, indices):
        size = blocks.shape[0]
        _, group = place_in(size)

        @pl.when(group == stage)
        def _():
            read_indices(blocks, indices, props.shape[0])
            waves[0] = entering[...]
            forward_steps(blocks, tails, waves, indices, props, rf)
            leaving[...] = waves[size]

        @pl.when(group != stage)
        def _():
            waves[...] = waves_in[...]

        @pl.when(group == 0)
        def _():
            spread_tails(blocks, first_tails)

    return kernel


def middle_kernel(groups):
    def kernel(waves, *refs):
        earlier, refs = refs[: groups - 1], refs[groups - 1 :]
        blocks, tails, props, lb, rb, left, right, right_conj, leaving, grads, lb_out, rb_out, observed, indices = refs
        size = blocks.shape[0]
        _, group = place_in(size)

        @pl.when(group == groups - 1)
        def _():
            read_indices(blocks, indices, props.shape[0])
            rows = earlier[0].shape[0]
            for n, near in enumerate(earlier):
                observed[n * rows : (n + 1) * rows, :] = near[...].astype(F32)
            observe(blocks, rows // size, observed, (groups - 1) * rows)
            g = detector(waves[size], observed[...], left, right, right_conj)
            leaving[...] = backward_steps(blocks, tails, waves, indices, lb, rb, grads, g)

        @pl.when(group < groups - 1)
        def _():
            backward_tables(props, lb_out, rb_out)

    return kernel


def backward_kernel(stage):
    def kernel(arriving, waves, blocks, tails, lb, rb, grads_in, leaving, grads, indices):
        _, group = place_in(blocks.shape[0])

        @pl.when(group == stage)
        def _():
            read_indices(blocks, indices, lb.shape[0])
            leaving[...] = backward_steps(blocks, tails, waves, indices, lb, rb, grads, arriving[...])

        @pl.when(group != stage)
        def _():
            grads[...] = grads_in[...]

    return kernel


def gather_kernel(offsets_ref, grads_ref, out_ref, planes, sems):
    positions = offsets_ref.shape[1]
    size, width, _ = grads_ref.shape
    extent = out_ref.shape[-1]
    _, group = place_in(size)
    flip = lax.rem(group, 2) * (size // 2)
    spread_out = []
    for p, slot in enumerate(slots_of(positions, size)):
        x0, x1, xt = halves(grads_ref[lax.bitwise_xor(slot, flip)])
        other = swapped(xt.astype(F32)).astype(BF16)
        both = jnp.concatenate(
            [jnp.concatenate([x0, xt], axis=1), jnp.concatenate([x1, other], axis=1)], axis=0
        )
        spread_out.append(dot(both, picker((2 * LANES, extent), offsets_ref[1, p])).astype(BF16))
    rows = jnp.concatenate(
        [row_picker((extent, width), -offsets_ref[0, p]) for p in range(positions)], axis=1
    )
    copies = []
    for c in range(2):
        here = slice(c * width, (c + 1) * width)
        planes[c] = dot(rows, jnp.concatenate([x[here] for x in spread_out], axis=0))
        copies.append(pltpu.make_async_copy(planes.at[c], out_ref.at[0, c], sems.at[c]))
        copies[-1].start()
    for copy in copies:
        copy.wait()


VMEM = pl.BlockSpec(memory_space=pltpu.VMEM)
SMEM = pl.BlockSpec(memory_space=pltpu.SMEM)
HBM = pl.BlockSpec(memory_space=pl.ANY)
ALONE = pltpu.CompilerParams(vmem_limit_bytes=60 * 1024 * 1024)
PARAMS = pltpu.CompilerParams(vmem_limit_bytes=20 * 1024 * 1024)


def shards(objects, propagators, prop_index, probes, probe_group, offsets, measured):
    sections = lax.axis_size("cuts")
    width = probes.shape[-1]
    kinds = propagators.shape[0]
    near_rows = measured.shape[1]
    size = GROUP
    groups = sections // size
    rows = width + EXTRA
    slots = slots_of(probe_group.shape[0], size)
    members = [list(range(first, first + size)) for first in range(0, sections, size)]

    def struct(*dims, kind=BF16):
        return jax.ShapeDtypeStruct(dims, kind)

    def exchanged(blocks):
        return lax.all_to_all(blocks, "cuts", 0, 0, axis_index_groups=members, tiled=True)

    def handed(block, stage, distance):
        ends = (slots_in(at, len(slots), size) for at in (stage, stage + distance))
        route = [(stage * size + l, (stage + distance) * size + m) for l, m in zip(*ends)]
        return lax.ppermute(block, "cuts", route)

    blocks = pl.pallas_call(
        window_kernel,
        out_shape=struct(size, rows, 2 * width),
        in_specs=[HBM, SMEM, HBM, HBM],
        out_specs=HBM,
        scratch_shapes=[
            pltpu.VMEM((size, rows, 2 * width), BF16),
            pltpu.SMEM(offsets.shape[::-1], jnp.int32),
            pltpu.VMEM(objects.shape[1:], BF16),
            pltpu.VMEM(measured.shape, F32),
            pltpu.VMEM((len(slots), 2, objects.shape[-1], 2 * LANES), BF16),
            pltpu.SemaphoreType.DMA((4 + len(slots),)),
        ],
        compiler_params=ALONE,
        name="windows",
    )(offsets.T, prop_index, objects, measured)
    blocks = exchanged(blocks)

    wave = struct(width, 2 * width)
    near = struct(size * near_rows, 2 * LANES)
    waves_shape = struct(size + 1, width, 2 * width)
    grads_shape = struct(size, width, 2 * width)
    tails_shape = struct(size, width, 2 * LANES)
    left_table = struct(kinds, 2 * width, width)
    square_table = struct(kinds, 2 * width, 2 * width)
    detector_left = struct(2, 2 * width, width)
    detector_right = struct(2, 2 * width, 2 * width)
    indices = pltpu.SMEM((size,), jnp.int32)

    def call(kernel, name, out_shape, in_specs, scratch_shapes, operands, slices=0):
        return pl.pallas_call(
            kernel,
            out_shape=out_shape,
            in_specs=in_specs,
            out_specs=[VMEM] * len(out_shape),
            scratch_shapes=scratch_shapes,
            compiler_params=PARAMS,
            cost_estimate=pl.CostEstimate(
                flops=16 * slices * width**3,
                bytes_accessed=sum(math.prod(x.shape) * x.dtype.itemsize for x in list(operands) + out_shape),
                transcendentals=0,
            ),
            name=name,
        )(*operands)

    leaving, waves, tails, lb, rf, rb, *dft = call(
        first_kernel,
        "first_forward",
        [wave, waves_shape, tails_shape, left_table, square_table, square_table]
        + [detector_left, detector_right, struct(2 * width, 2 * width)],
        [SMEM, HBM, VMEM, VMEM, VMEM],
        [pltpu.VMEM(probes.shape[1:], BF16), indices, pltpu.SemaphoreType.DMA],
        (probe_group, probes, blocks, propagators, jnp.asarray(dft_constant(width))),
        size,
    )
    entering = handed(leaving, 0, 1)
    (near_out,) = call(near_kernel, "near_rows", [near], [VMEM, HBM], [pltpu.VMEM(near.shape, F32)], (blocks, leaving))
    nears = [handed(near_out, stage, groups - 1 - stage) for stage in range(groups - 1)]
    for stage in range(1, groups):
        leaving, waves, first_tails = call(
            forward_kernel(stage),
            "forward",
            [wave, waves_shape, tails_shape],
            [VMEM] * 6,
            [indices],
            (entering, blocks, tails, propagators, rf, waves),
            size,
        )
        if stage < groups - 1:
            entering = handed(leaving, stage, 1)

    leaving, grads, lb, rb = call(
        middle_kernel(groups),
        "middle",
        [wave, grads_shape, left_table, square_table],
        [VMEM] * (groups + 8),
        [pltpu.VMEM((width, 2 * LANES), F32), indices],
        (waves, *nears, blocks, tails, propagators, lb, rb, *dft),
        size,
    )

    for stage in range(groups - 2, -1, -1):
        arriving = handed(leaving, stage + 1, -1)
        leaving, grads = call(
            backward_kernel(stage),
            "backward",
            [wave, grads_shape],
            [VMEM] * 7,
            [indices],
            (arriving, waves, blocks, first_tails if stage == 0 else tails, lb, rb, grads),
            size,
        )

    return pl.pallas_call(
        gather_kernel,
        out_shape=jax.ShapeDtypeStruct(objects.shape, F32),
        in_specs=[SMEM, VMEM],
        out_specs=HBM,
        scratch_shapes=[pltpu.VMEM(objects.shape[1:], F32), pltpu.SemaphoreType.DMA((2,))],
        compiler_params=PARAMS,
        name="sum_windows",
    )(offsets.T, exchanged(grads))


def solution(mesh):
    in_specs = (
        P(("parts", "cuts"), None, None, None),
        P(),
        P(("parts", "cuts")),
        P(),
        P(),
        P("parts", None),
        P("parts", "cuts", None),
    )
    out_specs = P(("parts", "cuts"), None, None, None)
    return jax.shard_map(shards, mesh=mesh, in_specs=in_specs, out_specs=out_specs, check_vma=False)
```

```python
import math

import jax
import jax.numpy as jnp
import numpy as np
from jax import lax
from jax.experimental import pallas as pl
from jax.experimental.pallas import tpu as pltpu
from jax.sharding import PartitionSpec as P

TRANSMIT = 0.985
GROUP = 8
LANES = 128
ROWS = 16
F32 = jnp.float32
BF16 = jnp.bfloat16


def dot(former, latter):
    return jnp.dot(former, latter, preferred_element_type=F32)


def halves(x):
    return x[:, :LANES], x[:, LANES : 2 * LANES], x[:, 2 * LANES :]


def swapped(tail):
    return pltpu.roll(tail, LANES // 2, 1)


def low_half(rows):
    return lax.broadcasted_iota(jnp.int32, (rows, LANES), 1) < LANES // 2


def spread(tail):
    other = swapped(tail)
    low = low_half(tail.shape[0])
    return jnp.where(low, tail, other), jnp.where(low, other, tail)


def signed(tail, minus_low):
    low = low_half(tail.shape[0])
    return jnp.where(low == minus_low, -tail, tail)


def factor(b):
    b0, b1, bt = halves(b)
    return (b0, b1) + spread(bt)


def times(a, parts):
    a0, a1, at = halves(a)
    b0, b1, b_real, b_imag = parts
    tail = at * b_real + signed(swapped(at), True) * b_imag
    return jnp.concatenate([a0 * b0 - a1 * b1, a1 * b0 + a0 * b1, tail], axis=1)


def times_conj(a, turned, parts):
    a0, a1, at = halves(a)
    b0, b1, b_real, b_imag = parts
    tail = at * b_real + turned * b_imag
    return jnp.concatenate([a0 * b0 + a1 * b1, a1 * b0 - a0 * b1, tail], axis=1)


def left_product(table, x, conj):
    width = x.shape[0]
    both = dot(table, x)
    u0, u1, ut = halves(both[:width])
    v0, v1, vt = halves(both[width:])
    turned = signed(swapped(vt), not conj)
    if conj:
        return jnp.concatenate([u0 + v1, u1 - v0, ut + turned], axis=1)
    return jnp.concatenate([u0 - v1, u1 + v0, ut + turned], axis=1)


def spread_tails(blocks, tails):
    size, _, columns = blocks.shape
    for k in range(size):
        pair = spread(blocks[k, : columns // 2, 2 * LANES :].astype(F32))
        tails[k] = jnp.concatenate(pair, axis=1).astype(BF16)


def transmission(blocks, tails, k):
    window = blocks[k, : blocks.shape[2] // 2, :].astype(F32)
    b0, b1, bt = halves(window)
    if tails is None:
        b_real, b_imag = spread(bt)
    else:
        pair = tails[k].astype(F32)
        b_real, b_imag = pair[:, :LANES], pair[:, LANES:]
    return TRANSMIT + b0, b1, TRANSMIT + b_real, b_imag


def split2(x):
    high = x.astype(BF16)
    return high, (x - high.astype(F32)).astype(BF16)


def picker(shape, start, high_tail=False):
    columns, across = (0, 1) if shape[0] > shape[1] else (1, 0)
    half = LANES // 2
    taken = lax.broadcasted_iota(jnp.int32, shape, columns) - start
    place = lax.broadcasted_iota(jnp.int32, shape, across)
    if high_tail:
        wanted = jnp.where(place < LANES, place, jnp.where(place < LANES + half, -shape[columns], place - half))
    else:
        wanted = jnp.where(place < LANES + half, place, -shape[columns])
    return jnp.where(taken == wanted, 1.0, 0.0).astype(BF16)


def row_picker(shape, distance):
    taken = lax.broadcasted_iota(jnp.int32, shape, 1)
    wanted = lax.broadcasted_iota(jnp.int32, shape, 0) + distance
    return jnp.where(taken == wanted, 1.0, 0.0).astype(BF16)


def rows_near(x, start, count):
    limit = x.shape[0] - count
    bit = 1 << (limit.bit_length() - 1)
    while bit >= ROWS:
        length = count + bit
        short = bit + length - x.shape[0]
        if short > 0:
            x = jnp.concatenate([x, jnp.zeros((short, x.shape[1]), x.dtype)], axis=0)
        x = jnp.where(lax.bitwise_and(start, bit) != 0, x[bit : bit + length], x[:length])
        bit //= 2
    return x


def packed(real, imag):
    return jnp.concatenate([real[:, :LANES], imag[:, :LANES], real[:, LANES:], imag[:, LANES:]], axis=1)


def dft_constant(width):
    counter = np.arange(width)
    angle = (counter[:, None] * counter[None, :] % width) * (2.0 * math.pi / width)
    return (np.stack([np.cos(angle), -np.sin(angle)]) / math.sqrt(width)).astype(np.float32)


def slots_of(positions, size):
    half = size // 2
    order = list(range(half, size)) + list(range(0, half, 2)) + list(range(1, half, 2))
    return order[:positions]


def slots_in(group, positions, size):
    flip = (group % 2) * (size // 2)
    return [slot ^ flip for slot in slots_of(positions, size)]


def window_kernel(offsets_in, index_ref, objects_in, measured_in, blocks_out, blocks, offsets_ref, objects, measured, pickers, sems):
    positions, near_rows, width = measured.shape
    extent = objects.shape[-1]
    copies = [
        pltpu.make_async_copy(objects_in.at[0, 0], objects.at[0], sems.at[0]),
        pltpu.make_async_copy(objects_in.at[0, 1], objects.at[1], sems.at[1]),
        pltpu.make_async_copy(measured_in, measured, sems.at[2]),
        pltpu.make_async_copy(offsets_in, offsets_ref, sems.at[3]),
    ]
    for copy in reversed(copies):
        copy.start()
    tag = jnp.full((ROWS, LANES), index_ref[0], jnp.int32).astype(F32)
    size = blocks_out.shape[0]
    _, group = place_in(size)
    flip = lax.rem(group, 2) * (size // 2)
    copies.pop().wait()
    for p in range(positions):
        for c in range(2):
            pickers[p, c] = picker((extent, 2 * LANES), offsets_ref[1, p], c == 1)
    for copy in copies:
        copy.wait()
    sending = []
    for p, slot in enumerate(slots_of(positions, size)):
        start = offsets_ref[0, p]
        real, imag = (
            dot(rows_near(objects[c], start, width), pickers[p, c])
            for c in range(2)
        )
        tail = real[:, LANES:] + imag[:, LANES:]
        window = jnp.concatenate([real[:, :LANES], imag[:, :LANES], tail], axis=1).astype(BF16)
        shift = lax.bitwise_and(start, ROWS - 1)
        blocks[p, :width, :] = dot(row_picker((width, width + ROWS), shift), window).astype(BF16)
        tail = measured[p, :, LANES:]
        seen = jnp.concatenate([measured[p, :, :LANES], tail, tail, tag[:near_rows]], axis=1)
        left_over = jnp.concatenate([tag[near_rows:]] * 3, axis=1)
        blocks[p, width:, :] = jnp.concatenate([seen, left_over], axis=0).astype(BF16)
        target = blocks_out.at[lax.bitwise_xor(slot, flip)]
        sending.append(pltpu.make_async_copy(blocks.at[p], target, sems.at[4 + p]))
        sending[-1].start()
    for copy in sending:
        copy.wait()


def right_table(real, imag):
    upper, lower = packed(real, imag), packed(-imag, real)
    return jnp.concatenate([upper[:LANES], lower[:LANES], upper[LANES:], lower[LANES:]], axis=0).astype(BF16)


def forward_tables(props, rf):
    for k in range(props.shape[0]):
        rf[k] = right_table(props[k, 0].astype(F32).T, props[k, 1].astype(F32).T)


def backward_tables(props, lb, rb):
    width = props.shape[-1]
    for k in range(props.shape[0]):
        real, imag = props[k, 0].astype(F32), props[k, 1].astype(F32)
        lb[k, :width, :] = real.T.astype(BF16)
        lb[k, width:, :] = imag.T.astype(BF16)
        rb[k] = right_table(real, -imag)


def detector_tables(dft, left, right, right_conj):
    width = dft.shape[-1]
    for n, (real, imag) in enumerate(zip(split2(dft[0]), split2(dft[1]))):
        left[n, :width, :] = real
        left[n, width:, :] = imag
        real, imag = real.astype(F32), imag.astype(F32)
        right[n] = right_table(real, imag)
        if n == 0:
            right_conj[...] = right_table(real, -imag)


def forward_steps(blocks, tails, waves, indices, lf, rf):
    sections, _, columns = blocks.shape
    width = columns // 2
    psi = waves[0]
    parts = transmission(blocks, tails, 0)
    for k in range(sections):
        which = indices[k]
        z = times(psi.astype(F32), parts).astype(BF16)
        h = left_product(lf[which].reshape(columns, width), z, False).astype(BF16)
        if k + 1 < sections:
            parts = transmission(blocks, tails, k + 1)
        psi = dot(h, rf[which]).astype(BF16)
        waves[k + 1] = psi


def backward_steps(blocks, tails, waves, indices, lb, rb, grads, g):
    sections, _, columns = blocks.shape
    width = columns // 2

    def leave(k, y, turned, wave_parts):
        grads[k] = times_conj(y, turned, wave_parts).astype(BF16)

    late = None
    for k in reversed(range(sections)):
        which = indices[k]
        c = left_product(lb[which], g, True).astype(BF16)
        if late is not None:
            leave(*late)
        wave_parts = factor(waves[k].astype(F32))
        window_parts = transmission(blocks, tails, k)
        y = dot(c, rb[which])
        turned = signed(swapped(halves(y)[2]), False)
        g = times_conj(y, turned, window_parts).astype(BF16)
        late = (k, y, turned, wave_parts)
    leave(*late)
    return g


def detector(psi, observed, left, right, right_conj):
    def product(ah, al, bh, bl):
        return dot(ah, bh) + (dot(ah, bl) + dot(al, bh))

    near = left_product(left[0], psi, False) + left_product(left[1], psi, False)
    far = product(*split2(near), right[0], right[1])
    f0, f1, ft = halves(far)
    other = swapped(ft)
    main = f0 * f0 + f1 * f1 - observed[:, :LANES]
    tail = ft * ft + other * other - observed[:, LANES:]
    push = jnp.concatenate([main * f0, main * f1, tail * ft], axis=1)
    back = left_product(left[0], push.astype(BF16), True)
    return dot(back.astype(BF16), right_conj[...]).astype(BF16)


def read_indices(blocks, indices, count):
    for k in range(blocks.shape[0]):
        tag = jnp.max(blocks[k, -ROWS:, 2 * LANES :].astype(F32))
        indices[k] = jnp.clip(tag.astype(jnp.int32), 0, count - 1)


def place_in(size):
    rank = lax.axis_index("cuts")
    return lax.rem(rank, size), lax.div(rank, size)


def observe(blocks, near_rows, observed, first):
    for k in range(blocks.shape[0]):
        at = first + k * near_rows
        observed[at : at + near_rows, :] = blocks[k, -ROWS:, : 2 * LANES].astype(F32)[:near_rows]


def near_kernel(blocks, props, _, near, tails, lb, rb, observed):
    _, group = place_in(blocks.shape[0])

    @pl.when(group == 0)
    def _():
        spread_tails(blocks, tails)
        backward_tables(props, lb, rb)

    observe(blocks, near.shape[0] // blocks.shape[0], observed, 0)
    near[...] = observed[...].astype(BF16)


def first_kernel(group_ref, probes, blocks, props, dft, leaving, waves, tails, lb, rf, rb, left, right, right_conj, probe, indices, sem):
    size = blocks.shape[0]
    slot, group = place_in(size)

    @pl.when(group == 0)
    def _():
        position = 0
        for p, held in enumerate(slots_of(group_ref.shape[0], size)):
            position = jnp.where(slot == held, p, position)
        which = group_ref[position]
        copy = pltpu.make_async_copy(probes.at[which], probe, sem)
        copy.start()
        forward_tables(props, rf)
        read_indices(blocks, indices, props.shape[0])
        copy.wait()
        waves[0] = packed(probe[0].astype(F32), probe[1].astype(F32)).astype(BF16)
        forward_steps(blocks, None, waves, indices, props, rf)
        leaving[...] = waves[size]

    @pl.when(group > 0)
    def _():
        spread_tails(blocks, tails)
        forward_tables(props, rf)
        backward_tables(props, lb, rb)
        detector_tables(dft, left, right, right_conj)


def forward_kernel(stage):
    def kernel(entering, blocks, tails, props, rf, waves_in, leaving, waves, indices):
        size = blocks.shape[0]
        _, group = place_in(size)

        @pl.when(group == stage)
        def _():
            read_indices(blocks, indices, props.shape[0])
            waves[0] = entering[...]
            forward_steps(blocks, tails, waves, indices, props, rf)
            leaving[...] = waves[size]

        @pl.when(group != stage)
        def _():
            waves[...] = waves_in[...]

    return kernel


def middle_kernel(groups):
    def kernel(waves, *refs):
        earlier, refs = refs[: groups - 1], refs[groups - 1 :]
        blocks, tails, props, lb, rb, left, right, right_conj, leaving, grads, observed, indices = refs
        size = blocks.shape[0]
        _, group = place_in(size)

        @pl.when(group == groups - 1)
        def _():
            read_indices(blocks, indices, props.shape[0])
            rows = earlier[0].shape[0]
            for n, near in enumerate(earlier):
                observed[n * rows : (n + 1) * rows, :] = near[...].astype(F32)
            observe(blocks, rows // size, observed, (groups - 1) * rows)
            g = detector(waves[size], observed[...], left, right, right_conj)
            leaving[...] = backward_steps(blocks, tails, waves, indices, lb, rb, grads, g)

    return kernel


def backward_kernel(stage):
    def kernel(arriving, waves, blocks, tails, lb, rb, grads_in, leaving, grads, indices):
        _, group = place_in(blocks.shape[0])

        @pl.when(group == stage)
        def _():
            read_indices(blocks, indices, lb.shape[0])
            leaving[...] = backward_steps(blocks, tails, waves, indices, lb, rb, grads, arriving[...])

        @pl.when(group != stage)
        def _():
            grads[...] = grads_in[...]

    return kernel


def gather_kernel(offsets_ref, grads_ref, out_ref, planes, sems):
    positions = offsets_ref.shape[1]
    size, width, _ = grads_ref.shape
    extent = out_ref.shape[-1]
    _, group = place_in(size)
    flip = lax.rem(group, 2) * (size // 2)
    spread_out = []
    for p, slot in enumerate(slots_of(positions, size)):
        x0, x1, xt = halves(grads_ref[lax.bitwise_xor(slot, flip)])
        other = swapped(xt.astype(F32)).astype(BF16)
        both = jnp.concatenate(
            [jnp.concatenate([x0, xt], axis=1), jnp.concatenate([x1, other], axis=1)], axis=0
        )
        spread_out.append(dot(both, picker((2 * LANES, extent), offsets_ref[1, p])).astype(BF16))
    rows = jnp.concatenate(
        [row_picker((extent, width), -offsets_ref[0, p]) for p in range(positions)], axis=1
    )
    copies = []
    for c in range(2):
        here = slice(c * width, (c + 1) * width)
        planes[c] = dot(rows, jnp.concatenate([x[here] for x in spread_out], axis=0))
        copies.append(pltpu.make_async_copy(planes.at[c], out_ref.at[0, c], sems.at[c]))
        copies[-1].start()
    for copy in copies:
        copy.wait()


VMEM = pl.BlockSpec(memory_space=pltpu.VMEM)
SMEM = pl.BlockSpec(memory_space=pltpu.SMEM)
HBM = pl.BlockSpec(memory_space=pl.ANY)
ALONE = pltpu.CompilerParams(vmem_limit_bytes=60 * 1024 * 1024)
PARAMS = pltpu.CompilerParams(vmem_limit_bytes=20 * 1024 * 1024)


def shards(objects, propagators, prop_index, probes, probe_group, offsets, measured):
    sections = lax.axis_size("cuts")
    width = probes.shape[-1]
    kinds = propagators.shape[0]
    near_rows = measured.shape[1]
    size = GROUP
    groups = sections // size
    rows = width + ROWS
    slots = slots_of(probe_group.shape[0], size)
    members = [list(range(first, first + size)) for first in range(0, sections, size)]

    def struct(*dims, kind=BF16):
        return jax.ShapeDtypeStruct(dims, kind)

    def exchanged(blocks):
        return lax.all_to_all(blocks, "cuts", 0, 0, axis_index_groups=members, tiled=True)

    def handed(block, stage, distance):
        ends = (slots_in(at, len(slots), size) for at in (stage, stage + distance))
        route = [(stage * size + l, (stage + distance) * size + m) for l, m in zip(*ends)]
        return lax.ppermute(block, "cuts", route)

    blocks = pl.pallas_call(
        window_kernel,
        out_shape=struct(size, rows, 2 * width),
        in_specs=[HBM, SMEM, HBM, HBM],
        out_specs=HBM,
        scratch_shapes=[
            pltpu.VMEM((size, rows, 2 * width), BF16),
            pltpu.SMEM(offsets.shape[::-1], jnp.int32),
            pltpu.VMEM(objects.shape[1:], BF16),
            pltpu.VMEM(measured.shape, F32),
            pltpu.VMEM((len(slots), 2, objects.shape[-1], 2 * LANES), BF16),
            pltpu.SemaphoreType.DMA((4 + len(slots),)),
        ],
        compiler_params=ALONE,
        name="windows",
    )(offsets.T, prop_index, objects, measured)
    blocks = exchanged(blocks)

    wave = struct(width, 2 * width)
    near = struct(size * near_rows, 2 * LANES)
    waves_shape = struct(size + 1, width, 2 * width)
    grads_shape = struct(size, width, 2 * width)
    tails_shape = struct(size, width, 2 * LANES)
    left_table = struct(kinds, 2 * width, width)
    square_table = struct(kinds, 2 * width, 2 * width)
    detector_left = struct(2, 2 * width, width)
    detector_right = struct(2, 2 * width, 2 * width)
    indices = pltpu.SMEM((size,), jnp.int32)

    def call(kernel, name, out_shape, in_specs, scratch_shapes, operands, slices=0):
        return pl.pallas_call(
            kernel,
            out_shape=out_shape,
            in_specs=in_specs,
            out_specs=[VMEM] * len(out_shape),
            scratch_shapes=scratch_shapes,
            compiler_params=PARAMS,
            cost_estimate=pl.CostEstimate(
                flops=16 * slices * width**3,
                bytes_accessed=sum(math.prod(x.shape) * x.dtype.itemsize for x in list(operands) + out_shape),
                transcendentals=0,
            ),
            name=name,
        )(*operands)

    leaving, waves, tails, lb, rf, rb, *dft = call(
        first_kernel,
        "first_forward",
        [wave, waves_shape, tails_shape, left_table, square_table, square_table]
        + [detector_left, detector_right, struct(2 * width, 2 * width)],
        [SMEM, HBM, VMEM, VMEM, VMEM],
        [pltpu.VMEM(probes.shape[1:], BF16), indices, pltpu.SemaphoreType.DMA],
        (probe_group, probes, blocks, propagators, jnp.asarray(dft_constant(width))),
        size,
    )
    entering = handed(leaving, 0, 1)
    near_out, *first_back = call(
        near_kernel,
        "near_rows",
        [near, tails_shape, left_table, square_table],
        [VMEM, VMEM, HBM],
        [pltpu.VMEM(near.shape, F32)],
        (blocks, propagators, leaving),
    )
    nears = [handed(near_out, stage, groups - 1 - stage) for stage in range(groups - 1)]
    for stage in range(1, groups):
        leaving, waves = call(
            forward_kernel(stage),
            "forward",
            [wave, waves_shape],
            [VMEM] * 6,
            [indices],
            (entering, blocks, tails, propagators, rf, waves),
            size,
        )
        if stage < groups - 1:
            entering = handed(leaving, stage, 1)

    leaving, grads = call(
        middle_kernel(groups),
        "middle",
        [wave, grads_shape],
        [VMEM] * (groups + 8),
        [pltpu.VMEM((width, 2 * LANES), F32), indices],
        (waves, *nears, blocks, tails, propagators, lb, rb, *dft),
        size,
    )

    for stage in range(groups - 2, -1, -1):
        arriving = handed(leaving, stage + 1, -1)
        leaving, grads = call(
            backward_kernel(stage),
            "backward",
            [wave, grads_shape],
            [VMEM] * 7,
            [indices],
            (arriving, waves, blocks, *(first_back if stage == 0 else (tails, lb, rb)), grads),
            size,
        )

    return pl.pallas_call(
        gather_kernel,
        out_shape=jax.ShapeDtypeStruct(objects.shape, F32),
        in_specs=[SMEM, VMEM],
        out_specs=HBM,
        scratch_shapes=[pltpu.VMEM(objects.shape[1:], F32), pltpu.SemaphoreType.DMA((2,))],
        compiler_params=PARAMS,
        name="sum_windows",
    )(offsets.T, exchanged(grads))


def solution(mesh):
    in_specs = (
        P(("parts", "cuts"), None, None, None),
        P(),
        P(("parts", "cuts")),
        P(),
        P(),
        P("parts", None),
        P("parts", "cuts", None),
    )
    out_specs = P(("parts", "cuts"), None, None, None)
    return jax.shard_map(shards, mesh=mesh, in_specs=in_specs, out_specs=out_specs, check_vma=False)
```

```python
import math

import jax
import jax.numpy as jnp
import numpy as np
from jax import lax
from jax.experimental import pallas as pl
from jax.experimental.pallas import tpu as pltpu
from jax.sharding import PartitionSpec as P

TRANSMIT = 0.985
GROUP = 8
LANES = 128
ROWS = 16
F32 = jnp.float32
BF16 = jnp.bfloat16


def dot(former, latter):
    return jnp.dot(former, latter, preferred_element_type=F32)


def halves(x):
    return x[:, :LANES], x[:, LANES : 2 * LANES], x[:, 2 * LANES :]


def swapped(tail):
    return pltpu.roll(tail, LANES // 2, 1)


def low_half(rows):
    return lax.broadcasted_iota(jnp.int32, (rows, LANES), 1) < LANES // 2


def spread(tail):
    other = swapped(tail)
    low = low_half(tail.shape[0])
    return jnp.where(low, tail, other), jnp.where(low, other, tail)


def signed(tail, minus_low):
    low = low_half(tail.shape[0])
    return jnp.where(low == minus_low, -tail, tail)


def factor(b):
    b0, b1, bt = halves(b)
    return (b0, b1) + spread(bt)


def times(a, parts):
    a0, a1, at = halves(a)
    b0, b1, b_real, b_imag = parts
    tail = at * b_real + signed(swapped(at), True) * b_imag
    return jnp.concatenate([a0 * b0 - a1 * b1, a1 * b0 + a0 * b1, tail], axis=1)


def times_conj(a, turned, parts):
    a0, a1, at = halves(a)
    b0, b1, b_real, b_imag = parts
    tail = at * b_real + turned * b_imag
    return jnp.concatenate([a0 * b0 + a1 * b1, a1 * b0 - a0 * b1, tail], axis=1)


def left_product(table, x, conj):
    width = x.shape[0]
    both = dot(table, x)
    u0, u1, ut = halves(both[:width])
    v0, v1, vt = halves(both[width:])
    turned = signed(swapped(vt), not conj)
    if conj:
        return jnp.concatenate([u0 + v1, u1 - v0, ut + turned], axis=1)
    return jnp.concatenate([u0 - v1, u1 + v0, ut + turned], axis=1)


def spread_tails(blocks, tails):
    size, _, columns = blocks.shape
    for k in range(size):
        pair = spread(blocks[k, : columns // 2, 2 * LANES :].astype(F32))
        tails[k] = jnp.concatenate(pair, axis=1).astype(BF16)


def transmission(blocks, tails, k):
    window = blocks[k, : blocks.shape[2] // 2, :].astype(F32)
    b0, b1, bt = halves(window)
    if tails is None:
        b_real, b_imag = spread(bt)
    else:
        pair = tails[k].astype(F32)
        b_real, b_imag = pair[:, :LANES], pair[:, LANES:]
    return TRANSMIT + b0, b1, TRANSMIT + b_real, b_imag


def split2(x):
    high = x.astype(BF16)
    return high, (x - high.astype(F32)).astype(BF16)


def picker(shape, start, high_tail=False):
    columns, across = (0, 1) if shape[0] > shape[1] else (1, 0)
    half = LANES // 2
    taken = lax.broadcasted_iota(jnp.int32, shape, columns) - start
    place = lax.broadcasted_iota(jnp.int32, shape, across)
    if high_tail:
        wanted = jnp.where(place < LANES, place, jnp.where(place < LANES + half, -shape[columns], place - half))
    else:
        wanted = jnp.where(place < LANES + half, place, -shape[columns])
    return jnp.where(taken == wanted, 1.0, 0.0).astype(BF16)


def row_picker(shape, distance):
    taken = lax.broadcasted_iota(jnp.int32, shape, 1)
    wanted = lax.broadcasted_iota(jnp.int32, shape, 0) + distance
    return jnp.where(taken == wanted, 1.0, 0.0).astype(BF16)


def rows_near(x, start, count):
    limit = x.shape[0] - count
    bit = 1 << (limit.bit_length() - 1)
    while bit >= ROWS:
        length = count + bit
        short = bit + length - x.shape[0]
        if short > 0:
            x = jnp.concatenate([x, jnp.zeros((short, x.shape[1]), x.dtype)], axis=0)
        x = jnp.where(lax.bitwise_and(start, bit) != 0, x[bit : bit + length], x[:length])
        bit //= 2
    return x


def packed(real, imag):
    return jnp.concatenate([real[:, :LANES], imag[:, :LANES], real[:, LANES:], imag[:, LANES:]], axis=1)


def dft_constant(width):
    counter = np.arange(width)
    angle = (counter[:, None] * counter[None, :] % width) * (2.0 * math.pi / width)
    return (np.stack([np.cos(angle), -np.sin(angle)]) / math.sqrt(width)).astype(np.float32)


def slots_of(positions, size):
    half = size // 2
    order = list(range(half, size)) + list(range(0, half, 2)) + list(range(1, half, 2))
    return order[:positions]


def slots_in(group, positions, size):
    flip = (group % 2) * (size // 2)
    return [slot ^ flip for slot in slots_of(positions, size)]


def window_kernel(offsets_in, index_ref, objects_in, measured_in, blocks_out, blocks, offsets_ref, objects, measured, pickers, sems):
    positions, near_rows, width = measured.shape
    extent = objects.shape[-1]
    copies = [
        pltpu.make_async_copy(objects_in.at[0, 0], objects.at[0], sems.at[0]),
        pltpu.make_async_copy(objects_in.at[0, 1], objects.at[1], sems.at[1]),
        pltpu.make_async_copy(measured_in, measured, sems.at[2]),
        pltpu.make_async_copy(offsets_in, offsets_ref, sems.at[3]),
    ]
    for copy in reversed(copies):
        copy.start()
    tag = jnp.full((ROWS, LANES), index_ref[0], jnp.int32).astype(F32)
    size = blocks_out.shape[0]
    _, group = place_in(size)
    flip = lax.rem(group, 2) * (size // 2)
    copies.pop().wait()
    for p in range(positions):
        for c in range(2):
            pickers[p, c] = picker((extent, 2 * LANES), offsets_ref[1, p], c == 1)
    for copy in copies:
        copy.wait()
    sending = []
    for p, slot in enumerate(slots_of(positions, size)):
        start = offsets_ref[0, p]
        real, imag = (
            dot(rows_near(objects[c], start, width), pickers[p, c])
            for c in range(2)
        )
        tail = real[:, LANES:] + imag[:, LANES:]
        window = jnp.concatenate([real[:, :LANES], imag[:, :LANES], tail], axis=1).astype(BF16)
        shift = lax.bitwise_and(start, ROWS - 1)
        blocks[p, :width, :] = dot(row_picker((width, width + ROWS), shift), window).astype(BF16)
        tail = measured[p, :, LANES:]
        seen = jnp.concatenate([measured[p, :, :LANES], tail, tail, tag[:near_rows]], axis=1)
        left_over = jnp.concatenate([tag[near_rows:]] * 3, axis=1)
        blocks[p, width:, :] = jnp.concatenate([seen, left_over], axis=0).astype(BF16)
        target = blocks_out.at[lax.bitwise_xor(slot, flip)]
        sending.append(pltpu.make_async_copy(blocks.at[p], target, sems.at[4 + p]))
        sending[-1].start()
    for copy in sending:
        copy.wait()


def right_table(real, imag):
    upper, lower = packed(real, imag), packed(-imag, real)
    return jnp.concatenate([upper[:LANES], lower[:LANES], upper[LANES:], lower[LANES:]], axis=0).astype(BF16)


def forward_tables(props, rf):
    for k in range(props.shape[0]):
        rf[k] = right_table(props[k, 0].astype(F32).T, props[k, 1].astype(F32).T)


def backward_tables(props, lb, rb):
    width = props.shape[-1]
    for k in range(props.shape[0]):
        real, imag = props[k, 0].astype(F32), props[k, 1].astype(F32)
        lb[k, :width, :] = real.T.astype(BF16)
        lb[k, width:, :] = imag.T.astype(BF16)
        rb[k] = right_table(real, -imag)


def detector_tables(dft, left, right, right_conj):
    width = dft.shape[-1]
    for n, (real, imag) in enumerate(zip(split2(dft[0]), split2(dft[1]))):
        left[n, :width, :] = real
        left[n, width:, :] = imag
        real, imag = real.astype(F32), imag.astype(F32)
        right[n] = right_table(real, imag)
        if n == 0:
            right_conj[...] = right_table(real, -imag)


def forward_steps(blocks, tails, waves, indices, lf, rf):
    sections, _, columns = blocks.shape
    width = columns // 2
    psi = waves[0]
    parts = transmission(blocks, tails, 0)
    for k in range(sections):
        which = indices[k]
        z = times(psi.astype(F32), parts).astype(BF16)
        h = left_product(lf[which].reshape(columns, width), z, False).astype(BF16)
        if k + 1 < sections:
            parts = transmission(blocks, tails, k + 1)
        psi = dot(h, rf[which]).astype(BF16)
        waves[k + 1] = psi


def backward_steps(blocks, tails, waves, indices, lb, rb, grads, g):
    sections, _, columns = blocks.shape
    width = columns // 2

    def leave(k, y, turned, wave_parts):
        grads[k] = times_conj(y, turned, wave_parts).astype(BF16)

    late = None
    for k in reversed(range(sections)):
        which = indices[k]
        c = left_product(lb[which], g, True).astype(BF16)
        if late is not None:
            leave(*late)
        wave_parts = factor(waves[k].astype(F32))
        window_parts = transmission(blocks, tails, k)
        y = dot(c, rb[which])
        turned = signed(swapped(halves(y)[2]), False)
        g = times_conj(y, turned, window_parts).astype(BF16)
        late = (k, y, turned, wave_parts)
    leave(*late)
    return g


def detector(psi, observed, left, right, right_conj):
    def product(ah, al, bh, bl):
        return dot(ah, bh) + (dot(ah, bl) + dot(al, bh))

    near = left_product(left[0], psi, False) + left_product(left[1], psi, False)
    far = product(*split2(near), right[0], right[1])
    f0, f1, ft = halves(far)
    other = swapped(ft)
    main = f0 * f0 + f1 * f1 - observed[:, :LANES]
    tail = ft * ft + other * other - observed[:, LANES:]
    push = jnp.concatenate([main * f0, main * f1, tail * ft], axis=1)
    back = left_product(left[0], push.astype(BF16), True)
    return dot(back.astype(BF16), right_conj[...]).astype(BF16)


def read_indices(blocks, indices, count):
    for k in range(blocks.shape[0]):
        tag = jnp.max(blocks[k, -ROWS:, 2 * LANES :].astype(F32))
        indices[k] = jnp.clip(tag.astype(jnp.int32), 0, count - 1)


def place_in(size):
    rank = lax.axis_index("cuts")
    return lax.rem(rank, size), lax.div(rank, size)


def observe(blocks, near_rows, observed, first):
    for k in range(blocks.shape[0]):
        at = first + k * near_rows
        observed[at : at + near_rows, :] = blocks[k, -ROWS:, : 2 * LANES].astype(F32)[:near_rows]


def near_kernel(blocks, _, near, observed):
    observe(blocks, near.shape[0] // blocks.shape[0], observed, 0)
    near[...] = observed[...].astype(BF16)


def first_kernel(group_ref, probes, blocks, props, dft, leaving, waves, tails, lb, rf, rb, left, right, right_conj, indices, probe, sem):
    size = blocks.shape[0]
    slot, group = place_in(size)
    read_indices(blocks, indices, props.shape[0])

    @pl.when(group == 0)
    def _():
        position = 0
        for p, held in enumerate(slots_of(group_ref.shape[0], size)):
            position = jnp.where(slot == held, p, position)
        which = group_ref[position]
        copy = pltpu.make_async_copy(probes.at[which], probe, sem)
        copy.start()
        forward_tables(props, rf)
        copy.wait()
        waves[0] = packed(probe[0].astype(F32), probe[1].astype(F32)).astype(BF16)
        forward_steps(blocks, None, waves, indices, props, rf)
        leaving[...] = waves[size]

    @pl.when(group > 0)
    def _():
        spread_tails(blocks, tails)
        forward_tables(props, rf)
        backward_tables(props, lb, rb)
        detector_tables(dft, left, right, right_conj)


def forward_kernel(stage):
    def kernel(indices, entering, blocks, tails, props, rf, waves_in, leaving, waves, first_tails):
        size = blocks.shape[0]
        _, group = place_in(size)

        @pl.when(group == stage)
        def _():
            waves[0] = entering[...]
            forward_steps(blocks, tails, waves, indices, props, rf)
            leaving[...] = waves[size]

        @pl.when(group != stage)
        def _():
            waves[...] = waves_in[...]

        @pl.when(group == 0)
        def _():
            spread_tails(blocks, first_tails)

    return kernel


def middle_kernel(groups):
    def kernel(indices, waves, *refs):
        earlier, refs = refs[: groups - 1], refs[groups - 1 :]
        blocks, tails, props, lb, rb, left, right, right_conj, leaving, grads, lb_out, rb_out, observed = refs
        size = blocks.shape[0]
        _, group = place_in(size)

        @pl.when(group == groups - 1)
        def _():
            rows = earlier[0].shape[0]
            for n, near in enumerate(earlier):
                observed[n * rows : (n + 1) * rows, :] = near[...].astype(F32)
            observe(blocks, rows // size, observed, (groups - 1) * rows)
            g = detector(waves[size], observed[...], left, right, right_conj)
            leaving[...] = backward_steps(blocks, tails, waves, indices, lb, rb, grads, g)

        @pl.when(group < groups - 1)
        def _():
            backward_tables(props, lb_out, rb_out)

    return kernel


def backward_kernel(stage):
    def kernel(indices, arriving, waves, blocks, tails, lb, rb, grads_in, leaving, grads):
        _, group = place_in(blocks.shape[0])

        @pl.when(group == stage)
        def _():
            leaving[...] = backward_steps(blocks, tails, waves, indices, lb, rb, grads, arriving[...])

        @pl.when(group != stage)
        def _():
            grads[...] = grads_in[...]

    return kernel


def gather_kernel(offsets_ref, grads_ref, out_ref, planes, sems):
    positions = offsets_ref.shape[1]
    size, width, _ = grads_ref.shape
    extent = out_ref.shape[-1]
    _, group = place_in(size)
    flip = lax.rem(group, 2) * (size // 2)
    spread_out = []
    for p, slot in enumerate(slots_of(positions, size)):
        x0, x1, xt = halves(grads_ref[lax.bitwise_xor(slot, flip)])
        other = swapped(xt.astype(F32)).astype(BF16)
        both = jnp.concatenate(
            [jnp.concatenate([x0, xt], axis=1), jnp.concatenate([x1, other], axis=1)], axis=0
        )
        spread_out.append(dot(both, picker((2 * LANES, extent), offsets_ref[1, p])).astype(BF16))
    rows = jnp.concatenate(
        [row_picker((extent, width), -offsets_ref[0, p]) for p in range(positions)], axis=1
    )
    copies = []
    for c in range(2):
        here = slice(c * width, (c + 1) * width)
        planes[c] = dot(rows, jnp.concatenate([x[here] for x in spread_out], axis=0))
        copies.append(pltpu.make_async_copy(planes.at[c], out_ref.at[0, c], sems.at[c]))
        copies[-1].start()
    for copy in copies:
        copy.wait()


VMEM = pl.BlockSpec(memory_space=pltpu.VMEM)
SMEM = pl.BlockSpec(memory_space=pltpu.SMEM)
HBM = pl.BlockSpec(memory_space=pl.ANY)
ALONE = pltpu.CompilerParams(vmem_limit_bytes=60 * 1024 * 1024)
PARAMS = pltpu.CompilerParams(vmem_limit_bytes=20 * 1024 * 1024)


def shards(objects, propagators, prop_index, probes, probe_group, offsets, measured):
    sections = lax.axis_size("cuts")
    width = probes.shape[-1]
    kinds = propagators.shape[0]
    near_rows = measured.shape[1]
    size = GROUP
    groups = sections // size
    rows = width + ROWS
    slots = slots_of(probe_group.shape[0], size)
    members = [list(range(first, first + size)) for first in range(0, sections, size)]

    def struct(*dims, kind=BF16):
        return jax.ShapeDtypeStruct(dims, kind)

    def exchanged(blocks):
        return lax.all_to_all(blocks, "cuts", 0, 0, axis_index_groups=members, tiled=True)

    def handed(block, stage, distance):
        ends = (slots_in(at, len(slots), size) for at in (stage, stage + distance))
        route = [(stage * size + l, (stage + distance) * size + m) for l, m in zip(*ends)]
        return lax.ppermute(block, "cuts", route)

    blocks = pl.pallas_call(
        window_kernel,
        out_shape=struct(size, rows, 2 * width),
        in_specs=[HBM, SMEM, HBM, HBM],
        out_specs=HBM,
        scratch_shapes=[
            pltpu.VMEM((size, rows, 2 * width), BF16),
            pltpu.SMEM(offsets.shape[::-1], jnp.int32),
            pltpu.VMEM(objects.shape[1:], BF16),
            pltpu.VMEM(measured.shape, F32),
            pltpu.VMEM((len(slots), 2, objects.shape[-1], 2 * LANES), BF16),
            pltpu.SemaphoreType.DMA((4 + len(slots),)),
        ],
        compiler_params=ALONE,
        name="windows",
    )(offsets.T, prop_index, objects, measured)
    blocks = exchanged(blocks)

    wave = struct(width, 2 * width)
    near = struct(size * near_rows, 2 * LANES)
    waves_shape = struct(size + 1, width, 2 * width)
    grads_shape = struct(size, width, 2 * width)
    tails_shape = struct(size, width, 2 * LANES)
    left_table = struct(kinds, 2 * width, width)
    square_table = struct(kinds, 2 * width, 2 * width)
    detector_left = struct(2, 2 * width, width)
    detector_right = struct(2, 2 * width, 2 * width)

    def call(kernel, name, out_shape, in_specs, scratch_shapes, operands, slices=0):
        return pl.pallas_call(
            kernel,
            out_shape=out_shape,
            in_specs=in_specs,
            out_specs=[SMEM if x.dtype == jnp.int32 else VMEM for x in out_shape],
            scratch_shapes=scratch_shapes,
            compiler_params=PARAMS,
            cost_estimate=pl.CostEstimate(
                flops=16 * slices * width**3,
                bytes_accessed=sum(math.prod(x.shape) * x.dtype.itemsize for x in list(operands) + out_shape),
                transcendentals=0,
            ),
            name=name,
        )(*operands)

    leaving, waves, tails, lb, rf, rb, *dft, indices = call(
        first_kernel,
        "first_forward",
        [wave, waves_shape, tails_shape, left_table, square_table, square_table]
        + [detector_left, detector_right, struct(2 * width, 2 * width), struct(size, kind=jnp.int32)],
        [SMEM, HBM, VMEM, VMEM, VMEM],
        [pltpu.VMEM(probes.shape[1:], BF16), pltpu.SemaphoreType.DMA],
        (probe_group, probes, blocks, propagators, jnp.asarray(dft_constant(width))),
        size,
    )
    entering = handed(leaving, 0, 1)
    (near_out,) = call(near_kernel, "near_rows", [near], [VMEM, HBM], [pltpu.VMEM(near.shape, F32)], (blocks, leaving))
    nears = [handed(near_out, stage, groups - 1 - stage) for stage in range(groups - 1)]
    for stage in range(1, groups):
        leaving, waves, first_tails = call(
            forward_kernel(stage),
            "forward",
            [wave, waves_shape, tails_shape],
            [SMEM] + [VMEM] * 6,
            [],
            (indices, entering, blocks, tails, propagators, rf, waves),
            size,
        )
        if stage < groups - 1:
            entering = handed(leaving, stage, 1)

    leaving, grads, lb, rb = call(
        middle_kernel(groups),
        "middle",
        [wave, grads_shape, left_table, square_table],
        [SMEM] + [VMEM] * (groups + 8),
        [pltpu.VMEM((width, 2 * LANES), F32)],
        (indices, waves, *nears, blocks, tails, propagators, lb, rb, *dft),
        size,
    )

    for stage in range(groups - 2, -1, -1):
        arriving = handed(leaving, stage + 1, -1)
        leaving, grads = call(
            backward_kernel(stage),
            "backward",
            [wave, grads_shape],
            [SMEM] + [VMEM] * 7,
            [],
            (indices, arriving, waves, blocks, first_tails if stage == 0 else tails, lb, rb, grads),
            size,
        )

    return pl.pallas_call(
        gather_kernel,
        out_shape=jax.ShapeDtypeStruct(objects.shape, F32),
        in_specs=[SMEM, VMEM],
        out_specs=HBM,
        scratch_shapes=[pltpu.VMEM(objects.shape[1:], F32), pltpu.SemaphoreType.DMA((2,))],
        compiler_params=PARAMS,
        name="sum_windows",
    )(offsets.T, exchanged(grads))


def solution(mesh):
    in_specs = (
        P(("parts", "cuts"), None, None, None),
        P(),
        P(("parts", "cuts")),
        P(),
        P(),
        P("parts", None),
        P("parts", "cuts", None),
    )
    out_specs = P(("parts", "cuts"), None, None, None)
    return jax.shard_map(shards, mesh=mesh, in_specs=in_specs, out_specs=out_specs, check_vma=False)
```

```python
import math

import jax
import jax.numpy as jnp
import numpy as np
from jax import lax
from jax.experimental import pallas as pl
from jax.experimental.pallas import tpu as pltpu
from jax.sharding import PartitionSpec as P

TRANSMIT = 0.985
GROUP = 8
LANES = 128
ROWS = 16
F32 = jnp.float32
BF16 = jnp.bfloat16


def dot(former, latter):
    return jnp.dot(former, latter, preferred_element_type=F32)


def halves(x):
    return x[:, :LANES], x[:, LANES : 2 * LANES], x[:, 2 * LANES :]


def swapped(tail):
    return pltpu.roll(tail, LANES // 2, 1)


def low_half(rows):
    return lax.broadcasted_iota(jnp.int32, (rows, LANES), 1) < LANES // 2


def spread(tail):
    other = swapped(tail)
    low = low_half(tail.shape[0])
    return jnp.where(low, tail, other), jnp.where(low, other, tail)


def signed(tail, minus_low):
    low = low_half(tail.shape[0])
    return jnp.where(low == minus_low, -tail, tail)


def factor(b):
    b0, b1, bt = halves(b)
    return (b0, b1) + spread(bt)


def times(a, parts):
    a0, a1, at = halves(a)
    b0, b1, b_real, b_imag = parts
    tail = at * b_real + signed(swapped(at), True) * b_imag
    return jnp.concatenate([a0 * b0 - a1 * b1, a1 * b0 + a0 * b1, tail], axis=1)


def times_conj(a, turned, parts):
    a0, a1, at = halves(a)
    b0, b1, b_real, b_imag = parts
    tail = at * b_real + turned * b_imag
    return jnp.concatenate([a0 * b0 + a1 * b1, a1 * b0 - a0 * b1, tail], axis=1)


def left_product(table, x, conj):
    width = x.shape[0]
    both = dot(table, x)
    u0, u1, ut = halves(both[:width])
    v0, v1, vt = halves(both[width:])
    turned = signed(swapped(vt), not conj)
    if conj:
        return jnp.concatenate([u0 + v1, u1 - v0, ut + turned], axis=1)
    return jnp.concatenate([u0 - v1, u1 + v0, ut + turned], axis=1)


def spread_tails(blocks, tails):
    size, _, columns = blocks.shape
    for k in range(size):
        pair = spread(blocks[k, : columns // 2, 2 * LANES :].astype(F32))
        tails[k] = jnp.concatenate(pair, axis=1).astype(BF16)


def transmission(blocks, tails, k):
    window = blocks[k, : blocks.shape[2] // 2, :].astype(F32)
    b0, b1, bt = halves(window)
    if tails is None:
        b_real, b_imag = spread(bt)
    else:
        pair = tails[k].astype(F32)
        b_real, b_imag = pair[:, :LANES], pair[:, LANES:]
    return TRANSMIT + b0, b1, TRANSMIT + b_real, b_imag


def split2(x):
    high = x.astype(BF16)
    return high, (x - high.astype(F32)).astype(BF16)


def picker(shape, start, high_tail=False):
    columns, across = (0, 1) if shape[0] > shape[1] else (1, 0)
    half = LANES // 2
    taken = lax.broadcasted_iota(jnp.int32, shape, columns) - start
    place = lax.broadcasted_iota(jnp.int32, shape, across)
    if high_tail:
        wanted = jnp.where(place < LANES, place, jnp.where(place < LANES + half, -shape[columns], place - half))
    else:
        wanted = jnp.where(place < LANES + half, place, -shape[columns])
    return jnp.where(taken == wanted, 1.0, 0.0).astype(BF16)


def row_picker(shape, distance):
    taken = lax.broadcasted_iota(jnp.int32, shape, 1)
    wanted = lax.broadcasted_iota(jnp.int32, shape, 0) + distance
    return jnp.where(taken == wanted, 1.0, 0.0).astype(BF16)


def rows_near(x, start, count):
    limit = x.shape[0] - count
    bit = 1 << (limit.bit_length() - 1)
    while bit >= ROWS:
        length = count + bit
        short = bit + length - x.shape[0]
        if short > 0:
            x = jnp.concatenate([x, jnp.zeros((short, x.shape[1]), x.dtype)], axis=0)
        x = jnp.where(lax.bitwise_and(start, bit) != 0, x[bit : bit + length], x[:length])
        bit //= 2
    return x


def packed(real, imag):
    return jnp.concatenate([real[:, :LANES], imag[:, :LANES], real[:, LANES:], imag[:, LANES:]], axis=1)


def dft_constant(width):
    counter = np.arange(width)
    angle = (counter[:, None] * counter[None, :] % width) * (2.0 * math.pi / width)
    return (np.stack([np.cos(angle), -np.sin(angle)]) / math.sqrt(width)).astype(np.float32)


def slots_of(positions, size):
    half = size // 2
    order = list(range(half, size)) + list(range(0, half, 2)) + list(range(1, half, 2))
    return order[:positions]


def slots_in(group, positions, size):
    flip = (group % 2) * (size // 2)
    return [slot ^ flip for slot in slots_of(positions, size)]


def window_kernel(offsets_in, index_ref, objects_in, measured_in, blocks_out, blocks, offsets_ref, objects, measured, pickers, sems):
    positions, near_rows, width = measured.shape
    extent = objects.shape[-1]
    copies = [
        pltpu.make_async_copy(objects_in.at[0, 0], objects.at[0], sems.at[0]),
        pltpu.make_async_copy(objects_in.at[0, 1], objects.at[1], sems.at[1]),
        pltpu.make_async_copy(measured_in, measured, sems.at[2]),
        pltpu.make_async_copy(offsets_in, offsets_ref, sems.at[3]),
    ]
    for copy in reversed(copies):
        copy.start()
    tag = jnp.full((ROWS, LANES), index_ref[0], jnp.int32).astype(F32)
    size = blocks_out.shape[0]
    _, group = place_in(size)
    flip = lax.rem(group, 2) * (size // 2)
    copies.pop().wait()
    for p in range(positions):
        for c in range(2):
            pickers[p, c] = picker((extent, 2 * LANES), offsets_ref[1, p], c == 1)
    for copy in copies:
        copy.wait()
    sending = []
    for p, slot in enumerate(slots_of(positions, size)):
        start = offsets_ref[0, p]
        real, imag = (
            dot(rows_near(objects[c], start, width), pickers[p, c])
            for c in range(2)
        )
        tail = real[:, LANES:] + imag[:, LANES:]
        window = jnp.concatenate([real[:, :LANES], imag[:, :LANES], tail], axis=1).astype(BF16)
        shift = lax.bitwise_and(start, ROWS - 1)
        blocks[p, :width, :] = dot(row_picker((width, width + ROWS), shift), window).astype(BF16)
        tail = measured[p, :, LANES:]
        seen = jnp.concatenate([measured[p, :, :LANES], tail, tail, tag[:near_rows]], axis=1)
        left_over = jnp.concatenate([tag[near_rows:]] * 3, axis=1)
        blocks[p, width:, :] = jnp.concatenate([seen, left_over], axis=0).astype(BF16)
        target = blocks_out.at[lax.bitwise_xor(slot, flip)]
        sending.append(pltpu.make_async_copy(blocks.at[p], target, sems.at[4 + p]))
        sending[-1].start()
    for copy in sending:
        copy.wait()


def right_table(real, imag):
    upper, lower = packed(real, imag), packed(-imag, real)
    return jnp.concatenate([upper[:LANES], lower[:LANES], upper[LANES:], lower[LANES:]], axis=0).astype(BF16)


def forward_tables(props, rf):
    for k in range(props.shape[0]):
        rf[k] = right_table(props[k, 0].astype(F32).T, props[k, 1].astype(F32).T)


def backward_tables(props, lb, rb):
    width = props.shape[-1]
    for k in range(props.shape[0]):
        real, imag = props[k, 0].astype(F32), props[k, 1].astype(F32)
        lb[k, :width, :] = real.T.astype(BF16)
        lb[k, width:, :] = imag.T.astype(BF16)
        rb[k] = right_table(real, -imag)


def detector_tables(dft, left, right, right_conj):
    width = dft.shape[-1]
    for n, (real, imag) in enumerate(zip(split2(dft[0]), split2(dft[1]))):
        left[n, :width, :] = real
        left[n, width:, :] = imag
        real, imag = real.astype(F32), imag.astype(F32)
        right[n] = right_table(real, imag)
        if n == 0:
            right_conj[...] = right_table(real, -imag)


def forward_steps(blocks, tails, waves, indices, lf, rf):
    sections, _, columns = blocks.shape
    width = columns // 2
    psi = waves[0]
    parts = transmission(blocks, tails, 0)
    for k in range(sections):
        which = indices[k]
        z = times(psi.astype(F32), parts).astype(BF16)
        h = left_product(lf[which].reshape(columns, width), z, False).astype(BF16)
        if k + 1 < sections:
            parts = transmission(blocks, tails, k + 1)
        psi = dot(h, rf[which]).astype(BF16)
        waves[k + 1] = psi


def backward_steps(blocks, tails, waves, indices, lb, rb, grads, g):
    sections, _, columns = blocks.shape
    width = columns // 2

    def leave(k, y, turned, wave_parts):
        grads[k] = times_conj(y, turned, wave_parts).astype(BF16)

    late = None
    for k in reversed(range(sections)):
        which = indices[k]
        c = left_product(lb[which], g, True).astype(BF16)
        if late is not None:
            leave(*late)
        wave_parts = factor(waves[k].astype(F32))
        window_parts = transmission(blocks, tails, k)
        y = dot(c, rb[which])
        turned = signed(swapped(halves(y)[2]), False)
        g = times_conj(y, turned, window_parts).astype(BF16)
        late = (k, y, turned, wave_parts)
    leave(*late)
    return g


def detector(psi, observed, left, right, right_conj):
    def product(ah, al, bh, bl):
        return dot(ah, bh) + (dot(ah, bl) + dot(al, bh))

    near = left_product(left[0], psi, False) + left_product(left[1], psi, False)
    far = product(*split2(near), right[0], right[1])
    f0, f1, ft = halves(far)
    other = swapped(ft)
    main = f0 * f0 + f1 * f1 - observed[:, :LANES]
    tail = ft * ft + other * other - observed[:, LANES:]
    push = jnp.concatenate([main * f0, main * f1, tail * ft], axis=1)
    back = left_product(left[0], push.astype(BF16), True)
    return dot(back.astype(BF16), right_conj[...]).astype(BF16)


def read_indices(blocks, indices, count):
    for k in range(blocks.shape[0]):
        tag = jnp.max(blocks[k, -ROWS:, 2 * LANES :].astype(F32))
        indices[k] = jnp.clip(tag.astype(jnp.int32), 0, count - 1)


def place_in(size):
    rank = lax.axis_index("cuts")
    return lax.rem(rank, size), lax.div(rank, size)


def observe(blocks, near_rows, observed, first):
    for k in range(blocks.shape[0]):
        at = first + k * near_rows
        observed[at : at + near_rows, :] = blocks[k, -ROWS:, : 2 * LANES].astype(F32)[:near_rows]


def near_kernel(blocks, _, near, observed):
    observe(blocks, near.shape[0] // blocks.shape[0], observed, 0)
    near[...] = observed[...].astype(BF16)


def first_kernel(group_in, probes, blocks, props, dft, leaving, waves, tails, lb, rf, rb, left, right, right_conj, group_ref, indices, sem):
    size = blocks.shape[0]
    slot, group = place_in(size)

    @pl.when(group == 0)
    def _():
        copy = pltpu.make_async_copy(group_in, group_ref, sem)
        copy.start()
        forward_tables(props, rf)
        read_indices(blocks, indices, props.shape[0])
        copy.wait()
        position = 0
        for p, held in enumerate(slots_of(group_ref.shape[0], size)):
            position = jnp.where(slot == held, p, position)
        which = group_ref[position]
        waves[0] = packed(probes[which, 0].astype(F32), probes[which, 1].astype(F32)).astype(BF16)
        forward_steps(blocks, None, waves, indices, props, rf)
        leaving[...] = waves[size]

    @pl.when(group > 0)
    def _():
        spread_tails(blocks, tails)
        forward_tables(props, rf)
        backward_tables(props, lb, rb)
        detector_tables(dft, left, right, right_conj)


def forward_kernel(stage):
    def kernel(entering, blocks, tails, props, rf, waves_in, leaving, waves, first_tails, indices):
        size = blocks.shape[0]
        _, group = place_in(size)

        @pl.when(group == stage)
        def _():
            read_indices(blocks, indices, props.shape[0])
            waves[0] = entering[...]
            forward_steps(blocks, tails, waves, indices, props, rf)
            leaving[...] = waves[size]

        @pl.when(group != stage)
        def _():
            waves[...] = waves_in[...]

        @pl.when(group == 0)
        def _():
            spread_tails(blocks, first_tails)

    return kernel


def middle_kernel(groups):
    def kernel(waves, *refs):
        earlier, refs = refs[: groups - 1], refs[groups - 1 :]
        blocks, tails, props, lb, rb, left, right, right_conj, leaving, grads, lb_out, rb_out, observed, indices = refs
        size = blocks.shape[0]
        _, group = place_in(size)

        @pl.when(group == groups - 1)
        def _():
            read_indices(blocks, indices, props.shape[0])
            rows = earlier[0].shape[0]
            for n, near in enumerate(earlier):
                observed[n * rows : (n + 1) * rows, :] = near[...].astype(F32)
            observe(blocks, rows // size, observed, (groups - 1) * rows)
            g = detector(waves[size], observed[...], left, right, right_conj)
            leaving[...] = backward_steps(blocks, tails, waves, indices, lb, rb, grads, g)

        @pl.when(group < groups - 1)
        def _():
            backward_tables(props, lb_out, rb_out)

    return kernel


def backward_kernel(stage):
    def kernel(arriving, waves, blocks, tails, lb, rb, grads_in, leaving, grads, indices):
        _, group = place_in(blocks.shape[0])

        @pl.when(group == stage)
        def _():
            read_indices(blocks, indices, lb.shape[0])
            leaving[...] = backward_steps(blocks, tails, waves, indices, lb, rb, grads, arriving[...])

        @pl.when(group != stage)
        def _():
            grads[...] = grads_in[...]

    return kernel


def gather_kernel(offsets_ref, grads_ref, out_ref, planes, sems):
    positions = offsets_ref.shape[1]
    size, width, _ = grads_ref.shape
    extent = out_ref.shape[-1]
    _, group = place_in(size)
    flip = lax.rem(group, 2) * (size // 2)
    spread_out = []
    for p, slot in enumerate(slots_of(positions, size)):
        x0, x1, xt = halves(grads_ref[lax.bitwise_xor(slot, flip)])
        other = swapped(xt.astype(F32)).astype(BF16)
        both = jnp.concatenate(
            [jnp.concatenate([x0, xt], axis=1), jnp.concatenate([x1, other], axis=1)], axis=0
        )
        spread_out.append(dot(both, picker((2 * LANES, extent), offsets_ref[1:2, p : p + 1])).astype(BF16))
    rows = jnp.concatenate(
        [row_picker((extent, width), -offsets_ref[0:1, p : p + 1]) for p in range(positions)], axis=1
    )
    copies = []
    for c in range(2):
        here = slice(c * width, (c + 1) * width)
        planes[c] = dot(rows, jnp.concatenate([x[here] for x in spread_out], axis=0))
        copies.append(pltpu.make_async_copy(planes.at[c], out_ref.at[0, c], sems.at[c]))
        copies[-1].start()
    for copy in copies:
        copy.wait()


VMEM = pl.BlockSpec(memory_space=pltpu.VMEM)
SMEM = pl.BlockSpec(memory_space=pltpu.SMEM)
HBM = pl.BlockSpec(memory_space=pl.ANY)
ALONE = pltpu.CompilerParams(vmem_limit_bytes=60 * 1024 * 1024)
PARAMS = pltpu.CompilerParams(vmem_limit_bytes=20 * 1024 * 1024)


def shards(objects, propagators, prop_index, probes, probe_group, offsets, measured):
    sections = lax.axis_size("cuts")
    width = probes.shape[-1]
    kinds = propagators.shape[0]
    near_rows = measured.shape[1]
    size = GROUP
    groups = sections // size
    rows = width + ROWS
    slots = slots_of(probe_group.shape[0], size)
    members = [list(range(first, first + size)) for first in range(0, sections, size)]

    def struct(*dims, kind=BF16):
        return jax.ShapeDtypeStruct(dims, kind)

    def exchanged(blocks):
        return lax.all_to_all(blocks, "cuts", 0, 0, axis_index_groups=members, tiled=True)

    def handed(block, stage, distance):
        ends = (slots_in(at, len(slots), size) for at in (stage, stage + distance))
        route = [(stage * size + l, (stage + distance) * size + m) for l, m in zip(*ends)]
        return lax.ppermute(block, "cuts", route)

    blocks = pl.pallas_call(
        window_kernel,
        out_shape=struct(size, rows, 2 * width),
        in_specs=[HBM, SMEM, HBM, HBM],
        out_specs=HBM,
        scratch_shapes=[
            pltpu.VMEM((size, rows, 2 * width), BF16),
            pltpu.SMEM(offsets.shape[::-1], jnp.int32),
            pltpu.VMEM(objects.shape[1:], BF16),
            pltpu.VMEM(measured.shape, F32),
            pltpu.VMEM((len(slots), 2, objects.shape[-1], 2 * LANES), BF16),
            pltpu.SemaphoreType.DMA((4 + len(slots),)),
        ],
        compiler_params=ALONE,
        name="windows",
    )(offsets.T, prop_index, objects, measured)
    blocks = exchanged(blocks)

    wave = struct(width, 2 * width)
    near = struct(size * near_rows, 2 * LANES)
    waves_shape = struct(size + 1, width, 2 * width)
    grads_shape = struct(size, width, 2 * width)
    tails_shape = struct(size, width, 2 * LANES)
    left_table = struct(kinds, 2 * width, width)
    square_table = struct(kinds, 2 * width, 2 * width)
    detector_left = struct(2, 2 * width, width)
    detector_right = struct(2, 2 * width, 2 * width)
    indices = pltpu.SMEM((size,), jnp.int32)

    def call(kernel, name, out_shape, in_specs, scratch_shapes, operands, slices=0):
        return pl.pallas_call(
            kernel,
            out_shape=out_shape,
            in_specs=in_specs,
            out_specs=[VMEM] * len(out_shape),
            scratch_shapes=scratch_shapes,
            compiler_params=PARAMS,
            cost_estimate=pl.CostEstimate(
                flops=16 * slices * width**3,
                bytes_accessed=sum(math.prod(x.shape) * x.dtype.itemsize for x in list(operands) + out_shape),
                transcendentals=0,
            ),
            name=name,
        )(*operands)

    leaving, waves, tails, lb, rf, rb, *dft = call(
        first_kernel,
        "first_forward",
        [wave, waves_shape, tails_shape, left_table, square_table, square_table]
        + [detector_left, detector_right, struct(2 * width, 2 * width)],
        [HBM, VMEM, VMEM, VMEM, VMEM],
        [pltpu.SMEM(probe_group.shape, jnp.int32), indices, pltpu.SemaphoreType.DMA],
        (probe_group, probes, blocks, propagators, jnp.asarray(dft_constant(width))),
        size,
    )
    entering = handed(leaving, 0, 1)
    (near_out,) = call(near_kernel, "near_rows", [near], [VMEM, HBM], [pltpu.VMEM(near.shape, F32)], (blocks, leaving))
    nears = [handed(near_out, stage, groups - 1 - stage) for stage in range(groups - 1)]
    for stage in range(1, groups):
        leaving, waves, first_tails = call(
            forward_kernel(stage),
            "forward",
            [wave, waves_shape, tails_shape],
            [VMEM] * 6,
            [indices],
            (entering, blocks, tails, propagators, rf, waves),
            size,
        )
        if stage < groups - 1:
            entering = handed(leaving, stage, 1)

    leaving, grads, lb, rb = call(
        middle_kernel(groups),
        "middle",
        [wave, grads_shape, left_table, square_table],
        [VMEM] * (groups + 8),
        [pltpu.VMEM((width, 2 * LANES), F32), indices],
        (waves, *nears, blocks, tails, propagators, lb, rb, *dft),
        size,
    )

    for stage in range(groups - 2, -1, -1):
        arriving = handed(leaving, stage + 1, -1)
        leaving, grads = call(
            backward_kernel(stage),
            "backward",
            [wave, grads_shape],
            [VMEM] * 7,
            [indices],
            (arriving, waves, blocks, first_tails if stage == 0 else tails, lb, rb, grads),
            size,
        )

    return pl.pallas_call(
        gather_kernel,
        out_shape=jax.ShapeDtypeStruct(objects.shape, F32),
        in_specs=[VMEM, VMEM],
        out_specs=HBM,
        scratch_shapes=[pltpu.VMEM(objects.shape[1:], F32), pltpu.SemaphoreType.DMA((2,))],
        compiler_params=PARAMS,
        name="sum_windows",
    )(offsets.T, exchanged(grads))


def solution(mesh):
    in_specs = (
        P(("parts", "cuts"), None, None, None),
        P(),
        P(("parts", "cuts")),
        P(),
        P(),
        P("parts", None),
        P("parts", "cuts", None),
    )
    out_specs = P(("parts", "cuts"), None, None, None)
    return jax.shard_map(shards, mesh=mesh, in_specs=in_specs, out_specs=out_specs, check_vma=False)
```

```python
import math

import jax
import jax.numpy as jnp
import numpy as np
from jax import lax
from jax.experimental import pallas as pl
from jax.experimental.pallas import tpu as pltpu
from jax.sharding import PartitionSpec as P

TRANSMIT = 0.985
GROUP = 8
LANES = 128
ROWS = 16
F32 = jnp.float32
BF16 = jnp.bfloat16


def dot(former, latter):
    return jnp.dot(former, latter, preferred_element_type=F32)


def halves(x):
    return x[:, :LANES], x[:, LANES : 2 * LANES], x[:, 2 * LANES :]


def swapped(tail):
    return pltpu.roll(tail, LANES // 2, 1)


def low_half(rows):
    return lax.broadcasted_iota(jnp.int32, (rows, LANES), 1) < LANES // 2


def spread(tail):
    other = swapped(tail)
    low = low_half(tail.shape[0])
    return jnp.where(low, tail, other), jnp.where(low, other, tail)


def signed(tail, minus_low):
    low = low_half(tail.shape[0])
    return jnp.where(low == minus_low, -tail, tail)


def factor(b):
    b0, b1, bt = halves(b)
    return (b0, b1) + spread(bt)


def times(a, parts):
    a0, a1, at = halves(a)
    b0, b1, b_real, b_imag = parts
    tail = at * b_real + signed(swapped(at), True) * b_imag
    return jnp.concatenate([a0 * b0 - a1 * b1, a1 * b0 + a0 * b1, tail], axis=1)


def times_conj(a, turned, parts):
    a0, a1, at = halves(a)
    b0, b1, b_real, b_imag = parts
    tail = at * b_real + turned * b_imag
    return jnp.concatenate([a0 * b0 + a1 * b1, a1 * b0 - a0 * b1, tail], axis=1)


def left_product(table, x, conj):
    width = x.shape[0]
    both = dot(table, x)
    u0, u1, ut = halves(both[:width])
    v0, v1, vt = halves(both[width:])
    turned = signed(swapped(vt), not conj)
    if conj:
        return jnp.concatenate([u0 + v1, u1 - v0, ut + turned], axis=1)
    return jnp.concatenate([u0 - v1, u1 + v0, ut + turned], axis=1)


def spread_tails(blocks, tails):
    size, _, columns = blocks.shape
    for k in range(size):
        pair = spread(blocks[k, : columns // 2, 2 * LANES :].astype(F32))
        tails[k] = jnp.concatenate(pair, axis=1).astype(BF16)


def transmission(blocks, tails, k):
    window = blocks[k, : blocks.shape[2] // 2, :].astype(F32)
    b0, b1, bt = halves(window)
    if tails is None:
        b_real, b_imag = spread(bt)
    else:
        pair = tails[k].astype(F32)
        b_real, b_imag = pair[:, :LANES], pair[:, LANES:]
    return TRANSMIT + b0, b1, TRANSMIT + b_real, b_imag


def split2(x):
    high = x.astype(BF16)
    return high, (x - high.astype(F32)).astype(BF16)


def picker(shape, start, high_tail=False):
    columns, across = (0, 1) if shape[0] > shape[1] else (1, 0)
    half = LANES // 2
    taken = lax.broadcasted_iota(jnp.int32, shape, columns) - start
    place = lax.broadcasted_iota(jnp.int32, shape, across)
    if high_tail:
        wanted = jnp.where(place < LANES, place, jnp.where(place < LANES + half, -shape[columns], place - half))
    else:
        wanted = jnp.where(place < LANES + half, place, -shape[columns])
    return jnp.where(taken == wanted, 1.0, 0.0).astype(BF16)


def row_picker(shape, distance):
    taken = lax.broadcasted_iota(jnp.int32, shape, 1)
    wanted = lax.broadcasted_iota(jnp.int32, shape, 0) + distance
    return jnp.where(taken == wanted, 1.0, 0.0).astype(BF16)


def rows_near(x, start, count):
    limit = x.shape[0] - count
    bit = 1 << (limit.bit_length() - 1)
    while bit >= ROWS:
        length = count + bit
        short = bit + length - x.shape[0]
        if short > 0:
            x = jnp.concatenate([x, jnp.zeros((short, x.shape[1]), x.dtype)], axis=0)
        x = jnp.where(lax.bitwise_and(start, bit) != 0, x[bit : bit + length], x[:length])
        bit //= 2
    return x


def packed(real, imag):
    return jnp.concatenate([real[:, :LANES], imag[:, :LANES], real[:, LANES:], imag[:, LANES:]], axis=1)


def dft_constant(width):
    counter = np.arange(width)
    angle = (counter[:, None] * counter[None, :] % width) * (2.0 * math.pi / width)
    return (np.stack([np.cos(angle), -np.sin(angle)]) / math.sqrt(width)).astype(np.float32)


def slots_of(positions, size):
    half = size // 2
    order = list(range(half, size)) + list(range(0, half, 2)) + list(range(1, half, 2))
    return order[:positions]


def slots_in(group, positions, size):
    flip = (group % 2) * (size // 2)
    return [slot ^ flip for slot in slots_of(positions, size)]


def window_kernel(offsets_in, index_in, objects_in, measured_in, blocks_out, blocks, index_ref, offsets_ref, objects, measured, pickers, sems):
    positions, near_rows, width = measured.shape
    extent = objects.shape[-1]
    copies = [
        pltpu.make_async_copy(objects_in.at[0, 0], objects.at[0], sems.at[0]),
        pltpu.make_async_copy(objects_in.at[0, 1], objects.at[1], sems.at[1]),
        pltpu.make_async_copy(measured_in, measured, sems.at[2]),
        pltpu.make_async_copy(index_in, index_ref, sems.at[4 + positions]),
        pltpu.make_async_copy(offsets_in, offsets_ref, sems.at[3]),
    ]
    for copy in reversed(copies):
        copy.start()
    size = blocks_out.shape[0]
    _, group = place_in(size)
    flip = lax.rem(group, 2) * (size // 2)
    copies.pop().wait()
    for p in range(positions):
        for c in range(2):
            pickers[p, c] = picker((extent, 2 * LANES), offsets_ref[1, p], c == 1)
    for copy in copies:
        copy.wait()
    tag = jnp.full((ROWS, LANES), index_ref[0], jnp.int32).astype(F32)
    sending = []
    for p, slot in enumerate(slots_of(positions, size)):
        start = offsets_ref[0, p]
        real, imag = (
            dot(rows_near(objects[c], start, width), pickers[p, c])
            for c in range(2)
        )
        tail = real[:, LANES:] + imag[:, LANES:]
        window = jnp.concatenate([real[:, :LANES], imag[:, :LANES], tail], axis=1).astype(BF16)
        shift = lax.bitwise_and(start, ROWS - 1)
        blocks[p, :width, :] = dot(row_picker((width, width + ROWS), shift), window).astype(BF16)
        tail = measured[p, :, LANES:]
        seen = jnp.concatenate([measured[p, :, :LANES], tail, tail, tag[:near_rows]], axis=1)
        left_over = jnp.concatenate([tag[near_rows:]] * 3, axis=1)
        blocks[p, width:, :] = jnp.concatenate([seen, left_over], axis=0).astype(BF16)
        target = blocks_out.at[lax.bitwise_xor(slot, flip)]
        sending.append(pltpu.make_async_copy(blocks.at[p], target, sems.at[4 + p]))
        sending[-1].start()
    for copy in sending:
        copy.wait()


def right_table(real, imag):
    upper, lower = packed(real, imag), packed(-imag, real)
    return jnp.concatenate([upper[:LANES], lower[:LANES], upper[LANES:], lower[LANES:]], axis=0).astype(BF16)


def forward_tables(props, rf):
    for k in range(props.shape[0]):
        rf[k] = right_table(props[k, 0].astype(F32).T, props[k, 1].astype(F32).T)


def backward_tables(props, lb, rb):
    width = props.shape[-1]
    for k in range(props.shape[0]):
        real, imag = props[k, 0].astype(F32), props[k, 1].astype(F32)
        lb[k, :width, :] = real.T.astype(BF16)
        lb[k, width:, :] = imag.T.astype(BF16)
        rb[k] = right_table(real, -imag)


def detector_tables(dft, left, right, right_conj):
    width = dft.shape[-1]
    for n, (real, imag) in enumerate(zip(split2(dft[0]), split2(dft[1]))):
        left[n, :width, :] = real
        left[n, width:, :] = imag
        real, imag = real.astype(F32), imag.astype(F32)
        right[n] = right_table(real, imag)
        if n == 0:
            right_conj[...] = right_table(real, -imag)


def forward_steps(blocks, tails, waves, indices, lf, rf):
    sections, _, columns = blocks.shape
    width = columns // 2
    psi = waves[0]
    parts = transmission(blocks, tails, 0)
    for k in range(sections):
        which = indices[k]
        z = times(psi.astype(F32), parts).astype(BF16)
        h = left_product(lf[which].reshape(columns, width), z, False).astype(BF16)
        if k + 1 < sections:
            parts = transmission(blocks, tails, k + 1)
        psi = dot(h, rf[which]).astype(BF16)
        waves[k + 1] = psi


def backward_steps(blocks, tails, waves, indices, lb, rb, grads, g):
    sections, _, columns = blocks.shape
    width = columns // 2

    def leave(k, y, turned, wave_parts):
        grads[k] = times_conj(y, turned, wave_parts).astype(BF16)

    late = None
    for k in reversed(range(sections)):
        which = indices[k]
        c = left_product(lb[which], g, True).astype(BF16)
        if late is not None:
            leave(*late)
        wave_parts = factor(waves[k].astype(F32))
        window_parts = transmission(blocks, tails, k)
        y = dot(c, rb[which])
        turned = signed(swapped(halves(y)[2]), False)
        g = times_conj(y, turned, window_parts).astype(BF16)
        late = (k, y, turned, wave_parts)
    leave(*late)
    return g


def detector(psi, observed, left, right, right_conj):
    def product(ah, al, bh, bl):
        return dot(ah, bh) + (dot(ah, bl) + dot(al, bh))

    near = left_product(left[0], psi, False) + left_product(left[1], psi, False)
    far = product(*split2(near), right[0], right[1])
    f0, f1, ft = halves(far)
    other = swapped(ft)
    main = f0 * f0 + f1 * f1 - observed[:, :LANES]
    tail = ft * ft + other * other - observed[:, LANES:]
    push = jnp.concatenate([main * f0, main * f1, tail * ft], axis=1)
    back = left_product(left[0], push.astype(BF16), True)
    return dot(back.astype(BF16), right_conj[...]).astype(BF16)


def read_indices(blocks, indices, count):
    for k in range(blocks.shape[0]):
        tag = jnp.max(blocks[k, -ROWS:, 2 * LANES :].astype(F32))
        indices[k] = jnp.clip(tag.astype(jnp.int32), 0, count - 1)


def place_in(size):
    rank = lax.axis_index("cuts")
    return lax.rem(rank, size), lax.div(rank, size)


def observe(blocks, near_rows, observed, first):
    for k in range(blocks.shape[0]):
        at = first + k * near_rows
        observed[at : at + near_rows, :] = blocks[k, -ROWS:, : 2 * LANES].astype(F32)[:near_rows]


def near_kernel(blocks, _, near, observed):
    observe(blocks, near.shape[0] // blocks.shape[0], observed, 0)
    near[...] = observed[...].astype(BF16)


def first_kernel(group_in, probes, blocks, props, dft, leaving, waves, tails, lb, rf, rb, left, right, right_conj, group_ref, indices, sem):
    size = blocks.shape[0]
    slot, group = place_in(size)

    @pl.when(group == 0)
    def _():
        copy = pltpu.make_async_copy(group_in, group_ref, sem)
        copy.start()
        forward_tables(props, rf)
        read_indices(blocks, indices, props.shape[0])
        copy.wait()
        position = 0
        for p, held in enumerate(slots_of(group_ref.shape[0], size)):
            position = jnp.where(slot == held, p, position)
        which = group_ref[position]
        waves[0] = packed(probes[which, 0].astype(F32), probes[which, 1].astype(F32)).astype(BF16)
        forward_steps(blocks, None, waves, indices, props, rf)
        leaving[...] = waves[size]

    @pl.when(group > 0)
    def _():
        spread_tails(blocks, tails)
        forward_tables(props, rf)
        backward_tables(props, lb, rb)
        detector_tables(dft, left, right, right_conj)


def forward_kernel(stage):
    def kernel(entering, blocks, tails, props, rf, waves_in, leaving, waves, first_tails, indices):
        size = blocks.shape[0]
        _, group = place_in(size)

        @pl.when(group == stage)
        def _():
            read_indices(blocks, indices, props.shape[0])
            waves[0] = entering[...]
            forward_steps(blocks, tails, waves, indices, props, rf)
            leaving[...] = waves[size]

        @pl.when(group != stage)
        def _():
            waves[...] = waves_in[...]

        @pl.when(group == 0)
        def _():
            spread_tails(blocks, first_tails)

    return kernel


def middle_kernel(groups):
    def kernel(waves, *refs):
        earlier, refs = refs[: groups - 1], refs[groups - 1 :]
        blocks, tails, props, lb, rb, left, right, right_conj, leaving, grads, lb_out, rb_out, observed, indices = refs
        size = blocks.shape[0]
        _, group = place_in(size)

        @pl.when(group == groups - 1)
        def _():
            read_indices(blocks, indices, props.shape[0])
            rows = earlier[0].shape[0]
            for n, near in enumerate(earlier):
                observed[n * rows : (n + 1) * rows, :] = near[...].astype(F32)
            observe(blocks, rows // size, observed, (groups - 1) * rows)
            g = detector(waves[size], observed[...], left, right, right_conj)
            leaving[...] = backward_steps(blocks, tails, waves, indices, lb, rb, grads, g)

        @pl.when(group < groups - 1)
        def _():
            backward_tables(props, lb_out, rb_out)

    return kernel


def backward_kernel(stage):
    def kernel(arriving, waves, blocks, tails, lb, rb, grads_in, leaving, grads, indices):
        _, group = place_in(blocks.shape[0])

        @pl.when(group == stage)
        def _():
            read_indices(blocks, indices, lb.shape[0])
            leaving[...] = backward_steps(blocks, tails, waves, indices, lb, rb, grads, arriving[...])

        @pl.when(group != stage)
        def _():
            grads[...] = grads_in[...]

    return kernel


def gather_kernel(offsets_ref, grads_ref, out_ref, planes, sems):
    positions = offsets_ref.shape[1]
    size, width, _ = grads_ref.shape
    extent = out_ref.shape[-1]
    _, group = place_in(size)
    flip = lax.rem(group, 2) * (size // 2)
    spread_out = []
    for p, slot in enumerate(slots_of(positions, size)):
        x0, x1, xt = halves(grads_ref[lax.bitwise_xor(slot, flip)])
        other = swapped(xt.astype(F32)).astype(BF16)
        both = jnp.concatenate(
            [jnp.concatenate([x0, xt], axis=1), jnp.concatenate([x1, other], axis=1)], axis=0
        )
        spread_out.append(dot(both, picker((2 * LANES, extent), offsets_ref[1:2, p : p + 1])).astype(BF16))
    rows = jnp.concatenate(
        [row_picker((extent, width), -offsets_ref[0:1, p : p + 1]) for p in range(positions)], axis=1
    )
    copies = []
    for c in range(2):
        here = slice(c * width, (c + 1) * width)
        planes[c] = dot(rows, jnp.concatenate([x[here] for x in spread_out], axis=0))
        copies.append(pltpu.make_async_copy(planes.at[c], out_ref.at[0, c], sems.at[c]))
        copies[-1].start()
    for copy in copies:
        copy.wait()


VMEM = pl.BlockSpec(memory_space=pltpu.VMEM)
SMEM = pl.BlockSpec(memory_space=pltpu.SMEM)
HBM = pl.BlockSpec(memory_space=pl.ANY)
ALONE = pltpu.CompilerParams(vmem_limit_bytes=60 * 1024 * 1024)
PARAMS = pltpu.CompilerParams(vmem_limit_bytes=20 * 1024 * 1024)


def shards(objects, propagators, prop_index, probes, probe_group, offsets, measured):
    sections = lax.axis_size("cuts")
    width = probes.shape[-1]
    kinds = propagators.shape[0]
    near_rows = measured.shape[1]
    size = GROUP
    groups = sections // size
    rows = width + ROWS
    slots = slots_of(probe_group.shape[0], size)
    members = [list(range(first, first + size)) for first in range(0, sections, size)]

    def struct(*dims, kind=BF16):
        return jax.ShapeDtypeStruct(dims, kind)

    def exchanged(blocks):
        return lax.all_to_all(blocks, "cuts", 0, 0, axis_index_groups=members, tiled=True)

    def handed(block, stage, distance):
        ends = (slots_in(at, len(slots), size) for at in (stage, stage + distance))
        route = [(stage * size + l, (stage + distance) * size + m) for l, m in zip(*ends)]
        return lax.ppermute(block, "cuts", route)

    blocks = pl.pallas_call(
        window_kernel,
        out_shape=struct(size, rows, 2 * width),
        in_specs=[HBM, HBM, HBM, HBM],
        out_specs=HBM,
        scratch_shapes=[
            pltpu.VMEM((size, rows, 2 * width), BF16),
            pltpu.SMEM(prop_index.shape, jnp.int32),
            pltpu.SMEM(offsets.shape[::-1], jnp.int32),
            pltpu.VMEM(objects.shape[1:], BF16),
            pltpu.VMEM(measured.shape, F32),
            pltpu.VMEM((len(slots), 2, objects.shape[-1], 2 * LANES), BF16),
            pltpu.SemaphoreType.DMA((5 + len(slots),)),
        ],
        compiler_params=ALONE,
        name="windows",
    )(offsets.T, prop_index, objects, measured)
    blocks = exchanged(blocks)

    wave = struct(width, 2 * width)
    near = struct(size * near_rows, 2 * LANES)
    waves_shape = struct(size + 1, width, 2 * width)
    grads_shape = struct(size, width, 2 * width)
    tails_shape = struct(size, width, 2 * LANES)
    left_table = struct(kinds, 2 * width, width)
    square_table = struct(kinds, 2 * width, 2 * width)
    detector_left = struct(2, 2 * width, width)
    detector_right = struct(2, 2 * width, 2 * width)
    indices = pltpu.SMEM((size,), jnp.int32)

    def call(kernel, name, out_shape, in_specs, scratch_shapes, operands, slices=0):
        return pl.pallas_call(
            kernel,
            out_shape=out_shape,
            in_specs=in_specs,
            out_specs=[VMEM] * len(out_shape),
            scratch_shapes=scratch_shapes,
            compiler_params=PARAMS,
            cost_estimate=pl.CostEstimate(
                flops=16 * slices * width**3,
                bytes_accessed=sum(math.prod(x.shape) * x.dtype.itemsize for x in list(operands) + out_shape),
                transcendentals=0,
            ),
            name=name,
        )(*operands)

    leaving, waves, tails, lb, rf, rb, *dft = call(
        first_kernel,
        "first_forward",
        [wave, waves_shape, tails_shape, left_table, square_table, square_table]
        + [detector_left, detector_right, struct(2 * width, 2 * width)],
        [HBM, VMEM, VMEM, VMEM, VMEM],
        [pltpu.SMEM(probe_group.shape, jnp.int32), indices, pltpu.SemaphoreType.DMA],
        (probe_group, probes, blocks, propagators, jnp.asarray(dft_constant(width))),
        size,
    )
    entering = handed(leaving, 0, 1)
    (near_out,) = call(near_kernel, "near_rows", [near], [VMEM, HBM], [pltpu.VMEM(near.shape, F32)], (blocks, leaving))
    nears = [handed(near_out, stage, groups - 1 - stage) for stage in range(groups - 1)]
    for stage in range(1, groups):
        leaving, waves, first_tails = call(
            forward_kernel(stage),
            "forward",
            [wave, waves_shape, tails_shape],
            [VMEM] * 6,
            [indices],
            (entering, blocks, tails, propagators, rf, waves),
            size,
        )
        if stage < groups - 1:
            entering = handed(leaving, stage, 1)

    leaving, grads, lb, rb = call(
        middle_kernel(groups),
        "middle",
        [wave, grads_shape, left_table, square_table],
        [VMEM] * (groups + 8),
        [pltpu.VMEM((width, 2 * LANES), F32), indices],
        (waves, *nears, blocks, tails, propagators, lb, rb, *dft),
        size,
    )

    for stage in range(groups - 2, -1, -1):
        arriving = handed(leaving, stage + 1, -1)
        leaving, grads = call(
            backward_kernel(stage),
            "backward",
            [wave, grads_shape],
            [VMEM] * 7,
            [indices],
            (arriving, waves, blocks, first_tails if stage == 0 else tails, lb, rb, grads),
            size,
        )

    return pl.pallas_call(
        gather_kernel,
        out_shape=jax.ShapeDtypeStruct(objects.shape, F32),
        in_specs=[VMEM, VMEM],
        out_specs=HBM,
        scratch_shapes=[pltpu.VMEM(objects.shape[1:], F32), pltpu.SemaphoreType.DMA((2,))],
        compiler_params=PARAMS,
        name="sum_windows",
    )(offsets.T, exchanged(grads))


def solution(mesh):
    in_specs = (
        P(("parts", "cuts"), None, None, None),
        P(),
        P(("parts", "cuts")),
        P(),
        P(),
        P("parts", None),
        P("parts", "cuts", None),
    )
    out_specs = P(("parts", "cuts"), None, None, None)
    return jax.shard_map(shards, mesh=mesh, in_specs=in_specs, out_specs=out_specs, check_vma=False)
```
